32 devices in a mesh: pair: 2 (over core), group: 2 (over x), rep: 8 (over z, y).
Axes of the slice: x: 2, y: 2, z: 4, core: 2. Of those that a mesh axis runs over, the one named last changes fastest.
Arguments:
- states: float32 [2, 2048, 4, 84, 84], P('pair', ('group', 'rep')), may hold values from 0 to 1
- actions: int32 [2, 2048], P('pair', ('group', 'rep')), may hold values from 0 to 17
- proj_lower: int32 [2048, 51], P(('group', 'rep')), may hold values from 0 to 49, as said below
- proj_upper: int32 [2048, 51], P(('group', 'rep')), may hold values from 1 to 50, as said below
- proj_weight: float32 [2048, 51], P(('group', 'rep')), may hold values from 0 to 1
- first_kernel: float32 [2, 32, 4, 8, 8], P('pair'), may hold values from -0.375 to 0.375
- first_bias: float32 [2, 32], P('pair'), may hold values from -3 to 3
- second_kernel: float32 [2, 64, 32, 4, 4], P('pair'), may hold values from -0.25 to 0.25
- second_bias: float32 [2, 64], P('pair'), may hold values from -3 to 3
- third_kernel: float32 [2, 64, 64, 3, 3], P('pair'), may hold values from -0.25 to 0.25
- third_bias: float32 [2, 64], P('pair'), may hold values from -3 to 3
- hidden_mean: float32 [2, 2, 3136, 512], P('pair'), may hold values from -0.109375 to 0.109375
- hidden_sigma: float32 [2, 2, 3136, 512], P('pair'), may hold values from -0.109375 to 0.109375
- hidden_bias_mean: float32 [2, 2, 512], P('pair'), may hold values from -3 to 3
- hidden_bias_sigma: float32 [2, 2, 512], P('pair'), may hold values from -3 to 3
- head_mean: float32 [2, 512, 969], P('pair'), may hold values from -0.25 to 0.25
- head_sigma: float32 [2, 512, 969], P('pair'), may hold values from -0.25 to 0.25
- head_bias_mean: float32 [2, 969], P('pair'), may hold values from -3 to 3
- head_bias_sigma: float32 [2, 969], P('pair'), may hold values from -3 to 3
- hidden_noise_in: float32 [2, 2, 3136], P('pair'), may hold values from -4 to 4
- hidden_noise_out: float32 [2, 2, 512], P('pair'), may hold values from -4 to 4
- head_noise_in: float32 [2, 2, 512], P('pair'), may hold values from -4 to 4
- head_noise_out: float32 [2, 969], P('pair'), may hold values from -4 to 4
Outputs:
- loss_value: float32 [], replicated
- states_grad: float32 [2048, 4, 84, 84], P(('group', 'rep'), 'pair')
- first_kernel_grad: float32 [32, 4, 8, 8], replicated
- first_bias_grad: float32 [32], replicated
- second_kernel_grad: float32 [64, 32, 4, 4], replicated
- second_bias_grad: float32 [64], replicated
- third_kernel_grad: float32 [64, 64, 3, 3], replicated
- third_bias_grad: float32 [64], replicated
- hidden_mean_grad: float32 [2, 3136, 512], P(None, ('pair', 'group'))
- hidden_sigma_grad: float32 [2, 3136, 512], P(None, ('pair', 'group'))
- hidden_bias_mean_grad: float32 [2, 512], replicated
- hidden_bias_sigma_grad: float32 [2, 512], replicated
- head_mean_grad: float32 [512, 969], P(('pair', 'group'))
- head_sigma_grad: float32 [512, 969], P(('pair', 'group'))
- head_bias_mean_grad: float32 [969], replicated
- head_bias_sigma_grad: float32 [969], replicated
The draws below stay inside these ranges and needn't reach their ends.
Inputs may be any that keep to these rules, and one draw needn't show every extreme that they name: proj_lower does not fall along the atoms of a transition. proj_upper = proj_lower + 1.
All inputs are finite; a program needn't handle non-finite values.
Results may differ from the reference program's by a relative error of at most 0.0003.
Values sent between devices are 32-bit elements; how exact they have to be, the bound alone decides.
A program may use at most 256 MiB of HBM per device.

```python
import jax
import jax.numpy as jnp
from jax import lax

FRAMES = 4
SIDE = 84
C1 = 32
C2 = 64
C3 = 64
HIDDEN_SIZE = 512
ATOMS = 51
ACTIONS = 18
B_DEV = 128
TOTAL = 2048
FEAT = 3136
OUTS = 969


def atom_lower(key):
    shift_vals = jax.random.randint(key, (TOTAL,), -(ATOMS // 5), ATOMS // 5 + 1)
    shift_vals = shift_vals.at[0].set(ATOMS // 5).at[1].set(-(ATOMS // 5))
    atom_index = jnp.arange(ATOMS)
    lower_idx = jnp.clip(shift_vals[:, None] + 97 * atom_index[None, :] // 100, 0, ATOMS - 2)
    return lower_idx.astype(jnp.int32)


def draw_proj_lower(key, part):
    return atom_lower(key)


def draw_proj_upper(key, part):
    return (atom_lower(key) + 1).astype(jnp.int32)


def set_ends(entries, stream_key, least, largest):
    index_at = [jax.random.randint(jax.random.fold_in(stream_key, axis), (), 0, length) for axis, length in enumerate(entries.shape)]
    main_axis = entries.shape.index(max(entries.shape))
    neighbour = index_at[:main_axis] + [(index_at[main_axis] + 1) % entries.shape[main_axis]] + index_at[main_axis + 1:]
    return entries.at[tuple(index_at)].set(least).at[tuple(neighbour)].set(largest)


def steps_of(own_key, extent, cuts, smallest, high):
    gain, own = 1.0, jax.random.fold_in(own_key, 6)
    for axis_at, parts in cuts:
        steps = jnp.exp(jax.random.uniform(jax.random.fold_in(own, axis_at), (parts,), jnp.float32, smallest / len(cuts), high / len(cuts)))
        gain = gain * jnp.repeat(steps, extent[axis_at] // parts).reshape([-1 if axis == axis_at else 1 for axis in range(len(extent))])
    return gain


def normal_values(rng, dims, width, limit, cuts=(), kind=jnp.bfloat16):
    factor_of = steps_of(rng, dims, cuts, -0.22, 0.18) if cuts else 1.0
    array = jax.random.normal(rng, dims, jnp.float32) * width * factor_of
    return jnp.minimum(jnp.maximum(array, -limit), limit).astype(kind)


def setup_inputs(seed: int = 0) -> dict:
    streams_of = jax.random.split(jax.random.key(seed), 24)
    states = jnp.clip(1.0 * jax.random.uniform(streams_of[0], (2, TOTAL, FRAMES, SIDE, SIDE), jnp.float32) ** steps_of(streams_of[0], (2, TOTAL, FRAMES, SIDE, SIDE), ((0, 2), (1, 16)), -0.2, 0.2), 0.0, 1.0)
    actions = set_ends(jax.random.randint(streams_of[1], (2, TOTAL), 0, ACTIONS), jax.random.fold_in(streams_of[1], 1), 0, ACTIONS - 1).astype(jnp.int32)
    proj_lower = draw_proj_lower(jax.random.fold_in(streams_of[23], 71), 0)
    proj_upper = draw_proj_upper(jax.random.fold_in(streams_of[23], 71), 0)
    proj_weight = jnp.clip(1.0 * jax.random.uniform(streams_of[4], (TOTAL, ATOMS), jnp.float32) ** steps_of(streams_of[4], (TOTAL, ATOMS), ((0, 16),), -0.2, 0.2), 0.0, 1.0)
    first_kernel = normal_values(streams_of[5], (2, C1, FRAMES, 8, 8), (FRAMES * 64) ** -0.5, 0.375, ((0, 2),), jnp.float32)
    first_bias = normal_values(streams_of[6], (2, C1), 0.5, 3.0, ((0, 2),), jnp.float32)
    second_kernel = normal_values(streams_of[7], (2, C2, C1, 4, 4), (C1 * 16) ** -0.5, 0.25, ((0, 2),), jnp.float32)
    second_bias = normal_values(streams_of[8], (2, C2), 0.5, 3.0, ((0, 2),), jnp.float32)
    third_kernel = normal_values(streams_of[9], (2, C3, C2, 3, 3), (C2 * 9) ** -0.5, 0.25, ((0, 2),), jnp.float32)
    third_bias = normal_values(streams_of[10], (2, C3), 0.5, 3.0, ((0, 2),), jnp.float32)
    hidden_mean = normal_values(streams_of[11], (2, 2, FEAT, HIDDEN_SIZE), FEAT ** -0.5, 0.109375, ((0, 2),), jnp.float32)
    hidden_sigma = normal_values(streams_of[12], (2, 2, FEAT, HIDDEN_SIZE), FEAT ** -0.5, 0.109375, ((0, 2),), jnp.float32)
    hidden_bias_mean = normal_values(streams_of[13], (2, 2, HIDDEN_SIZE), 0.5, 3.0, ((0, 2),), jnp.float32)
    hidden_bias_sigma = normal_values(streams_of[14], (2, 2, HIDDEN_SIZE), 0.5, 3.0, ((0, 2),), jnp.float32)
    head_mean = normal_values(streams_of[15], (2, HIDDEN_SIZE, OUTS), HIDDEN_SIZE ** -0.5, 0.25, ((0, 2),), jnp.float32)
    head_sigma = normal_values(streams_of[16], (2, HIDDEN_SIZE, OUTS), HIDDEN_SIZE ** -0.5, 0.25, ((0, 2),), jnp.float32)
    head_bias_mean = normal_values(streams_of[17], (2, OUTS), 0.5, 3.0, ((0, 2),), jnp.float32)
    head_bias_sigma = normal_values(streams_of[18], (2, OUTS), 0.5, 3.0, ((0, 2),), jnp.float32)
    hidden_noise_in = normal_values(streams_of[19], (2, 2, FEAT), 1.0, 4.0, ((0, 2),), jnp.float32)
    hidden_noise_out = normal_values(streams_of[20], (2, 2, HIDDEN_SIZE), 1.0, 4.0, ((0, 2),), jnp.float32)
    head_noise_in = normal_values(streams_of[21], (2, 2, HIDDEN_SIZE), 1.0, 4.0, ((0, 2),), jnp.float32)
    head_noise_out = normal_values(streams_of[22], (2, OUTS), 1.0, 4.0, ((0, 2),), jnp.float32)
    return {"states": states, "actions": actions, "proj_lower": proj_lower, "proj_upper": proj_upper, "proj_weight": proj_weight, "first_kernel": first_kernel, "first_bias": first_bias, "second_kernel": second_kernel, "second_bias": second_bias, "third_kernel": third_kernel, "third_bias": third_bias, "hidden_mean": hidden_mean, "hidden_sigma": hidden_sigma, "hidden_bias_mean": hidden_bias_mean, "hidden_bias_sigma": hidden_bias_sigma, "head_mean": head_mean, "head_sigma": head_sigma, "head_bias_mean": head_bias_mean, "head_bias_sigma": head_bias_sigma, "hidden_noise_in": hidden_noise_in, "hidden_noise_out": hidden_noise_out, "head_noise_in": head_noise_in, "head_noise_out": head_noise_out}


@jax.custom_vjp
def low(v):
    return lax.optimization_barrier(v.astype(jnp.bfloat16)).astype(jnp.float32)

@jax.custom_vjp
def low_back(v):
    return v

def low_keep(v):
    return (low(v), None)

def low_pass(kept, grad):
    return (grad,)

def back_keep(v):
    return (v, None)

def back_low(kept, grad):
    return (low(grad),)
low.defvjp(low_keep, low_pass)
low_back.defvjp(back_keep, back_low)
HIGHEST = lax.Precision.HIGHEST

def smooth(values):
    return values * jax.nn.sigmoid(values)

def conv_layer(inputs, kernel, offset, stride):
    output = lax.conv_general_dilated(inputs, kernel, (stride, stride), 'VALID', dimension_numbers=('NCHW', 'OIHW', 'NCHW'), precision=HIGHEST)
    return smooth(output + offset[None, :, None, None])

def network(weights, noises, frames, chosen):
    torso_out = conv_layer(frames, weights[0], weights[1], 4)
    torso_out = conv_layer(torso_out, weights[2], weights[3], 2)
    torso_out = conv_layer(torso_out, weights[4], weights[5], 1)
    features = torso_out.reshape(torso_out.shape[0], -1)
    hidden_in, hidden_out, head_in, head_out = noises
    hidden_w = weights[6] + weights[7] * (hidden_in[:, :, None] * hidden_out[:, None, :])
    hidden_b = weights[8] + weights[9] * hidden_out
    hidden = smooth(jnp.einsum('bf,sfh->sbh', features, hidden_w, precision=HIGHEST) + hidden_b[:, None, :])
    column = jnp.arange(head_out.shape[0])
    head_noise = jnp.where(column[None, :] < ATOMS, head_in[0][:, None], head_in[1][:, None])
    head_w = weights[10] + weights[11] * head_noise * head_out[None, :]
    head_b = weights[12] + weights[13] * head_out
    value_part = jnp.dot(hidden[0], head_w[:, :ATOMS], precision=HIGHEST) + head_b[:ATOMS]
    advantage = (jnp.dot(hidden[1], head_w[:, ATOMS:], precision=HIGHEST) + head_b[ATOMS:]).reshape(-1, ACTIONS, ATOMS)
    logits = value_part[:, None, :] + advantage - lax.optimization_barrier(jnp.mean(advantage, axis=1, keepdims=True))
    action_hot = (chosen[:, None] == jnp.arange(ACTIONS)[None, :]).astype(logits.dtype)
    picked = lax.optimization_barrier(jnp.sum(action_hot[:, :, None] * logits, axis=1))
    return jax.nn.log_softmax(picked, axis=-1)

def project(probabilities, lower_idx, upper_idx, upper_share):
    atom_index = jnp.arange(ATOMS)
    lower_hot = (lower_idx[:, :, None] == atom_index[None, None, :]).astype(probabilities.dtype)
    upper_hot = (upper_idx[:, :, None] == atom_index[None, None, :]).astype(probabilities.dtype)
    lower_mass = jnp.einsum('bi,bij->bj', probabilities * (1.0 - upper_share), lower_hot, precision=HIGHEST)
    upper_mass = jnp.einsum('bi,bij->bj', probabilities * upper_share, upper_hot, precision=HIGHEST)
    return lower_mass + upper_mass

def reference(states, actions, proj_lower, proj_upper, proj_weight, first_kernel, first_bias, second_kernel, second_bias, third_kernel, third_bias, hidden_mean, hidden_sigma, hidden_bias_mean, hidden_bias_sigma, head_mean, head_sigma, head_bias_mean, head_bias_sigma, hidden_noise_in, hidden_noise_out, head_noise_in, head_noise_out):
    stacked = (first_kernel, first_bias, second_kernel, second_bias, third_kernel, third_bias, hidden_mean, hidden_sigma, hidden_bias_mean, hidden_bias_sigma, head_mean, head_sigma, head_bias_mean, head_bias_sigma)
    noise_sets = (hidden_noise_in, hidden_noise_out, head_noise_in, head_noise_out)
    online = tuple((array_item[0] for array_item in stacked))
    target = tuple((array_item[1] for array_item in stacked))
    online_noise = tuple((array_item[0] for array_item in noise_sets))
    target_noise = tuple((array_item[1] for array_item in noise_sets))
    target_logp = network(target, target_noise, states[1], actions[1])
    target_dist = project(jnp.exp(target_logp), proj_lower, proj_upper, proj_weight)

    def online_loss(weights, frames):
        log_probs = network(weights, online_noise, frames, actions[0])
        return -jnp.sum(target_dist * log_probs) / B_DEV
    total_loss, pullback = jax.vjp(online_loss, online, states[0])
    weight_grads, frame_grads = pullback(jnp.ones_like(total_loss))
    return (total_loss, frame_grads, weight_grads[0], weight_grads[1], weight_grads[2], weight_grads[3], weight_grads[4], weight_grads[5], weight_grads[6], weight_grads[7], weight_grads[8], weight_grads[9], weight_grads[10], weight_grads[11], weight_grads[12], weight_grads[13])
```

```python
import jax
import jax.numpy as jnp
from jax import lax
from jax.experimental import pallas as pl
from jax.experimental.pallas import tpu as pltpu
from jax.sharding import PartitionSpec as P

BF = jnp.bfloat16
F32 = jnp.float32
NN=(((1,),(0,)),((),()))
NT=(((1,),(1,)),((),()))
TN=(((0,),(0,)),((),()))

def split(v):
    hi = v.astype(BF)
    return hi, (v - hi.astype(F32)).astype(BF)

def dot(a, b, dims=NN):
    return lax.dot_general(a, b, dims, preferred_element_type=F32)

def dot3(a, b, dims=NN):
    ah, al = a; bh, bl = b
    return dot(ah, bh, dims) + (dot(ah, bl, dims) + dot(al, bh, dims))

def silu(v):
    return v * jax.nn.sigmoid(v)

def fwd_weights(k1, k2, k3):
    a = jnp.transpose(k1, (0, 2, 3, 1)).reshape(32, 2, 4, 32)
    a = jnp.stack([jnp.pad(a, ((0, 0), (0, 0), (0, 0), (16 * w, 32 - 16 * w))) for w in range(3)])
    w1 = jnp.transpose(a, (2, 0, 1, 3, 4)).reshape(192, 256)
    w2 = jnp.transpose(k2.reshape(64, 32, 2, 2, 4), (2, 0, 3, 4, 1)).reshape(128, 256)
    a = jnp.transpose(k3, (2, 0, 3, 1)).reshape(3, 64, 192)
    a = jnp.stack([jnp.pad(a, ((0, 0), (0, 0), (64 * w, 64 - 64 * w))) for w in range(2)])
    w3 = jnp.transpose(a, (1, 0, 2, 3)).reshape(384, 256)
    return w1, w2, w3

def fwd_kernel(x_ref, w1_ref, w2_ref, w3_ref, b1_ref, b2_ref, b3_ref, pre1_ref, pre2_ref, pre3_ref, f_ref,
               xh, xl, ws1, top1, top2, acc3, h1h, h1l, h2h, h2l):
    j = pl.program_id(0)
    @pl.when(j == 0)
    def _():
        xh[:, 336:, :] = jnp.zeros((4, 16, 128), BF)
        xl[:, 336:, :] = jnp.zeros((4, 16, 128), BF)
        top1[...] = jnp.zeros_like(top1)
        top2[...] = jnp.zeros_like(top2)
        acc3[...] = jnp.zeros_like(acc3)
        hi, lo = split(w1_ref[...])
        ws1[0] = hi
        ws1[1] = lo
        h2h[:, 576:, :] = jnp.zeros((9, 64, 128), BF)
        h2l[:, 576:, :] = jnp.zeros((9, 64, 128), BF)
    v = x_ref[...]
    hi = v.astype(BF)
    xh[:, 0:336, :] = hi
    xl[:, 0:336, :] = (v - hi.astype(F32)).astype(BF)
    rh = jnp.concatenate([xh[:, 48 * i:48 * i + 64, :].reshape(256, 128) for i in range(7)], axis=1)
    rl = jnp.concatenate([xl[:, 48 * i:48 * i + 64, :].reshape(256, 128) for i in range(7)], axis=1)
    r = dot3((ws1[0], ws1[1]), (rh, rl))
    out = top1[...] + r[96:]
    top1[...] = r[:96]
    b1 = b1_ref[...]
    row = jnp.maximum(j - 1, 0)
    for i in range(7):
        n = 96 if i < 6 else 64
        p = out[:n, 128 * i:128 * i + 128] + b1[:n]
        pre1_ref[0, 96 * i:96 * i + n, :] = p
        hh, hl = split(silu(p))
        h1h[row, 96 * i:96 * i + n, :] = hh
        h1l[row, 96 * i:96 * i + n, :] = hl

    @pl.when(j == pl.num_programs(0) - 1)
    def _():
        w2 = split(w2_ref[...])
        b2 = b2_ref[...]
        def step2(y, carry):
            rh = jnp.concatenate([h1h[pl.ds(2 * y, 2), 64 * i:64 * i + 128, :].reshape(256, 128) for i in range(9)], axis=1)
            rl = jnp.concatenate([h1l[pl.ds(2 * y, 2), 64 * i:64 * i + 128, :].reshape(256, 128) for i in range(9)], axis=1)
            r = dot3(w2, (rh, rl))
            o = top2[...] + r[64:]
            top2[...] = r[:64]
            row = jnp.maximum(y - 1, 0)
            for i in range(9):
                p = o[:, 128 * i:128 * i + 128] + b2
                pre2_ref[row, 64 * i:64 * i + 64, :] = p
                hh, hl = split(silu(p))
                h2h[row, 64 * i:64 * i + 64, :] = hh
                h2l[row, 64 * i:64 * i + 64, :] = hl
            return carry
        lax.fori_loop(0, 10, step2, 0)
        w3 = split(w3_ref[...])
        b3 = b3_ref[...]
        def step3(y, carry):
            rh = jnp.concatenate([h2h[y, 128 * i:128 * i + 256, :] for i in range(4)], axis=1)
            rl = jnp.concatenate([h2l[y, 128 * i:128 * i + 256, :] for i in range(4)], axis=1)
            r = dot3(w3, (rh, rl))
            for ky in range(3):
                for i in range(4):
                    acc3[y - ky + 2, 128 * i:128 * i + 128, :] += r[128 * ky:128 * ky + 128, 128 * i:128 * i + 128]
            return carry
        lax.fori_loop(0, 9, step3, 0)
        for y in range(7):
            for x in range(7):
                p = acc3[y + 2, 64 * x:64 * x + 64, :] + b3
                pre3_ref[pl.ds(y * 7 + x, 64, stride=49), :] = p
                f_ref[pl.ds(y * 7 + x, 64, stride=49), :] = silu(p)

def forward(x, w1, w2, w3, b1, b2, b3):
    full = lambda *s: pl.BlockSpec(s, lambda j: (0,) * len(s))
    return pl.pallas_call(
        fwd_kernel,
        grid=(21,),
        in_specs=[pl.BlockSpec((4, 336, 128), lambda j: (j, 0, 0)), full(192, 256), full(128, 256), full(384, 256),
                  full(96, 128), full(64, 128), full(64, 128)],
        out_specs=[pl.BlockSpec((1, 640, 128), lambda j: (jnp.maximum(j - 1, 0), 0, 0)), full(9, 576, 128),
                   full(3136, 128), full(3136, 128)],
        out_shape=[jax.ShapeDtypeStruct((20, 640, 128), F32), jax.ShapeDtypeStruct((9, 576, 128), F32),
                   jax.ShapeDtypeStruct((3136, 128), F32), jax.ShapeDtypeStruct((3136, 128), F32)],
        scratch_shapes=[pltpu.VMEM((4, 352, 128), BF), pltpu.VMEM((4, 352, 128), BF), pltpu.VMEM((2, 192, 256), BF),
                        pltpu.VMEM((96, 896), F32), pltpu.VMEM((64, 1152), F32), pltpu.VMEM((11, 512, 128), F32),
                        pltpu.VMEM((20, 640, 128), BF), pltpu.VMEM((20, 640, 128), BF),
                        pltpu.VMEM((9, 640, 128), BF), pltpu.VMEM((9, 640, 128), BF)],
        compiler_params=pltpu.CompilerParams(vmem_limit_bytes=60 * 2**20),
    )(x, w1, w2, w3, b1, b2, b3)


def dsilu(v):
    s = jax.nn.sigmoid(v)
    return s * (1.0 + v * (1.0 - s))

def bwd_weights(k1, k2, k3):
    a = jnp.transpose(k1.reshape(32, 2, 2, 2, 4, 2, 4), (1, 4, 6, 2, 3, 5, 0))
    cols = []
    for q in range(4):
        parts = []
        for xb in range(3):
            o = xb - q + 1
            parts.append(a[:, :, :, :, ::-1, o, :] if 0 <= o <= 1 else jnp.zeros((2, 4, 4, 2, 2, 32), F32))
        cols.append(jnp.stack(parts, axis=2))
    w1 = jnp.stack(cols, axis=6).reshape(192, 256)
    a = jnp.transpose(k2.reshape(64, 32, 2, 2, 2, 2), (3, 5, 1, 2, 4, 0))[:, :, :, ::-1, ::-1]
    w2 = a.reshape(128, 256)
    cols = []
    for q in range(4):
        parts = []
        for w in range(2):
            kx = w + 2 - q
            parts.append(jnp.transpose(k3[:, :, :, kx], (2, 1, 0)) if 0 <= kx <= 2 else jnp.zeros((3, 64, 64), F32))
        cols.append(jnp.stack(parts, axis=1))
    w3 = jnp.stack(cols, axis=3).reshape(384, 256)
    return w1, w2, w3

def bwd_kernel(x_ref, pre1_ref, pre2_ref, pre3_ref, df_ref, w1_ref, w2_ref, w3_ref,
               lo_ref, up_ref, g1_ref, g2_ref, g3_ref, gb1_ref, gb2_ref, gb3_ref,
               xh, xl, ws1, d3f, d3h, d3l, d2h, d2l, d1h, d1l, h2h, h2l, acc2, a1, a2, a3):
    j = pl.program_id(0)
    @pl.when(j == 0)
    def _():
        xh[:, 336:, :] = jnp.zeros((4, 16, 128), BF)
        xl[:, 336:, :] = jnp.zeros((4, 16, 128), BF)
        hi, lo = split(w1_ref[...])
        ws1[0] = hi
        ws1[1] = lo
        for ref in (d3h, d3l, d2h, d2l, acc2, a1, a2, a3):
            ref[...] = jnp.zeros_like(ref)
        for ref in (d1h, d1l):
            ref[0] = jnp.zeros((704, 128), BF)
            ref[21] = jnp.zeros((704, 128), BF)
            ref[:, 0:32, :] = jnp.zeros((22, 32, 128), BF)
            ref[:, 672:704, :] = jnp.zeros((22, 32, 128), BF)
        d3f[...] = df_ref[...] * dsilu(pre3_ref[...])
        total = jnp.zeros((64, 128), F32)
        for y in range(7):
            for x in range(7):
                d = d3f[pl.ds(y * 7 + x, 64, stride=49), :]
                total = total + d
                hi, lo = split(d)
                d3h[y + 2, 64 * (x + 2):64 * (x + 3), :] = hi
                d3l[y + 2, 64 * (x + 2):64 * (x + 3), :] = lo
        gb3_ref[...] = jnp.sum(total, axis=1, keepdims=True)
        w3 = split(w3_ref[...])
        h2h[:, 576:, :] = jnp.zeros((9, 64, 128), BF)
        h2l[:, 576:, :] = jnp.zeros((9, 64, 128), BF)
        def split2(y, c):
            hi, lo = split(silu(pre2_ref[y]))
            h2h[y, 0:576, :] = hi
            h2l[y, 0:576, :] = lo
            return c
        lax.fori_loop(0, 9, split2, 0)
        def dgrad3(y, c):
            rh = jnp.concatenate([d3h[y + 2, 128 * i:128 * i + 256, :] for i in range(5)], axis=1)
            rl = jnp.concatenate([d3l[y + 2, 128 * i:128 * i + 256, :] for i in range(5)], axis=1)
            r = dot3(w3, (rh, rl))
            for ky in range(3):
                for i in range(5):
                    acc2[y + ky, 128 * i:128 * i + 128, :] += r[128 * ky:128 * ky + 128, 128 * i:128 * i + 128]
            return c
        lax.fori_loop(0, 7, dgrad3, 0)
        def wgrad3(y, c):
            def lhs(ref):
                return jnp.concatenate([jnp.concatenate([ref[y - ky + 2, 128 * (i + 1):128 * (i + 2), :] for i in range(4)], axis=1) for ky in range(3)], axis=0)
            def rhs(ref):
                return jnp.concatenate([ref[y, 128 * i:128 * i + 256, :] for i in range(4)], axis=1)
            a3[...] += dot3((lhs(d3h), lhs(d3l)), (rhs(h2h), rhs(h2l)), NT)
            return c
        lax.fori_loop(0, 9, wgrad3, 0)
        for ky in range(3):
            g3_ref[ky] = a3[128 * ky:128 * ky + 64, 0:192] + a3[128 * ky + 64:128 * ky + 128, 64:256]
        w2 = split(w2_ref[...])
        def step2(y, total):
            for x in range(9):
                d = acc2[y, 64 * x:64 * x + 64, :] * dsilu(pre2_ref[y, 64 * x:64 * x + 64, :])
                total = total + d
                hi, lo = split(d)
                d2h[y + 1, 64 * (x + 1):64 * (x + 2), :] = hi
                d2l[y + 1, 64 * (x + 1):64 * (x + 2), :] = lo
            return total
        total = lax.fori_loop(0, 9, step2, jnp.zeros((64, 128), F32))
        gb2_ref[...] = jnp.sum(total, axis=1, keepdims=True)
        def block2(y, total):
            rh = jnp.concatenate([d2h[pl.ds(y, 2), 64 * i:64 * i + 128, :].reshape(256, 128) for i in range(10)], axis=1)
            rl = jnp.concatenate([d2l[pl.ds(y, 2), 64 * i:64 * i + 128, :].reshape(256, 128) for i in range(10)], axis=1)
            r = dot3(w2, (rh, rl))
            h1h, h1l = [], []
            for py in range(2):
                rowh, rowl = [], []
                for i in range(10):
                    p = pre1_ref[2 * y + py, 64 * i:64 * i + 64, :]
                    s = jax.nn.sigmoid(p)
                    h = p * s
                    d = r[64 * py:64 * py + 64, 128 * i:128 * i + 128] * (s * (1.0 + p * (1.0 - s)))
                    total = total + d[0:32] + d[32:64]
                    hi, lo = split(d)
                    d1h[2 * y + py + 1, 64 * i + 32:64 * i + 96, :] = hi
                    d1l[2 * y + py + 1, 64 * i + 32:64 * i + 96, :] = lo
                    hi, lo = split(h)
                    rowh.append(hi)
                    rowl.append(lo)
                h1h.append(rowh)
                h1l.append(rowl)
            def lhs(ref):
                return jnp.concatenate([jnp.concatenate([ref[y + 1 - h, 64 * (i + 1):64 * (i + 2), :] for i in range(9)], axis=1) for h in range(2)], axis=0)
            def rhs(rows):
                return jnp.concatenate([jnp.concatenate([rows[0][i], rows[0][i + 1], rows[1][i], rows[1][i + 1]], axis=0) for i in range(9)], axis=1)
            a2[...] += dot3((lhs(d2h), lhs(d2l)), (rhs(h1h), rhs(h1l)), NT)
            return total
        total = lax.fori_loop(0, 10, block2, jnp.zeros((32, 128), F32))
        gb1_ref[...] = jnp.sum(total, axis=1, keepdims=True)
        g2_ref[...] = a2[...]
    v = x_ref[...]
    hi = v.astype(BF)
    xh[:, 0:336, :] = hi
    xl[:, 0:336, :] = (v - hi.astype(F32)).astype(BF)
    rh = jnp.concatenate([d1h[pl.ds(j, 2), 96 * i:96 * i + 128, :].reshape(256, 128) for i in range(7)], axis=1)
    rl = jnp.concatenate([d1l[pl.ds(j, 2), 96 * i:96 * i + 128, :].reshape(256, 128) for i in range(7)], axis=1)
    r = dot3((ws1[0], ws1[1]), (rh, rl))
    for ky in range(4):
        for i in range(7):
            lo_ref[ky, 24 * i:24 * i + 24, :] = r[24 * ky:24 * ky + 24, 128 * i:128 * i + 128]
            up_ref[ky, 24 * i:24 * i + 24, :] = r[96 + 24 * ky:96 + 24 * ky + 24, 128 * i:128 * i + 128]
    def lhs(ref):
        return jnp.concatenate([jnp.concatenate([ref[j + 1 - h, 96 * i + 32:96 * i + 128, :] for i in range(7)], axis=1) for h in range(2)], axis=0)
    def rhs(ref):
        return jnp.concatenate([ref[:, 48 * i:48 * i + 64, :].reshape(256, 128) for i in range(7)], axis=1)
    a1[...] += dot3((lhs(d1h), lhs(d1l)), (rhs(xh), rhs(xl)), NT)
    @pl.when(j == pl.num_programs(0) - 1)
    def _():
        for h in range(2):
            for ky in range(4):
                g = a1[96 * h:96 * h + 32, 64 * ky:64 * ky + 32]
                g = g + a1[96 * h + 32:96 * h + 64, 64 * ky + 16:64 * ky + 48]
                g = g + a1[96 * h + 64:96 * h + 96, 64 * ky + 32:64 * ky + 64]
                g1_ref[4 * h + ky] = g

def backward(x, pre1, pre2, pre3, df, w1, w2, w3):
    full = lambda *s: pl.BlockSpec(s, lambda j: (0,) * len(s))
    one = lambda *s: pl.BlockSpec(s, lambda j: (0,) * len(s), pipeline_mode=pl.Buffered(1))
    sds = lambda *s: jax.ShapeDtypeStruct(s, F32)
    half = pl.BlockSpec((4, 168, 128), lambda j: (j, 0, 0))
    return pl.pallas_call(
        bwd_kernel,
        grid=(21,),
        in_specs=[pl.BlockSpec((4, 336, 128), lambda j: (j, 0, 0)), one(20, 640, 128), one(9, 576, 128), one(3136, 128), one(3136, 128),
                  one(192, 256), one(128, 256), one(384, 256)],
        out_specs=[half, half, full(8, 32, 32), full(128, 256), full(3, 64, 192), full(32, 1), full(64, 1), full(64, 1)],
        out_shape=[sds(84, 168, 128), sds(84, 168, 128), sds(8, 32, 32), sds(128, 256), sds(3, 64, 192), sds(32, 1), sds(64, 1), sds(64, 1)],
        scratch_shapes=[pltpu.VMEM((4, 352, 128), BF), pltpu.VMEM((4, 352, 128), BF), pltpu.VMEM((2, 192, 256), BF),
                        pltpu.VMEM((3136, 128), F32), pltpu.VMEM((11, 768, 128), BF), pltpu.VMEM((11, 768, 128), BF),
                        pltpu.VMEM((11, 704, 128), BF), pltpu.VMEM((11, 704, 128), BF),
                        pltpu.VMEM((22, 704, 128), BF), pltpu.VMEM((22, 704, 128), BF),
                        pltpu.VMEM((9, 640, 128), BF), pltpu.VMEM((9, 640, 128), BF),
                        pltpu.VMEM((9, 640, 128), F32), pltpu.VMEM((192, 256), F32), pltpu.VMEM((128, 256), F32), pltpu.VMEM((384, 256), F32)],
        compiler_params=pltpu.CompilerParams(vmem_limit_bytes=60 * 2**20),
    )(x, pre1, pre2, pre3, df, w1, w2, w3)

def torso_grads(g1, g2, g3):
    k1 = jnp.transpose(g1.reshape(8, 32, 8, 4), (1, 3, 0, 2))
    k2 = jnp.transpose(g2.reshape(2, 64, 2, 4, 32), (1, 4, 0, 2, 3)).reshape(64, 32, 4, 4)
    k3 = jnp.transpose(g3.reshape(3, 64, 3, 64), (1, 3, 0, 2))
    return k1, k2, k3

ATOMS, ACTIONS, PAD = 51, 18, 56
STEPS = 7

def column(row, lanes):
    tall = jnp.transpose(jnp.broadcast_to(row, (128, row.shape[1])))
    return jnp.concatenate([tall] * (lanes // 128), axis=1)

def noisy(mean_ref, sigma_ref, nin_ref, nout_ref, s):
    return mean_ref[s] + sigma_ref[s] * (column(nin_ref[0, s:s + 1, :], 512) * nout_ref[s:s + 1, :])

def mask_of(chosen, a):
    return jnp.where(chosen == a, 1.0 - 1.0 / ACTIONS, -1.0 / ACTIONS)

def hid_kernel(f_ref, m_ref, s_ref, nin_ref, nout_ref, hb_ref, wo_ref, bo_ref, c_ref, pl_ref, pw_ref,
               h_ref, g_ref, logp_ref, dist_ref, acc):
    j = pl.program_id(0)
    @pl.when(j == 0)
    def _():
        acc[...] = jnp.zeros_like(acc)
    f = split(f_ref[...])
    for s in range(2):
        w = split(noisy(m_ref, s_ref, nin_ref, nout_ref, s))
        acc[:, 512 * s:512 * s + 512] += dot3(f, w, TN)
    @pl.when(j == pl.num_programs(0) - 1)
    def _():
        h = acc[...] + hb_ref[...]
        h_ref[...] = h
        g = silu(h)
        g_ref[...] = g
        gt = jnp.transpose(g)
        wo = wo_ref[...]
        v = dot3(split(wo[0]), split(gt[:512])) + bo_ref[0]
        a = dot3(split(wo[1:].reshape(ACTIONS * PAD, 512)), split(gt[512:]))
        chosen = c_ref[...]
        z = v
        for i in range(ACTIONS):
            z = z + mask_of(chosen, i) * (a[PAD * i:PAD * i + PAD] + bo_ref[i + 1])
        row = lax.broadcasted_iota(jnp.int32, (PAD, 128), 0)
        z = jnp.where(row < ATOMS, z, -1e30)
        top = jnp.max(z, axis=0, keepdims=True)
        e = jnp.exp(z - top)
        tot = jnp.sum(e, axis=0, keepdims=True)
        logp_ref[...] = (z - top) - jnp.log(tot)
        p = e / tot
        dist = jnp.zeros((PAD, 128), F32)
        for i in range(ATOMS):
            lower = pl_ref[i:i + 1, :]
            share = pw_ref[i:i + 1, :]
            pi = p[i:i + 1, :]
            dist = dist + jnp.where(row == lower, pi * (1.0 - share), 0.0) + jnp.where(row == lower + 1, pi * share, 0.0)
        dist_ref[...] = dist

def hidden(f, m, s, nin, nout, hb, wo, bo, c, plow, pw):
    full = lambda *t: pl.BlockSpec(t, lambda j: (0,) * len(t))
    sds = lambda *t: jax.ShapeDtypeStruct(t, F32)
    k = 3136 // STEPS
    wspec = pl.BlockSpec((2, k, 512), lambda j: (0, j, 0))
    return pl.pallas_call(
        hid_kernel, grid=(STEPS,),
        in_specs=[pl.BlockSpec((k, 128), lambda j: (j, 0)), wspec, wspec, pl.BlockSpec((1, 2, k), lambda j: (j, 0, 0)), full(2, 512), full(1, 1024),
                  full(19, PAD, 512), full(19, PAD, 128), full(1, 128), full(ATOMS, 128), full(ATOMS, 128)],
        out_specs=[full(128, 1024), full(128, 1024), full(PAD, 128), full(PAD, 128)],
        out_shape=[sds(128, 1024), sds(128, 1024), sds(PAD, 128), sds(PAD, 128)],
        scratch_shapes=[pltpu.VMEM((128, 1024), F32)],
        compiler_params=pltpu.CompilerParams(vmem_limit_bytes=60 * 2**20),
    )(f, m, s, nin, nout, hb, wo, bo, c, plow, pw)

def hid_bwd_kernel(t_ref, logp_ref, h_ref, m_ref, s_ref, nin_ref, nout_ref, wo_ref, c_ref,
                   df_ref, dp_ref, dz_ref, loss_ref, bo_ref, dth, dtl):
    j = pl.program_id(0)
    @pl.when(j == 0)
    def _():
        t = t_ref[...]
        logp = logp_ref[...]
        chosen = c_ref[...]
        row = lax.broadcasted_iota(jnp.int32, (PAD, 128), 0)
        d = (jnp.exp(logp) * jnp.sum(t, axis=0, keepdims=True) - t) * (1.0 / 128)
        loss = -jnp.sum(jnp.where(row < ATOMS, t * logp, 0.0), axis=1, keepdims=True) * (1.0 / 128)
        loss_ref[...] = jnp.sum(loss, axis=0, keepdims=True)
        dz_ref[...] = jnp.where(row == ATOMS, chosen.astype(F32), d)
        bo_ref[0] = jnp.sum(d, axis=1, keepdims=True)
        parts = []
        for i in range(ACTIONS):
            p = mask_of(chosen, i) * d
            bo_ref[i + 1] = jnp.sum(p, axis=1, keepdims=True)
            parts.append(p)
        da = jnp.concatenate(parts, axis=0)
        wo = wo_ref[...]
        g0 = dot3(split(d), split(wo[0]), TN)
        g1 = dot3(split(da), split(wo[1:].reshape(ACTIONS * PAD, 512)), TN)
        for s, g in enumerate((g0, g1)):
            dp = g * dsilu(h_ref[:, 512 * s:512 * s + 512])
            dp_ref[:, 512 * s:512 * s + 512] = dp
            hi, lo = split(jnp.transpose(dp))
            dth[s] = hi
            dtl[s] = lo
    out = None
    for s in range(2):
        w = split(noisy(m_ref, s_ref, nin_ref, nout_ref, s))
        r = dot3(w, (dth[s], dtl[s]))
        out = r if out is None else out + r
    df_ref[...] = out

def hidden_bwd(t, logp, h, m, s, nin, nout, wo, c):
    full = lambda *u: pl.BlockSpec(u, lambda j: (0,) * len(u))
    sds = lambda *u: jax.ShapeDtypeStruct(u, F32)
    k = 3136 // STEPS
    wspec = pl.BlockSpec((2, k, 512), lambda j: (0, j, 0))
    return pl.pallas_call(
        hid_bwd_kernel, grid=(STEPS,),
        in_specs=[full(PAD, 128), full(PAD, 128), full(128, 1024), wspec, wspec, pl.BlockSpec((1, 2, k), lambda j: (j, 0, 0)), full(2, 512),
                  full(19, PAD, 512), full(1, 128)],
        out_specs=[pl.BlockSpec((k, 128), lambda j: (j, 0)), full(128, 1024), full(PAD, 128), full(1, 1), full(19, PAD, 1)],
        out_shape=[sds(3136, 128), sds(128, 1024), sds(PAD, 128), sds(1, 1), sds(19, PAD, 1)],
        scratch_shapes=[pltpu.VMEM((2, 512, 128), BF), pltpu.VMEM((2, 512, 128), BF)],
        compiler_params=pltpu.CompilerParams(vmem_limit_bytes=60 * 2**20),
    )(t, logp, h, m, s, nin, nout, wo, c)

def online_only(value):
    other = lax.ppermute(value, "pair", [(0, 1)])
    return jnp.where(lax.axis_index("pair") == 0, value, other)

def exchange(parts):
    groups = lax.axis_size("group")
    p, g = lax.axis_index("pair"), lax.axis_index("group")
    got = []
    for k in range(groups):
        to = (g + k) % groups
        mine = parts(0, to)
        if k:
            mine = lax.ppermute(mine, ("pair", "group"), [(i, (i + k) % groups) for i in range(groups)])
        theirs = lax.ppermute(parts(1, to), ("pair", "group"), [(i, groups + (i + k) % groups) for i in range(groups)])
        got.append(jnp.where(p == 0, mine, theirs))
    return got

HIGH = lax.Precision.HIGH

def local(states, actions, proj_lower, proj_upper, proj_weight, first_kernel, first_bias, second_kernel, second_bias,
          third_kernel, third_bias, hidden_mean, hidden_sigma, hidden_bias_mean, hidden_bias_sigma, head_mean, head_sigma,
          head_bias_mean, head_bias_sigma, hidden_noise_in, hidden_noise_out, head_noise_in, head_noise_out):
    pair = lax.axis_index("pair")
    groups = lax.axis_size("group")
    shards = 2 * groups
    n_in, n_out, e_in, e_out = hidden_noise_in[0], hidden_noise_out[0], head_noise_in[0], head_noise_out[0]
    noise = online_only(jnp.concatenate([v.reshape(-1) for v in (n_in, n_out, e_in, e_out)]))
    on_in = noise[:6272].reshape(2, 3136)
    on_out = noise[6272:7296].reshape(2, 512)
    on_ein = noise[7296:8320].reshape(2, 512)
    on_eout = noise[8320:]
    shard = pair * groups + lax.axis_index("group")

    x = jnp.transpose(states[0], (2, 3, 1, 0)).reshape(84, 336, 128)
    k1, k2, k3 = first_kernel[0], second_kernel[0], third_kernel[0]
    spread = lambda b, n: jnp.broadcast_to(jnp.tile(b, n)[:, None], (b.shape[0] * n, 128))
    pre1, pre2, pre3, feats = forward(x, *fwd_weights(k1, k2, k3), spread(first_bias[0], 3), spread(second_bias[0], 1), spread(third_bias[0], 1))
    feat_q = 3136 // shards
    f_got = exchange(lambda p, g: lax.dynamic_slice_in_dim(feats, (p * groups + g) * feat_q, feat_q, axis=0))

    wide = lambda v: jnp.pad(v.reshape(19, ATOMS, -1), ((0, 0), (0, PAD - ATOMS), (0, 0)))
    e_rows = jnp.concatenate([e_in[0:1], jnp.broadcast_to(e_in[1:2], (ACTIONS, 512))])
    wo = wide(head_mean[0].T) + wide(head_sigma[0].T) * (e_rows[:, None, :] * wide(e_out[:, None]))
    bo = jnp.broadcast_to(wide((head_bias_mean[0] + head_bias_sigma[0] * e_out)[:, None]), (19, PAD, 128))
    hb = (hidden_bias_mean[0] + hidden_bias_sigma[0] * n_out).reshape(1, 1024)
    nin = jnp.transpose(n_in.reshape(2, STEPS, 3136 // STEPS), (1, 0, 2))
    h, hid, logp, dist = hidden(feats, hidden_mean[0], hidden_sigma[0], nin, n_out, hb, wo, bo, actions, proj_lower.T, proj_weight.T)
    hid_q = 512 // shards
    hid_got = exchange(lambda p, g: lax.dynamic_slice_in_dim(hid.reshape(128, 2, 512), (p * groups + g) * hid_q, hid_q, axis=2))
    target = lax.ppermute(dist, "pair", [(1, 0)])
    df, dpre, dz, loss, bo_sum = hidden_bwd(target, logp, h, hidden_mean[0], hidden_sigma[0], nin, n_out, wo, actions)
    d_got = exchange(lambda p, g: jnp.concatenate([dpre, dz.T, jnp.zeros((128, 72), F32)], axis=1))
    d_all = jnp.concatenate(d_got, axis=0)
    f_all = jnp.concatenate(f_got, axis=1)
    hid_all = jnp.concatenate(hid_got, axis=0)
    part_hidden = jnp.einsum("fb,bsh->sfh", f_all, d_all[:, :1024].reshape(-1, 2, 512), precision=HIGH)
    dz_all = d_all[:, 1024:1024 + ATOMS]
    picked = d_all[:, 1024 + ATOMS]
    mask = jnp.where(picked[None, :] == jnp.arange(ACTIONS, dtype=F32)[:, None], 1.0 - 1.0 / ACTIONS, -1.0 / ACTIONS)
    da = (mask[:, None, :] * dz_all.T[None]).reshape(ACTIONS * ATOMS, -1)
    part_head = jnp.concatenate([jnp.dot(dz_all.T, hid_all[:, 0], precision=HIGH), jnp.dot(da, hid_all[:, 1], precision=HIGH)], axis=0)
    part_hidden, part_head, df = lax.optimization_barrier((part_hidden, part_head, df))
    hidden_grad, head_grad = lax.psum((part_hidden, part_head), "rep")

    lo, up, g1, g2, g3, gb1, gb2, gb3 = backward(x, pre1, pre2, pre3, df, *bwd_weights(k1, k2, k3))
    moved = lax.ppermute(up, "pair", [(0, 1)])
    grad_rows = jnp.where(pair == 0, lo, moved)
    states_grad = jnp.transpose(grad_rows.reshape(84, 84, 2, 128), (3, 2, 0, 1))
    small = [g1, g2, g3, gb1, gb2, gb3, jnp.sum(dpre, axis=0), bo_sum[:, :ATOMS], loss]
    flat = lax.psum(jnp.concatenate([v.reshape(-1) for v in small]), ("pair", "group", "rep"))
    out, at = [], 0
    for v in small:
        out.append(flat[at:at + v.size].reshape(v.shape))
        at += v.size
    g1, g2, g3, gb1, gb2, gb3, hb_grad, bo_grad, loss = out
    gk1, gk2, gk3 = torso_grads(g1, g2, g3)
    hb_grad = hb_grad.reshape(2, 512)
    bo_grad = bo_grad.reshape(-1)

    in_q = lax.dynamic_slice_in_dim(on_in, shard * feat_q, feat_q, axis=1)
    hidden_sigma_grad = hidden_grad * (in_q[:, :, None] * on_out[:, None, :])
    e_q = lax.dynamic_slice_in_dim(on_ein, shard * hid_q, hid_q, axis=1)
    column_of = jnp.arange(on_eout.shape[0])[:, None]
    head_sigma_grad = head_grad * (jnp.where(column_of < ATOMS, e_q[0:1], e_q[1:2]) * on_eout[:, None])
    return (loss.reshape(()), states_grad, gk1, gb1.reshape(-1), gk2, gb2.reshape(-1), gk3, gb3.reshape(-1), hidden_grad, hidden_sigma_grad,
            hb_grad, hb_grad * on_out, head_grad.T, head_sigma_grad.T, bo_grad, bo_grad * on_eout)


def solution(mesh):
    placed = (
        P("pair", ("group", "rep"), None, None, None),
        P("pair", ("group", "rep")),
        P(("group", "rep"), None),
        P(("group", "rep"), None),
        P(("group", "rep"), None),
        P("pair", None, None, None, None),
        P("pair", None),
        P("pair", None, None, None, None),
        P("pair", None),
        P("pair", None, None, None, None),
        P("pair", None),
        P("pair", None, None, None),
        P("pair", None, None, None),
        P("pair", None, None),
        P("pair", None, None),
        P("pair", None, None),
        P("pair", None, None),
        P("pair", None),
        P("pair", None),
        P("pair", None, None),
        P("pair", None, None),
        P("pair", None, None),
        P("pair", None),
    )
    return jax.shard_map(
        local,
        mesh=mesh,
        in_specs=placed,
        out_specs=(
            P(),
            P(("group", "rep"), "pair", None, None),
            P(),
            P(),
            P(),
            P(),
            P(),
            P(),
            P(None, ("pair", "group"), None),
            P(None, ("pair", "group"), None),
            P(),
            P(),
            P(("pair", "group"), None),
            P(("pair", "group"), None),
            P(),
            P(),
        ),
        check_vma=False,
    )
```

```python
import functools
import jax
import jax.numpy as jnp
from jax import lax
from jax.experimental import pallas as pl
from jax.experimental.pallas import tpu as pltpu
from jax.sharding import PartitionSpec as P

BF = jnp.bfloat16
F32 = jnp.float32
NN=(((1,),(0,)),((),()))
NT=(((1,),(1,)),((),()))
TN=(((0,),(0,)),((),()))

def split(v):
    hi = v.astype(BF)
    return hi, (v - hi.astype(F32)).astype(BF)

def dot(a, b, dims=NN):
    return lax.dot_general(a, b, dims, preferred_element_type=F32)

def dot3(a, b, dims=NN):
    ah, al = a; bh, bl = b
    return dot(ah, bh, dims) + (dot(ah, bl, dims) + dot(al, bh, dims))

def silu(v):
    return v * jax.nn.sigmoid(v)

def fwd_weights(k1, k2, k3):
    a = jnp.transpose(k1, (0, 2, 3, 1)).reshape(32, 2, 4, 32)
    a = jnp.stack([jnp.pad(a, ((0, 0), (0, 0), (0, 0), (16 * w, 32 - 16 * w))) for w in range(3)])
    w1 = jnp.transpose(a, (2, 0, 1, 3, 4)).reshape(192, 256)
    w2 = jnp.transpose(k2.reshape(64, 32, 2, 2, 4), (2, 0, 3, 4, 1)).reshape(128, 256)
    a = jnp.transpose(k3, (2, 0, 3, 1)).reshape(3, 64, 192)
    a = jnp.stack([jnp.pad(a, ((0, 0), (0, 0), (64 * w, 64 - 64 * w))) for w in range(2)])
    w3 = jnp.transpose(a, (1, 0, 2, 3)).reshape(384, 256)
    return w1, w2, w3

def fwd_kernel(x_ref, w1_ref, w2_ref, w3_ref, b1_ref, b2_ref, b3_ref, pre1_ref, pre2_ref, pre3_ref, f_ref,
               xh, xl, ws1, top1, top2, acc3, h1h, h1l, h2h, h2l):
    j = pl.program_id(0)
    @pl.when(j == 0)
    def _():
        xh[:, 336:, :] = jnp.zeros((4, 16, 128), BF)
        xl[:, 336:, :] = jnp.zeros((4, 16, 128), BF)
        top1[...] = jnp.zeros_like(top1)
        top2[...] = jnp.zeros_like(top2)
        acc3[...] = jnp.zeros_like(acc3)
        hi, lo = split(w1_ref[...])
        ws1[0] = hi
        ws1[1] = lo
        h2h[:, 576:, :] = jnp.zeros((9, 64, 128), BF)
        h2l[:, 576:, :] = jnp.zeros((9, 64, 128), BF)
    v = x_ref[...]
    hi = v.astype(BF)
    xh[:, 0:336, :] = hi
    xl[:, 0:336, :] = (v - hi.astype(F32)).astype(BF)
    rh = jnp.concatenate([xh[:, 48 * i:48 * i + 64, :].reshape(256, 128) for i in range(7)], axis=1)
    rl = jnp.concatenate([xl[:, 48 * i:48 * i + 64, :].reshape(256, 128) for i in range(7)], axis=1)
    r = dot3((ws1[0], ws1[1]), (rh, rl))
    out = top1[...] + r[96:]
    top1[...] = r[:96]
    b1 = b1_ref[...]
    row = jnp.maximum(j - 1, 0)
    for i in range(7):
        n = 96 if i < 6 else 64
        p = out[:n, 128 * i:128 * i + 128] + b1[:n]
        pre1_ref[0, 96 * i:96 * i + n, :] = p
        hh, hl = split(silu(p))
        h1h[row, 96 * i:96 * i + n, :] = hh
        h1l[row, 96 * i:96 * i + n, :] = hl

    @pl.when(j == pl.num_programs(0) - 1)
    def _():
        w2 = split(w2_ref[...])
        b2 = b2_ref[...]
        def step2(y, carry):
            rh = jnp.concatenate([h1h[pl.ds(2 * y, 2), 64 * i:64 * i + 128, :].reshape(256, 128) for i in range(9)], axis=1)
            rl = jnp.concatenate([h1l[pl.ds(2 * y, 2), 64 * i:64 * i + 128, :].reshape(256, 128) for i in range(9)], axis=1)
            r = dot3(w2, (rh, rl))
            o = top2[...] + r[64:]
            top2[...] = r[:64]
            row = jnp.maximum(y - 1, 0)
            for i in range(9):
                p = o[:, 128 * i:128 * i + 128] + b2
                pre2_ref[row, 64 * i:64 * i + 64, :] = p
                hh, hl = split(silu(p))
                h2h[row, 64 * i:64 * i + 64, :] = hh
                h2l[row, 64 * i:64 * i + 64, :] = hl
            return carry
        lax.fori_loop(0, 10, step2, 0)
        w3 = split(w3_ref[...])
        b3 = b3_ref[...]
        def step3(y, carry):
            rh = jnp.concatenate([h2h[y, 128 * i:128 * i + 256, :] for i in range(4)], axis=1)
            rl = jnp.concatenate([h2l[y, 128 * i:128 * i + 256, :] for i in range(4)], axis=1)
            r = dot3(w3, (rh, rl))
            for ky in range(3):
                for i in range(4):
                    acc3[y - ky + 2, 128 * i:128 * i + 128, :] += r[128 * ky:128 * ky + 128, 128 * i:128 * i + 128]
            return carry
        lax.fori_loop(0, 9, step3, 0)
        for y in range(7):
            for x in range(7):
                p = acc3[y + 2, 64 * x:64 * x + 64, :] + b3
                pre3_ref[pl.ds(y * 7 + x, 64, stride=49), :] = p
                f_ref[pl.ds(y * 7 + x, 64, stride=49), :] = silu(p)

def forward(x, w1, w2, w3, b1, b2, b3):
    full = lambda *s: pl.BlockSpec(s, lambda j: (0,) * len(s))
    return pl.pallas_call(
        fwd_kernel,
        grid=(21,),
        in_specs=[pl.BlockSpec((4, 336, 128), lambda j: (j, 0, 0)), full(192, 256), full(128, 256), full(384, 256),
                  full(96, 128), full(64, 128), full(64, 128)],
        out_specs=[pl.BlockSpec((1, 640, 128), lambda j: (jnp.maximum(j - 1, 0), 0, 0)), full(9, 576, 128),
                   full(3136, 128), full(3136, 128)],
        out_shape=[jax.ShapeDtypeStruct((20, 640, 128), F32), jax.ShapeDtypeStruct((9, 576, 128), F32),
                   jax.ShapeDtypeStruct((3136, 128), F32), jax.ShapeDtypeStruct((3136, 128), F32)],
        scratch_shapes=[pltpu.VMEM((4, 352, 128), BF), pltpu.VMEM((4, 352, 128), BF), pltpu.VMEM((2, 192, 256), BF),
                        pltpu.VMEM((96, 896), F32), pltpu.VMEM((64, 1152), F32), pltpu.VMEM((11, 512, 128), F32),
                        pltpu.VMEM((20, 640, 128), BF), pltpu.VMEM((20, 640, 128), BF),
                        pltpu.VMEM((9, 640, 128), BF), pltpu.VMEM((9, 640, 128), BF)],
        compiler_params=pltpu.CompilerParams(vmem_limit_bytes=60 * 2**20),
    )(x, w1, w2, w3, b1, b2, b3)


MESH_ID = pl.DeviceIdType.MESH


def coords():
    r = lax.axis_index("rep")
    return lax.axis_index("pair"), lax.axis_index("group"), r // 2, r % 2


def at(p, g, z, y):
    return (p, g, z * 2 + y)


def flip(z, k):
    return (z, z + 1 - 2 * (z % 2), z + 2 - 4 * (z // 2), 3 - z)[k]


def line(p, g, z, y):
    return [at(q, g, flip(z, k), y) for k in range(4) for q in ((p, 1 - p) if k else (1 - p,))]


def plane(p, g, z, y):
    return [at(p, g, z, 1 - y), at(p, 1 - g, z, y), at(p, 1 - g, z, 1 - y)]


def greet(devices):
    barrier = pltpu.get_barrier_semaphore()
    for device in devices:
        pl.semaphore_signal(barrier, inc=1, device_id=device, device_id_type=MESH_ID)
    pl.semaphore_wait(barrier, len(devices))


def remote(src, dst, send, recv, device):
    return pltpu.make_async_remote_copy(src_ref=src, dst_ref=dst, send_sem=send, recv_sem=recv, device_id=device, device_id_type=MESH_ID)


class Scatter:
    def __init__(self, parts, src, dst, send, recv, own):
        self.parts, self.src, self.dst, self.send, self.recv, self.own = parts, src, dst, send, recv, own
        self.p, self.g, self.z, self.y = coords()

    def copies(self):
        for k in range(4):
            for q in range(2):
                for i in range(self.parts):
                    zd = flip(self.z, k)
                    if k == 0 and q == 0:
                        yield pltpu.make_async_copy(self.src(q, zd, i), self.dst(self.z, i), self.own.at[i]), True
                    else:
                        yield remote(self.src(q, zd, i), self.dst(self.z, i), self.send.at[k * 2 + q, i], self.recv.at[k, i], at(q, self.g, zd, self.y)), False

    def start(self):
        @pl.when(self.p == 0)
        def _():
            for copy, own in self.copies():
                copy.start()

    def arrived(self, k):
        for i in range(self.parts):
            zs = flip(self.z, k)
            wait = remote(self.src(0, zs, i), self.dst(zs, i), self.send.at[0, i], self.recv.at[k, i], at(1 - self.p, self.g, self.z, self.y)).wait_recv
            if k:
                wait()
            else:
                pl.when(self.p == 1)(wait)
                pl.when(self.p == 0)(pltpu.make_async_copy(self.src(0, zs, i), self.dst(zs, i), self.own.at[i]).wait)

    def sent(self):
        @pl.when(self.p == 0)
        def _():
            for copy, own in self.copies():
                if not own:
                    copy.wait_send()


def scatter_sems(parts):
    return [pltpu.SemaphoreType.DMA((8, parts)), pltpu.SemaphoreType.DMA((4, parts)), pltpu.SemaphoreType.DMA((parts,))]


def f_scatter(f_ref, f1_ref, sems):
    def src(q, zd, i):
        return f_ref.at[pl.ds(pl.multiple_of((2 * q + i) * 784 + jnp.minimum(200 * zd, 584), 8), 200)]
    return Scatter(2, src, lambda z, i: f1_ref.at[i, z], *sems)


def g_scatter(hid_ref, g1_ref, sems):
    return Scatter(1, lambda q, zd, i: hid_ref.at[q, zd], lambda z, i: g1_ref.at[z], *sems)


def d_scatter(msg_ref, d1_ref, sems):
    return Scatter(1, lambda q, zd, i: msg_ref.at[q], lambda z, i: d1_ref.at[z], *sems)


def spread_plane(p, g, z, y, src, dst, send, recv):
    places = [(g, y), (g, 1 - y), (1 - g, y), (1 - g, 1 - y)]
    out = [pltpu.make_async_copy(src(*places[0]), dst(0), send.at[0])]
    for m in range(1, 4):
        out.append(remote(src(*places[m]), dst(m), send.at[m], recv.at[m], at(p, places[m][0], z, places[m][1])))
    return out
ATOMS, ACTIONS, PAD = 51, 18, 56
STEPS = 7

def column(row, lanes):
    tall = jnp.transpose(jnp.broadcast_to(row, (128, row.shape[1])))
    return jnp.concatenate([tall] * (lanes // 128), axis=1)

def noisy(mean_ref, sigma_ref, nin_ref, nout_ref, s):
    return mean_ref[s] + sigma_ref[s] * (column(nin_ref[0, s:s + 1, :], 512) * nout_ref[s:s + 1, :])

def mask_of(chosen, a):
    return jnp.where(chosen == a, 1.0 - 1.0 / ACTIONS, -1.0 / ACTIONS)

def hid_kernel(net, f_ref, m_ref, s_ref, nin_ref, nout_ref, hb_ref, wo_ref, bo_ref, c_ref, pl_ref, pw_ref, *rest):
    if net:
        f_all, h_ref, g_ref, logp_ref, dist_ref, f1_ref, acc = rest[:7]
        wire = f_scatter(f_all, f1_ref, rest[7:])
    else:
        h_ref, g_ref, logp_ref, dist_ref, acc = rest
    j = pl.program_id(0)
    @pl.when(j == 0)
    def _():
        if net:
            greet(line(*coords()))
            wire.start()
        acc[...] = jnp.zeros_like(acc)
    f = split(f_ref[...])
    for s in range(2):
        w = split(noisy(m_ref, s_ref, nin_ref, nout_ref, s))
        acc[:, 512 * s:512 * s + 512] += dot3(f, w, TN)
    @pl.when(j == pl.num_programs(0) - 1)
    def _():
        h = acc[...] + hb_ref[...]
        h_ref[...] = h
        gt = jnp.transpose(silu(h))
        for s in range(2):
            for q in range(2):
                for gg in range(2):
                    for z in range(4):
                        at_row = 512 * s + 256 * q + 128 * gg + 32 * z
                        g_ref[q, z, gg, s] = gt[at_row:at_row + 32]
        wo = wo_ref[...]
        v = dot3(split(wo[0]), split(gt[:512])) + bo_ref[0]
        a = dot3(split(wo[1:].reshape(ACTIONS * PAD, 512)), split(gt[512:]))
        chosen = c_ref[...]
        z = v
        for i in range(ACTIONS):
            z = z + mask_of(chosen, i) * (a[PAD * i:PAD * i + PAD] + bo_ref[i + 1])
        row = lax.broadcasted_iota(jnp.int32, (PAD, 128), 0)
        z = jnp.where(row < ATOMS, z, -1e30)
        top = jnp.max(z, axis=0, keepdims=True)
        e = jnp.exp(z - top)
        tot = jnp.sum(e, axis=0, keepdims=True)
        logp_ref[...] = (z - top) - jnp.log(tot)
        p = e / tot
        dist = jnp.zeros((PAD, 128), F32)
        for i in range(ATOMS):
            lower = pl_ref[i:i + 1, :]
            share = pw_ref[i:i + 1, :]
            pi = p[i:i + 1, :]
            dist = dist + jnp.where(row == lower, pi * (1.0 - share), 0.0) + jnp.where(row == lower + 1, pi * share, 0.0)
        dist_ref[...] = dist
        if net:
            for k in range(4):
                wire.arrived(k)
            wire.sent()

ANY = pl.BlockSpec(memory_space=pl.ANY)

def hidden(net, f, m, s, nin, nout, hb, wo, bo, c, plow, pw):
    full = lambda *t: pl.BlockSpec(t, lambda j: (0,) * len(t))
    sds = lambda *t: jax.ShapeDtypeStruct(t, F32)
    k = 3136 // STEPS
    wspec = pl.BlockSpec((2, k, 512), lambda j: (0, j, 0))
    return pl.pallas_call(
        functools.partial(hid_kernel, net), grid=(STEPS,),
        in_specs=[pl.BlockSpec((k, 128), lambda j: (j, 0)), wspec, wspec, pl.BlockSpec((1, 2, k), lambda j: (j, 0, 0)), full(2, 512), full(1, 1024),
                  full(19, PAD, 512), full(19, PAD, 128), full(1, 128), full(ATOMS, 128), full(ATOMS, 128)] + [ANY] * net,
        out_specs=[full(128, 1024), full(2, 4, 2, 2, 32, 128), full(PAD, 128), full(PAD, 128)] + [ANY] * net,
        out_shape=[sds(128, 1024), sds(2, 4, 2, 2, 32, 128), sds(PAD, 128), sds(PAD, 128)] + [sds(2, 4, 200, 128)] * net,
        scratch_shapes=[pltpu.VMEM((128, 1024), F32)] + scatter_sems(2) * net,
        compiler_params=pltpu.CompilerParams(vmem_limit_bytes=60 * 2**20, **(dict(collective_id=1, has_side_effects=True) if net else {})),
    )(f, m, s, nin, nout, hb, wo, bo, c, plow, pw, *([f] * net))

def hid_bwd_kernel(net, t_ref, logp_ref, h_ref, m_ref, s_ref, nin_ref, nout_ref, wo_ref, c_ref, *rest):
    if net:
        f1_ref, hid_ref, df_ref, msg_ref, small_ref, f2_ref, g1_ref, dth, dtl, fs, fr = rest[:11]
        wire = g_scatter(hid_ref, g1_ref, rest[11:])
        p, g, z, y = coords()
        fan = spread_plane(p, g, z, y, lambda gd, yd: f1_ref.at[gd], lambda m: f2_ref.at[m], fs, fr)
    else:
        df_ref, msg_ref, small_ref, dth, dtl = rest
    j = pl.program_id(0)
    @pl.when(j == 0)
    def _():
        if net:
            greet(line(p, g, z, y) + plane(p, g, z, y))
            for copy in fan:
                copy.start()
            wire.start()
        t = t_ref[...]
        logp = logp_ref[...]
        chosen = c_ref[...]
        row = lax.broadcasted_iota(jnp.int32, (PAD, 128), 0)
        d = (jnp.exp(logp) * jnp.sum(t, axis=0, keepdims=True) - t) * (1.0 / 128)
        loss = -jnp.sum(jnp.where(row < ATOMS, t * logp, 0.0), axis=1, keepdims=True) * (1.0 / 128)
        dz = jnp.where(row == ATOMS, chosen.astype(F32), d)
        da = jnp.concatenate([mask_of(chosen, i) * d for i in range(ACTIONS)], axis=0)
        wo = wo_ref[...]
        d2, da2 = split(d), split(da)
        g0 = dot3(d2, split(wo[0]), TN)
        g1 = dot3(da2, split(wo[1:].reshape(ACTIONS * PAD, 512)), TN)
        small_ref[...] = jnp.zeros_like(small_ref)
        for s, grad in enumerate((g0, g1)):
            dp = grad * dsilu(h_ref[:, 512 * s:512 * s + 512])
            total = jnp.sum(dp, axis=0, keepdims=True)
            for c in range(4):
                msg_ref[c // 2, s, 128 * (c % 2):128 * (c % 2) + 128, :] = dp[:, 128 * c:128 * c + 128]
                small_ref[4 * s + c:4 * s + c + 1, :] = total[:, 128 * c:128 * c + 128]
            for ph in range(2):
                msg_ref[ph, s, 256:312, :] = dz
            hi, lo = split(jnp.transpose(dp))
            dth[s] = hi
            dtl[s] = lo
        ones = jnp.ones((8, 128), BF)
        every = jnp.concatenate([d, da, jnp.zeros((1152 - 19 * PAD, 128), F32)], axis=0)
        eh, el = split(every)
        rest_ = (every - eh.astype(F32)) - el.astype(F32)
        rows = dot(ones, eh, NT) + dot(ones, el, NT) + dot(ones, rest_.astype(BF), NT)
        for c in range(9):
            small_ref[8 + c:9 + c, :] = rows[0:1, 128 * c:128 * c + 128]
        small_ref[17:18, :] = jnp.broadcast_to(jnp.sum(loss, axis=0, keepdims=True), (1, 128))
    out = None
    for s in range(2):
        w = split(noisy(m_ref, s_ref, nin_ref, nout_ref, s))
        r = dot3(w, (dth[s], dtl[s]))
        out = r if out is None else out + r
    df_ref[...] = out
    if net:
        @pl.when(j == pl.num_programs(0) - 1)
        def _():
            fan[0].wait()
            for copy in fan[1:]:
                copy.wait()
            for k in range(4):
                wire.arrived(k)
            wire.sent()

def hidden_bwd(net, t, logp, h, m, s, nin, nout, wo, c, *wired):
    full = lambda *u: pl.BlockSpec(u, lambda j: (0,) * len(u))
    sds = lambda *u: jax.ShapeDtypeStruct(u, F32)
    k = 3136 // STEPS
    wspec = pl.BlockSpec((2, k, 512), lambda j: (0, j, 0))
    return pl.pallas_call(
        functools.partial(hid_bwd_kernel, net), grid=(STEPS,),
        in_specs=[full(PAD, 128), full(PAD, 128), full(128, 1024), wspec, wspec, pl.BlockSpec((1, 2, k), lambda j: (j, 0, 0)), full(2, 512),
                  full(19, PAD, 512), full(1, 128)] + [ANY, ANY] * net,
        out_specs=[pl.BlockSpec((k, 128), lambda j: (j, 0)), full(2, 2, 312, 128), full(24, 128)] + [ANY, ANY] * net,
        out_shape=[sds(3136, 128), sds(2, 2, 312, 128), sds(24, 128)] + [sds(4, 4, 200, 128), sds(4, 2, 2, 32, 128)] * net,
        scratch_shapes=[pltpu.VMEM((2, 512, 128), BF), pltpu.VMEM((2, 512, 128), BF)]
        + ([pltpu.SemaphoreType.DMA((4,)), pltpu.SemaphoreType.DMA((4,))] + scatter_sems(1)) * net,
        compiler_params=pltpu.CompilerParams(vmem_limit_bytes=60 * 2**20, **(dict(collective_id=2, has_side_effects=True) if net else {})),
    )(t, logp, h, m, s, nin, nout, wo, c, *wired)

def dsilu(v):
    s = jax.nn.sigmoid(v)
    return s * (1.0 + v * (1.0 - s))

def bwd_weights(k1, k2, k3):
    a = jnp.transpose(k1.reshape(32, 2, 2, 2, 4, 2, 4), (1, 4, 6, 2, 3, 5, 0))
    cols = []
    for q in range(4):
        parts = []
        for xb in range(3):
            o = xb - q + 1
            parts.append(a[:, :, :, :, ::-1, o, :] if 0 <= o <= 1 else jnp.zeros((2, 4, 4, 2, 2, 32), F32))
        cols.append(jnp.stack(parts, axis=2))
    w1 = jnp.stack(cols, axis=6).reshape(192, 256)
    a = jnp.transpose(k2.reshape(64, 32, 2, 2, 2, 2), (3, 5, 1, 2, 4, 0))[:, :, :, ::-1, ::-1]
    w2 = a.reshape(128, 256)
    cols = []
    for q in range(4):
        parts = []
        for w in range(2):
            kx = w + 2 - q
            parts.append(jnp.transpose(k3[:, :, :, kx], (2, 1, 0)) if 0 <= kx <= 2 else jnp.zeros((3, 64, 64), F32))
        cols.append(jnp.stack(parts, axis=1))
    w3 = jnp.stack(cols, axis=3).reshape(384, 256)
    return w1, w2, w3


def low_kernel(net, pre1_ref, pre2_ref, pre3_ref, df_ref, w2_ref, w3_ref, *rest):
    if net:
        msg_ref, g1_ref, d1h, d1l, small_ref, d1_ref, d2_ref, d3_ref, g2_ref = rest[:9]
        d3f, d3h, d3l, d2h, d2l, h2h, h2l, acc2, a2, a3 = rest[9:19]
        ps, pr, gs, gr, ss, sr = rest[19:25]
        wire = d_scatter(msg_ref, d1_ref, rest[25:])
        p, g, z, y = coords()
        greet(line(p, g, z, y) + plane(p, g, z, y))
        wire.start()
        def fan(k):
            zs = flip(z, k)
            return (spread_plane(p, g, z, y, lambda gd, yd: d1_ref.at[zs, yd], lambda m: d2_ref.at[m, zs], ps.at[k], pr.at[k])
                    + spread_plane(p, g, z, y, lambda gd, yd: g1_ref.at[zs, gd, yd], lambda m: g2_ref.at[m, zs], gs.at[k], gr.at[k]))
        def forward(k):
            wire.arrived(k)
            for copy in fan(k):
                copy.start()
    else:
        d1h, d1l, small_ref, d3f, d3h, d3l, d2h, d2l, h2h, h2l, acc2, a2, a3 = rest
    def upper():
        for ref in (d3h, d3l, d2h, d2l, acc2, a2, a3):
            ref[...] = jnp.zeros_like(ref)
        small_ref[...] = jnp.zeros_like(small_ref)
        for ref in (d1h, d1l):
            ref[0] = jnp.zeros((704, 128), BF)
            ref[21] = jnp.zeros((704, 128), BF)
            ref[:, 0:32, :] = jnp.zeros((22, 32, 128), BF)
            ref[:, 672:704, :] = jnp.zeros((22, 32, 128), BF)
        d3f[...] = df_ref[...] * dsilu(pre3_ref[...])
        total = jnp.zeros((64, 128), F32)
        for y in range(7):
            for x in range(7):
                d = d3f[pl.ds(y * 7 + x, 64, stride=49), :]
                total = total + d
                hi, lo = split(d)
                d3h[y + 2, 64 * (x + 2):64 * (x + 3), :] = hi
                d3l[y + 2, 64 * (x + 2):64 * (x + 3), :] = lo
        small_ref[640:641, 0:64] = jnp.sum(jnp.transpose(total), axis=0, keepdims=True)
        w3 = split(w3_ref[...])
        h2h[:, 576:, :] = jnp.zeros((9, 64, 128), BF)
        h2l[:, 576:, :] = jnp.zeros((9, 64, 128), BF)
        def split2(y, c):
            hi, lo = split(silu(pre2_ref[y]))
            h2h[y, 0:576, :] = hi
            h2l[y, 0:576, :] = lo
            return c
        lax.fori_loop(0, 9, split2, 0)
        def dgrad3(y, c):
            rh = jnp.concatenate([d3h[y + 2, 128 * i:128 * i + 256, :] for i in range(5)], axis=1)
            rl = jnp.concatenate([d3l[y + 2, 128 * i:128 * i + 256, :] for i in range(5)], axis=1)
            r = dot3(w3, (rh, rl))
            for ky in range(3):
                for i in range(5):
                    acc2[y + ky, 128 * i:128 * i + 128, :] += r[128 * ky:128 * ky + 128, 128 * i:128 * i + 128]
            return c
        lax.fori_loop(0, 7, dgrad3, 0)
        def wgrad3(y, c):
            def lhs(ref):
                return jnp.concatenate([jnp.concatenate([ref[y - ky + 2, 128 * (i + 1):128 * (i + 2), :] for i in range(4)], axis=1) for ky in range(3)], axis=0)
            def rhs(ref):
                return jnp.concatenate([ref[y, 128 * i:128 * i + 256, :] for i in range(4)], axis=1)
            a3[...] += dot3((lhs(d3h), lhs(d3l)), (rhs(h2h), rhs(h2l)), NT)
            return c
        lax.fori_loop(0, 9, wgrad3, 0)
        for ky in range(3):
            grad = a3[128 * ky:128 * ky + 64, 0:192] + a3[128 * ky + 64:128 * ky + 128, 64:256]
            small_ref[256 + 64 * ky:320 + 64 * ky, :] = grad[:, 0:128]
            small_ref[448 + 64 * ky:512 + 64 * ky, 0:64] = grad[:, 128:192]
        def step2(y, total):
            for x in range(9):
                d = acc2[y, 64 * x:64 * x + 64, :] * dsilu(pre2_ref[y, 64 * x:64 * x + 64, :])
                total = total + d
                hi, lo = split(d)
                d2h[y + 1, 64 * (x + 1):64 * (x + 2), :] = hi
                d2l[y + 1, 64 * (x + 1):64 * (x + 2), :] = lo
            return total
        total = lax.fori_loop(0, 9, step2, jnp.zeros((64, 128), F32))
        small_ref[641:642, 0:64] = jnp.sum(jnp.transpose(total), axis=0, keepdims=True)
    def block2(y, total):
        w2 = split(w2_ref[...])
        rh = jnp.concatenate([d2h[pl.ds(y, 2), 64 * i:64 * i + 128, :].reshape(256, 128) for i in range(10)], axis=1)
        rl = jnp.concatenate([d2l[pl.ds(y, 2), 64 * i:64 * i + 128, :].reshape(256, 128) for i in range(10)], axis=1)
        r = dot3(w2, (rh, rl))
        h1h, h1l = [], []
        for py in range(2):
            rowh, rowl = [], []
            for i in range(10):
                v = pre1_ref[2 * y + py, 64 * i:64 * i + 64, :]
                s = jax.nn.sigmoid(v)
                d = r[64 * py:64 * py + 64, 128 * i:128 * i + 128] * (s * (1.0 + v * (1.0 - s)))
                total = total + d[0:32] + d[32:64]
                hi, lo = split(d)
                d1h[2 * y + py + 1, 64 * i + 32:64 * i + 96, :] = hi
                d1l[2 * y + py + 1, 64 * i + 32:64 * i + 96, :] = lo
                hi, lo = split(v * s)
                rowh.append(hi)
                rowl.append(lo)
            h1h.append(rowh)
            h1l.append(rowl)
        def lhs(ref):
            return jnp.concatenate([jnp.concatenate([ref[y + 1 - h, 64 * (i + 1):64 * (i + 2), :] for i in range(9)], axis=1) for h in range(2)], axis=0)
        def rhs(rows):
            return jnp.concatenate([jnp.concatenate([rows[0][i], rows[0][i + 1], rows[1][i], rows[1][i + 1]], axis=0) for i in range(9)], axis=1)
        a2[...] += dot3((lhs(d2h), lhs(d2l)), (rhs(h1h), rhs(h1l)), NT)
        return total
    def lower():
        total = lax.fori_loop(0, 10, block2, jnp.zeros((32, 128), F32))
        small_ref[642:643, 0:32] = jnp.sum(jnp.transpose(total), axis=0, keepdims=True)
        small_ref[0:128, :] = a2[:, 0:128]
        small_ref[128:256, :] = a2[:, 128:256]
    if not net:
        upper()
        lower()
        return
    pl.when(p == 0)(upper)
    for k in range(4):
        forward(k)
    pl.when(p == 0)(lower)
    fans = [fan(k) for k in range(4)]
    swaps = []
    for m in range(4):
        for k in range(4):
            for copy in (fans[k][m], fans[k][4 + m]):
                if m:
                    copy.wait_recv()
                else:
                    copy.wait()
        swap = remote(d2_ref.at[m, :, pl.ds(0, 256)], d3_ref.at[m], ss.at[m], sr.at[m], at(1 - p, g, z, y))
        swap.start()
        swaps.append(swap)
    for m in range(1, 4):
        for k in range(4):
            fans[k][m].wait_send()
            fans[k][4 + m].wait_send()
    for swap in swaps:
        swap.wait()
    wire.sent()

def lower_backward(net, pre1, pre2, pre3, df, w2, w3, *wired):
    one = lambda *s: pl.BlockSpec(s, lambda j: (0,) * len(s), pipeline_mode=pl.Buffered(1))
    sds = lambda *s: jax.ShapeDtypeStruct(s, F32)
    bfs = lambda *s: jax.ShapeDtypeStruct(s, BF)
    vmb = lambda *s: pltpu.VMEM(s, BF)
    dma = pltpu.SemaphoreType.DMA
    return pl.pallas_call(
        functools.partial(low_kernel, net),
        grid=(1,),
        in_specs=[one(20, 640, 128), one(9, 576, 128), one(3136, 128), one(3136, 128), one(128, 256), one(384, 256)] + [ANY, ANY] * net,
        out_specs=[one(22, 704, 128), one(22, 704, 128), one(648, 128)] + [ANY] * (4 * net),
        out_shape=[bfs(22, 704, 128), bfs(22, 704, 128), sds(648, 128)]
        + [sds(4, 2, 312, 128), sds(4, 4, 312, 128), sds(4, 4, 256, 128), sds(4, 4, 32, 128)] * net,
        scratch_shapes=[pltpu.VMEM((3136, 128), F32), vmb(11, 768, 128), vmb(11, 768, 128), vmb(11, 704, 128), vmb(11, 704, 128),
                        vmb(9, 640, 128), vmb(9, 640, 128), pltpu.VMEM((9, 640, 128), F32), pltpu.VMEM((128, 256), F32), pltpu.VMEM((384, 256), F32)]
        + ([dma((4, 4)), dma((4, 4)), dma((4, 4)), dma((4, 4)), dma((4,)), dma((4,))] + scatter_sems(1)) * net,
        compiler_params=pltpu.CompilerParams(vmem_limit_bytes=60 * 2**20, **(dict(collective_id=3, has_side_effects=True) if net else {})),
    )(pre1, pre2, pre3, df, w2, w3, *wired)

def first_kernel_bwd(net, x_ref, dha_ref, dhb_ref, dla_ref, dlb_ref, w1_ref, *rest):
    if net:
        r_ref, q_ref, small_ref, sg_ref, ag_ref, ah_ref, xh, xl, ws1, a1, lob, upb, ls, us, ur, zs_, zr, ys, yr, own = rest
        p, g, z, y = coords()
        def along_z(k):
            to = at(p, g, flip(z, k), y)
            if k:
                return [remote(r_ref, ag_ref.at[y, z], zs_.at[k, 0], zr.at[k, 0], to), remote(q_ref, ah_ref.at[y, z], zs_.at[k, 1], zr.at[k, 1], to)]
            return [pltpu.make_async_copy(r_ref, ag_ref.at[y, z], own.at[0]), pltpu.make_async_copy(q_ref, ah_ref.at[y, z], own.at[1])]
        def along_y(k):
            zs = flip(z, k)
            a, b = (ag_ref.at[y, zs], ah_ref.at[y, zs]) if k else (r_ref, q_ref)
            to = at(p, g, z, 1 - y)
            return [remote(a, ag_ref.at[y, zs], ys.at[k, 0], yr.at[k, 0], to), remote(b, ah_ref.at[y, zs], ys.at[k, 1], yr.at[k, 1], to)]
        def states_out(j, slot):
            return (pltpu.make_async_copy(lob.at[slot], sg_ref.at[pl.ds(4 * j, 4)], ls.at[slot]),
                    remote(upb.at[slot], sg_ref.at[pl.ds(4 * j, 4)], us.at[slot], ur.at[j], at(1 - p, g, z, y)))
    else:
        small_ref, lo_ref, up_ref, xh, xl, ws1, a1 = rest
    j = pl.program_id(0)
    last = pl.num_programs(0) - 1
    @pl.when(j == 0)
    def _():
        if net:
            greet([at(q, g, flip(z, k), y) for k in range(1, 4) for q in (p,)] + [at(p, g, z, 1 - y), at(1 - p, g, z, y)])
            for k in (1, 2, 3, 0):
                for copy in along_z(k):
                    copy.start()
            for copy in along_y(0):
                copy.start()
        xh[:, 336:, :] = jnp.zeros((4, 16, 128), BF)
        xl[:, 336:, :] = jnp.zeros((4, 16, 128), BF)
        hi, lo = split(w1_ref[...])
        ws1[0] = hi
        ws1[1] = lo
        a1[...] = jnp.zeros_like(a1)
    def work():
        v = x_ref[...]
        hi = v.astype(BF)
        xh[:, 0:336, :] = hi
        xl[:, 0:336, :] = (v - hi.astype(F32)).astype(BF)
        def both(a, b):
            return jnp.concatenate([jnp.concatenate([a[0, 96 * i:96 * i + 128, :], b[0, 96 * i:96 * i + 128, :]], axis=0) for i in range(7)], axis=1)
        r = dot3((ws1[0], ws1[1]), (both(dha_ref, dhb_ref), both(dla_ref, dlb_ref)))
        if net:
            slot = j % 2
            @pl.when(j >= 2)
            def _():
                a, b = states_out(j - 2, slot)
                a.wait()
                b.wait_send()
            lo_to, up_to = lob.at[slot], upb.at[slot]
        else:
            lo_to, up_to = lo_ref, up_ref
        for ky in range(4):
            for i in range(7):
                lo_to[ky, 24 * i:24 * i + 24, :] = r[24 * ky:24 * ky + 24, 128 * i:128 * i + 128]
                up_to[ky, 24 * i:24 * i + 24, :] = r[96 + 24 * ky:96 + 24 * ky + 24, 128 * i:128 * i + 128]
        if net:
            for copy in states_out(j, slot):
                copy.start()
        def lhs(a, b):
            return jnp.concatenate([jnp.concatenate([ref[0, 96 * i + 32:96 * i + 128, :] for i in range(7)], axis=1) for ref in (b, a)], axis=0)
        def rhs(ref):
            return jnp.concatenate([ref[:, 48 * i:48 * i + 64, :].reshape(256, 128) for i in range(7)], axis=1)
        a1[...] += dot3((lhs(dha_ref, dhb_ref), lhs(dla_ref, dlb_ref)), (rhs(xh), rhs(xl)), NT)
    if net:
        pl.when(p == 0)(work)
        for k, step in ((1, 6), (2, 11), (3, 16)):
            @pl.when(j == step)
            def _():
                for copy in along_z(k):
                    copy.wait_recv()
                for copy in along_y(k):
                    copy.start()
    else:
        work()
    @pl.when(j == last)
    def _():
        for h in range(2):
            for ky in range(4):
                grad = a1[96 * h:96 * h + 32, 64 * ky:64 * ky + 32]
                grad = grad + a1[96 * h + 32:96 * h + 64, 64 * ky + 16:64 * ky + 48]
                grad = grad + a1[96 * h + 64:96 * h + 96, 64 * ky + 32:64 * ky + 64]
                small_ref[32 * h:32 * h + 32, 32 * ky:32 * ky + 32] = grad
        if net:
            @pl.when(p == 0)
            def _():
                for back in (1, 0):
                    a, b = states_out(j - back, (j - back) % 2)
                    a.wait()
                    b.wait_send()
            @pl.when(p == 1)
            def _():
                def arrive(i, c):
                    states_out(i, 0)[1].wait_recv()
                    return c
                lax.fori_loop(0, last + 1, arrive, 0)
            for k in range(4):
                for copy in along_z(k):
                    if k:
                        copy.wait_send()
                    else:
                        copy.wait()
                for copy in along_y(k):
                    copy.wait()

def first_backward(net, x, dh, dl, w1, *wired):
    full = lambda *s: pl.BlockSpec(s, lambda j: (0,) * len(s))
    sds = lambda *s: jax.ShapeDtypeStruct(s, F32)
    vmb = lambda *s: pltpu.VMEM(s, BF)
    dma = pltpu.SemaphoreType.DMA
    half = pl.BlockSpec((4, 168, 128), lambda j: (j, 0, 0))
    row = pl.BlockSpec((1, 704, 128), lambda j: (j, 0, 0))
    next_row = pl.BlockSpec((1, 704, 128), lambda j: (j + 1, 0, 0))
    return pl.pallas_call(
        functools.partial(first_kernel_bwd, net),
        grid=(21,),
        in_specs=[pl.BlockSpec((4, 336, 128), lambda j: (j, 0, 0)), row, next_row, row, next_row, full(192, 256)] + [ANY, ANY] * net,
        out_specs=[full(64, 128)] + ([ANY] * 3 if net else [half, half]),
        out_shape=[sds(64, 128)] + ([sds(84, 168, 128), sds(2, 4, 200, 512), sds(2, 4, 32, 1152)] if net else [sds(84, 168, 128), sds(84, 168, 128)]),
        scratch_shapes=[vmb(4, 352, 128), vmb(4, 352, 128), vmb(2, 192, 256), pltpu.VMEM((192, 256), F32)]
        + [pltpu.VMEM((2, 4, 168, 128), F32), pltpu.VMEM((2, 4, 168, 128), F32), dma((2,)), dma((2,)), dma((21,)),
           dma((4, 2)), dma((4, 2)), dma((4, 2)), dma((4, 2)), dma((2,))] * net,
        compiler_params=pltpu.CompilerParams(vmem_limit_bytes=60 * 2**20, **(dict(collective_id=4, has_side_effects=True) if net else {})),
    )(x, dh, dh, dl, dl, w1, *wired)

def wide_kernel(f_ref, d_ref, e_ref, g_ref, r_ref, q_ref, acc, acq):
    m = pl.program_id(0)
    p = lax.axis_index("pair")
    @pl.when(m == 0)
    def _():
        acc[...] = jnp.zeros_like(acc)
        acq[...] = jnp.zeros_like(acq)
    f = split(jnp.concatenate([f_ref[0, i] for i in range(4)], axis=1))
    def block(ref):
        return jnp.concatenate([jnp.concatenate([ref[0, i, 128 * c:128 * c + 128, :] for c in range(2)], axis=1) for i in range(4)], axis=0)
    acc[0] += dot3(f, split(block(d_ref)))
    acc[1] += dot3(f, split(block(e_ref)))
    dz = jnp.concatenate([d_ref[0, i, 256:312, :] for i in range(4)], axis=1)
    row = lax.broadcasted_iota(jnp.int32, (PAD, 512), 0)
    chosen = dz[ATOMS:ATOMS + 1].astype(jnp.int32)
    d = jnp.where(row < ATOMS, dz, 0.0)
    da = jnp.concatenate([d] + [mask_of(chosen, i) * d for i in range(ACTIONS)] + [jnp.zeros((1152 - 19 * PAD, 512), F32)], axis=0)
    g = split(jnp.concatenate([g_ref[0, i] for i in range(4)], axis=1))
    acq[...] += dot3(g, split(da), NT)
    @pl.when(m == 3)
    def _():
        r_ref[:, 0:256] = jnp.where(p == 0, acc[0], acc[1])
        r_ref[:, 256:512] = jnp.where(p == 0, acc[1], acc[0])
        q_ref[...] = acq[...]

def wide_grads(f2, d2, d3, g2):
    full = lambda *s: pl.BlockSpec(s, lambda j: (0,) * len(s))
    part = lambda n: pl.BlockSpec((1, 4, n, 128), lambda j: (j, 0, 0, 0))
    sds = lambda *s: jax.ShapeDtypeStruct(s, F32)
    return pl.pallas_call(
        wide_kernel, grid=(4,),
        in_specs=[part(200), part(312), part(256), part(32)],
        out_specs=[full(200, 512), full(32, 1152)],
        out_shape=[sds(200, 512), sds(32, 1152)],
        scratch_shapes=[pltpu.VMEM((2, 200, 256), F32), pltpu.VMEM((32, 1152), F32)],
        compiler_params=pltpu.CompilerParams(vmem_limit_bytes=60 * 2**20),
    )(f2, d2, d3, g2)

ROWS = 768

def sum_kernel(ag_ref, in_ref, out_ref, s0_ref, s1_ref, s2_ref, mean_ref, sigma_ref, tot_ref, pay, got, red, ss, sr, ts, tr, own):
    p, g = lax.axis_index("pair"), lax.axis_index("group")
    reps = lax.axis_size("rep")
    r = lax.axis_index("rep")
    me = (p * 2 + g) * reps + r
    chip = g * reps + r
    count = 4 * reps
    size = ROWS // count
    def spot(i):
        return (i // (2 * reps), (i // reps) % 2, i % reps)
    barrier = pltpu.get_barrier_semaphore()
    for k in range(1, count):
        pl.semaphore_signal(barrier, inc=1, device_id=spot((me + k) % count), device_id_type=MESH_ID)
    pl.semaphore_wait(barrier, count - 1)
    pay[0:24, :] = s0_ref[...]
    pay[24:672, :] = s1_ref[...]
    pay[672:736, :] = s2_ref[...]
    pay[736:, :] = jnp.zeros((ROWS - 736, 128), F32)
    def first(k):
        to = (me + k) % count
        src, dst = pay.at[pl.ds(pl.multiple_of(to * size, 8), size)], got.at[chip]
        return remote(src, dst, ss.at[k], sr.at[chip], spot(to)) if k else pltpu.make_async_copy(src, dst, own)
    @pl.when(p == 0)
    def _():
        for k in range(count):
            first(k).start()
    row_in = in_ref[...]
    for s in range(2):
        tall = column(in_ref[s:s + 1, :], 512) * out_ref[s:s + 1, :]
        for z, (start, n) in enumerate(((0, 200), (200, 200), (400, 184), (584, 200))):
            v = ag_ref[s, z, 0:n, :]
            mean_ref[s, start:start + n, :] = v
            sigma_ref[s, start:start + n, :] = v * tall[start:start + n]
    @pl.when(p == 0)
    def _():
        for k in range(1, count):
            first(k).wait_send()
        first(0).wait()
    for c in range(2 * reps):
        wait = remote(pay.at[pl.ds(0, size)], got.at[c], ss.at[0], sr.at[c], spot((me + 1) % count)).wait_recv
        pl.when(jnp.logical_or(p == 1, chip != c))(wait)
    red[...] = jnp.sum(got[...], axis=0)
    here = pl.ds(pl.multiple_of(me * size, 8), size)
    sends = [remote(red, tot_ref.at[here], ts.at[k], tr.at[me], spot((me + k) % count)) for k in range(1, count)]
    for copy in sends:
        copy.start()
    tot_ref[here, :] = red[...]
    for copy in sends:
        copy.wait_send()
    for k in range(1, count):
        who = (me + k) % count
        remote(red, tot_ref.at[pl.ds(pl.multiple_of(who * size, 8), size)], ts.at[k], tr.at[who], spot(who)).wait_recv()

def sum_all(ag, n_in, n_out, s0, s1, s2):
    vm = pl.BlockSpec(memory_space=pltpu.VMEM)
    sds = lambda *s: jax.ShapeDtypeStruct(s, F32)
    dma = pltpu.SemaphoreType.DMA
    return pl.pallas_call(
        sum_kernel,
        in_specs=[vm] * 6, out_specs=[vm] * 3,
        out_shape=[sds(2, 784, 512), sds(2, 784, 512), sds(ROWS, 128)],
        scratch_shapes=[pltpu.VMEM((ROWS, 128), F32), pltpu.VMEM((16, 24, 128), F32), pltpu.VMEM((24, 128), F32),
                        dma((32,)), dma((16,)), dma((32,)), dma((32,)), dma],
        compiler_params=pltpu.CompilerParams(vmem_limit_bytes=60 * 2**20, collective_id=5, has_side_effects=True),
    )(ag, n_in, n_out, s0, s1, s2)

def torso_grads(total):
    g1 = total[672:736].reshape(2, 32, 4, 8, 4)
    k1 = jnp.transpose(g1, (1, 4, 0, 2, 3)).reshape(32, 4, 8, 8)
    g2 = total[24:280].reshape(2, 2, 64, 4, 32)
    k2 = jnp.transpose(g2, (2, 4, 1, 0, 3)).reshape(64, 32, 4, 4)
    g3 = jnp.concatenate([total[280:472], total[472:664, 0:64]], axis=1).reshape(3, 64, 3, 64)
    k3 = jnp.transpose(g3, (1, 3, 0, 2))
    return k1, total[666, 0:32], k2, total[665, 0:64], k3, total[664, 0:64]

def online_only(value):
    other = lax.ppermute(value, "pair", [(0, 1)])
    return jnp.where(lax.axis_index("pair") == 0, value, other)

def exchange(parts):
    groups = lax.axis_size("group")
    p, g = lax.axis_index("pair"), lax.axis_index("group")
    got = []
    for k in range(groups):
        to = (g + k) % groups
        mine = parts(0, to)
        if k:
            mine = lax.ppermute(mine, ("pair", "group"), [(i, (i + k) % groups) for i in range(groups)])
        theirs = lax.ppermute(parts(1, to), ("pair", "group"), [(i, groups + (i + k) % groups) for i in range(groups)])
        got.append(jnp.where(p == 0, mine, theirs))
    return got

HIGH = lax.Precision.HIGH

def local(states, actions, proj_lower, proj_upper, proj_weight, first_kernel, first_bias, second_kernel, second_bias,
          third_kernel, third_bias, hidden_mean, hidden_sigma, hidden_bias_mean, hidden_bias_sigma, head_mean, head_sigma,
          head_bias_mean, head_bias_sigma, hidden_noise_in, hidden_noise_out, head_noise_in, head_noise_out):
    pair = lax.axis_index("pair")
    groups = lax.axis_size("group")
    shards = 2 * groups
    net = int(groups == 2 and lax.axis_size("rep") == 8)
    n_in, n_out, e_in, e_out = hidden_noise_in[0], hidden_noise_out[0], head_noise_in[0], head_noise_out[0]
    noise = online_only(jnp.concatenate([v.reshape(-1) for v in (n_in, n_out, e_in, e_out)]))
    on_in = noise[:6272].reshape(2, 3136)
    on_out = noise[6272:7296].reshape(2, 512)
    on_ein = noise[7296:8320].reshape(2, 512)
    on_eout = noise[8320:]
    shard = pair * groups + lax.axis_index("group")
    feat_q, hid_q = 3136 // shards, 512 // shards
    in_q = lax.dynamic_slice_in_dim(on_in, shard * feat_q, feat_q, axis=1)
    e_q = lax.dynamic_slice_in_dim(on_ein, shard * hid_q, hid_q, axis=1)

    x = jnp.transpose(states[0], (2, 3, 1, 0)).reshape(84, 336, 128)
    k1, k2, k3 = first_kernel[0], second_kernel[0], third_kernel[0]
    spread = lambda b, n: jnp.broadcast_to(jnp.tile(b, n)[:, None], (b.shape[0] * n, 128))
    pre1, pre2, pre3, feats = forward(x, *fwd_weights(k1, k2, k3), spread(first_bias[0], 3), spread(second_bias[0], 1), spread(third_bias[0], 1))

    wide = lambda v: jnp.pad(v.reshape(19, ATOMS, -1), ((0, 0), (0, PAD - ATOMS), (0, 0)))
    e_rows = jnp.concatenate([e_in[0:1], jnp.broadcast_to(e_in[1:2], (ACTIONS, 512))])
    wo = wide(head_mean[0].T) + wide(head_sigma[0].T) * (e_rows[:, None, :] * wide(e_out[:, None]))
    bo = jnp.broadcast_to(wide((head_bias_mean[0] + head_bias_sigma[0] * e_out)[:, None]), (19, PAD, 128))
    hb = (hidden_bias_mean[0] + hidden_bias_sigma[0] * n_out).reshape(1, 1024)
    nin = jnp.transpose(n_in.reshape(2, STEPS, 3136 // STEPS), (1, 0, 2))
    bw1, bw2, bw3 = bwd_weights(k1, k2, k3)
    h, hid, logp, dist, *f1 = hidden(net, feats, hidden_mean[0], hidden_sigma[0], nin, n_out, hb, wo, bo, actions, proj_lower.T, proj_weight.T)
    target = lax.ppermute(dist, "pair", [(1, 0)])
    df, msg, small_b, *f2g1 = hidden_bwd(net, target, logp, h, hidden_mean[0], hidden_sigma[0], nin, n_out, wo, actions, *f1, *([hid] * net))
    if net:
        f2, g1 = f2g1
        dh, dl, small_d, _, d2, d3, g2 = lower_backward(net, pre1, pre2, pre3, df, bw2, bw3, msg, g1)
        part_r, part_q = wide_grads(f2, d2, d3, g2)
        small_f, grad_rows, ag, ah = first_backward(net, x, dh, dl, bw1, part_r, part_q)
        hidden_grad, hidden_sigma_grad, total = sum_all(ag, in_q, on_out, small_b, small_d, small_f)
        value_part = jnp.transpose(ah[0].reshape(128, 1152)[:, :ATOMS])
        adv_part = jnp.transpose(ah[1].reshape(128, 1152)[:, PAD:19 * PAD].reshape(128, ACTIONS, PAD)[:, :, :ATOMS], (1, 2, 0)).reshape(ACTIONS * ATOMS, 128)
        head_grad = jnp.concatenate([value_part, adv_part], axis=0)
    else:
        f_got = exchange(lambda p, g: lax.dynamic_slice_in_dim(feats, (p * groups + g) * feat_q, feat_q, axis=0))
        hid = jnp.transpose(hid, (3, 0, 2, 1, 4, 5)).reshape(1024, 128).T
        hid_got = exchange(lambda p, g: lax.dynamic_slice_in_dim(hid.reshape(128, 2, 512), (p * groups + g) * hid_q, hid_q, axis=2))
        dpre = jnp.transpose(msg[:, :, :256].reshape(2, 2, 2, 128, 128), (3, 1, 0, 2, 4)).reshape(128, 1024)
        dz = msg[0, 0, 256:]
        d_all = jnp.concatenate(exchange(lambda p, g: jnp.concatenate([dpre, dz.T, jnp.zeros((128, 72), F32)], axis=1)), axis=0)
        f_all = jnp.concatenate(f_got, axis=1)
        hid_all = jnp.concatenate(hid_got, axis=0)
        part_hidden = jnp.einsum("fb,bsh->sfh", f_all, d_all[:, :1024].reshape(-1, 2, 512), precision=HIGH)
        dz_all = d_all[:, 1024:1024 + ATOMS]
        picked = d_all[:, 1024 + ATOMS]
        mask = jnp.where(picked[None, :] == jnp.arange(ACTIONS, dtype=F32)[:, None], 1.0 - 1.0 / ACTIONS, -1.0 / ACTIONS)
        da = (mask[:, None, :] * dz_all.T[None]).reshape(ACTIONS * ATOMS, -1)
        part_head = jnp.concatenate([jnp.dot(dz_all.T, hid_all[:, 0], precision=HIGH), jnp.dot(da, hid_all[:, 1], precision=HIGH)], axis=0)
        hidden_grad, head_grad = lax.psum((part_hidden, part_head), "rep")
        dh, dl, small_d = lower_backward(net, pre1, pre2, pre3, df, bw2, bw3)
        small_f, lo, up = first_backward(net, x, dh, dl, bw1)
        grad_rows = jnp.where(pair == 0, lo, lax.ppermute(up, "pair", [(0, 1)]))
        total = lax.psum(jnp.concatenate([small_b, small_d, small_f], axis=0), ("pair", "group", "rep"))
        hidden_sigma_grad = hidden_grad * (in_q[:, :, None] * on_out[:, None, :])
    states_grad = jnp.transpose(grad_rows.reshape(84, 84, 2, 128), (3, 2, 0, 1))
    gk1, gb1, gk2, gb2, gk3, gb3 = torso_grads(total)
    hb_grad = total[0:8].reshape(2, 512)
    bo_grad = total[8:17].reshape(-1)[:19 * PAD].reshape(19, PAD)[:, :ATOMS].reshape(-1)
    loss = total[17, 0]
    column_of = jnp.arange(on_eout.shape[0])[:, None]
    head_sigma_grad = head_grad * (jnp.where(column_of < ATOMS, e_q[0:1], e_q[1:2]) * on_eout[:, None])
    return (loss, states_grad, gk1, gb1, gk2, gb2, gk3, gb3, hidden_grad, hidden_sigma_grad,
            hb_grad, hb_grad * on_out, head_grad.T, head_sigma_grad.T, bo_grad, bo_grad * on_eout)


def solution(mesh):
    placed = (
        P("pair", ("group", "rep"), None, None, None),
        P("pair", ("group", "rep")),
        P(("group", "rep"), None),
        P(("group", "rep"), None),
        P(("group", "rep"), None),
        P("pair", None, None, None, None),
        P("pair", None),
        P("pair", None, None, None, None),
        P("pair", None),
        P("pair", None, None, None, None),
        P("pair", None),
        P("pair", None, None, None),
        P("pair", None, None, None),
        P("pair", None, None),
        P("pair", None, None),
        P("pair", None, None),
        P("pair", None, None),
        P("pair", None),
        P("pair", None),
        P("pair", None, None),
        P("pair", None, None),
        P("pair", None, None),
        P("pair", None),
    )
    return jax.shard_map(
        local,
        mesh=mesh,
        in_specs=placed,
        out_specs=(
            P(),
            P(("group", "rep"), "pair", None, None),
            P(),
            P(),
            P(),
            P(),
            P(),
            P(),
            P(None, ("pair", "group"), None),
            P(None, ("pair", "group"), None),
            P(),
            P(),
            P(("pair", "group"), None),
            P(("pair", "group"), None),
            P(),
            P(),
        ),
        check_vma=False,
    )
```

```python
import functools
import jax
import jax.numpy as jnp
from jax import lax
from jax.experimental import pallas as pl
from jax.experimental.pallas import tpu as pltpu
from jax.sharding import PartitionSpec as P

BF = jnp.bfloat16
F32 = jnp.float32
NN=(((1,),(0,)),((),()))
NT=(((1,),(1,)),((),()))
TN=(((0,),(0,)),((),()))

def split(v):
    hi = v.astype(BF)
    return hi, (v - hi.astype(F32)).astype(BF)

def dot(a, b, dims=NN):
    return lax.dot_general(a, b, dims, preferred_element_type=F32)

def dot3(a, b, dims=NN):
    ah, al = a; bh, bl = b
    return dot(ah, bh, dims) + (dot(ah, bl, dims) + dot(al, bh, dims))

def silu(v):
    return v * jax.nn.sigmoid(v)

def prep_kernel(k1_ref, k2_ref, k3_ref, b1_ref, b2_ref, b3_ref, f1_ref, f2_ref, f3_ref, r1_ref, r2_ref, r3_ref, c1_ref, c2_ref, c3_ref,
                t1a, t1b, u1a, u1b, m2, m3, n2, n3):
    for ref in (t1a, t1b, u1a, u1b, m2, m3, n2, n3):
        ref[...] = jnp.zeros_like(ref)
    def put(ref, start, stride, v, lane):
        n = v.shape[0]
        pieces = [jnp.zeros((n, lane), F32)] * (lane > 0) + [v] + [jnp.zeros((n, 96 - lane), F32)] * (lane < 96)
        rows = pl.ds(start, n, stride=stride)
        ref[rows, :] = ref[rows, :] + jnp.concatenate(pieces, axis=1)
    for c in range(4):
        for ky in range(8):
            v = k1_ref[c, ky]
            h, kq = ky // 4, ky % 4
            for w in range(3):
                put((t1a, t1b)[h], kq * 64 + 16 * w + c, 4, v, 32 * w)
            base = (c // 2) * 96 + kq * 24 + c % 2
            for q in range(4):
                if q == 0:
                    put((u1b, u1a)[h], base, 2, v[4:8], 0)
                elif q == 3:
                    put((u1b, u1a)[h], base + 16, 2, v[0:4], 96)
                else:
                    put((u1b, u1a)[h], base + 8 * (q - 1), 2, v, 32 * q)
    for ky in range(4):
        for kx in range(4):
            v = k2_ref[:, ky, kx, :]
            h, py, wx, px = ky // 2, ky % 2, 1 - kx // 2, kx % 2
            m2[py * 128 + kx * 32:py * 128 + kx * 32 + 32, 64 * h:64 * h + 64] = v
            n2[(py * 2 + px) * 32:(py * 2 + px) * 32 + 32, 128 * (1 - h) + 64 * wx:128 * (1 - h) + 64 * wx + 64] = v
    for ky in range(3):
        for kx in range(3):
            v = k3_ref[ky, kx]
            vt = jnp.transpose(v)
            for w in range(2):
                m3[ky * 128 + w * 64:ky * 128 + w * 64 + 64, 64 * (w + kx):64 * (w + kx) + 64] = v
                q = w + 2 - kx
                n3[ky * 128 + w * 64:ky * 128 + w * 64 + 64, 64 * q:64 * q + 64] = vt
    w1 = jnp.concatenate([jnp.transpose(t1a[...])[0:96], jnp.transpose(t1b[...])[0:96]], axis=0)
    pairs = ((f1_ref, w1), (f2_ref, jnp.transpose(m2[...])), (f3_ref, m3[...]), (r1_ref, jnp.concatenate([u1a[...], u1b[...]], axis=1)), (r2_ref, n2[...]), (r3_ref, n3[...]))
    for ref, v in pairs:
        hi, lo = split(v)
        ref[0] = hi
        ref[1] = lo
    for ref, b_ref, n, times in ((c1_ref, b1_ref, 32, 3), (c2_ref, b2_ref, 64, 1), (c3_ref, b3_ref, 64, 1)):
        col = jnp.transpose(jnp.broadcast_to(b_ref[...], (128, n)))
        for i in range(times):
            ref[n * i:n * i + n, :] = col

def prepare(k1, k2, k3, b1, b2, b3):
    vm = pl.BlockSpec(memory_space=pltpu.VMEM)
    bfs = lambda *s: jax.ShapeDtypeStruct(s, BF)
    sds = lambda *s: jax.ShapeDtypeStruct(s, F32)
    f32 = lambda *s: pltpu.VMEM(s, F32)
    return pl.pallas_call(
        prep_kernel, in_specs=[vm] * 6, out_specs=[vm] * 9,
        out_shape=[bfs(2, 192, 256), bfs(2, 128, 256), bfs(2, 384, 256), bfs(2, 192, 256), bfs(2, 128, 256), bfs(2, 384, 256), sds(96, 128), sds(64, 128), sds(64, 128)],
        scratch_shapes=[f32(256, 128), f32(256, 128), f32(192, 128), f32(192, 128), f32(256, 128), f32(384, 256), f32(128, 256), f32(384, 256)],
        compiler_params=pltpu.CompilerParams(vmem_limit_bytes=60 * 2**20),
    )(jnp.transpose(k1, (1, 2, 3, 0)), jnp.transpose(k2, (1, 2, 3, 0)), jnp.transpose(k3, (2, 3, 0, 1)), b1, b2, b3)

def fwd_kernel(x_ref, w1_ref, w2_ref, w3_ref, b1_ref, b2_ref, b3_ref, pre1_ref, pre2_ref, pre3_ref, f_ref,
               xh, xl, top1, top2, acc3, h1h, h1l, h2h, h2l):
    j = pl.program_id(0)
    @pl.when(j == 0)
    def _():
        xh[:, 336:, :] = jnp.zeros((4, 16, 128), BF)
        xl[:, 336:, :] = jnp.zeros((4, 16, 128), BF)
        top1[...] = jnp.zeros_like(top1)
        top2[...] = jnp.zeros_like(top2)
        acc3[...] = jnp.zeros_like(acc3)
        h2h[:, 576:, :] = jnp.zeros((9, 64, 128), BF)
        h2l[:, 576:, :] = jnp.zeros((9, 64, 128), BF)
    v = x_ref[...]
    hi = v.astype(BF)
    xh[:, 0:336, :] = hi
    xl[:, 0:336, :] = (v - hi.astype(F32)).astype(BF)
    rh = jnp.concatenate([xh[:, 48 * i:48 * i + 64, :].reshape(256, 128) for i in range(7)], axis=1)
    rl = jnp.concatenate([xl[:, 48 * i:48 * i + 64, :].reshape(256, 128) for i in range(7)], axis=1)
    r = dot3((w1_ref[0], w1_ref[1]), (rh, rl))
    out = top1[...] + r[96:]
    top1[...] = r[:96]
    b1 = b1_ref[...]
    row = jnp.maximum(j - 1, 0)
    for i in range(7):
        n = 96 if i < 6 else 64
        p = out[:n, 128 * i:128 * i + 128] + b1[:n]
        pre1_ref[0, 96 * i:96 * i + n, :] = p
        hh, hl = split(silu(p))
        h1h[row, 96 * i:96 * i + n, :] = hh
        h1l[row, 96 * i:96 * i + n, :] = hl

    @pl.when(j == pl.num_programs(0) - 1)
    def _():
        w2 = (w2_ref[0], w2_ref[1])
        b2 = b2_ref[...]
        def step2(y, carry):
            rh = jnp.concatenate([h1h[pl.ds(2 * y, 2), 64 * i:64 * i + 128, :].reshape(256, 128) for i in range(9)], axis=1)
            rl = jnp.concatenate([h1l[pl.ds(2 * y, 2), 64 * i:64 * i + 128, :].reshape(256, 128) for i in range(9)], axis=1)
            r = dot3(w2, (rh, rl))
            o = top2[...] + r[64:]
            top2[...] = r[:64]
            row = jnp.maximum(y - 1, 0)
            for i in range(9):
                p = o[:, 128 * i:128 * i + 128] + b2
                pre2_ref[row, 64 * i:64 * i + 64, :] = p
                hh, hl = split(silu(p))
                h2h[row, 64 * i:64 * i + 64, :] = hh
                h2l[row, 64 * i:64 * i + 64, :] = hl
            return carry
        lax.fori_loop(0, 10, step2, 0)
        w3 = (w3_ref[0], w3_ref[1])
        b3 = b3_ref[...]
        def step3(y, carry):
            rh = jnp.concatenate([h2h[y, 128 * i:128 * i + 256, :] for i in range(4)], axis=1)
            rl = jnp.concatenate([h2l[y, 128 * i:128 * i + 256, :] for i in range(4)], axis=1)
            r = dot3(w3, (rh, rl))
            for ky in range(3):
                for i in range(4):
                    acc3[y - ky + 2, 128 * i:128 * i + 128, :] += r[128 * ky:128 * ky + 128, 128 * i:128 * i + 128]
            return carry
        lax.fori_loop(0, 9, step3, 0)
        for y in range(7):
            for x in range(7):
                p = acc3[y + 2, 64 * x:64 * x + 64, :] + b3
                pre3_ref[pl.ds(y * 7 + x, 64, stride=49), :] = p
                f_ref[pl.ds(y * 7 + x, 64, stride=49), :] = silu(p)

def forward(x, w1, w2, w3, b1, b2, b3):
    full = lambda *s: pl.BlockSpec(s, lambda j: (0,) * len(s))
    return pl.pallas_call(
        fwd_kernel,
        grid=(21,),
        in_specs=[pl.BlockSpec((4, 336, 128), lambda j: (j, 0, 0)), full(2, 192, 256), full(2, 128, 256), full(2, 384, 256),
                  full(96, 128), full(64, 128), full(64, 128)],
        out_specs=[pl.BlockSpec((1, 640, 128), lambda j: (jnp.maximum(j - 1, 0), 0, 0)), full(9, 576, 128),
                   full(3136, 128), full(3136, 128)],
        out_shape=[jax.ShapeDtypeStruct((20, 640, 128), F32), jax.ShapeDtypeStruct((9, 576, 128), F32),
                   jax.ShapeDtypeStruct((3136, 128), F32), jax.ShapeDtypeStruct((3136, 128), F32)],
        scratch_shapes=[pltpu.VMEM((4, 352, 128), BF), pltpu.VMEM((4, 352, 128), BF),
                        pltpu.VMEM((96, 896), F32), pltpu.VMEM((64, 1152), F32), pltpu.VMEM((11, 512, 128), F32),
                        pltpu.VMEM((20, 640, 128), BF), pltpu.VMEM((20, 640, 128), BF),
                        pltpu.VMEM((9, 640, 128), BF), pltpu.VMEM((9, 640, 128), BF)],
        compiler_params=pltpu.CompilerParams(vmem_limit_bytes=60 * 2**20),
    )(x, w1, w2, w3, b1, b2, b3)


MESH_ID = pl.DeviceIdType.MESH


def coords():
    r = lax.axis_index("rep")
    return lax.axis_index("pair"), lax.axis_index("group"), r // 2, r % 2


def at(p, g, z, y):
    return (p, g, z * 2 + y)


def flip(z, k):
    return (z, z + 1 - 2 * (z % 2), z + 2 - 4 * (z // 2), 3 - z)[k]


def line(p, g, z, y):
    return [at(q, g, flip(z, k), y) for k in range(4) for q in ((p, 1 - p) if k else (1 - p,))]


def plane(p, g, z, y):
    return [at(p, g, z, 1 - y), at(p, 1 - g, z, y), at(p, 1 - g, z, 1 - y)]


def greet(devices):
    barrier = pltpu.get_barrier_semaphore()
    for device in devices:
        pl.semaphore_signal(barrier, inc=1, device_id=device, device_id_type=MESH_ID)
    pl.semaphore_wait(barrier, len(devices))


def remote(src, dst, send, recv, device):
    return pltpu.make_async_remote_copy(src_ref=src, dst_ref=dst, send_sem=send, recv_sem=recv, device_id=device, device_id_type=MESH_ID)


class Scatter:
    def __init__(self, parts, src, dst, send, recv, own, cores=2):
        self.parts, self.src, self.dst, self.send, self.recv, self.own, self.cores = parts, src, dst, send, recv, own, cores
        self.p, self.g, self.z, self.y = coords()

    def copies(self):
        for k in range(4):
            for q in range(self.cores):
                for i in range(self.parts):
                    zd = flip(self.z, k)
                    if k == 0 and q == 0:
                        yield pltpu.make_async_copy(self.src(q, zd, i), self.dst(self.z, i), self.own.at[i]), True
                    else:
                        yield remote(self.src(q, zd, i), self.dst(self.z, i), self.send.at[k * 2 + q, i], self.recv.at[k, i], at(q, self.g, zd, self.y)), False

    def start(self):
        @pl.when(self.p == 0)
        def _():
            for copy, own in self.copies():
                copy.start()

    def arrived(self, k):
        if self.cores == 1:
            pl.when(self.p == 0)(lambda: self.landed(k))
        else:
            self.landed(k)

    def landed(self, k):
        for i in range(self.parts):
            zs = flip(self.z, k)
            wait = remote(self.src(0, zs, i), self.dst(zs, i), self.send.at[0, i], self.recv.at[k, i], at(1 - self.p, self.g, self.z, self.y)).wait_recv
            local = pltpu.make_async_copy(self.src(0, zs, i), self.dst(zs, i), self.own.at[i]).wait
            if k:
                wait()
            elif self.cores == 1:
                local()
            else:
                pl.when(self.p == 1)(wait)
                pl.when(self.p == 0)(local)

    def sent(self):
        @pl.when(self.p == 0)
        def _():
            for copy, own in self.copies():
                if not own:
                    copy.wait_send()


def scatter_sems(parts):
    return [pltpu.SemaphoreType.DMA((8, parts)), pltpu.SemaphoreType.DMA((4, parts)), pltpu.SemaphoreType.DMA((parts,))]


def f_scatter(f_ref, f1_ref, sems):
    def src(q, zd, i):
        return f_ref.at[pl.ds(pl.multiple_of((2 * q + i) * 784 + jnp.minimum(200 * zd, 584), 8), 200)]
    return Scatter(2, src, lambda z, i: f1_ref.at[i, z], *sems)


def g_scatter(hid_ref, g1_ref, sems):
    return Scatter(1, lambda q, zd, i: hid_ref.at[q, zd], lambda z, i: g1_ref.at[z], *sems)


def d_scatter(msg_ref, d1_ref, sems):
    return Scatter(1, lambda q, zd, i: msg_ref.at[q], lambda z, i: d1_ref.at[z], *sems)


def z_scatter(dz_ref, dz1_ref, sems):
    return Scatter(1, lambda q, zd, i: dz_ref, lambda z, i: dz1_ref.at[z], *sems, cores=1)


def spread_plane(p, g, z, y, src, dst, send, recv):
    places = [(g, y), (g, 1 - y), (1 - g, y), (1 - g, 1 - y)]
    out = [pltpu.make_async_copy(src(*places[0]), dst(0), send.at[0])]
    for m in range(1, 4):
        out.append(remote(src(*places[m]), dst(m), send.at[m], recv.at[m], at(p, places[m][0], z, places[m][1])))
    return out
ATOMS, ACTIONS, PAD = 51, 18, 56
OUTS, OUTP = 969, 976
STEPS = 7
ANY = pl.BlockSpec(memory_space=pl.ANY)
VMEM = pl.BlockSpec(memory_space=pltpu.VMEM)

def column(row, lanes):
    tall = jnp.transpose(jnp.broadcast_to(row, (128, row.shape[1])))
    return jnp.concatenate([tall] * (lanes // 128), axis=1)

def noisy(mean_ref, sigma_ref, nin_ref, nout_ref, s):
    return mean_ref[s] + sigma_ref[s] * (column(nin_ref[0, s:s + 1, :], 512) * nout_ref[s:s + 1, :])

def mask_of(chosen, a):
    return jnp.where(chosen == a, 1.0 - 1.0 / ACTIONS, -1.0 / ACTIONS)

def hid_kernel(net, f_ref, m_ref, s_ref, nin_ref, nout_ref, hb_ref, wo_ref, bo_ref, c_ref, pl_ref, pw_ref, *rest):
    if net:
        f_all, h_ref, g_ref, logp_ref, dist_ref, f1_ref, acc, adv = rest[:8]
        wire = f_scatter(f_all, f1_ref, rest[8:])
    else:
        h_ref, g_ref, logp_ref, dist_ref, acc, adv = rest
    j = pl.program_id(0)
    @pl.when(j == 0)
    def _():
        if net:
            greet(line(*coords()))
            wire.start()
        acc[...] = jnp.zeros_like(acc)
    f = split(f_ref[...])
    for s in range(2):
        w = split(noisy(m_ref, s_ref, nin_ref, nout_ref, s))
        acc[:, 512 * s:512 * s + 512] += dot3(f, w, TN)
    @pl.when(j == pl.num_programs(0) - 1)
    def _():
        h = acc[...] + hb_ref[...]
        h_ref[...] = h
        gt = jnp.transpose(silu(h))
        for s in range(2):
            for q in range(2):
                for gg in range(2):
                    for z in range(4):
                        at_row = 512 * s + 256 * q + 128 * gg + 32 * z
                        g_ref[q, z, gg, s] = gt[at_row:at_row + 32]
        both = dot3(split(wo_ref[...]), split(jnp.concatenate([gt[:512], gt[512:]], axis=1)))
        bias = column(bo_ref[...], 128)
        adv[...] = both[:, 128:] + bias
        z = both[0:PAD, 0:128] + bias[0:PAD]
        chosen = c_ref[...]
        for i in range(ACTIONS):
            z = z + mask_of(chosen, i) * adv[ATOMS * (i + 1):ATOMS * (i + 1) + PAD, :]
        row = lax.broadcasted_iota(jnp.int32, (PAD, 128), 0)
        z = jnp.where(row < ATOMS, z, -1e30)
        top = jnp.max(z, axis=0, keepdims=True)
        e = jnp.exp(z - top)
        tot = jnp.sum(e, axis=0, keepdims=True)
        logp_ref[...] = (z - top) - jnp.log(tot)
        p = e / tot
        dist = jnp.zeros((PAD, 128), F32)
        for i in range(ATOMS):
            lower = pl_ref[i:i + 1, :]
            share = pw_ref[i:i + 1, :]
            pi = p[i:i + 1, :]
            dist = dist + jnp.where(row == lower, pi * (1.0 - share), 0.0) + jnp.where(row == lower + 1, pi * share, 0.0)
        dist_ref[...] = dist
        if net:
            for k in range(4):
                wire.arrived(k)
            wire.sent()

def hidden(net, f, m, s, nin, nout, hb, wo, bo, c, plow, pw):
    full = lambda *t: pl.BlockSpec(t, lambda j: (0,) * len(t))
    sds = lambda *t: jax.ShapeDtypeStruct(t, F32)
    k = 3136 // STEPS
    wspec = pl.BlockSpec((2, k, 512), lambda j: (0, j, 0))
    return pl.pallas_call(
        functools.partial(hid_kernel, net), grid=(STEPS,),
        in_specs=[pl.BlockSpec((k, 128), lambda j: (j, 0)), wspec, wspec, pl.BlockSpec((1, 2, k), lambda j: (j, 0, 0)), full(2, 512), full(1, 1024),
                  full(OUTP, 512), full(1, OUTP), full(1, 128), full(ATOMS, 128), full(ATOMS, 128)] + [ANY] * net,
        out_specs=[full(128, 1024), full(2, 4, 2, 2, 32, 128), full(PAD, 128), full(PAD, 128)] + [ANY] * net,
        out_shape=[sds(128, 1024), sds(2, 4, 2, 2, 32, 128), sds(PAD, 128), sds(PAD, 128)] + [sds(2, 4, 200, 128)] * net,
        scratch_shapes=[pltpu.VMEM((128, 1024), F32), pltpu.VMEM((OUTP, 128), F32)] + scatter_sems(2) * net,
        compiler_params=pltpu.CompilerParams(vmem_limit_bytes=60 * 2**20, **(dict(collective_id=1, has_side_effects=True) if net else {})),
    )(f, m, s, nin, nout, hb, wo, bo, c, plow, pw, *([f] * net))

def hid_bwd_kernel(net, t_ref, logp_ref, h_ref, m_ref, s_ref, nin_ref, nout_ref, wo_ref, c_ref, *rest):
    if net:
        f1_ref, hid_ref, df_ref, small_ref, f2_ref, g1_ref, d1_ref, dz1_ref, dth, dtl, da, msg, dz_to, t_got, fs, fr, ts, tr = rest[:18]
        g_wire = g_scatter(hid_ref, g1_ref, rest[18:21])
        d_wire = d_scatter(msg, d1_ref, rest[21:24])
        z_wire = z_scatter(dz_to, dz1_ref, rest[24:27])
        wires = (g_wire, d_wire, z_wire)
        p, g, z, y = coords()
        fan = spread_plane(p, g, z, y, lambda gd, yd: f1_ref.at[gd], lambda m: f2_ref.at[m], fs, fr)
        target = remote(t_ref, t_got, ts, tr, at(1 - p, g, z, y))
    else:
        df_ref, small_ref, msg, dz_to, dth, dtl, da = rest
        t_got = t_ref
    j = pl.program_id(0)
    def begin():
        t = t_got[...]
        logp = logp_ref[...]
        chosen = c_ref[...]
        row = lax.broadcasted_iota(jnp.int32, (PAD, 128), 0)
        d = (jnp.exp(logp) * jnp.sum(t, axis=0, keepdims=True) - t) * (1.0 / 128)
        loss = -jnp.sum(jnp.where(row < ATOMS, t * logp, 0.0), axis=1, keepdims=True) * (1.0 / 128)
        dz_to[...] = jnp.where(row == ATOMS, chosen.astype(F32), d)
        da[...] = jnp.zeros_like(da)
        da[0:PAD, 0:128] = d
        for i in range(ACTIONS):
            da[ATOMS * (i + 1):ATOMS * (i + 1) + PAD, 128:256] = mask_of(chosen, i) * d
        every = da[...]
        eh, el = split(every)
        grads = dot3((eh, el), split(wo_ref[...]), TN)
        small_ref[...] = jnp.zeros_like(small_ref)
        for s in range(2):
            dp = grads[128 * s:128 * s + 128] * dsilu(h_ref[:, 512 * s:512 * s + 512])
            total = jnp.sum(dp, axis=0, keepdims=True)
            for c in range(4):
                msg[c // 2, s, 128 * (c % 2):128 * (c % 2) + 128, :] = dp[:, 128 * c:128 * c + 128]
                small_ref[4 * s + c:4 * s + c + 1, :] = total[:, 128 * c:128 * c + 128]
            hi, lo = split(jnp.transpose(dp))
            dth[s] = hi
            dtl[s] = lo
        if net:
            d_wire.start()
            z_wire.start()
        ones = jnp.ones((8, 256), BF)
        left = (every - eh.astype(F32)) - el.astype(F32)
        rows = dot(ones, eh, NT) + dot(ones, el, NT) + dot(ones, left.astype(BF), NT)
        for c in range(8):
            n = min(128, OUTP - 128 * c)
            small_ref[8 + c:9 + c, 0:n] = rows[0:1, 128 * c:128 * c + n]
        small_ref[16:17, :] = jnp.broadcast_to(jnp.sum(loss, axis=0, keepdims=True), (1, 128))
    def step():
        out = None
        for s in range(2):
            w = split(noisy(m_ref, s_ref, nin_ref, nout_ref, s))
            r = dot3(w, (dth[s], dtl[s]))
            out = r if out is None else out + r
        df_ref[...] = out
    if not net:
        pl.when(j == 0)(begin)
        step()
        return
    @pl.when(j == 0)
    def _():
        greet(line(p, g, z, y) + plane(p, g, z, y))
        pl.when(p == 1)(target.start)
        for copy in fan:
            copy.start()
        g_wire.start()
        @pl.when(p == 0)
        def _():
            target.wait_recv()
            begin()
    pl.when(p == 0)(step)
    @pl.when(j == pl.num_programs(0) - 1)
    def _():
        pl.when(p == 1)(target.wait_send)
        for copy in fan:
            copy.wait()
        for wire in wires:
            for k in range(4):
                wire.arrived(k)
            wire.sent()

def hidden_bwd(net, t, logp, h, m, s, nin, nout, wo, c, *wired):
    full = lambda *u: pl.BlockSpec(u, lambda j: (0,) * len(u))
    sds = lambda *u: jax.ShapeDtypeStruct(u, F32)
    dma = pltpu.SemaphoreType.DMA
    k = 3136 // STEPS
    wspec = pl.BlockSpec((2, k, 512), lambda j: (0, j, 0))
    return pl.pallas_call(
        functools.partial(hid_bwd_kernel, net), grid=(STEPS,),
        in_specs=[full(PAD, 128), full(PAD, 128), full(128, 1024), wspec, wspec, pl.BlockSpec((1, 2, k), lambda j: (j, 0, 0)), full(2, 512),
                  full(OUTP, 512), full(1, 128)] + [ANY, ANY] * net,
        out_specs=[pl.BlockSpec((k, 128), lambda j: (j, 0)), full(24, 128)] + ([ANY] * 4 if net else [full(2, 2, 256, 128), full(PAD, 128)]),
        out_shape=[sds(3136, 128), sds(24, 128)] + ([sds(4, 4, 200, 128), sds(4, 2, 2, 32, 128), sds(4, 2, 256, 128), sds(4, PAD, 128)] if net
                                                    else [sds(2, 2, 256, 128), sds(PAD, 128)]),
        scratch_shapes=[pltpu.VMEM((2, 512, 128), BF), pltpu.VMEM((2, 512, 128), BF), pltpu.VMEM((OUTP, 256), F32)]
        + ([pltpu.VMEM((2, 2, 256, 128), F32), pltpu.VMEM((PAD, 128), F32), pltpu.VMEM((PAD, 128), F32), dma((4,)), dma((4,)), dma, dma]
           + scatter_sems(1) * 3) * net,
        compiler_params=pltpu.CompilerParams(vmem_limit_bytes=60 * 2**20, **(dict(collective_id=2, has_side_effects=True) if net else {})),
    )(t, logp, h, m, s, nin, nout, wo, c, *wired)

def dsilu(v):
    s = jax.nn.sigmoid(v)
    return s * (1.0 + v * (1.0 - s))

def low_kernel(net, pre1_ref, pre2_ref, pre3_ref, df_ref, w2_ref, w3_ref, *rest):
    if net:
        d1_ref, g1_ref, dz1_ref, d1h, d1l, small_ref, d2_ref, d3_ref, g2_ref, dz2_ref = rest[:10]
        d3f, d3h, d3l, d2h, d2l, h2h, h2l, acc2, a2, a3 = rest[10:20]
        ps, pr, gs, gr, qs, qr, ss, sr, ts, tr = rest[20:]
        p, g, z, y = coords()
        greet(plane(p, g, z, y) + [at(1 - p, g, z, y)])
        fan_d = spread_plane(p, g, z, y, lambda gd, yd: d1_ref.at[:, yd], lambda m: d2_ref.at[m], ps, pr)
        fan_g = spread_plane(p, g, z, y, lambda gd, yd: g1_ref.at[:, gd, yd], lambda m: g2_ref.at[m], gs, gr)
        fan_z = spread_plane(p, g, z, y, lambda gd, yd: dz1_ref, lambda m: dz2_ref.at[m], qs, qr)
        swaps = [remote(d2_ref.at[m], d3_ref.at[m], ss.at[m], sr.at[m], at(1 - p, g, z, y)) for m in range(4)]
        hand = remote(dz2_ref, dz2_ref, ts, tr, at(1 - p, g, z, y))
        for copy in fan_d + fan_g:
            copy.start()
        @pl.when(p == 0)
        def _():
            for copy in fan_z:
                copy.start()
        fan_d[0].wait()
        swaps[0].start()
    else:
        d1h, d1l, small_ref, d3f, d3h, d3l, d2h, d2l, h2h, h2l, acc2, a2, a3 = rest
    def upper():
        for ref in (d3h, d3l, d2h, d2l, acc2, a2, a3):
            ref[...] = jnp.zeros_like(ref)
        small_ref[...] = jnp.zeros_like(small_ref)
        for ref in (d1h, d1l):
            ref[0] = jnp.zeros((704, 128), BF)
            ref[21] = jnp.zeros((704, 128), BF)
            ref[:, 0:32, :] = jnp.zeros((22, 32, 128), BF)
            ref[:, 672:704, :] = jnp.zeros((22, 32, 128), BF)
        d3f[...] = df_ref[...] * dsilu(pre3_ref[...])
        total = jnp.zeros((64, 128), F32)
        for y in range(7):
            for x in range(7):
                d = d3f[pl.ds(y * 7 + x, 64, stride=49), :]
                total = total + d
                hi, lo = split(d)
                d3h[y + 2, 64 * (x + 2):64 * (x + 3), :] = hi
                d3l[y + 2, 64 * (x + 2):64 * (x + 3), :] = lo
        small_ref[640:641, 0:64] = jnp.sum(jnp.transpose(total), axis=0, keepdims=True)
        w3 = (w3_ref[0], w3_ref[1])
        h2h[:, 576:, :] = jnp.zeros((9, 64, 128), BF)
        h2l[:, 576:, :] = jnp.zeros((9, 64, 128), BF)
        def split2(y, c):
            hi, lo = split(silu(pre2_ref[y]))
            h2h[y, 0:576, :] = hi
            h2l[y, 0:576, :] = lo
            return c
        lax.fori_loop(0, 9, split2, 0)
        def dgrad3(y, c):
            rh = jnp.concatenate([d3h[y + 2, 128 * i:128 * i + 256, :] for i in range(5)], axis=1)
            rl = jnp.concatenate([d3l[y + 2, 128 * i:128 * i + 256, :] for i in range(5)], axis=1)
            r = dot3(w3, (rh, rl))
            for ky in range(3):
                for i in range(5):
                    acc2[y + ky, 128 * i:128 * i + 128, :] += r[128 * ky:128 * ky + 128, 128 * i:128 * i + 128]
            return c
        lax.fori_loop(0, 7, dgrad3, 0)
        def wgrad3(y, c):
            def lhs(ref):
                return jnp.concatenate([jnp.concatenate([ref[y - ky + 2, 128 * (i + 1):128 * (i + 2), :] for i in range(4)], axis=1) for ky in range(3)], axis=0)
            def rhs(ref):
                return jnp.concatenate([ref[y, 128 * i:128 * i + 256, :] for i in range(4)], axis=1)
            a3[...] += dot3((lhs(d3h), lhs(d3l)), (rhs(h2h), rhs(h2l)), NT)
            return c
        lax.fori_loop(0, 9, wgrad3, 0)
        for ky in range(3):
            grad = a3[128 * ky:128 * ky + 64, 0:192] + a3[128 * ky + 64:128 * ky + 128, 64:256]
            small_ref[256 + 64 * ky:320 + 64 * ky, :] = grad[:, 0:128]
            small_ref[448 + 64 * ky:512 + 64 * ky, 0:64] = grad[:, 128:192]
        def step2(y, total):
            for x in range(9):
                d = acc2[y, 64 * x:64 * x + 64, :] * dsilu(pre2_ref[y, 64 * x:64 * x + 64, :])
                total = total + d
                hi, lo = split(d)
                d2h[y + 1, 64 * (x + 1):64 * (x + 2), :] = hi
                d2l[y + 1, 64 * (x + 1):64 * (x + 2), :] = lo
            return total
        total = lax.fori_loop(0, 9, step2, jnp.zeros((64, 128), F32))
        small_ref[641:642, 0:64] = jnp.sum(jnp.transpose(total), axis=0, keepdims=True)
    def block2(y, total):
        w2 = (w2_ref[0], w2_ref[1])
        rh = jnp.concatenate([d2h[pl.ds(y, 2), 64 * i:64 * i + 128, :].reshape(256, 128) for i in range(10)], axis=1)
        rl = jnp.concatenate([d2l[pl.ds(y, 2), 64 * i:64 * i + 128, :].reshape(256, 128) for i in range(10)], axis=1)
        r = dot3(w2, (rh, rl))
        h1h, h1l = [], []
        for py in range(2):
            rowh, rowl = [], []
            for i in range(10):
                v = pre1_ref[2 * y + py, 64 * i:64 * i + 64, :]
                s = jax.nn.sigmoid(v)
                d = r[64 * py:64 * py + 64, 128 * i:128 * i + 128] * (s * (1.0 + v * (1.0 - s)))
                total = total + d[0:32] + d[32:64]
                hi, lo = split(d)
                d1h[2 * y + py + 1, 64 * i + 32:64 * i + 96, :] = hi
                d1l[2 * y + py + 1, 64 * i + 32:64 * i + 96, :] = lo
                hi, lo = split(v * s)
                rowh.append(hi)
                rowl.append(lo)
            h1h.append(rowh)
            h1l.append(rowl)
        def lhs(ref):
            return jnp.concatenate([jnp.concatenate([ref[y + 1 - h, 64 * (i + 1):64 * (i + 2), :] for i in range(9)], axis=1) for h in range(2)], axis=0)
        def rhs(rows):
            return jnp.concatenate([jnp.concatenate([rows[0][i], rows[0][i + 1], rows[1][i], rows[1][i + 1]], axis=0) for i in range(9)], axis=1)
        a2[...] += dot3((lhs(d2h), lhs(d2l)), (rhs(h1h), rhs(h1l)), NT)
        return total
    def lower():
        total = lax.fori_loop(0, 10, block2, jnp.zeros((32, 128), F32))
        small_ref[642:643, 0:32] = jnp.sum(jnp.transpose(total), axis=0, keepdims=True)
        small_ref[0:128, :] = a2[:, 0:128]
        small_ref[128:256, :] = a2[:, 128:256]
    if not net:
        upper()
        lower()
        return
    @pl.when(p == 0)
    def _():
        upper()
        lower()
    for m in range(1, 4):
        fan_d[m].wait_recv()
        swaps[m].start()
    @pl.when(p == 0)
    def _():
        for copy in fan_z:
            copy.wait()
        hand.start()
        hand.wait_send()
    pl.when(p == 1)(hand.wait_recv)
    for copy in fan_g:
        copy.wait()
    for m in range(1, 4):
        fan_d[m].wait_send()
    for swap in swaps:
        swap.wait()

def lower_backward(net, pre1, pre2, pre3, df, w2, w3, *wired):
    one = lambda *s: pl.BlockSpec(s, lambda j: (0,) * len(s), pipeline_mode=pl.Buffered(1))
    sds = lambda *s: jax.ShapeDtypeStruct(s, F32)
    bfs = lambda *s: jax.ShapeDtypeStruct(s, BF)
    vmb = lambda *s: pltpu.VMEM(s, BF)
    dma = pltpu.SemaphoreType.DMA
    return pl.pallas_call(
        functools.partial(low_kernel, net),
        grid=(1,),
        in_specs=[one(20, 640, 128), one(9, 576, 128), one(3136, 128), one(3136, 128), one(2, 128, 256), one(2, 384, 256)] + [ANY] * (3 * net),
        out_specs=[one(22, 704, 128), one(22, 704, 128), one(648, 128)] + [ANY] * (4 * net),
        out_shape=[bfs(22, 704, 128), bfs(22, 704, 128), sds(648, 128)]
        + [sds(4, 4, 256, 128), sds(4, 4, 256, 128), sds(4, 4, 32, 128), sds(4, 4, PAD, 128)] * net,
        scratch_shapes=[pltpu.VMEM((3136, 128), F32), vmb(11, 768, 128), vmb(11, 768, 128), vmb(11, 704, 128), vmb(11, 704, 128),
                        vmb(9, 640, 128), vmb(9, 640, 128), pltpu.VMEM((9, 640, 128), F32), pltpu.VMEM((128, 256), F32), pltpu.VMEM((384, 256), F32)]
        + ([dma((4,))] * 8 + [dma, dma]) * net,
        compiler_params=pltpu.CompilerParams(vmem_limit_bytes=60 * 2**20, **(dict(collective_id=3, has_side_effects=True) if net else {})),
    )(pre1, pre2, pre3, df, w2, w3, *wired)

def first_kernel_bwd(net, x_ref, dha_ref, dhb_ref, dla_ref, dlb_ref, w1_ref, *rest):
    if net:
        r_ref, q_ref, s0_ref, s1_ref, tot_ref, sg_ref, ag_ref, ah_ref, xh, xl, a1, lob, upb, pay, got, red, tot, ls, us, ur, zs_, zr, ys, yr, own = rest[:25]
        as_, ar, bs, br, cs, cr, one_ = rest[25:]
        p, g, z, y = coords()
        reps = lax.axis_size("rep")
        chips = 2 * reps
        me = g * reps + lax.axis_index("rep")
        size = ROWS // chips
        def chip(i):
            return (0, i // reps, i % reps)
        def part(i):
            return pl.ds(pl.multiple_of(i * size, 8), size)
        def give(k):
            to = (me + k) % chips
            if k:
                return remote(pay.at[part(to)], got.at[me], as_.at[k], ar.at[k], chip(to))
            return pltpu.make_async_copy(pay.at[part(me)], got.at[me], one_)
        def given(k):
            who = (me + chips - k) % chips
            return remote(pay.at[part(me)], got.at[who], as_.at[k], ar.at[k], chip(who))
        def tell(k):
            return remote(red, tot.at[part(me)], bs.at[k], br.at[k], chip((me + k) % chips))
        def told(k):
            who = (me + chips - k) % chips
            return remote(red, tot.at[part(who)], bs.at[k], br.at[k], chip(who))
        hand = remote(tot, tot, cs, cr, at(1 - p, g, z, y))
        small_ref = pay.at[pl.ds(672, 64)]
        def rows_of(zz):
            return pl.ds(pl.multiple_of(32 * zz, 8), 32)
        def head_at(yy, zz):
            return ah_ref.at[pl.ds(yy, 1 + 7 * yy), rows_of(zz)]
        def along_z(k, yy):
            to = at(p, g, flip(z, k), y)
            a, b = (r_ref, ag_ref.at[yy, z]), (q_ref.at[pl.ds(yy, 1 + 7 * yy)], head_at(yy, z))
            if k:
                return [remote(*a, zs_.at[k, 0], zr.at[k, 0], to), remote(*b, zs_.at[k, 1], zr.at[k, 1], to)]
            return [pltpu.make_async_copy(*a, own.at[0]), pltpu.make_async_copy(*b, own.at[1])]
        def along_y(k, yy):
            zs = flip(z, k)
            a, b = (ag_ref.at[yy, zs], head_at(yy, zs)) if k else (r_ref, q_ref.at[pl.ds(yy, 1 + 7 * yy)])
            to = at(p, g, z, 1 - y)
            return [remote(a, ag_ref.at[yy, zs], ys.at[k, 0], yr.at[k, 0], to), remote(b, head_at(yy, zs), ys.at[k, 1], yr.at[k, 1], to)]
        def each(do, flipped=False):
            for yy in range(2):
                pl.when(y == (1 - yy if flipped else yy))(functools.partial(do, yy))
        def states_out(j, slot):
            return (pltpu.make_async_copy(lob.at[slot], sg_ref.at[pl.ds(4 * j, 4)], ls.at[slot]),
                    remote(upb.at[slot], sg_ref.at[pl.ds(4 * j, 4)], us.at[slot], ur.at[j], at(1 - p, g, z, y)))
    else:
        small_ref, lo_ref, up_ref, xh, xl, a1 = rest
    j = pl.program_id(0)
    last = pl.num_programs(0) - 1
    @pl.when(j == 0)
    def _():
        if net:
            pl.when(p == 0)(lambda: greet([chip((me + k) % chips) for k in range(1, chips)] + [at(1, g, z, y)]))
            pl.when(p == 1)(lambda: greet([at(1, g, flip(z, k), y) for k in range(1, 4)] + [at(1, g, z, 1 - y), at(0, g, z, y)]))
            pay[0:24, :] = s0_ref[...]
            pay[24:672, :] = s1_ref[...]
            pay[736:, :] = jnp.zeros((ROWS - 736, 128), F32)
            def begin(yy):
                for copy in along_z(1, yy) + along_y(0, yy) + along_z(2, yy) + along_z(3, yy) + along_z(0, yy):
                    copy.start()
            each(begin)
        xh[:, 336:, :] = jnp.zeros((4, 16, 128), BF)
        xl[:, 336:, :] = jnp.zeros((4, 16, 128), BF)
        a1[...] = jnp.zeros_like(a1)
    def work():
        v = x_ref[...]
        hi = v.astype(BF)
        xh[:, 0:336, :] = hi
        xl[:, 0:336, :] = (v - hi.astype(F32)).astype(BF)
        def both(a, b):
            return jnp.concatenate([jnp.concatenate([a[0, 96 * i:96 * i + 128, :], b[0, 96 * i:96 * i + 128, :]], axis=0) for i in range(7)], axis=1)
        r = dot3((w1_ref[0], w1_ref[1]), (both(dha_ref, dhb_ref), both(dla_ref, dlb_ref)))
        if net:
            slot = j % 2
            @pl.when(j >= 2)
            def _():
                a, b = states_out(j - 2, slot)
                a.wait()
                b.wait_send()
            lo_to, up_to = lob.at[slot], upb.at[slot]
        else:
            lo_to, up_to = lo_ref, up_ref
        for ky in range(4):
            for i in range(7):
                lo_to[ky, 24 * i:24 * i + 24, :] = r[24 * ky:24 * ky + 24, 128 * i:128 * i + 128]
                up_to[ky, 24 * i:24 * i + 24, :] = r[96 + 24 * ky:96 + 24 * ky + 24, 128 * i:128 * i + 128]
        if net:
            for copy in states_out(j, slot):
                copy.start()
        def lhs(a, b):
            return jnp.concatenate([jnp.concatenate([ref[0, 96 * i + 32:96 * i + 128, :] for i in range(7)], axis=1) for ref in (b, a)], axis=0)
        def rhs(ref):
            return jnp.concatenate([ref[:, 48 * i:48 * i + 64, :].reshape(256, 128) for i in range(7)], axis=1)
        a1[...] += dot3((lhs(dha_ref, dhb_ref), lhs(dla_ref, dlb_ref)), (rhs(xh), rhs(xl)), NT)
    if net:
        pl.when(p == 0)(work)
        def pass_on(k, yy):
            for copy in along_z(k, yy):
                copy.wait_recv()
            for copy in along_y(k, yy):
                copy.start()
        for k, step in ((1, 9), (2, 18)):
            pl.when(j == step)(lambda: each(functools.partial(pass_on, k)))
    else:
        work()
    @pl.when(j == last)
    def _():
        for h in range(2):
            for ky in range(4):
                grad = a1[96 * h:96 * h + 32, 64 * ky:64 * ky + 32]
                grad = grad + a1[96 * h + 32:96 * h + 64, 64 * ky + 16:64 * ky + 48]
                grad = grad + a1[96 * h + 64:96 * h + 96, 64 * ky + 32:64 * ky + 64]
                small_ref[32 * h:32 * h + 32, 32 * ky:32 * ky + 32] = grad
        if net:
            @pl.when(p == 0)
            def _():
                for k in range(chips):
                    give(k).start()
            each(functools.partial(pass_on, 3))
            @pl.when(p == 0)
            def _():
                give(0).wait()
                for k in range(1, chips):
                    given(k).wait_recv()
                red[...] = jnp.sum(got[...], axis=0)
                tot[part(me), :] = red[...]
                for k in range(1, chips):
                    tell(k).start()
                for k in range(1, chips):
                    told(k).wait_recv()
                hand.start()
                for k in range(1, chips):
                    give(k).wait_send()
                    tell(k).wait_send()
                hand.wait_send()
                for back in (1, 0):
                    a, b = states_out(j - back, (j - back) % 2)
                    a.wait()
                    b.wait_send()
            @pl.when(p == 1)
            def _():
                hand.wait_recv()
                def arrive(i, c):
                    states_out(i, 0)[1].wait_recv()
                    return c
                lax.fori_loop(0, last + 1, arrive, 0)
            tot_ref[...] = tot[...]
            def sent(yy):
                for k in range(4):
                    for copy in along_z(k, yy):
                        if k:
                            copy.wait_send()
                        else:
                            copy.wait()
                    for copy in along_y(k, yy):
                        copy.wait_send()
            each(sent)
            def came(yy):
                for k in range(4):
                    for copy in along_y(k, yy):
                        copy.wait_recv()
            each(came, flipped=True)

def first_backward(net, x, dh, dl, w1, *wired):
    full = lambda *s: pl.BlockSpec(s, lambda j: (0,) * len(s))
    sds = lambda *s: jax.ShapeDtypeStruct(s, F32)
    vmb = lambda *s: pltpu.VMEM(s, BF)
    dma = pltpu.SemaphoreType.DMA
    half = pl.BlockSpec((4, 168, 128), lambda j: (j, 0, 0))
    row = pl.BlockSpec((1, 704, 128), lambda j: (j, 0, 0))
    next_row = pl.BlockSpec((1, 704, 128), lambda j: (j + 1, 0, 0))
    return pl.pallas_call(
        functools.partial(first_kernel_bwd, net),
        grid=(21,),
        in_specs=[pl.BlockSpec((4, 336, 128), lambda j: (j, 0, 0)), row, next_row, row, next_row, full(2, 192, 256)] + [ANY, ANY, full(24, 128), full(648, 128)] * net,
        out_specs=[full(ROWS, 128)] + [ANY] * 3 if net else [full(64, 128), half, half],
        out_shape=[sds(ROWS, 128), sds(84, 168, 128), sds(2, 4, 200, 512), sds(9, 128, 128)] if net else [sds(64, 128), sds(84, 168, 128), sds(84, 168, 128)],
        scratch_shapes=[vmb(4, 352, 128), vmb(4, 352, 128), pltpu.VMEM((192, 256), F32)]
        + [pltpu.VMEM((2, 4, 168, 128), F32), pltpu.VMEM((2, 4, 168, 128), F32), pltpu.VMEM((ROWS, 128), F32), pltpu.VMEM((16, ROWS // 16, 128), F32),
           pltpu.VMEM((ROWS // 16, 128), F32), pltpu.VMEM((ROWS, 128), F32), dma((2,)), dma((2,)), dma((21,)),
           dma((4, 2)), dma((4, 2)), dma((4, 2)), dma((4, 2)), dma((2,)), dma((16,)), dma((16,)), dma((16,)), dma((16,)), dma, dma, dma] * net,
        compiler_params=pltpu.CompilerParams(vmem_limit_bytes=60 * 2**20, **(dict(collective_id=4, has_side_effects=True) if net else {})),
    )(x, dh, dh, dl, dl, w1, *wired)

ROWS = 768

def wide_kernel(f_ref, d_ref, e_ref, g_ref, z_ref, r_ref, q_ref, acc, acq, da):
    m = pl.program_id(0)
    p = lax.axis_index("pair")
    @pl.when(m == 0)
    def _():
        acc[...] = jnp.zeros_like(acc)
        acq[...] = jnp.zeros_like(acq)
        da[...] = jnp.zeros_like(da)
    f = split(jnp.concatenate([f_ref[0, i] for i in range(4)], axis=1))
    def block(ref):
        return jnp.concatenate([jnp.concatenate([ref[0, i, 128 * c:128 * c + 128, :] for c in range(2)], axis=1) for i in range(4)], axis=0)
    acc[0] += dot3(f, split(block(d_ref)))
    acc[1] += dot3(f, split(block(e_ref)))
    dz = jnp.concatenate([z_ref[0, i] for i in range(4)], axis=1)
    row = lax.broadcasted_iota(jnp.int32, (PAD, 512), 0)
    chosen = dz[ATOMS:ATOMS + 1].astype(jnp.int32)
    d = jnp.where(row < ATOMS, dz, 0.0)
    da[0:PAD, :] = d
    for i in range(ACTIONS):
        da[128 + ATOMS * i:128 + ATOMS * i + PAD, :] = mask_of(chosen, i) * d
    g = split(jnp.concatenate([g_ref[0, i] for i in range(4)], axis=1))
    acq[...] += dot3(g, split(da[...]), NT)
    @pl.when(m == 3)
    def _():
        r_ref[:, 0:256] = jnp.where(p == 0, acc[0], acc[1])
        r_ref[:, 256:512] = jnp.where(p == 0, acc[1], acc[0])
        for c in range(9):
            q_ref[c] = acq[:, 128 * c:128 * c + 128]

def wide_grads(f2, d2, d3, g2, z2):
    full = lambda *s: pl.BlockSpec(s, lambda j: (0,) * len(s))
    part = lambda n: pl.BlockSpec((1, 4, n, 128), lambda j: (j, 0, 0, 0))
    sds = lambda *s: jax.ShapeDtypeStruct(s, F32)
    return pl.pallas_call(
        wide_kernel, grid=(4,),
        in_specs=[part(200), part(256), part(256), part(32), part(PAD)],
        out_specs=[full(200, 512), full(9, 32, 128)],
        out_shape=[sds(200, 512), sds(9, 32, 128)],
        scratch_shapes=[pltpu.VMEM((2, 200, 256), F32), pltpu.VMEM((32, 1152), F32), pltpu.VMEM((1152, 512), F32)],
        compiler_params=pltpu.CompilerParams(vmem_limit_bytes=60 * 2**20),
    )(f2, d2, d3, g2, z2)

def torso_out(tot, k1_ref, k2_ref, k3_ref, b1_ref, b2_ref, b3_ref, t1, t2):
    t1[:, 0:64] = jnp.transpose(tot[672:736, :])
    t1[:, 64:128] = jnp.zeros((128, 64), F32)
    for ky in range(4):
        for c in range(4):
            v = t1[pl.ds(32 * ky + c, 8, stride=4), :]
            for h in range(2):
                k1_ref[c, 4 * h + ky] = v[:, 32 * h:32 * h + 32]
    for py in range(2):
        t2[...] = jnp.transpose(tot[24 + 128 * py:152 + 128 * py, :])
        for h in range(2):
            for kx in range(4):
                k2_ref[:, 2 * h + py, kx, :] = t2[32 * kx:32 * kx + 32, 64 * h:64 * h + 64]
    for ky in range(3):
        for kx in range(3):
            base = (280 if kx < 2 else 472) + 64 * ky
            k3_ref[ky, kx] = tot[base:base + 64, 64 * (kx % 2):64 * (kx % 2) + 64]
    b3_ref[...] = tot[664:665, 0:64]
    b2_ref[...] = tot[665:666, 0:64]
    b1_ref[...] = tot[666:667, 0:32]

def finish_kernel(ag_ref, ah_ref, tot_ref, in_ref, out_ref, ein_ref, eout_ref, mean_ref, sigma_ref, hm_ref, hs_ref, k1_ref, k2_ref, k3_ref, b1_ref, b2_ref, b3_ref,
                  hb_ref, hbs_ref, bo_ref, bos_ref, loss_ref, t1, t2):
    for s in range(2):
        tall = column(in_ref[s:s + 1, :], 512) * out_ref[s:s + 1, :]
        for z, (start, n) in enumerate(((0, 200), (200, 200), (400, 184), (584, 200))):
            v = ag_ref[s, z, 0:n, :]
            mean_ref[s, start:start + n, :] = v
            sigma_ref[s, start:start + n, :] = v * tall[start:start + n]
    noise = column(eout_ref[...], 128)
    for c in range(9):
        start = 0 if c == 0 else ATOMS + 128 * (c - 1)
        n = min(128, (ATOMS if c == 0 else OUTS) - start)
        v = jnp.transpose(ah_ref[c])[0:n]
        hm_ref[start:start + n, :] = v
        hs_ref[start:start + n, :] = v * (noise[start:start + n] * ein_ref[min(c, 1):min(c, 1) + 1, :])
    torso_out(tot_ref, k1_ref, k2_ref, k3_ref, b1_ref, b2_ref, b3_ref, t1, t2)
    for s in range(2):
        for c in range(4):
            v = tot_ref[4 * s + c:4 * s + c + 1, :]
            hb_ref[s:s + 1, 128 * c:128 * c + 128] = v
            hbs_ref[s:s + 1, 128 * c:128 * c + 128] = v * out_ref[s:s + 1, 128 * c:128 * c + 128]
    for c in range(8):
        n = min(128, OUTS - 128 * c)
        v = tot_ref[8 + c:9 + c, 0:n]
        bo_ref[:, 128 * c:128 * c + n] = v
        bos_ref[:, 128 * c:128 * c + n] = v * eout_ref[:, 128 * c:128 * c + n]
    loss_ref[...] = tot_ref[16:17, :]

def finish(ag, ah, tot, n_in, n_out, e_in, e_out):
    sds = lambda *s: jax.ShapeDtypeStruct(s, F32)
    return pl.pallas_call(
        finish_kernel, in_specs=[VMEM] * 7, out_specs=[VMEM] * 15,
        out_shape=[sds(2, 784, 512), sds(2, 784, 512), sds(OUTS, 128), sds(OUTS, 128), sds(4, 8, 8, 32), sds(32, 4, 4, 64), sds(3, 3, 64, 64), sds(1, 32), sds(1, 64), sds(1, 64),
                   sds(2, 512), sds(2, 512), sds(1, OUTS), sds(1, OUTS), sds(1, 128)],
        scratch_shapes=[pltpu.VMEM((128, 128), F32), pltpu.VMEM((128, 128), F32)],
        compiler_params=pltpu.CompilerParams(vmem_limit_bytes=60 * 2**20),
    )(ag, ah, tot, n_in, n_out, e_in, e_out)

def small_finish_kernel(tot_ref, k1_ref, k2_ref, k3_ref, b1_ref, b2_ref, b3_ref, t1, t2):
    torso_out(tot_ref, k1_ref, k2_ref, k3_ref, b1_ref, b2_ref, b3_ref, t1, t2)

def small_finish(tot):
    sds = lambda *s: jax.ShapeDtypeStruct(s, F32)
    return pl.pallas_call(
        small_finish_kernel, in_specs=[VMEM], out_specs=[VMEM] * 6,
        out_shape=[sds(4, 8, 8, 32), sds(32, 4, 4, 64), sds(3, 3, 64, 64), sds(1, 32), sds(1, 64), sds(1, 64)],
        scratch_shapes=[pltpu.VMEM((128, 128), F32), pltpu.VMEM((128, 128), F32)],
    )(tot)

def online_only(value):
    other = lax.ppermute(value, "pair", [(0, 1)])
    return jnp.where(lax.axis_index("pair") == 0, value, other)

def exchange(parts):
    groups = lax.axis_size("group")
    p, g = lax.axis_index("pair"), lax.axis_index("group")
    got = []
    for k in range(groups):
        to = (g + k) % groups
        mine = parts(0, to)
        if k:
            mine = lax.ppermute(mine, ("pair", "group"), [(i, (i + k) % groups) for i in range(groups)])
        theirs = lax.ppermute(parts(1, to), ("pair", "group"), [(i, groups + (i + k) % groups) for i in range(groups)])
        got.append(jnp.where(p == 0, mine, theirs))
    return got

HIGH = lax.Precision.HIGH

def local(states, actions, proj_lower, proj_upper, proj_weight, first_kernel, first_bias, second_kernel, second_bias,
          third_kernel, third_bias, hidden_mean, hidden_sigma, hidden_bias_mean, hidden_bias_sigma, head_mean, head_sigma,
          head_bias_mean, head_bias_sigma, hidden_noise_in, hidden_noise_out, head_noise_in, head_noise_out):
    pair = lax.axis_index("pair")
    groups = lax.axis_size("group")
    shards = 2 * groups
    net = int(groups == 2 and lax.axis_size("rep") == 8)
    n_in, n_out, e_in, e_out = hidden_noise_in[0], hidden_noise_out[0], head_noise_in[0], head_noise_out[0]
    noise = online_only(jnp.concatenate([v.reshape(-1) for v in (n_in, n_out, e_in, e_out)]))
    on_in = noise[:6272].reshape(2, 3136)
    on_out = noise[6272:7296].reshape(2, 512)
    on_ein = noise[7296:8320].reshape(2, 512)
    on_eout = noise[8320:]
    shard = pair * groups + lax.axis_index("group")
    feat_q, hid_q = 3136 // shards, 512 // shards
    in_q = lax.dynamic_slice_in_dim(on_in, shard * feat_q, feat_q, axis=1)
    e_q = lax.dynamic_slice_in_dim(on_ein, shard * hid_q, hid_q, axis=1)

    x = jnp.transpose(states[0], (2, 3, 1, 0)).reshape(84, 336, 128)
    fw1, fw2, fw3, bw1, bw2, bw3, c1, c2, c3 = prepare(first_kernel[0], second_kernel[0], third_kernel[0], first_bias, second_bias, third_bias)
    e_out = e_out[None]
    e_rows = jnp.where(jnp.arange(OUTS)[:, None] < ATOMS, e_in[0:1], e_in[1:2])
    wo = jnp.pad(head_mean[0].T + head_sigma[0].T * (e_rows * e_out.T), ((0, OUTP - OUTS), (0, 0)))
    bo = jnp.pad(head_bias_mean + head_bias_sigma * e_out, ((0, 0), (0, OUTP - OUTS)))
    hb = (hidden_bias_mean[0] + hidden_bias_sigma[0] * n_out).reshape(1, 1024)
    nin = jnp.transpose(n_in.reshape(2, STEPS, 3136 // STEPS), (1, 0, 2))
    pre1, pre2, pre3, feats = forward(x, fw1, fw2, fw3, c1, c2, c3)
    h, hid, logp, dist, *f1 = hidden(net, feats, hidden_mean[0], hidden_sigma[0], nin, n_out, hb, wo, bo, actions, proj_lower.T, proj_weight.T)
    back = (logp, h, hidden_mean[0], hidden_sigma[0], nin, n_out, wo, actions)
    if net:
        df, small_b, f2, g1, d1, dz1 = hidden_bwd(net, dist, *back, *f1, hid)
        dh, dl, small_d, d2, d3, g2, z2 = lower_backward(net, pre1, pre2, pre3, df, bw2, bw3, d1, g1, dz1)
        part_r, part_q = wide_grads(f2, d2, d3, g2, z2)
        total, grad_rows, ag, ah = first_backward(net, x, dh, dl, bw1, part_r, part_q, small_b, small_d)
        (hidden_grad, hidden_sigma_grad, head_t, head_sigma_t, gk1, gk2, gk3, gb1, gb2, gb3, hb_grad, hbs_grad, bo_grad, bos_grad,
         loss) = finish(ag, ah, total, in_q, on_out, e_q, on_eout[None])
    else:
        df, small_b, msg, dz = hidden_bwd(net, lax.ppermute(dist, "pair", [(1, 0)]), *back)
        f_got = exchange(lambda p, g: lax.dynamic_slice_in_dim(feats, (p * groups + g) * feat_q, feat_q, axis=0))
        hid = jnp.transpose(hid, (3, 0, 2, 1, 4, 5)).reshape(1024, 128).T
        hid_got = exchange(lambda p, g: lax.dynamic_slice_in_dim(hid.reshape(128, 2, 512), (p * groups + g) * hid_q, hid_q, axis=2))
        dpre = jnp.transpose(msg.reshape(2, 2, 2, 128, 128), (3, 1, 0, 2, 4)).reshape(128, 1024)
        d_all = jnp.concatenate(exchange(lambda p, g: jnp.concatenate([dpre, dz.T, jnp.zeros((128, 72), F32)], axis=1)), axis=0)
        f_all = jnp.concatenate(f_got, axis=1)
        hid_all = jnp.concatenate(hid_got, axis=0)
        part_hidden = jnp.einsum("fb,bsh->sfh", f_all, d_all[:, :1024].reshape(-1, 2, 512), precision=HIGH)
        dz_all = d_all[:, 1024:1024 + ATOMS]
        picked = d_all[:, 1024 + ATOMS]
        mask = jnp.where(picked[None, :] == jnp.arange(ACTIONS, dtype=F32)[:, None], 1.0 - 1.0 / ACTIONS, -1.0 / ACTIONS)
        da = (mask[:, None, :] * dz_all.T[None]).reshape(ACTIONS * ATOMS, -1)
        part_head = jnp.concatenate([jnp.dot(dz_all.T, hid_all[:, 0], precision=HIGH), jnp.dot(da, hid_all[:, 1], precision=HIGH)], axis=0)
        hidden_grad, head_t = lax.psum((part_hidden, part_head), "rep")
        dh, dl, small_d = lower_backward(net, pre1, pre2, pre3, df, bw2, bw3)
        small_f, lo, up = first_backward(net, x, dh, dl, bw1)
        grad_rows = jnp.where(pair == 0, lo, lax.ppermute(up, "pair", [(0, 1)]))
        total = lax.psum(jnp.concatenate([small_b, small_d, small_f], axis=0), ("pair", "group", "rep"))
        hidden_sigma_grad = hidden_grad * (in_q[:, :, None] * on_out[:, None, :])
        head_sigma_t = head_t * (jnp.where(jnp.arange(OUTS)[:, None] < ATOMS, e_q[0:1], e_q[1:2]) * on_eout[:, None])
        gk1, gk2, gk3, gb1, gb2, gb3 = small_finish(total)
        hb_grad = total[0:8].reshape(2, 512)
        bo_grad = total[8:16].reshape(1, -1)[:, :OUTS]
        hbs_grad, bos_grad = hb_grad * on_out, bo_grad * on_eout
        loss = total[16:17]
    states_grad = jnp.transpose(grad_rows.reshape(84, 84, 2, 128), (3, 2, 0, 1))
    return (loss[0, 0], states_grad, jnp.transpose(gk1, (3, 0, 1, 2)), gb1[0], jnp.transpose(gk2, (3, 0, 1, 2)), gb2[0], jnp.transpose(gk3, (2, 3, 0, 1)), gb3[0],
            hidden_grad, hidden_sigma_grad, hb_grad, hbs_grad, head_t.T, head_sigma_t.T, bo_grad[0], bos_grad[0])


def solution(mesh):
    placed = (
        P("pair", ("group", "rep"), None, None, None),
        P("pair", ("group", "rep")),
        P(("group", "rep"), None),
        P(("group", "rep"), None),
        P(("group", "rep"), None),
        P("pair", None, None, None, None),
        P("pair", None),
        P("pair", None, None, None, None),
        P("pair", None),
        P("pair", None, None, None, None),
        P("pair", None),
        P("pair", None, None, None),
        P("pair", None, None, None),
        P("pair", None, None),
        P("pair", None, None),
        P("pair", None, None),
        P("pair", None, None),
        P("pair", None),
        P("pair", None),
        P("pair", None, None),
        P("pair", None, None),
        P("pair", None, None),
        P("pair", None),
    )
    return jax.shard_map(
        local,
        mesh=mesh,
        in_specs=placed,
        out_specs=(
            P(),
            P(("group", "rep"), "pair", None, None),
            P(),
            P(),
            P(),
            P(),
            P(),
            P(),
            P(None, ("pair", "group"), None),
            P(None, ("pair", "group"), None),
            P(),
            P(),
            P(("pair", "group"), None),
            P(("pair", "group"), None),
            P(),
            P(),
        ),
        check_vma=False,
    )
```

```python
import functools
import jax
import jax.numpy as jnp
from jax import lax
from jax.experimental import pallas as pl
from jax.experimental.pallas import tpu as pltpu
from jax.sharding import PartitionSpec as P

BF = jnp.bfloat16
F32 = jnp.float32
NN=(((1,),(0,)),((),()))
NT=(((1,),(1,)),((),()))
TN=(((0,),(0,)),((),()))

def split(v):
    hi = v.astype(BF)
    return hi, (v - hi.astype(F32)).astype(BF)

def dot(a, b, dims=NN):
    return lax.dot_general(a, b, dims, preferred_element_type=F32)

def dot3(a, b, dims=NN):
    ah, al = a; bh, bl = b
    return dot(ah, bh, dims) + (dot(ah, bl, dims) + dot(al, bh, dims))

def silu(v):
    return v * jax.nn.sigmoid(v)

def prep_kernel(k1_ref, k2_ref, k3_ref, b1_ref, b2_ref, b3_ref, f1_ref, f2_ref, f3_ref, r1_ref, r2_ref, r3_ref, c1_ref, c2_ref, c3_ref,
                t1a, t1b, u1a, u1b, m2, m3, n2, n3):
    for ref in (t1a, t1b, u1a, u1b, m2, m3, n2, n3):
        ref[...] = jnp.zeros_like(ref)
    def put(ref, start, stride, v, lane):
        n = v.shape[0]
        pieces = [jnp.zeros((n, lane), F32)] * (lane > 0) + [v] + [jnp.zeros((n, 96 - lane), F32)] * (lane < 96)
        rows = pl.ds(start, n, stride=stride)
        ref[rows, :] = ref[rows, :] + jnp.concatenate(pieces, axis=1)
    for c in range(4):
        for ky in range(8):
            v = k1_ref[c, ky]
            h, kq = ky // 4, ky % 4
            for w in range(3):
                put((t1a, t1b)[h], kq * 64 + 16 * w + c, 4, v, 32 * w)
            base = (c // 2) * 96 + kq * 24 + c % 2
            for q in range(4):
                if q == 0:
                    put((u1b, u1a)[h], base, 2, v[4:8], 0)
                elif q == 3:
                    put((u1b, u1a)[h], base + 16, 2, v[0:4], 96)
                else:
                    put((u1b, u1a)[h], base + 8 * (q - 1), 2, v, 32 * q)
    for ky in range(4):
        for kx in range(4):
            v = k2_ref[:, ky, kx, :]
            h, py, wx, px = ky // 2, ky % 2, 1 - kx // 2, kx % 2
            m2[py * 128 + kx * 32:py * 128 + kx * 32 + 32, 64 * h:64 * h + 64] = v
            n2[(py * 2 + px) * 32:(py * 2 + px) * 32 + 32, 128 * (1 - h) + 64 * wx:128 * (1 - h) + 64 * wx + 64] = v
    for ky in range(3):
        for kx in range(3):
            v = k3_ref[ky, kx]
            vt = jnp.transpose(v)
            for w in range(2):
                m3[ky * 128 + w * 64:ky * 128 + w * 64 + 64, 64 * (w + kx):64 * (w + kx) + 64] = v
                q = w + 2 - kx
                n3[ky * 128 + w * 64:ky * 128 + w * 64 + 64, 64 * q:64 * q + 64] = vt
    w1 = jnp.concatenate([jnp.transpose(t1a[...])[0:96], jnp.transpose(t1b[...])[0:96]], axis=0)
    pairs = ((f1_ref, w1), (f2_ref, jnp.transpose(m2[...])), (f3_ref, m3[...]), (r1_ref, jnp.concatenate([u1a[...], u1b[...]], axis=1)), (r2_ref, n2[...]), (r3_ref, n3[...]))
    for ref, v in pairs:
        hi, lo = split(v)
        ref[0] = hi
        ref[1] = lo
    for ref, b_ref, n, times in ((c1_ref, b1_ref, 32, 3), (c2_ref, b2_ref, 64, 1), (c3_ref, b3_ref, 64, 1)):
        col = jnp.transpose(jnp.broadcast_to(b_ref[...], (128, n)))
        for i in range(times):
            ref[n * i:n * i + n, :] = col

def prepare(k1, k2, k3, b1, b2, b3):
    vm = pl.BlockSpec(memory_space=pltpu.VMEM)
    bfs = lambda *s: jax.ShapeDtypeStruct(s, BF)
    sds = lambda *s: jax.ShapeDtypeStruct(s, F32)
    f32 = lambda *s: pltpu.VMEM(s, F32)
    return pl.pallas_call(
        prep_kernel, in_specs=[vm] * 6, out_specs=[vm] * 9,
        out_shape=[bfs(2, 192, 256), bfs(2, 128, 256), bfs(2, 384, 256), bfs(2, 192, 256), bfs(2, 128, 256), bfs(2, 384, 256), sds(96, 128), sds(64, 128), sds(64, 128)],
        scratch_shapes=[f32(256, 128), f32(256, 128), f32(192, 128), f32(192, 128), f32(256, 128), f32(384, 256), f32(128, 256), f32(384, 256)],
        compiler_params=pltpu.CompilerParams(vmem_limit_bytes=60 * 2**20),
    )(jnp.transpose(k1, (1, 2, 3, 0)), jnp.transpose(k2, (1, 2, 3, 0)), jnp.transpose(k3, (2, 3, 0, 1)), b1, b2, b3)

def fwd_kernel(x_ref, w1_ref, w2_ref, w3_ref, b1_ref, b2_ref, b3_ref, pre1_hbm, pre2_hbm, pre3_ref, f_ref,
               xs, pre1_ref, pre2_ref, xh, xl, top1, top2, acc3, h1h, h1l, h2h, h2l, x_sem, sem1, sem2):
    def x_in(j):
        return pltpu.make_async_copy(x_ref.at[pl.ds(4 * j, 4)], xs.at[pl.ds(4 * j, 4)], x_sem.at[j])
    def row_out(row):
        return pltpu.make_async_copy(pre1_ref.at[row], pre1_hbm.at[row], sem1.at[row])
    for j in range(21):
        x_in(j).start()
    xh[:, 336:, :] = jnp.zeros((4, 16, 128), BF)
    xl[:, 336:, :] = jnp.zeros((4, 16, 128), BF)
    top1[...] = jnp.zeros_like(top1)
    top2[...] = jnp.zeros_like(top2)
    acc3[...] = jnp.zeros_like(acc3)
    h2h[:, 576:, :] = jnp.zeros((9, 64, 128), BF)
    h2l[:, 576:, :] = jnp.zeros((9, 64, 128), BF)
    def step1(j, carry):
        x_in(j).wait()
        v = xs[pl.ds(4 * j, 4)]
        hi = v.astype(BF)
        xh[:, 0:336, :] = hi
        xl[:, 0:336, :] = (v - hi.astype(F32)).astype(BF)
        rh = jnp.concatenate([xh[:, 48 * i:48 * i + 64, :].reshape(256, 128) for i in range(7)], axis=1)
        rl = jnp.concatenate([xl[:, 48 * i:48 * i + 64, :].reshape(256, 128) for i in range(7)], axis=1)
        r = dot3((w1_ref[0], w1_ref[1]), (rh, rl))
        out = top1[...] + r[96:]
        top1[...] = r[:96]
        b1 = b1_ref[...]
        row = jnp.maximum(j - 1, 0)
        for i in range(7):
            n = 96 if i < 6 else 64
            p = out[:n, 128 * i:128 * i + 128] + b1[:n]
            pre1_ref[row, 96 * i:96 * i + n, :] = p
            hh, hl = split(silu(p))
            h1h[row, 96 * i:96 * i + n, :] = hh
            h1l[row, 96 * i:96 * i + n, :] = hl
        pl.when(j >= 1)(lambda: row_out(row).start())
        return carry
    lax.fori_loop(0, 21, step1, 0)
    w2 = (w2_ref[0], w2_ref[1])
    b2 = b2_ref[...]
    def step2(y, carry):
        rh = jnp.concatenate([h1h[pl.ds(2 * y, 2), 64 * i:64 * i + 128, :].reshape(256, 128) for i in range(9)], axis=1)
        rl = jnp.concatenate([h1l[pl.ds(2 * y, 2), 64 * i:64 * i + 128, :].reshape(256, 128) for i in range(9)], axis=1)
        r = dot3(w2, (rh, rl))
        o = top2[...] + r[64:]
        top2[...] = r[:64]
        row = jnp.maximum(y - 1, 0)
        for i in range(9):
            p = o[:, 128 * i:128 * i + 128] + b2
            pre2_ref[row, 64 * i:64 * i + 64, :] = p
            hh, hl = split(silu(p))
            h2h[row, 64 * i:64 * i + 64, :] = hh
            h2l[row, 64 * i:64 * i + 64, :] = hl
        return carry
    lax.fori_loop(0, 10, step2, 0)
    pre2_out = pltpu.make_async_copy(pre2_ref, pre2_hbm, sem2)
    pre2_out.start()
    w3 = (w3_ref[0], w3_ref[1])
    b3 = b3_ref[...]
    def step3(y, carry):
        rh = jnp.concatenate([h2h[y, 128 * i:128 * i + 256, :] for i in range(4)], axis=1)
        rl = jnp.concatenate([h2l[y, 128 * i:128 * i + 256, :] for i in range(4)], axis=1)
        r = dot3(w3, (rh, rl))
        for ky in range(3):
            for i in range(4):
                acc3[y - ky + 2, 128 * i:128 * i + 128, :] += r[128 * ky:128 * ky + 128, 128 * i:128 * i + 128]
        return carry
    lax.fori_loop(0, 9, step3, 0)
    for y in range(7):
        for x in range(7):
            p = acc3[y + 2, 64 * x:64 * x + 64, :] + b3
            pre3_ref[pl.ds(y * 7 + x, 64, stride=49), :] = p
            f_ref[pl.ds(y * 7 + x, 64, stride=49), :] = silu(p)
    pre2_out.wait()
    for row in range(20):
        row_out(row).wait()

def forward(x, w1, w2, w3, b1, b2, b3):
    vm = pl.BlockSpec(memory_space=pltpu.VMEM)
    hbm = pl.BlockSpec(memory_space=pl.ANY)
    sds = lambda *s: jax.ShapeDtypeStruct(s, F32)
    f32 = lambda *s: pltpu.VMEM(s, F32)
    bf = lambda *s: pltpu.VMEM(s, BF)
    dma = pltpu.SemaphoreType.DMA
    return pl.pallas_call(
        fwd_kernel,
        in_specs=[hbm] + [vm] * 6,
        out_specs=[hbm, hbm, vm, vm],
        out_shape=[sds(20, 640, 128), sds(9, 576, 128), sds(3136, 128), sds(3136, 128)],
        scratch_shapes=[f32(84, 336, 128), f32(20, 640, 128), f32(9, 576, 128), bf(4, 352, 128), bf(4, 352, 128),
                        f32(96, 896), f32(64, 1152), f32(11, 512, 128), bf(20, 640, 128), bf(20, 640, 128), bf(9, 640, 128), bf(9, 640, 128),
                        dma((21,)), dma((20,)), dma],
        compiler_params=pltpu.CompilerParams(vmem_limit_bytes=60 * 2**20),
    )(x, w1, w2, w3, b1, b2, b3)


MESH_ID = pl.DeviceIdType.MESH


def coords():
    r = lax.axis_index("rep")
    return lax.axis_index("pair"), lax.axis_index("group"), r // 2, r % 2


def at(p, g, z, y):
    return (p, g, z * 2 + y)


def flip(z, k):
    return (z, z + 1 - 2 * (z % 2), z + 2 - 4 * (z // 2), 3 - z)[k]


def line(p, g, z, y):
    return [at(q, g, flip(z, k), y) for k in range(4) for q in ((p, 1 - p) if k else (1 - p,))]


def plane(p, g, z, y):
    return [at(p, g, z, 1 - y), at(p, 1 - g, z, y), at(p, 1 - g, z, 1 - y)]


def greet(devices):
    barrier = pltpu.get_barrier_semaphore()
    for device in devices:
        pl.semaphore_signal(barrier, inc=1, device_id=device, device_id_type=MESH_ID)
    pl.semaphore_wait(barrier, len(devices))


def remote(src, dst, send, recv, device):
    return pltpu.make_async_remote_copy(src_ref=src, dst_ref=dst, send_sem=send, recv_sem=recv, device_id=device, device_id_type=MESH_ID)


class Scatter:
    def __init__(self, parts, src, dst, send, recv, own, cores=2):
        self.parts, self.src, self.dst, self.send, self.recv, self.own, self.cores = parts, src, dst, send, recv, own, cores
        self.p, self.g, self.z, self.y = coords()

    def copies(self):
        for k in range(4):
            for q in range(self.cores):
                for i in range(self.parts):
                    zd = flip(self.z, k)
                    if k == 0 and q == 0:
                        yield pltpu.make_async_copy(self.src(q, zd, i), self.dst(self.z, i), self.own.at[i]), True
                    else:
                        yield remote(self.src(q, zd, i), self.dst(self.z, i), self.send.at[k * 2 + q, i], self.recv.at[k, i], at(q, self.g, zd, self.y)), False

    def start(self):
        @pl.when(self.p == 0)
        def _():
            for copy, own in self.copies():
                copy.start()

    def arrived(self, k):
        if self.cores == 1:
            pl.when(self.p == 0)(lambda: self.landed(k))
        else:
            self.landed(k)

    def landed(self, k):
        for i in range(self.parts):
            zs = flip(self.z, k)
            wait = remote(self.src(0, zs, i), self.dst(zs, i), self.send.at[0, i], self.recv.at[k, i], at(1 - self.p, self.g, self.z, self.y)).wait_recv
            local = pltpu.make_async_copy(self.src(0, zs, i), self.dst(zs, i), self.own.at[i]).wait
            if k:
                wait()
            elif self.cores == 1:
                local()
            else:
                pl.when(self.p == 1)(wait)
                pl.when(self.p == 0)(local)

    def sent(self):
        @pl.when(self.p == 0)
        def _():
            for copy, own in self.copies():
                if not own:
                    copy.wait_send()


def scatter_sems(parts):
    return [pltpu.SemaphoreType.DMA((8, parts)), pltpu.SemaphoreType.DMA((4, parts)), pltpu.SemaphoreType.DMA((parts,))]


FIRST = 104


def f_scatter(f_ref, f1_ref, half, sems):
    start, rows = (0, FIRST) if half == 0 else (FIRST, 200 - FIRST)
    def src(q, zd, i):
        return f_ref.at[pl.ds(pl.multiple_of((2 * q + i) * 784 + jnp.minimum(200 * zd, 584) + start, 8), rows)]
    return Scatter(2, src, lambda z, i: f1_ref.at[i, z], *sems)


def f_fan(f1_ref, f2_ref, send, recv):
    return spread_plane(*coords(), lambda gd, yd: f1_ref.at[gd], lambda m: f2_ref.at[m], send, recv)


class Line:
    def __init__(self, parts, own, slot, send, recv):
        self.parts, self.own, self.slot, self.send, self.recv = parts, own, slot, send, recv
        self.p, self.g, self.z, self.y = coords()

    def block(self, t, way):
        return jnp.maximum(self.z - t, 0) if way == 0 else jnp.minimum(self.z + t, 3)

    def there(self, t, way):
        return self.z >= t if way == 0 else self.z + t <= 3

    def copies(self, t, way):
        to = at(self.p, self.g, jnp.minimum(self.z + 1, 3) if way == 0 else jnp.maximum(self.z - 1, 0), self.y)
        zz = self.block(t, way)
        return [remote(self.own(i) if t == 0 else self.slot(zz, i), self.slot(zz, i), self.send.at[t, way, i], self.recv.at[t, way, i], to) for i in range(self.parts)]

    def goes(self, t, way):
        return jnp.logical_and(self.there(t, way), self.z <= 2 if way == 0 else self.z >= 1)

    def start(self, t):
        for way in range(2):
            def go():
                for copy in self.copies(t, way):
                    copy.start()
            pl.when(self.goes(t, way))(go)

    def arrive(self, t, then):
        for way in range(2):
            def come():
                zz = self.block(t, way)
                for i in range(self.parts):
                    remote(self.slot(zz, i), self.slot(zz, i), self.send.at[t - 1, way, i], self.recv.at[t - 1, way, i], at(1 - self.p, self.g, self.z, self.y)).wait_recv()
                if t < 3:
                    def go():
                        for copy in self.copies(t, way):
                            copy.start()
                    pl.when(self.goes(t, way))(go)
                then(2 * t - 1 + way, zz)
            pl.when(self.there(t, way))(come)

    def each(self, do):
        do(0, self.z)
        for t in range(1, 4):
            for way in range(2):
                pl.when(self.there(t, way))(lambda: do(2 * t - 1 + way, self.block(t, way)))

    def sent(self):
        for t in range(3):
            for way in range(2):
                def done():
                    for copy in self.copies(t, way):
                        copy.wait_send()
                pl.when(self.goes(t, way))(done)


def line_sems(parts):
    return [pltpu.SemaphoreType.DMA((3, 2, parts)), pltpu.SemaphoreType.DMA((3, 2, parts))]


def g_scatter(hid_ref, g1_ref, sems):
    return Scatter(1, lambda q, zd, i: hid_ref.at[q, zd], lambda z, i: g1_ref.at[z], *sems)


def z_scatter(dz_ref, dz1_ref, sems):
    return Scatter(1, lambda q, zd, i: dz_ref, lambda z, i: dz1_ref.at[z], *sems, cores=1)


def spread_plane(p, g, z, y, src, dst, send, recv):
    places = [(g, y), (g, 1 - y), (1 - g, y), (1 - g, 1 - y)]
    out = [pltpu.make_async_copy(src(*places[0]), dst(0), send.at[0])]
    for m in range(1, 4):
        out.append(remote(src(*places[m]), dst(m), send.at[m], recv.at[m], at(p, places[m][0], z, places[m][1])))
    return out
ATOMS, ACTIONS, PAD = 51, 18, 56
OUTS, OUTP = 969, 976
STEPS = 7
ANY = pl.BlockSpec(memory_space=pl.ANY)
VMEM = pl.BlockSpec(memory_space=pltpu.VMEM)

def column(row, lanes):
    tall = jnp.transpose(jnp.broadcast_to(row, (128, row.shape[1])))
    return jnp.concatenate([tall] * (lanes // 128), axis=1)

def noisy(mean_ref, sigma_ref, nin_ref, nout_ref, s):
    return mean_ref[s] + sigma_ref[s] * (column(nin_ref[0, s:s + 1, :], 512) * nout_ref[s:s + 1, :])

def mask_of(chosen, a):
    return jnp.where(chosen == a, 1.0 - 1.0 / ACTIONS, -1.0 / ACTIONS)

def hid_kernel(net, f_ref, m_ref, s_ref, nin_ref, nout_ref, hb_ref, wo_ref, bo_ref, c_ref, pl_ref, pw_ref, *rest):
    if net:
        f_all, h_ref, g_ref, logp_ref, dist_ref, f1a_ref, f1b_ref, f2_ref, acc, adv, fs, fr = rest[:12]
        wires = f_scatter(f_all, f1a_ref, 0, rest[12:15]), f_scatter(f_all, f1b_ref, 1, rest[15:18])
        fan = f_fan(f1a_ref, f2_ref, fs, fr)
        p, g, z, y = coords()
    else:
        h_ref, g_ref, logp_ref, dist_ref, acc, adv = rest
    j = pl.program_id(0)
    @pl.when(j == 0)
    def _():
        if net:
            greet(line(p, g, z, y) + plane(p, g, z, y))
            wires[0].start()
        acc[...] = jnp.zeros_like(acc)
    if net:
        @pl.when(j == 4)
        def _():
            wires[0].sent()
            wires[1].start()
            for k in range(4):
                wires[0].arrived(k)
            for copy in fan:
                copy.start()
    f = split(f_ref[...])
    for s in range(2):
        w = split(noisy(m_ref, s_ref, nin_ref, nout_ref, s))
        acc[:, 512 * s:512 * s + 512] += dot3(f, w, TN)
    @pl.when(j == pl.num_programs(0) - 1)
    def _():
        h = acc[...] + hb_ref[...]
        h_ref[...] = h
        gt = jnp.transpose(silu(h))
        for s in range(2):
            for q in range(2):
                for gg in range(2):
                    for z in range(4):
                        at_row = 512 * s + 256 * q + 128 * gg + 32 * z
                        g_ref[q, z, gg, s] = gt[at_row:at_row + 32]
        both = dot3(split(wo_ref[...]), split(jnp.concatenate([gt[:512], gt[512:]], axis=1)))
        bias = column(bo_ref[...], 128)
        adv[...] = both[:, 128:] + bias
        z = both[0:PAD, 0:128] + bias[0:PAD]
        chosen = c_ref[...]
        for i in range(ACTIONS):
            z = z + mask_of(chosen, i) * adv[ATOMS * (i + 1):ATOMS * (i + 1) + PAD, :]
        row = lax.broadcasted_iota(jnp.int32, (PAD, 128), 0)
        z = jnp.where(row < ATOMS, z, -1e30)
        top = jnp.max(z, axis=0, keepdims=True)
        e = jnp.exp(z - top)
        tot = jnp.sum(e, axis=0, keepdims=True)
        logp_ref[...] = (z - top) - jnp.log(tot)
        p = e / tot
        dist = jnp.zeros((PAD, 128), F32)
        for i in range(ATOMS):
            lower = pl_ref[i:i + 1, :]
            share = pw_ref[i:i + 1, :]
            pi = p[i:i + 1, :]
            dist = dist + jnp.where(row == lower, pi * (1.0 - share), 0.0) + jnp.where(row == lower + 1, pi * share, 0.0)
        dist_ref[...] = dist
        if net:
            for k in range(4):
                wires[1].arrived(k)
            wires[1].sent()
            for copy in fan:
                copy.wait()

def hidden(net, f, m, s, nin, nout, hb, wo, bo, c, plow, pw):
    full = lambda *t: pl.BlockSpec(t, lambda j: (0,) * len(t))
    sds = lambda *t: jax.ShapeDtypeStruct(t, F32)
    k = 3136 // STEPS
    wspec = pl.BlockSpec((2, k, 512), lambda j: (0, j, 0))
    return pl.pallas_call(
        functools.partial(hid_kernel, net), grid=(STEPS,),
        in_specs=[pl.BlockSpec((k, 128), lambda j: (j, 0)), wspec, wspec, pl.BlockSpec((1, 2, k), lambda j: (j, 0, 0)), full(2, 512), full(1, 1024),
                  full(OUTP, 512), full(1, OUTP), full(1, 128), full(ATOMS, 128), full(ATOMS, 128)] + [ANY] * net,
        out_specs=[full(128, 1024), full(2, 4, 2, 2, 32, 128), full(PAD, 128), full(PAD, 128)] + [ANY, ANY, ANY] * net,
        out_shape=[sds(128, 1024), sds(2, 4, 2, 2, 32, 128), sds(PAD, 128), sds(PAD, 128)]
        + [sds(2, 4, FIRST, 128), sds(2, 4, 200 - FIRST, 128), sds(4, 4, FIRST, 128)] * net,
        scratch_shapes=[pltpu.VMEM((128, 1024), F32), pltpu.VMEM((OUTP, 128), F32)] + ([pltpu.SemaphoreType.DMA((4,))] * 2 + scatter_sems(2) * 2) * net,
        compiler_params=pltpu.CompilerParams(vmem_limit_bytes=60 * 2**20, **(dict(collective_id=1, has_side_effects=True) if net else {})),
    )(f, m, s, nin, nout, hb, wo, bo, c, plow, pw, *([f] * net))

def hid_bwd_kernel(net, t_ref, logp_ref, h_ref, m_ref, s_ref, nin_ref, nout_ref, wo_ref, c_ref, *rest):
    if net:
        f1b_ref, hid_ref, df_ref, small_ref, f2b_ref, g1_ref, d1_ref, dz1_ref, g2_ref, d2_ref, dz2_ref, d3_ref = rest[:12]
        dth, dtl, da, msg, dz_to, t_got = rest[12:18]
        ds, dr, gs, gr, qs, qr, fs, fr, ts, tr, hs, hr, ss, sr, ps, pr, own = rest[18:35]
        g_wire = g_scatter(hid_ref, g1_ref, rest[35:38])
        z_wire = z_scatter(dz_to, dz1_ref, rest[38:41])
        p, g, z, y = coords()
        d_line = Line(1, lambda i: d1_ref.at[z], lambda zz, i: d1_ref.at[zz], rest[41], rest[42])
        partner = at(1 - p, g, z, y)
        target = remote(t_ref, t_got, ts, tr, partner)
        hand = remote(dz2_ref, dz2_ref, hs, hr, partner)
        give = remote(msg.at[1], d1_ref.at[z], ps, pr, partner)
        keep = pltpu.make_async_copy(msg.at[0], d1_ref.at[z], own)
        fan_f = f_fan(f1b_ref, f2b_ref, fs, fr)
        fan_g = spread_plane(p, g, z, y, lambda gd, yd: g1_ref.at[:, gd, yd], lambda m: g2_ref.at[m], gs, gr)
        fan_z = spread_plane(p, g, z, y, lambda gd, yd: dz1_ref, lambda m: dz2_ref.at[m], qs, qr)
        def fan_d(place, zz):
            return spread_plane(p, g, z, y, lambda gd, yd: d1_ref.at[zz, yd], lambda m: d2_ref.at[m, zz], ds.at[place], dr.at[place])
        def swap(place, zz):
            return remote(d2_ref.at[:, zz], d3_ref.at[:, zz], ss.at[place], sr.at[place], partner)
        def forward(place, zz):
            for copy in fan_d(place, zz):
                copy.start()
        def forward_small():
            for k in range(4):
                g_wire.arrived(k)
            for copy in fan_g:
                copy.start()
            for k in range(4):
                z_wire.arrived(k)
            @pl.when(p == 0)
            def _():
                for copy in fan_z:
                    copy.start()
    else:
        df_ref, small_ref, msg, dz_to, dth, dtl, da = rest
        t_got = t_ref
    j = pl.program_id(0)
    def begin():
        t = t_got[...]
        logp = logp_ref[...]
        chosen = c_ref[...]
        row = lax.broadcasted_iota(jnp.int32, (PAD, 128), 0)
        d = (jnp.exp(logp) * jnp.sum(t, axis=0, keepdims=True) - t) * (1.0 / 128)
        loss = -jnp.sum(jnp.where(row < ATOMS, t * logp, 0.0), axis=1, keepdims=True) * (1.0 / 128)
        dz_to[...] = jnp.where(row == ATOMS, chosen.astype(F32), d)
        da[...] = jnp.zeros_like(da)
        da[0:PAD, 0:128] = d
        for i in range(ACTIONS):
            da[ATOMS * (i + 1):ATOMS * (i + 1) + PAD, 128:256] = mask_of(chosen, i) * d
        every = da[...]
        eh, el = split(every)
        grads = dot3((eh, el), split(wo_ref[...]), TN)
        small_ref[...] = jnp.zeros_like(small_ref)
        for s in range(2):
            dp = grads[128 * s:128 * s + 128] * dsilu(h_ref[:, 512 * s:512 * s + 512])
            total = jnp.sum(dp, axis=0, keepdims=True)
            for c in range(4):
                msg[c // 2, s, 128 * (c % 2):128 * (c % 2) + 128, :] = dp[:, 128 * c:128 * c + 128]
                small_ref[4 * s + c:4 * s + c + 1, :] = total[:, 128 * c:128 * c + 128]
            hi, lo = split(jnp.transpose(dp))
            dth[s] = hi
            dtl[s] = lo
        if net:
            give.start()
            keep.start()
            z_wire.start()
            keep.wait()
        ones = jnp.ones((8, 256), BF)
        left = (every - eh.astype(F32)) - el.astype(F32)
        rows = dot(ones, eh, NT) + dot(ones, el, NT) + dot(ones, left.astype(BF), NT)
        for c in range(8):
            n = min(128, OUTP - 128 * c)
            small_ref[8 + c:9 + c, 0:n] = rows[0:1, 128 * c:128 * c + n]
        small_ref[16:17, :] = jnp.broadcast_to(jnp.sum(loss, axis=0, keepdims=True), (1, 128))
    def step():
        out = None
        for s in range(2):
            w = split(noisy(m_ref, s_ref, nin_ref, nout_ref, s))
            r = dot3(w, (dth[s], dtl[s]))
            out = r if out is None else out + r
        df_ref[...] = out
    if not net:
        pl.when(j == 0)(begin)
        step()
        return
    @pl.when(j == 0)
    def _():
        greet(line(p, g, z, y) + plane(p, g, z, y))
        pl.when(p == 1)(target.start)
        for copy in fan_f:
            copy.start()
        g_wire.start()
        @pl.when(p == 0)
        def _():
            target.wait_recv()
            begin()
        pl.when(p == 1)(give.wait_recv)
        d_line.start(0)
        forward(0, z)
    pl.when(p == 0)(step)
    pl.when(j == 3)(forward_small)
    @pl.when(j == pl.num_programs(0) - 1)
    def _():
        for t in range(1, 4):
            d_line.arrive(t, forward)
        pl.when(p == 1)(target.wait_send)
        @pl.when(p == 0)
        def _():
            for copy in fan_z:
                copy.wait()
            hand.start()
        def landed(place, zz):
            copies = fan_d(place, zz)
            copies[0].wait()
            for copy in copies[1:]:
                copy.wait_recv()
            swap(place, zz).start()
        d_line.each(landed)
        for copy in fan_f + fan_g:
            copy.wait()
        def gone(place, zz):
            for copy in fan_d(place, zz)[1:]:
                copy.wait_send()
            swap(place, zz).wait()
        d_line.each(gone)
        d_line.sent()
        @pl.when(p == 0)
        def _():
            give.wait_send()
            hand.wait_send()
        pl.when(p == 1)(hand.wait_recv)
        for wire in (g_wire, z_wire):
            wire.sent()

def hidden_bwd(net, t, logp, h, m, s, nin, nout, wo, c, *wired):
    full = lambda *u: pl.BlockSpec(u, lambda j: (0,) * len(u))
    sds = lambda *u: jax.ShapeDtypeStruct(u, F32)
    dma = pltpu.SemaphoreType.DMA
    k = 3136 // STEPS
    wspec = pl.BlockSpec((2, k, 512), lambda j: (0, j, 0))
    return pl.pallas_call(
        functools.partial(hid_bwd_kernel, net), grid=(STEPS,),
        in_specs=[full(PAD, 128), full(PAD, 128), full(128, 1024), wspec, wspec, pl.BlockSpec((1, 2, k), lambda j: (j, 0, 0)), full(2, 512),
                  full(OUTP, 512), full(1, 128)] + [ANY, ANY] * net,
        out_specs=[pl.BlockSpec((k, 128), lambda j: (j, 0)), full(24, 128)] + ([ANY] * 8 if net else [full(2, 2, 256, 128), full(PAD, 128)]),
        out_shape=[sds(3136, 128), sds(24, 128)] + ([sds(4, 4, 200 - FIRST, 128), sds(4, 2, 2, 32, 128), sds(4, 2, 256, 128), sds(4, PAD, 128), sds(4, 4, 32, 128), sds(4, 4, 256, 128),
                                                     sds(4, 4, PAD, 128), sds(4, 4, 256, 128)] if net else [sds(2, 2, 256, 128), sds(PAD, 128)]),
        scratch_shapes=[pltpu.VMEM((2, 512, 128), BF), pltpu.VMEM((2, 512, 128), BF), pltpu.VMEM((OUTP, 256), F32)]
        + ([pltpu.VMEM((2, 2, 256, 128), F32), pltpu.VMEM((PAD, 128), F32), pltpu.VMEM((PAD, 128), F32), dma((7, 4)), dma((7, 4))] + [dma((4,))] * 6 + [dma] * 4 + [dma((7,)), dma((7,)), dma, dma, dma]
           + scatter_sems(1) * 2 + line_sems(1)) * net,
        compiler_params=pltpu.CompilerParams(vmem_limit_bytes=60 * 2**20, **(dict(collective_id=2, has_side_effects=True) if net else {})),
    )(t, logp, h, m, s, nin, nout, wo, c, *wired)

def dsilu(v):
    s = jax.nn.sigmoid(v)
    return s * (1.0 + v * (1.0 - s))


ROWS = 768

def bwd_kernel(net, x_ref, pre1_hbm, pre2_ref, pre3_ref, df_ref, w1_ref, w2_ref, w3_ref, *rest):
    if net:
        r_ref, q_ref, s0_ref, tot_ref, sg_ref, ag_ref, ah_ref, bg_ref, bh_ref = rest[:9]
        xs, pre1_ref, xh, xl, d3f, d3h, d3l, d2h, d2l, d1h, d1l, h2h, h2l, acc2, a1, a2, a3, pay, lob, upb, x_sem, sem1, ls, us = rest[9:33]
        got, got1, red, tot, ur, zs_, zr, ys, yr, own, gs, gr, ws, wr, as_, ar, bs, br, es, er, cs, cr, one_ = rest[33:]
        p, g, z, y = coords()
        reps = lax.axis_size("rep")
        chips = 2 * reps
        me = g * reps + lax.axis_index("rep")
        size = ROWS // chips
        def chip(i):
            return (0, i // reps, i % reps)
        def part(i):
            return pl.ds(pl.multiple_of(i * size, 8), size)
        def give(k):
            to = (me + k) % chips
            if k:
                return remote(pay.at[part(to)], got.at[me], as_.at[k], ar.at[k], chip(to))
            return pltpu.make_async_copy(pay.at[part(me)], got.at[me], one_)
        def given(k):
            who = (me + chips - k) % chips
            return remote(pay.at[part(me)], got.at[who], as_.at[k], ar.at[k], chip(who))
        def show(k):
            return remote(pay.at[pl.ds(672, 64)], got1.at[me], es.at[k], er.at[k], chip((me + k) % chips))
        def shown(k):
            who = (me + chips - k) % chips
            return remote(pay.at[pl.ds(672, 64)], got1.at[who], es.at[k], er.at[k], chip(who))
        def tell(k):
            return remote(red, tot.at[part(me)], bs.at[k], br.at[k], chip((me + k) % chips))
        def told(k):
            who = (me + chips - k) % chips
            return remote(red, tot.at[part(who)], bs.at[k], br.at[k], chip(who))
        hand = remote(tot, tot, cs, cr, at(1 - p, g, z, y))
        def head_at(ref, yy, zz):
            return ref.at[pl.ds(yy, 1 + 7 * yy), pl.ds(pl.multiple_of(32 * zz, 8), 32)]
        def head_of(yy):
            return q_ref.at[pl.ds(yy, 1 + 7 * yy)]
        def slots(yy, zz):
            return ag_ref.at[yy, zz], head_at(ah_ref, yy, zz), bg_ref.at[yy, zz], head_at(bh_ref, yy, zz)
        def lines(yy):
            mine = (r_ref, head_of(yy)) + slots(yy, z)[2:]
            return Line(4, lambda i: mine[i], lambda zz, i: slots(yy, zz)[i], zs_, zr)
        def keep(yy):
            a, b, _, _ = slots(yy, z)
            return [pltpu.make_async_copy(r_ref, a, own.at[0]), pltpu.make_async_copy(head_of(yy), b, own.at[1])]
        def give_own(yy):
            _, _, a, b = slots(yy, z)
            return [remote(r_ref, a, gs.at[0], gr.at[0], at(1, g, z, y)), remote(head_of(yy), b, gs.at[1], gr.at[1], at(1, g, z, y))]
        def along_y(place, zz, yy):
            src = slots(yy, zz) if place else (r_ref, head_of(yy)) + slots(yy, z)[2:]
            return [remote(src[i], slots(yy, zz)[i], ys.at[place, i], yr.at[place, i], at(p, g, z, 1 - y)) for i in range(4)]
        def bring(place, zz, yy):
            a, b, c, d = slots(yy, zz)
            return [remote(c, a, ws.at[yy, place, 0], wr.at[yy, place, 0], at(0, g, z, y)), remote(d, b, ws.at[yy, place, 1], wr.at[yy, place, 1], at(0, g, z, y))]
        def each(do, flipped=False):
            for yy in range(2):
                pl.when(y == (1 - yy if flipped else yy))(functools.partial(do, yy))
        def states_out(j, slot):
            return (pltpu.make_async_copy(lob.at[slot], sg_ref.at[pl.ds(4 * j, 4)], ls.at[slot]),
                    remote(upb.at[slot], sg_ref.at[pl.ds(4 * j, 4)], us.at[slot], ur.at[j], at(1 - p, g, z, y)))
        def gather(yy):
            def then(place, zz):
                for copy in along_y(place, zz, yy) + bring(place, zz, yy):
                    copy.start()
            for copy in give_own(yy):
                copy.wait_recv()
            lines(yy).start(0)
            then(0, z)
            for copy in keep(yy):
                copy.start()
            for t in range(1, 4):
                lines(yy).arrive(t, then)
        def second(yy):
            def landed(place, zz):
                for copy in along_y(place, zz, yy):
                    copy.wait_recv()
                for copy in bring(place, zz, yy):
                    copy.start()
            lines(yy).each(landed)
        def finished(yy):
            def gone(place, zz):
                for copy in along_y(place, zz, yy) + bring(place, zz, yy):
                    copy.wait_send()
            for copy in keep(yy):
                copy.wait()
            lines(yy).sent()
            lines(yy).each(gone)
        def second_sent(yy):
            def gone(place, zz):
                for copy in bring(place, zz, yy):
                    copy.wait_send()
            lines(yy).each(gone)
        def brought(yy):
            def came(place, zz):
                for copy in bring(place, zz, yy):
                    copy.wait_recv()
            lines(yy).each(came)
    else:
        tot_ref, lo_ref, up_ref, xs, pre1_ref, xh, xl, d3f, d3h, d3l, d2h, d2l, d1h, d1l, h2h, h2l, acc2, a1, a2, a3, pay, lob, upb, x_sem, sem1, ls, us = rest
        def states_out(j, slot):
            return (pltpu.make_async_copy(lob.at[slot], lo_ref.at[pl.ds(4 * j, 4)], ls.at[slot]),
                    pltpu.make_async_copy(upb.at[slot], up_ref.at[pl.ds(4 * j, 4)], us.at[slot]))
    small_ref = pay.at[pl.ds(24, 648)]
    last = 20
    def x_in(j):
        return pltpu.make_async_copy(x_ref.at[pl.ds(4 * j, 4)], xs.at[pl.ds(4 * j, 4)], x_sem.at[j])
    pre1_in = pltpu.make_async_copy(pre1_hbm, pre1_ref, sem1)
    def fetch():
        pre1_in.start()
        for j in range(21):
            x_in(j).start()
    def upper():
        for ref in (d3h, d3l, d2h, d2l, acc2, a2, a3):
            ref[...] = jnp.zeros_like(ref)
        small_ref[...] = jnp.zeros((648, 128), F32)
        for ref in (d1h, d1l):
            ref[0] = jnp.zeros((704, 128), BF)
            ref[21] = jnp.zeros((704, 128), BF)
            ref[:, 0:32, :] = jnp.zeros((22, 32, 128), BF)
            ref[:, 672:704, :] = jnp.zeros((22, 32, 128), BF)
        d3f[...] = df_ref[...] * dsilu(pre3_ref[...])
        total = jnp.zeros((64, 128), F32)
        for y in range(7):
            for x in range(7):
                d = d3f[pl.ds(y * 7 + x, 64, stride=49), :]
                total = total + d
                hi, lo = split(d)
                d3h[y + 2, 64 * (x + 2):64 * (x + 3), :] = hi
                d3l[y + 2, 64 * (x + 2):64 * (x + 3), :] = lo
        small_ref[640:641, 0:64] = jnp.sum(jnp.transpose(total), axis=0, keepdims=True)
        w3 = (w3_ref[0], w3_ref[1])
        h2h[:, 576:, :] = jnp.zeros((9, 64, 128), BF)
        h2l[:, 576:, :] = jnp.zeros((9, 64, 128), BF)
        def split2(y, c):
            hi, lo = split(silu(pre2_ref[y]))
            h2h[y, 0:576, :] = hi
            h2l[y, 0:576, :] = lo
            return c
        lax.fori_loop(0, 9, split2, 0)
        def dgrad3(y, c):
            rh = jnp.concatenate([d3h[y + 2, 128 * i:128 * i + 256, :] for i in range(5)], axis=1)
            rl = jnp.concatenate([d3l[y + 2, 128 * i:128 * i + 256, :] for i in range(5)], axis=1)
            r = dot3(w3, (rh, rl))
            for ky in range(3):
                for i in range(5):
                    acc2[y + ky, 128 * i:128 * i + 128, :] += r[128 * ky:128 * ky + 128, 128 * i:128 * i + 128]
            return c
        lax.fori_loop(0, 7, dgrad3, 0)
        def wgrad3(y, c):
            def lhs(ref):
                return jnp.concatenate([jnp.concatenate([ref[y - ky + 2, 128 * (i + 1):128 * (i + 2), :] for i in range(4)], axis=1) for ky in range(3)], axis=0)
            def rhs(ref):
                return jnp.concatenate([ref[y, 128 * i:128 * i + 256, :] for i in range(4)], axis=1)
            a3[...] += dot3((lhs(d3h), lhs(d3l)), (rhs(h2h), rhs(h2l)), NT)
            return c
        lax.fori_loop(0, 9, wgrad3, 0)
        for ky in range(3):
            grad = a3[128 * ky:128 * ky + 64, 0:192] + a3[128 * ky + 64:128 * ky + 128, 64:256]
            small_ref[256 + 64 * ky:320 + 64 * ky, :] = grad[:, 0:128]
            small_ref[448 + 64 * ky:512 + 64 * ky, 0:64] = grad[:, 128:192]
        def step2(y, total):
            for x in range(9):
                d = acc2[y, 64 * x:64 * x + 64, :] * dsilu(pre2_ref[y, 64 * x:64 * x + 64, :])
                total = total + d
                hi, lo = split(d)
                d2h[y + 1, 64 * (x + 1):64 * (x + 2), :] = hi
                d2l[y + 1, 64 * (x + 1):64 * (x + 2), :] = lo
            return total
        total = lax.fori_loop(0, 9, step2, jnp.zeros((64, 128), F32))
        small_ref[641:642, 0:64] = jnp.sum(jnp.transpose(total), axis=0, keepdims=True)
    def block2(y, total):
        w2 = (w2_ref[0], w2_ref[1])
        rh = jnp.concatenate([d2h[pl.ds(y, 2), 64 * i:64 * i + 128, :].reshape(256, 128) for i in range(10)], axis=1)
        rl = jnp.concatenate([d2l[pl.ds(y, 2), 64 * i:64 * i + 128, :].reshape(256, 128) for i in range(10)], axis=1)
        r = dot3(w2, (rh, rl))
        h1h, h1l = [], []
        for py in range(2):
            rowh, rowl = [], []
            for i in range(10):
                v = pre1_ref[2 * y + py, 64 * i:64 * i + 64, :]
                s = jax.nn.sigmoid(v)
                d = r[64 * py:64 * py + 64, 128 * i:128 * i + 128] * (s * (1.0 + v * (1.0 - s)))
                total = total + d[0:32] + d[32:64]
                hi, lo = split(d)
                d1h[2 * y + py + 1, 64 * i + 32:64 * i + 96, :] = hi
                d1l[2 * y + py + 1, 64 * i + 32:64 * i + 96, :] = lo
                hi, lo = split(v * s)
                rowh.append(hi)
                rowl.append(lo)
            h1h.append(rowh)
            h1l.append(rowl)
        def lhs(ref):
            return jnp.concatenate([jnp.concatenate([ref[y + 1 - h, 64 * (i + 1):64 * (i + 2), :] for i in range(9)], axis=1) for h in range(2)], axis=0)
        def rhs(rows):
            return jnp.concatenate([jnp.concatenate([rows[0][i], rows[0][i + 1], rows[1][i], rows[1][i + 1]], axis=0) for i in range(9)], axis=1)
        a2[...] += dot3((lhs(d2h), lhs(d2l)), (rhs(h1h), rhs(h1l)), NT)
        return total
    def lower():
        pre1_in.wait()
        total = lax.fori_loop(0, 10, block2, jnp.zeros((32, 128), F32))
        small_ref[642:643, 0:32] = jnp.sum(jnp.transpose(total), axis=0, keepdims=True)
        small_ref[0:128, :] = a2[:, 0:128]
        small_ref[128:256, :] = a2[:, 128:256]
    def states_gone(j, slot):
        a, b = states_out(j, slot)
        a.wait()
        if net:
            b.wait_send()
        else:
            b.wait()
    def work(j, carry):
        x_in(j).wait()
        v = xs[pl.ds(4 * j, 4)]
        hi = v.astype(BF)
        xh[:, 0:336, :] = hi
        xl[:, 0:336, :] = (v - hi.astype(F32)).astype(BF)
        def both(ref):
            return jnp.concatenate([ref[pl.ds(j, 2), 96 * i:96 * i + 128, :].reshape(256, 128) for i in range(7)], axis=1)
        r = dot3((w1_ref[0], w1_ref[1]), (both(d1h), both(d1l)))
        slot = j % 2
        pl.when(j >= 2)(lambda: states_gone(j - 2, slot))
        lo_to, up_to = lob.at[slot], upb.at[slot]
        for ky in range(4):
            for i in range(7):
                lo_to[ky, 24 * i:24 * i + 24, :] = r[24 * ky:24 * ky + 24, 128 * i:128 * i + 128]
                up_to[ky, 24 * i:24 * i + 24, :] = r[96 + 24 * ky:96 + 24 * ky + 24, 128 * i:128 * i + 128]
        for copy in states_out(j, slot):
            copy.start()
        def lhs(ref):
            return jnp.concatenate([jnp.concatenate([ref[j + 1 - h, 96 * i + 32:96 * i + 128, :] for i in range(7)], axis=1) for h in range(2)], axis=0)
        def rhs(ref):
            return jnp.concatenate([ref[:, 48 * i:48 * i + 64, :].reshape(256, 128) for i in range(7)], axis=1)
        a1[...] += dot3((lhs(d1h), lhs(d1l)), (rhs(xh), rhs(xl)), NT)
        return carry
    if net:
        pl.when(p == 0)(fetch)
        pl.when(p == 0)(lambda: greet([chip((me + k) % chips) for k in range(1, chips)] + [at(1, g, z, y)]))
        pl.when(p == 1)(lambda: greet([at(1, g, flip(z, k), y) for k in range(1, 4)] + [at(1, g, z, 1 - y), at(0, g, z, y)]))
        def begin(yy):
            for copy in give_own(yy):
                copy.start()
        pl.when(p == 0)(lambda: each(begin))
        @pl.when(p == 1)
        def _():
            each(gather)
            each(second, flipped=True)
        pay[0:24, :] = s0_ref[...]
    else:
        pay[0:24, :] = jnp.zeros((24, 128), F32)
    pay[672:, :] = jnp.zeros((ROWS - 672, 128), F32)
    xh[:, 336:, :] = jnp.zeros((4, 16, 128), BF)
    xl[:, 336:, :] = jnp.zeros((4, 16, 128), BF)
    a1[...] = jnp.zeros_like(a1)
    if net:
        pl.when(p == 0)(upper)
        pl.when(p == 0)(lower)
        @pl.when(p == 0)
        def _():
            for k in range(chips):
                give(k).start()
    else:
        fetch()
        upper()
        lower()
    if net:
        @pl.when(p == 0)
        def _():
            lax.fori_loop(0, 7, work, 0)
            give(0).wait()
            for k in range(1, chips):
                give(k).wait_send()
            for k in range(1, chips):
                given(k).wait_recv()
            red[...] = jnp.sum(got[...], axis=0)
            tot[part(me), :] = red[...]
            for k in range(1, chips):
                tell(k).start()
            lax.fori_loop(7, 21, work, 0)
    else:
        lax.fori_loop(0, 21, work, 0)
        for j in (last - 1, last):
            states_gone(j, j % 2)
    for h in range(2):
        for ky in range(4):
            grad = a1[96 * h:96 * h + 32, 64 * ky:64 * ky + 32]
            grad = grad + a1[96 * h + 32:96 * h + 64, 64 * ky + 16:64 * ky + 48]
            grad = grad + a1[96 * h + 64:96 * h + 96, 64 * ky + 32:64 * ky + 64]
            pay[672 + 32 * h:704 + 32 * h, 32 * ky:32 * ky + 32] = grad
    if net:
        @pl.when(p == 0)
        def _():
            for k in range(1, chips):
                show(k).start()
            got1[me] = pay[672:736, :]
        @pl.when(p == 0)
        def _():
            for k in range(1, chips):
                told(k).wait_recv()
            for k in range(1, chips):
                shown(k).wait_recv()
            tot[672:736, :] = jnp.sum(got1[...], axis=0)
            hand.start()
            for k in range(1, chips):
                tell(k).wait_send()
                show(k).wait_send()
            hand.wait_send()
            for j in (last - 1, last):
                states_gone(j, j % 2)
        @pl.when(p == 1)
        def _():
            hand.wait_recv()
            def arrive(i, c):
                states_out(i, 0)[1].wait_recv()
                return c
            lax.fori_loop(0, last + 1, arrive, 0)
        tot_ref[...] = tot[...]
        @pl.when(p == 0)
        def _():
            def given_own(yy):
                for copy in give_own(yy):
                    copy.wait_send()
            each(given_own)
            brought(0)
            brought(1)
        @pl.when(p == 1)
        def _():
            each(finished)
            each(second_sent, flipped=True)
    else:
        tot_ref[...] = pay[...]

def backward(net, x, pre1, pre2, pre3, df, w1, w2, w3, *wired):
    sds = lambda *s: jax.ShapeDtypeStruct(s, F32)
    vmb = lambda *s: pltpu.VMEM(s, BF)
    f32 = lambda *s: pltpu.VMEM(s, F32)
    dma = pltpu.SemaphoreType.DMA
    return pl.pallas_call(
        functools.partial(bwd_kernel, net),
        in_specs=[ANY, ANY] + [VMEM] * 6 + [ANY, ANY, VMEM] * net,
        out_specs=[VMEM] + [ANY] * (5 if net else 2),
        out_shape=[sds(ROWS, 128)] + ([sds(84, 168, 128)] + [sds(2, 4, 200, 512), sds(9, 128, 128)] * 2 if net else [sds(84, 168, 128), sds(84, 168, 128)]),
        scratch_shapes=[f32(84, 336, 128), f32(20, 640, 128), vmb(4, 352, 128), vmb(4, 352, 128), f32(3136, 128), vmb(11, 768, 128), vmb(11, 768, 128), vmb(11, 704, 128),
                        vmb(11, 704, 128), vmb(22, 704, 128), vmb(22, 704, 128), vmb(9, 640, 128), vmb(9, 640, 128), f32(9, 640, 128), f32(192, 256), f32(128, 256),
                        f32(384, 256), f32(ROWS, 128), f32(2, 4, 168, 128), f32(2, 4, 168, 128), dma((21,)), dma, dma((2,)), dma((2,))]
        + ([f32(16, ROWS // 16, 128), f32(16, 64, 128), f32(ROWS // 16, 128), f32(ROWS, 128), dma((21,))]
           + line_sems(4) + [dma((7, 4))] * 2 + [dma((2,))] * 3 + [dma((2, 7, 2))] * 2 + [dma((16,))] * 6 + [dma] * 3) * net,
        compiler_params=pltpu.CompilerParams(vmem_limit_bytes=62 * 2**20, **(dict(collective_id=3, has_side_effects=True) if net else {})),
    )(x, pre1, pre2, pre3, df, w1, w2, w3, *wired)

def wide_kernel(fa_ref, fb_ref, d_ref, e_ref, g_ref, z_ref, r_ref, q_ref, acc, acq, da):
    m = pl.program_id(0)
    p = lax.axis_index("pair")
    @pl.when(m == 0)
    def _():
        acc[...] = jnp.zeros_like(acc)
        acq[...] = jnp.zeros_like(acq)
        da[...] = jnp.zeros_like(da)
    f = split(jnp.concatenate([jnp.concatenate([fa_ref[0, i], fb_ref[0, i]], axis=0) for i in range(4)], axis=1))
    def block(ref):
        return jnp.concatenate([jnp.concatenate([ref[0, i, 128 * c:128 * c + 128, :] for c in range(2)], axis=1) for i in range(4)], axis=0)
    acc[0] += dot3(f, split(block(d_ref)))
    acc[1] += dot3(f, split(block(e_ref)))
    dz = jnp.concatenate([z_ref[0, i] for i in range(4)], axis=1)
    row = lax.broadcasted_iota(jnp.int32, (PAD, 512), 0)
    chosen = dz[ATOMS:ATOMS + 1].astype(jnp.int32)
    d = jnp.where(row < ATOMS, dz, 0.0)
    da[0:PAD, :] = d
    for i in range(ACTIONS):
        da[128 + ATOMS * i:128 + ATOMS * i + PAD, :] = mask_of(chosen, i) * d
    g = split(jnp.concatenate([g_ref[0, i] for i in range(4)], axis=1))
    acq[...] += dot3(g, split(da[...]), NT)
    @pl.when(m == 3)
    def _():
        r_ref[:, 0:256] = jnp.where(p == 0, acc[0], acc[1])
        r_ref[:, 256:512] = jnp.where(p == 0, acc[1], acc[0])
        for c in range(9):
            q_ref[c] = acq[:, 128 * c:128 * c + 128]

def wide_grads(f2a, f2b, d2, d3, g2, z2):
    full = lambda *s: pl.BlockSpec(s, lambda j: (0,) * len(s))
    part = lambda n: pl.BlockSpec((1, 4, n, 128), lambda j: (j, 0, 0, 0))
    sds = lambda *s: jax.ShapeDtypeStruct(s, F32)
    return pl.pallas_call(
        wide_kernel, grid=(4,),
        in_specs=[part(FIRST), part(200 - FIRST), part(256), part(256), part(32), part(PAD)],
        out_specs=[full(200, 512), full(9, 32, 128)],
        out_shape=[sds(200, 512), sds(9, 32, 128)],
        scratch_shapes=[pltpu.VMEM((2, 200, 256), F32), pltpu.VMEM((32, 1152), F32), pltpu.VMEM((1152, 512), F32)],
        compiler_params=pltpu.CompilerParams(vmem_limit_bytes=60 * 2**20),
    )(f2a, f2b, d2, d3, g2, z2)

def torso_out(tot, k1_ref, k2_ref, k3_ref, b1_ref, b2_ref, b3_ref, t1, t2):
    t1[:, 0:64] = jnp.transpose(tot[672:736, :])
    t1[:, 64:128] = jnp.zeros((128, 64), F32)
    for ky in range(4):
        for c in range(4):
            v = t1[pl.ds(32 * ky + c, 8, stride=4), :]
            for h in range(2):
                k1_ref[c, 4 * h + ky] = v[:, 32 * h:32 * h + 32]
    for py in range(2):
        t2[...] = jnp.transpose(tot[24 + 128 * py:152 + 128 * py, :])
        for h in range(2):
            for kx in range(4):
                k2_ref[:, 2 * h + py, kx, :] = t2[32 * kx:32 * kx + 32, 64 * h:64 * h + 64]
    for ky in range(3):
        for kx in range(3):
            base = (280 if kx < 2 else 472) + 64 * ky
            k3_ref[ky, kx] = tot[base:base + 64, 64 * (kx % 2):64 * (kx % 2) + 64]
    b3_ref[...] = tot[664:665, 0:64]
    b2_ref[...] = tot[665:666, 0:64]
    b1_ref[...] = tot[666:667, 0:32]

def finish_kernel(ag_ref, ah_ref, tot_ref, in_ref, out_ref, ein_ref, eout_ref, mean_ref, sigma_ref, hm_ref, hs_ref, k1_ref, k2_ref, k3_ref, b1_ref, b2_ref, b3_ref,
                  hb_ref, hbs_ref, bo_ref, bos_ref, loss_ref, t1, t2):
    for s in range(2):
        tall = column(in_ref[s:s + 1, :], 512) * out_ref[s:s + 1, :]
        for z, (start, n) in enumerate(((0, 200), (200, 200), (400, 184), (584, 200))):
            v = ag_ref[s, z, 0:n, :]
            mean_ref[s, start:start + n, :] = v
            sigma_ref[s, start:start + n, :] = v * tall[start:start + n]
    noise = column(eout_ref[...], 128)
    for c in range(9):
        start = 0 if c == 0 else ATOMS + 128 * (c - 1)
        n = min(128, (ATOMS if c == 0 else OUTS) - start)
        v = jnp.transpose(ah_ref[c])[0:n]
        hm_ref[start:start + n, :] = v
        hs_ref[start:start + n, :] = v * (noise[start:start + n] * ein_ref[min(c, 1):min(c, 1) + 1, :])
    torso_out(tot_ref, k1_ref, k2_ref, k3_ref, b1_ref, b2_ref, b3_ref, t1, t2)
    for s in range(2):
        for c in range(4):
            v = tot_ref[4 * s + c:4 * s + c + 1, :]
            hb_ref[s:s + 1, 128 * c:128 * c + 128] = v
            hbs_ref[s:s + 1, 128 * c:128 * c + 128] = v * out_ref[s:s + 1, 128 * c:128 * c + 128]
    for c in range(8):
        n = min(128, OUTS - 128 * c)
        v = tot_ref[8 + c:9 + c, 0:n]
        bo_ref[:, 128 * c:128 * c + n] = v
        bos_ref[:, 128 * c:128 * c + n] = v * eout_ref[:, 128 * c:128 * c + n]
    loss_ref[...] = tot_ref[16:17, :]

def finish(ag, ah, tot, n_in, n_out, e_in, e_out):
    sds = lambda *s: jax.ShapeDtypeStruct(s, F32)
    return pl.pallas_call(
        finish_kernel, in_specs=[VMEM] * 7, out_specs=[VMEM] * 15,
        out_shape=[sds(2, 784, 512), sds(2, 784, 512), sds(OUTS, 128), sds(OUTS, 128), sds(4, 8, 8, 32), sds(32, 4, 4, 64), sds(3, 3, 64, 64), sds(1, 32), sds(1, 64), sds(1, 64),
                   sds(2, 512), sds(2, 512), sds(1, OUTS), sds(1, OUTS), sds(1, 128)],
        scratch_shapes=[pltpu.VMEM((128, 128), F32), pltpu.VMEM((128, 128), F32)],
        compiler_params=pltpu.CompilerParams(vmem_limit_bytes=60 * 2**20),
    )(ag, ah, tot, n_in, n_out, e_in, e_out)

def small_finish_kernel(tot_ref, k1_ref, k2_ref, k3_ref, b1_ref, b2_ref, b3_ref, t1, t2):
    torso_out(tot_ref, k1_ref, k2_ref, k3_ref, b1_ref, b2_ref, b3_ref, t1, t2)

def small_finish(tot):
    sds = lambda *s: jax.ShapeDtypeStruct(s, F32)
    return pl.pallas_call(
        small_finish_kernel, in_specs=[VMEM], out_specs=[VMEM] * 6,
        out_shape=[sds(4, 8, 8, 32), sds(32, 4, 4, 64), sds(3, 3, 64, 64), sds(1, 32), sds(1, 64), sds(1, 64)],
        scratch_shapes=[pltpu.VMEM((128, 128), F32), pltpu.VMEM((128, 128), F32)],
    )(tot)

def online_only(value):
    other = lax.ppermute(value, "pair", [(0, 1)])
    return jnp.where(lax.axis_index("pair") == 0, value, other)

def exchange(parts):
    groups = lax.axis_size("group")
    p, g = lax.axis_index("pair"), lax.axis_index("group")
    got = []
    for k in range(groups):
        to = (g + k) % groups
        mine = parts(0, to)
        if k:
            mine = lax.ppermute(mine, ("pair", "group"), [(i, (i + k) % groups) for i in range(groups)])
        theirs = lax.ppermute(parts(1, to), ("pair", "group"), [(i, groups + (i + k) % groups) for i in range(groups)])
        got.append(jnp.where(p == 0, mine, theirs))
    return got

HIGH = lax.Precision.HIGH

def local(states, actions, proj_lower, proj_upper, proj_weight, first_kernel, first_bias, second_kernel, second_bias,
          third_kernel, third_bias, hidden_mean, hidden_sigma, hidden_bias_mean, hidden_bias_sigma, head_mean, head_sigma,
          head_bias_mean, head_bias_sigma, hidden_noise_in, hidden_noise_out, head_noise_in, head_noise_out):
    pair = lax.axis_index("pair")
    groups = lax.axis_size("group")
    shards = 2 * groups
    net = int(groups == 2 and lax.axis_size("rep") == 8)
    n_in, n_out, e_in, e_out = hidden_noise_in[0], hidden_noise_out[0], head_noise_in[0], head_noise_out[0]
    noise = online_only(jnp.concatenate([v.reshape(-1) for v in (n_in, n_out, e_in, e_out)]))
    on_in = noise[:6272].reshape(2, 3136)
    on_out = noise[6272:7296].reshape(2, 512)
    on_ein = noise[7296:8320].reshape(2, 512)
    on_eout = noise[8320:]
    shard = pair * groups + lax.axis_index("group")
    feat_q, hid_q = 3136 // shards, 512 // shards
    in_q = lax.dynamic_slice_in_dim(on_in, shard * feat_q, feat_q, axis=1)
    e_q = lax.dynamic_slice_in_dim(on_ein, shard * hid_q, hid_q, axis=1)

    x = jnp.transpose(states[0], (2, 3, 1, 0)).reshape(84, 336, 128)
    fw1, fw2, fw3, bw1, bw2, bw3, c1, c2, c3 = prepare(first_kernel[0], second_kernel[0], third_kernel[0], first_bias, second_bias, third_bias)
    e_out = e_out[None]
    e_rows = jnp.where(jnp.arange(OUTS)[:, None] < ATOMS, e_in[0:1], e_in[1:2])
    wo = jnp.pad(head_mean[0].T + head_sigma[0].T * (e_rows * e_out.T), ((0, OUTP - OUTS), (0, 0)))
    bo = jnp.pad(head_bias_mean + head_bias_sigma * e_out, ((0, 0), (0, OUTP - OUTS)))
    hb = (hidden_bias_mean[0] + hidden_bias_sigma[0] * n_out).reshape(1, 1024)
    nin = jnp.transpose(n_in.reshape(2, STEPS, 3136 // STEPS), (1, 0, 2))
    pre1, pre2, pre3, feats = forward(x, fw1, fw2, fw3, c1, c2, c3)
    h, hid, logp, dist, *f12 = hidden(net, feats, hidden_mean[0], hidden_sigma[0], nin, n_out, hb, wo, bo, actions, proj_lower.T, proj_weight.T)
    back = (logp, h, hidden_mean[0], hidden_sigma[0], nin, n_out, wo, actions)
    if net:
        df, small_b, f2b, _, _, _, g2, d2, z2, d3 = hidden_bwd(net, dist, *back, f12[1], hid)
        part_r, part_q = wide_grads(f12[2], f2b, d2, d3, g2, z2)
        total, grad_rows, ag, ah, _, _ = backward(net, x, pre1, pre2, pre3, df, bw1, bw2, bw3, part_r, part_q, small_b)
        (hidden_grad, hidden_sigma_grad, head_t, head_sigma_t, gk1, gk2, gk3, gb1, gb2, gb3, hb_grad, hbs_grad, bo_grad, bos_grad,
         loss) = finish(ag, ah, total, in_q, on_out, e_q, on_eout[None])
    else:
        df, small_b, msg, dz = hidden_bwd(net, lax.ppermute(dist, "pair", [(1, 0)]), *back)
        f_got = exchange(lambda p, g: lax.dynamic_slice_in_dim(feats, (p * groups + g) * feat_q, feat_q, axis=0))
        hid = jnp.transpose(hid, (3, 0, 2, 1, 4, 5)).reshape(1024, 128).T
        hid_got = exchange(lambda p, g: lax.dynamic_slice_in_dim(hid.reshape(128, 2, 512), (p * groups + g) * hid_q, hid_q, axis=2))
        dpre = jnp.transpose(msg.reshape(2, 2, 2, 128, 128), (3, 1, 0, 2, 4)).reshape(128, 1024)
        d_all = jnp.concatenate(exchange(lambda p, g: jnp.concatenate([dpre, dz.T, jnp.zeros((128, 72), F32)], axis=1)), axis=0)
        f_all = jnp.concatenate(f_got, axis=1)
        hid_all = jnp.concatenate(hid_got, axis=0)
        part_hidden = jnp.einsum("fb,bsh->sfh", f_all, d_all[:, :1024].reshape(-1, 2, 512), precision=HIGH)
        dz_all = d_all[:, 1024:1024 + ATOMS]
        picked = d_all[:, 1024 + ATOMS]
        mask = jnp.where(picked[None, :] == jnp.arange(ACTIONS, dtype=F32)[:, None], 1.0 - 1.0 / ACTIONS, -1.0 / ACTIONS)
        da = (mask[:, None, :] * dz_all.T[None]).reshape(ACTIONS * ATOMS, -1)
        part_head = jnp.concatenate([jnp.dot(dz_all.T, hid_all[:, 0], precision=HIGH), jnp.dot(da, hid_all[:, 1], precision=HIGH)], axis=0)
        hidden_grad, head_t = lax.psum((part_hidden, part_head), "rep")
        small_d, lo, up = backward(net, x, pre1, pre2, pre3, df, bw1, bw2, bw3)
        grad_rows = jnp.where(pair == 0, lo, lax.ppermute(up, "pair", [(0, 1)]))
        total = lax.psum(small_d + jnp.pad(small_b, ((0, ROWS - 24), (0, 0))), ("pair", "group", "rep"))
        hidden_sigma_grad = hidden_grad * (in_q[:, :, None] * on_out[:, None, :])
        head_sigma_t = head_t * (jnp.where(jnp.arange(OUTS)[:, None] < ATOMS, e_q[0:1], e_q[1:2]) * on_eout[:, None])
        gk1, gk2, gk3, gb1, gb2, gb3 = small_finish(total)
        hb_grad = total[0:8].reshape(2, 512)
        bo_grad = total[8:16].reshape(1, -1)[:, :OUTS]
        hbs_grad, bos_grad = hb_grad * on_out, bo_grad * on_eout
        loss = total[16:17]
    states_grad = jnp.transpose(grad_rows.reshape(84, 84, 2, 128), (3, 2, 0, 1))
    return (loss[0, 0], states_grad, jnp.transpose(gk1, (3, 0, 1, 2)), gb1[0], jnp.transpose(gk2, (3, 0, 1, 2)), gb2[0], jnp.transpose(gk3, (2, 3, 0, 1)), gb3[0],
            hidden_grad, hidden_sigma_grad, hb_grad, hbs_grad, head_t.T, head_sigma_t.T, bo_grad[0], bos_grad[0])


def solution(mesh):
    placed = (
        P("pair", ("group", "rep"), None, None, None),
        P("pair", ("group", "rep")),
        P(("group", "rep"), None),
        P(("group", "rep"), None),
        P(("group", "rep"), None),
        P("pair", None, None, None, None),
        P("pair", None),
        P("pair", None, None, None, None),
        P("pair", None),
        P("pair", None, None, None, None),
        P("pair", None),
        P("pair", None, None, None),
        P("pair", None, None, None),
        P("pair", None, None),
        P("pair", None, None),
        P("pair", None, None),
        P("pair", None, None),
        P("pair", None),
        P("pair", None),
        P("pair", None, None),
        P("pair", None, None),
        P("pair", None, None),
        P("pair", None),
    )
    return jax.shard_map(
        local,
        mesh=mesh,
        in_specs=placed,
        out_specs=(
            P(),
            P(("group", "rep"), "pair", None, None),
            P(),
            P(),
            P(),
            P(),
            P(),
            P(),
            P(None, ("pair", "group"), None),
            P(None, ("pair", "group"), None),
            P(),
            P(),
            P(("pair", "group"), None),
            P(("pair", "group"), None),
            P(),
            P(),
        ),
        check_vma=False,
    )
```

```python
import functools
import jax
import jax.numpy as jnp
from jax import lax
from jax.experimental import pallas as pl
from jax.experimental.pallas import tpu as pltpu
from jax.sharding import PartitionSpec as P

BF = jnp.bfloat16
F32 = jnp.float32
NN=(((1,),(0,)),((),()))
NT=(((1,),(1,)),((),()))
TN=(((0,),(0,)),((),()))

def split(v):
    hi = v.astype(BF)
    return hi, (v - hi.astype(F32)).astype(BF)

def dot(a, b, dims=NN):
    return lax.dot_general(a, b, dims, preferred_element_type=F32)

def dot3(a, b, dims=NN):
    ah, al = a; bh, bl = b
    return dot(ah, bh, dims) + (dot(ah, bl, dims) + dot(al, bh, dims))

def silu(v):
    return v * jax.nn.sigmoid(v)

def prep_kernel(k1_ref, k2_ref, k3_ref, b1_ref, b2_ref, b3_ref, f1_ref, f2_ref, f3_ref, r1_ref, r2_ref, r3_ref, c1_ref, c2_ref, c3_ref,
                t1a, t1b, u1a, u1b, m2, m3, n2, n3):
    for ref in (t1a, t1b, u1a, u1b, m2, m3, n2, n3):
        ref[...] = jnp.zeros_like(ref)
    def put(ref, start, stride, v, lane):
        n = v.shape[0]
        pieces = [jnp.zeros((n, lane), F32)] * (lane > 0) + [v] + [jnp.zeros((n, 96 - lane), F32)] * (lane < 96)
        rows = pl.ds(start, n, stride=stride)
        ref[rows, :] = ref[rows, :] + jnp.concatenate(pieces, axis=1)
    for c in range(4):
        for ky in range(8):
            v = k1_ref[c, ky]
            h, kq = ky // 4, ky % 4
            for w in range(3):
                put((t1a, t1b)[h], kq * 64 + 16 * w + c, 4, v, 32 * w)
            base = (c // 2) * 96 + kq * 24 + c % 2
            for q in range(4):
                if q == 0:
                    put((u1b, u1a)[h], base, 2, v[4:8], 0)
                elif q == 3:
                    put((u1b, u1a)[h], base + 16, 2, v[0:4], 96)
                else:
                    put((u1b, u1a)[h], base + 8 * (q - 1), 2, v, 32 * q)
    for ky in range(4):
        for kx in range(4):
            v = k2_ref[:, ky, kx, :]
            h, py, wx, px = ky // 2, ky % 2, 1 - kx // 2, kx % 2
            m2[py * 128 + kx * 32:py * 128 + kx * 32 + 32, 64 * h:64 * h + 64] = v
            n2[(py * 2 + px) * 32:(py * 2 + px) * 32 + 32, 128 * (1 - h) + 64 * wx:128 * (1 - h) + 64 * wx + 64] = v
    for ky in range(3):
        for kx in range(3):
            v = k3_ref[ky, kx]
            vt = jnp.transpose(v)
            for w in range(2):
                m3[ky * 128 + w * 64:ky * 128 + w * 64 + 64, 64 * (w + kx):64 * (w + kx) + 64] = v
                q = w + 2 - kx
                n3[ky * 128 + w * 64:ky * 128 + w * 64 + 64, 64 * q:64 * q + 64] = vt
    w1 = jnp.concatenate([jnp.transpose(t1a[...])[0:96], jnp.transpose(t1b[...])[0:96]], axis=0)
    pairs = ((f1_ref, w1), (f2_ref, jnp.transpose(m2[...])), (f3_ref, m3[...]), (r1_ref, jnp.concatenate([u1a[...], u1b[...]], axis=1)), (r2_ref, n2[...]), (r3_ref, n3[...]))
    for ref, v in pairs:
        hi, lo = split(v)
        ref[0] = hi
        ref[1] = lo
    for ref, b_ref, n, times in ((c1_ref, b1_ref, 32, 3), (c2_ref, b2_ref, 64, 1), (c3_ref, b3_ref, 64, 1)):
        col = jnp.transpose(jnp.broadcast_to(b_ref[...], (128, n)))
        for i in range(times):
            ref[n * i:n * i + n, :] = col

def prepare(k1, k2, k3, b1, b2, b3):
    vm = pl.BlockSpec(memory_space=pltpu.VMEM)
    bfs = lambda *s: jax.ShapeDtypeStruct(s, BF)
    sds = lambda *s: jax.ShapeDtypeStruct(s, F32)
    f32 = lambda *s: pltpu.VMEM(s, F32)
    return pl.pallas_call(
        prep_kernel, in_specs=[vm] * 6, out_specs=[vm] * 9,
        out_shape=[bfs(2, 192, 256), bfs(2, 128, 256), bfs(2, 384, 256), bfs(2, 192, 256), bfs(2, 128, 256), bfs(2, 384, 256), sds(96, 128), sds(64, 128), sds(64, 128)],
        scratch_shapes=[f32(256, 128), f32(256, 128), f32(192, 128), f32(192, 128), f32(256, 128), f32(384, 256), f32(128, 256), f32(384, 256)],
        compiler_params=pltpu.CompilerParams(vmem_limit_bytes=60 * 2**20),
    )(jnp.transpose(k1, (1, 2, 3, 0)), jnp.transpose(k2, (1, 2, 3, 0)), jnp.transpose(k3, (2, 3, 0, 1)), b1, b2, b3)

def fwd_kernel(x_ref, w1_ref, w2_ref, w3_ref, b1_ref, b2_ref, b3_ref, pre1_hbm, pre2_hbm, pre3_ref, f_ref,
               xs, pre1_ref, pre2_ref, xh, xl, top1, top2, acc3, h1h, h1l, h2h, h2l, x_sem, sem1, sem2):
    def x_in(j):
        return pltpu.make_async_copy(x_ref.at[pl.ds(4 * j, 4)], xs.at[pl.ds(4 * j, 4)], x_sem.at[j])
    def row_out(row):
        return pltpu.make_async_copy(pre1_ref.at[row], pre1_hbm.at[row], sem1.at[row])
    for j in range(21):
        x_in(j).start()
    xh[:, 336:, :] = jnp.zeros((4, 16, 128), BF)
    xl[:, 336:, :] = jnp.zeros((4, 16, 128), BF)
    top1[...] = jnp.zeros_like(top1)
    top2[...] = jnp.zeros_like(top2)
    acc3[...] = jnp.zeros_like(acc3)
    h2h[:, 576:, :] = jnp.zeros((9, 64, 128), BF)
    h2l[:, 576:, :] = jnp.zeros((9, 64, 128), BF)
    def step1(j, carry):
        x_in(j).wait()
        v = xs[pl.ds(4 * j, 4)]
        hi = v.astype(BF)
        xh[:, 0:336, :] = hi
        xl[:, 0:336, :] = (v - hi.astype(F32)).astype(BF)
        rh = jnp.concatenate([xh[:, 48 * i:48 * i + 64, :].reshape(256, 128) for i in range(7)], axis=1)
        rl = jnp.concatenate([xl[:, 48 * i:48 * i + 64, :].reshape(256, 128) for i in range(7)], axis=1)
        r = dot3((w1_ref[0], w1_ref[1]), (rh, rl))
        out = top1[...] + r[96:]
        top1[...] = r[:96]
        b1 = b1_ref[...]
        row = jnp.maximum(j - 1, 0)
        for i in range(7):
            n = 96 if i < 6 else 64
            p = out[:n, 128 * i:128 * i + 128] + b1[:n]
            pre1_ref[row, 96 * i:96 * i + n, :] = p
            hh, hl = split(silu(p))
            h1h[row, 96 * i:96 * i + n, :] = hh
            h1l[row, 96 * i:96 * i + n, :] = hl
        pl.when(j >= 1)(lambda: row_out(row).start())
        return carry
    lax.fori_loop(0, 21, step1, 0)
    w2 = (w2_ref[0], w2_ref[1])
    b2 = b2_ref[...]
    def step2(y, carry):
        rh = jnp.concatenate([h1h[pl.ds(2 * y, 2), 64 * i:64 * i + 128, :].reshape(256, 128) for i in range(9)], axis=1)
        rl = jnp.concatenate([h1l[pl.ds(2 * y, 2), 64 * i:64 * i + 128, :].reshape(256, 128) for i in range(9)], axis=1)
        r = dot3(w2, (rh, rl))
        o = top2[...] + r[64:]
        top2[...] = r[:64]
        row = jnp.maximum(y - 1, 0)
        for i in range(9):
            p = o[:, 128 * i:128 * i + 128] + b2
            pre2_ref[row, 64 * i:64 * i + 64, :] = p
            hh, hl = split(silu(p))
            h2h[row, 64 * i:64 * i + 64, :] = hh
            h2l[row, 64 * i:64 * i + 64, :] = hl
        return carry
    lax.fori_loop(0, 10, step2, 0)
    pre2_out = pltpu.make_async_copy(pre2_ref, pre2_hbm, sem2)
    pre2_out.start()
    w3 = (w3_ref[0], w3_ref[1])
    b3 = b3_ref[...]
    def step3(y, carry):
        rh = jnp.concatenate([h2h[y, 128 * i:128 * i + 256, :] for i in range(4)], axis=1)
        rl = jnp.concatenate([h2l[y, 128 * i:128 * i + 256, :] for i in range(4)], axis=1)
        r = dot3(w3, (rh, rl))
        for ky in range(3):
            for i in range(4):
                acc3[y - ky + 2, 128 * i:128 * i + 128, :] += r[128 * ky:128 * ky + 128, 128 * i:128 * i + 128]
        return carry
    lax.fori_loop(0, 9, step3, 0)
    for y in range(7):
        for x in range(7):
            p = acc3[y + 2, 64 * x:64 * x + 64, :] + b3
            pre3_ref[pl.ds(y * 7 + x, 64, stride=49), :] = p
            f_ref[pl.ds(y * 7 + x, 64, stride=49), :] = silu(p)
    pre2_out.wait()
    for row in range(20):
        row_out(row).wait()

def forward(x, w1, w2, w3, b1, b2, b3):
    vm = pl.BlockSpec(memory_space=pltpu.VMEM)
    hbm = pl.BlockSpec(memory_space=pl.ANY)
    sds = lambda *s: jax.ShapeDtypeStruct(s, F32)
    f32 = lambda *s: pltpu.VMEM(s, F32)
    bf = lambda *s: pltpu.VMEM(s, BF)
    dma = pltpu.SemaphoreType.DMA
    return pl.pallas_call(
        fwd_kernel,
        in_specs=[hbm] + [vm] * 6,
        out_specs=[hbm, hbm, vm, vm],
        out_shape=[sds(20, 640, 128), sds(9, 576, 128), sds(3136, 128), sds(3136, 128)],
        scratch_shapes=[f32(84, 336, 128), f32(20, 640, 128), f32(9, 576, 128), bf(4, 352, 128), bf(4, 352, 128),
                        f32(96, 896), f32(64, 1152), f32(11, 512, 128), bf(20, 640, 128), bf(20, 640, 128), bf(9, 640, 128), bf(9, 640, 128),
                        dma((21,)), dma((20,)), dma],
        compiler_params=pltpu.CompilerParams(vmem_limit_bytes=60 * 2**20),
    )(x, w1, w2, w3, b1, b2, b3)


MESH_ID = pl.DeviceIdType.MESH


def coords():
    r = lax.axis_index("rep")
    return lax.axis_index("pair"), lax.axis_index("group"), r // 2, r % 2


def at(p, g, z, y):
    return (p, g, z * 2 + y)


def flip(z, k):
    return (z, z + 1 - 2 * (z % 2), z + 2 - 4 * (z // 2), 3 - z)[k]


def line(p, g, z, y):
    return [at(q, g, flip(z, k), y) for k in range(4) for q in ((p, 1 - p) if k else (1 - p,))]


def plane(p, g, z, y):
    return [at(p, g, z, 1 - y), at(p, 1 - g, z, y), at(p, 1 - g, z, 1 - y)]


def greet(devices):
    barrier = pltpu.get_barrier_semaphore()
    for device in devices:
        pl.semaphore_signal(barrier, inc=1, device_id=device, device_id_type=MESH_ID)
    pl.semaphore_wait(barrier, len(devices))


def remote(src, dst, send, recv, device):
    return pltpu.make_async_remote_copy(src_ref=src, dst_ref=dst, send_sem=send, recv_sem=recv, device_id=device, device_id_type=MESH_ID)


class Scatter:
    def __init__(self, parts, src, dst, send, recv, own, hold=None, cores=2):
        self.parts, self.src, self.dst, self.send, self.recv, self.own, self.hold, self.cores = parts, src, dst, send, recv, own, hold, cores
        self.p, self.g, self.z, self.y = coords()

    def copies(self):
        for k in range(4):
            for q in range(self.cores):
                for i in range(self.parts):
                    zd = flip(self.z, k)
                    if k == 0 and q == 0:
                        yield pltpu.make_async_copy(self.src(q, zd, i), self.dst(self.z, i) if self.hold is None else self.hold.at[i], self.own.at[i]), True
                    else:
                        yield remote(self.src(q, zd, i), self.dst(self.z, i), self.send.at[k * 2 + q, i], self.recv.at[k, i], at(q, self.g, zd, self.y)), False

    def start(self):
        @pl.when(self.p == 0)
        def _():
            for copy, own in self.copies():
                copy.start()

    def arrived(self, k):
        if self.cores == 1:
            pl.when(self.p == 0)(lambda: self.landed(k))
        else:
            self.landed(k)

    def landed(self, k):
        for i in range(self.parts):
            zs = flip(self.z, k)
            wait = remote(self.src(0, zs, i), self.dst(zs, i), self.send.at[0, i], self.recv.at[k, i], at(1 - self.p, self.g, self.z, self.y)).wait_recv
            def local():
                if self.hold is None:
                    pltpu.make_async_copy(self.src(0, zs, i), self.dst(zs, i), self.own.at[i]).wait()
                else:
                    pltpu.make_async_copy(self.src(0, zs, i), self.hold.at[i], self.own.at[i]).wait()
                    out = pltpu.make_async_copy(self.hold.at[i], self.dst(zs, i), self.own.at[i])
                    out.start()
                    out.wait()
            if k:
                wait()
            elif self.cores == 1:
                local()
            else:
                pl.when(self.p == 1)(wait)
                pl.when(self.p == 0)(local)

    def sent(self):
        @pl.when(self.p == 0)
        def _():
            for copy, own in self.copies():
                if not own:
                    copy.wait_send()


def scatter_sems(parts, *hold):
    return [pltpu.SemaphoreType.DMA((8, parts)), pltpu.SemaphoreType.DMA((4, parts)), pltpu.SemaphoreType.DMA((parts,))] + [pltpu.VMEM((parts,) + hold, F32)] * bool(hold)


FIRST = 104


def f_scatter(f_ref, f1_ref, half, sems):
    start, rows = (0, FIRST) if half == 0 else (FIRST, 200 - FIRST)
    def src(q, zd, i):
        return f_ref.at[pl.ds(pl.multiple_of((2 * q + i) * 784 + jnp.minimum(200 * zd, 584) + start, 8), rows)]
    return Scatter(2, src, lambda z, i: f1_ref.at[i, z], *sems)


def f_fan(f1_ref, f2_ref, send, recv):
    return spread_plane(*coords(), lambda gd, yd: f1_ref.at[gd], lambda m: f2_ref.at[m], send, recv)


class Line:
    def __init__(self, parts, own, slot, send, recv):
        self.parts, self.own, self.slot, self.send, self.recv = parts, own, slot, send, recv
        self.p, self.g, self.z, self.y = coords()

    def block(self, t, way):
        return jnp.maximum(self.z - t, 0) if way == 0 else jnp.minimum(self.z + t, 3)

    def there(self, t, way):
        return self.z >= t if way == 0 else self.z + t <= 3

    def copies(self, t, way):
        to = at(self.p, self.g, jnp.minimum(self.z + 1, 3) if way == 0 else jnp.maximum(self.z - 1, 0), self.y)
        zz = self.block(t, way)
        return [remote(self.own(i) if t == 0 else self.slot(zz, i), self.slot(zz, i), self.send.at[t, way, i], self.recv.at[t, way, i], to) for i in range(self.parts)]

    def goes(self, t, way):
        return jnp.logical_and(self.there(t, way), self.z <= 2 if way == 0 else self.z >= 1)

    def start(self, t):
        for way in range(2):
            def go():
                for copy in self.copies(t, way):
                    copy.start()
            pl.when(self.goes(t, way))(go)

    def arrive(self, t, then):
        for i in range(self.parts):
            for way in range(2):
                def come():
                    zz = self.block(t, way)
                    remote(self.slot(zz, i), self.slot(zz, i), self.send.at[t - 1, way, i], self.recv.at[t - 1, way, i], at(1 - self.p, self.g, self.z, self.y)).wait_recv()
                    if t < 3:
                        pl.when(self.goes(t, way))(self.copies(t, way)[i].start)
                    then(2 * t - 1 + way, zz, i)
                pl.when(self.there(t, way))(come)

    def each(self, do):
        do(0, self.z)
        for t in range(1, 4):
            for way in range(2):
                pl.when(self.there(t, way))(lambda: do(2 * t - 1 + way, self.block(t, way)))

    def sent(self):
        for t in range(3):
            for way in range(2):
                def done():
                    for copy in self.copies(t, way):
                        copy.wait_send()
                pl.when(self.goes(t, way))(done)


def line_sems(parts):
    return [pltpu.SemaphoreType.DMA((3, 2, parts)), pltpu.SemaphoreType.DMA((3, 2, parts))]


def g_scatter(hid_ref, g1_ref, sems):
    return Scatter(1, lambda q, zd, i: hid_ref.at[q, zd], lambda z, i: g1_ref.at[z], *sems)


def z_scatter(dz_ref, dz1_ref, sems):
    return Scatter(1, lambda q, zd, i: dz_ref, lambda z, i: dz1_ref.at[z], *sems, cores=1)


def spread_plane(p, g, z, y, src, dst, send, recv):
    places = [(g, 1 - y), (1 - g, y), (1 - g, 1 - y)]
    return [remote(src(*to), dst(m), send.at[m], recv.at[m], at(p, to[0], z, to[1])) for m, to in enumerate(places)]
ATOMS, ACTIONS, PAD = 51, 18, 56
OUTS, OUTP = 969, 976
STEPS = 7
ANY = pl.BlockSpec(memory_space=pl.ANY)
VMEM = pl.BlockSpec(memory_space=pltpu.VMEM)

def column(row, lanes):
    tall = jnp.transpose(jnp.broadcast_to(row, (128, row.shape[1])))
    return jnp.concatenate([tall] * (lanes // 128), axis=1)

def noisy(mean_ref, sigma_ref, nin_ref, nout_ref, s):
    return mean_ref[s] + sigma_ref[s] * (column(nin_ref[0, s:s + 1, :], 512) * nout_ref[s:s + 1, :])

def mask_of(chosen, a):
    return jnp.where(chosen == a, 1.0 - 1.0 / ACTIONS, -1.0 / ACTIONS)

def hid_kernel(net, f_ref, m_ref, s_ref, nin_ref, nout_ref, hb_ref, wo_ref, bo_ref, c_ref, pl_ref, pw_ref, *rest):
    if net:
        f_all, h_ref, g_ref, logp_ref, dist_ref, f1a_ref, f1b_ref, f2_ref, acc, adv, fs, fr = rest[:12]
        wires = f_scatter(f_all, f1a_ref, 0, rest[12:16]), f_scatter(f_all, f1b_ref, 1, rest[16:20])
        fan = f_fan(f1a_ref, f2_ref, fs, fr)
        p, g, z, y = coords()
    else:
        h_ref, g_ref, logp_ref, dist_ref, acc, adv = rest
    j = pl.program_id(0)
    @pl.when(j == 0)
    def _():
        if net:
            greet(line(p, g, z, y) + plane(p, g, z, y))
            wires[0].start()
        acc[...] = jnp.zeros_like(acc)
    if net:
        @pl.when(j == 4)
        def _():
            wires[0].sent()
            wires[1].start()
            for k in range(4):
                wires[0].arrived(k)
            for copy in fan:
                copy.start()
    f = split(f_ref[...])
    for s in range(2):
        w = split(noisy(m_ref, s_ref, nin_ref, nout_ref, s))
        acc[:, 512 * s:512 * s + 512] += dot3(f, w, TN)
    @pl.when(j == pl.num_programs(0) - 1)
    def _():
        h = acc[...] + hb_ref[...]
        h_ref[...] = h
        gt = jnp.transpose(silu(h))
        for s in range(2):
            for q in range(2):
                for gg in range(2):
                    for z in range(4):
                        at_row = 512 * s + 256 * q + 128 * gg + 32 * z
                        g_ref[q, z, gg, s] = gt[at_row:at_row + 32]
        both = dot3(split(wo_ref[...]), split(jnp.concatenate([gt[:512], gt[512:]], axis=1)))
        bias = column(bo_ref[...], 128)
        adv[...] = both[:, 128:] + bias
        z = both[0:PAD, 0:128] + bias[0:PAD]
        chosen = c_ref[...]
        for i in range(ACTIONS):
            z = z + mask_of(chosen, i) * adv[ATOMS * (i + 1):ATOMS * (i + 1) + PAD, :]
        row = lax.broadcasted_iota(jnp.int32, (PAD, 128), 0)
        z = jnp.where(row < ATOMS, z, -1e30)
        top = jnp.max(z, axis=0, keepdims=True)
        e = jnp.exp(z - top)
        tot = jnp.sum(e, axis=0, keepdims=True)
        logp_ref[...] = (z - top) - jnp.log(tot)
        p = e / tot
        dist = jnp.zeros((PAD, 128), F32)
        for i in range(ATOMS):
            lower = pl_ref[i:i + 1, :]
            share = pw_ref[i:i + 1, :]
            pi = p[i:i + 1, :]
            dist = dist + jnp.where(row == lower, pi * (1.0 - share), 0.0) + jnp.where(row == lower + 1, pi * share, 0.0)
        dist_ref[...] = dist
        if net:
            for k in range(4):
                wires[1].arrived(k)
            wires[1].sent()
            for copy in fan:
                copy.wait()

def hidden(net, f, m, s, nin, nout, hb, wo, bo, c, plow, pw):
    full = lambda *t: pl.BlockSpec(t, lambda j: (0,) * len(t))
    sds = lambda *t: jax.ShapeDtypeStruct(t, F32)
    k = 3136 // STEPS
    wspec = pl.BlockSpec((2, k, 512), lambda j: (0, j, 0))
    return pl.pallas_call(
        functools.partial(hid_kernel, net), grid=(STEPS,),
        in_specs=[pl.BlockSpec((k, 128), lambda j: (j, 0)), wspec, wspec, pl.BlockSpec((1, 2, k), lambda j: (j, 0, 0)), full(2, 512), full(1, 1024),
                  full(OUTP, 512), full(1, OUTP), full(1, 128), full(ATOMS, 128), full(ATOMS, 128)] + [ANY] * net,
        out_specs=[full(128, 1024), full(2, 4, 2, 2, 32, 128), full(PAD, 128), full(PAD, 128)] + [ANY, ANY, ANY] * net,
        out_shape=[sds(128, 1024), sds(2, 4, 2, 2, 32, 128), sds(PAD, 128), sds(PAD, 128)]
        + [sds(2, 4, FIRST, 128), sds(2, 4, 200 - FIRST, 128), sds(3, 4, FIRST, 128)] * net,
        scratch_shapes=[pltpu.VMEM((128, 1024), F32), pltpu.VMEM((OUTP, 128), F32)] + ([pltpu.SemaphoreType.DMA((3,))] * 2 + scatter_sems(2, FIRST, 128) + scatter_sems(2, 200 - FIRST, 128)) * net,
        compiler_params=pltpu.CompilerParams(vmem_limit_bytes=60 * 2**20, **(dict(collective_id=1, has_side_effects=True) if net else {})),
    )(f, m, s, nin, nout, hb, wo, bo, c, plow, pw, *([f] * net))

def hid_bwd_kernel(net, t_ref, logp_ref, h_ref, m_ref, s_ref, nin_ref, nout_ref, wo_ref, c_ref, *rest):
    if net:
        noise, rest = list(zip(rest[2:6], rest[16:20])), rest[:2] + rest[6:16] + rest[20:]
        f1b_ref, hid_ref, df_ref, small_ref, f2b_ref, g1_ref, d1_ref, dz1_ref, g2_ref, d2_ref, dz2_ref, d3_ref = rest[:12]
        dth, dtl, da, msg, dz_to, t_got = rest[12:18]
        ds, dr, gs, gr, qs, qr, fs, fr, ts, tr, hs, hr, ss, sr, ps, pr, own = rest[18:35]
        g_wire = g_scatter(hid_ref, g1_ref, rest[35:39])
        z_wire = z_scatter(dz_to, dz1_ref, rest[39:42])
        p, g, z, y = coords()
        d_line = Line(2, lambda i: d1_ref.at[z, i], lambda zz, i: d1_ref.at[zz, i], rest[42], rest[43])
        partner = at(1 - p, g, z, y)
        target = remote(t_ref, t_got, ts, tr, partner)
        hands = [remote(dz2_ref, dz2_ref, hs.at[0], hr.at[0], partner), remote(dz1_ref, dz1_ref, hs.at[1], hr.at[1], partner)]
        tells = [remote(src, dst, rest[44].at[i], rest[45].at[i], partner) for i, (src, dst) in enumerate(noise)]
        give = remote(msg.at[1], d1_ref.at[z], ps, pr, partner)
        keep = pltpu.make_async_copy(msg.at[0], d1_ref.at[z], own)
        fan_f = f_fan(f1b_ref, f2b_ref, fs, fr)
        fan_g = spread_plane(p, g, z, y, lambda gd, yd: g1_ref.at[:, gd], lambda m: g2_ref.at[m], gs, gr)
        fan_z = spread_plane(p, g, z, y, lambda gd, yd: dz1_ref, lambda m: dz2_ref.at[m], qs, qr)
        def fan_d(place, zz):
            return spread_plane(p, g, z, y, lambda gd, yd: d1_ref.at[zz, yd], lambda m: d2_ref.at[m, zz], ds.at[place], dr.at[place])
        def swap_own(place, zz):
            return remote(d1_ref.at[zz, y], d3_ref.at[3, zz], ss.at[place, 0], sr.at[place, 0], partner)
        def swap(place, zz):
            return remote(d2_ref.at[:, zz], d3_ref.at[pl.ds(0, 3), zz], ss.at[place, 1], sr.at[place, 1], partner)
        def forward(place, zz, s):
            along_y, along_x, both = fan_d(place, zz)
            @pl.when(y == s)
            def _():
                along_x.start()
                swap_own(place, zz).start()
            @pl.when(y != s)
            def _():
                both.start()
                along_y.start()
        def forward_small():
            for k in range(4):
                g_wire.arrived(k)
            for copy in fan_g:
                copy.start()
            for k in range(4):
                z_wire.arrived(k)
            @pl.when(p == 0)
            def _():
                for copy in fan_z:
                    copy.start()
    else:
        df_ref, small_ref, msg, dz_to, dth, dtl, da = rest
        t_got = t_ref
    j = pl.program_id(0)
    def begin():
        t = t_got[...]
        logp = logp_ref[...]
        chosen = c_ref[...]
        row = lax.broadcasted_iota(jnp.int32, (PAD, 128), 0)
        d = (jnp.exp(logp) * jnp.sum(t, axis=0, keepdims=True) - t) * (1.0 / 128)
        loss = -jnp.sum(jnp.where(row < ATOMS, t * logp, 0.0), axis=1, keepdims=True) * (1.0 / 128)
        dz_to[...] = jnp.where(row == ATOMS, chosen.astype(F32), d)
        da[...] = jnp.zeros_like(da)
        da[0:PAD, 0:128] = d
        for i in range(ACTIONS):
            da[ATOMS * (i + 1):ATOMS * (i + 1) + PAD, 128:256] = mask_of(chosen, i) * d
        every = da[...]
        eh, el = split(every)
        grads = dot3((eh, el), split(wo_ref[...]), TN)
        small_ref[...] = jnp.zeros_like(small_ref)
        for s in range(2):
            dp = grads[128 * s:128 * s + 128] * dsilu(h_ref[:, 512 * s:512 * s + 512])
            total = jnp.sum(dp, axis=0, keepdims=True)
            for c in range(4):
                msg[c // 2, s, 128 * (c % 2):128 * (c % 2) + 128, :] = dp[:, 128 * c:128 * c + 128]
                small_ref[4 * s + c:4 * s + c + 1, :] = total[:, 128 * c:128 * c + 128]
            hi, lo = split(jnp.transpose(dp))
            dth[s] = hi
            dtl[s] = lo
        if net:
            give.start()
            keep.start()
            z_wire.start()
            keep.wait()
        ones = jnp.ones((8, 256), BF)
        left = (every - eh.astype(F32)) - el.astype(F32)
        rows = dot(ones, eh, NT) + dot(ones, el, NT) + dot(ones, left.astype(BF), NT)
        for c in range(8):
            n = min(128, OUTP - 128 * c)
            small_ref[8 + c:9 + c, 0:n] = rows[0:1, 128 * c:128 * c + n]
        small_ref[16:17, :] = jnp.broadcast_to(jnp.sum(loss, axis=0, keepdims=True), (1, 128))
    def step():
        out = None
        for s in range(2):
            w = split(noisy(m_ref, s_ref, nin_ref, nout_ref, s))
            r = dot3(w, (dth[s], dtl[s]))
            out = r if out is None else out + r
        df_ref[...] = out
    if not net:
        pl.when(j == 0)(begin)
        step()
        return
    @pl.when(j == 0)
    def _():
        greet(line(p, g, z, y) + plane(p, g, z, y))
        pl.when(p == 1)(target.start)
        for copy in fan_f:
            copy.start()
        g_wire.start()
        @pl.when(p == 0)
        def _():
            target.wait_recv()
            begin()
            for copy in tells:
                copy.start()
        pl.when(p == 1)(give.wait_recv)
        d_line.start(0)
        for s in range(2):
            forward(0, z, s)
    pl.when(p == 0)(step)
    pl.when(j == 3)(forward_small)
    @pl.when(j == pl.num_programs(0) - 1)
    def _():
        for t in range(1, 4):
            d_line.arrive(t, forward)
        pl.when(p == 1)(target.wait_send)
        @pl.when(p == 0)
        def _():
            for copy in fan_z:
                copy.wait()
            for copy in hands:
                copy.start()
        def landed(place, zz):
            for copy in fan_d(place, zz):
                copy.wait_recv()
            swap(place, zz).start()
        d_line.each(landed)
        for copy in fan_f + fan_g:
            copy.wait()
        def gone(place, zz):
            for copy in fan_d(place, zz):
                copy.wait_send()
            swap(place, zz).wait()
            swap_own(place, zz).wait()
        d_line.each(gone)
        d_line.sent()
        @pl.when(p == 0)
        def _():
            give.wait_send()
            for copy in hands + tells:
                copy.wait_send()
        @pl.when(p == 1)
        def _():
            for copy in hands + tells:
                copy.wait_recv()
        for wire in (g_wire, z_wire):
            wire.sent()

def hidden_bwd(net, t, logp, h, m, s, nin, nout, wo, c, *wired):
    full = lambda *u: pl.BlockSpec(u, lambda j: (0,) * len(u))
    sds = lambda *u: jax.ShapeDtypeStruct(u, F32)
    dma = pltpu.SemaphoreType.DMA
    k = 3136 // STEPS
    wspec = pl.BlockSpec((2, k, 512), lambda j: (0, j, 0))
    return pl.pallas_call(
        functools.partial(hid_bwd_kernel, net), grid=(STEPS,),
        in_specs=[full(PAD, 128), full(PAD, 128), full(128, 1024), wspec, wspec, pl.BlockSpec((1, 2, k), lambda j: (j, 0, 0)), full(2, 512),
                  full(OUTP, 512), full(1, 128)] + [ANY] * (6 * net),
        out_specs=[pl.BlockSpec((k, 128), lambda j: (j, 0)), full(24, 128)] + ([ANY] * 12 if net else [full(2, 2, 256, 128), full(PAD, 128)]),
        out_shape=[sds(3136, 128), sds(24, 128)] + ([sds(3, 4, 200 - FIRST, 128), sds(4, 2, 2, 32, 128), sds(4, 2, 256, 128), sds(4, PAD, 128), sds(3, 4, 2, 32, 128), sds(3, 4, 256, 128),
                                                     sds(3, 4, PAD, 128), sds(4, 4, 256, 128), sds(2, 3136), sds(2, 512), sds(2, 512), sds(1, OUTS)] if net else [sds(2, 2, 256, 128), sds(PAD, 128)]),
        scratch_shapes=[pltpu.VMEM((2, 512, 128), BF), pltpu.VMEM((2, 512, 128), BF), pltpu.VMEM((OUTP, 256), F32)]
        + ([pltpu.VMEM((2, 2, 256, 128), F32), pltpu.VMEM((PAD, 128), F32), pltpu.VMEM((PAD, 128), F32), dma((7, 3)), dma((7, 3))] + [dma((3,))] * 6 + [dma, dma, dma((2,)), dma((2,)), dma((7, 2)), dma((7, 2)), dma, dma, dma]
           + scatter_sems(1, 2, 2, 32, 128) + scatter_sems(1) + line_sems(2) + [dma((4,)), dma((4,))]) * net,
        compiler_params=pltpu.CompilerParams(vmem_limit_bytes=60 * 2**20, **(dict(collective_id=2, has_side_effects=True) if net else {})),
    )(t, logp, h, m, s, nin, nout, wo, c, *wired)

def dsilu(v):
    s = jax.nn.sigmoid(v)
    return s * (1.0 + v * (1.0 - s))


ROWS = 768

def bwd_kernel(net, x_ref, pre1_hbm, pre2_ref, pre3_ref, df_ref, w1_ref, w2_ref, w3_ref, *rest):
    if net:
        r_ref, q_ref, s0_ref, tot_ref, sg_ref, ag_ref, ah_ref, bg_ref, bh_ref = rest[:9]
        xs, pre1_ref, xh, xl, d3f, d3h, d3l, d2h, d2l, d1h, d1l, h2h, h2l, acc2, a1, a2, a3, pay, lob, upb, x_sem, sem1, ls, us = rest[9:33]
        got, got1, red, tot, ur, zs_, zr, ys, yr, own, gs, gr, ws, wr, as_, ar, bs, br, es, er, cs, cr, one_ = rest[33:]
        p, g, z, y = coords()
        reps = lax.axis_size("rep")
        chips = 2 * reps
        me = g * reps + lax.axis_index("rep")
        size = ROWS // chips
        def chip(i):
            return (0, i // reps, i % reps)
        def part(i):
            return pl.ds(pl.multiple_of(i * size, 8), size)
        def give(k):
            to = (me + k) % chips
            if k:
                return remote(pay.at[part(to)], got.at[me], as_.at[k], ar.at[k], chip(to))
            return pltpu.make_async_copy(pay.at[part(me)], got.at[me], one_)
        def given(k):
            who = (me + chips - k) % chips
            return remote(pay.at[part(me)], got.at[who], as_.at[k], ar.at[k], chip(who))
        def show(k):
            return remote(pay.at[pl.ds(672, 64)], got1.at[me], es.at[k], er.at[k], chip((me + k) % chips))
        def shown(k):
            who = (me + chips - k) % chips
            return remote(pay.at[pl.ds(672, 64)], got1.at[who], es.at[k], er.at[k], chip(who))
        def tell(k):
            return remote(red, tot.at[part(me)], bs.at[k], br.at[k], chip((me + k) % chips))
        def told(k):
            who = (me + chips - k) % chips
            return remote(red, tot.at[part(who)], bs.at[k], br.at[k], chip(who))
        hand = remote(tot, tot, cs, cr, at(1 - p, g, z, y))
        def head_at(ref, yy, zz):
            return ref.at[zz, pl.ds(5 * yy, 5 - yy)]
        def head_of(yy):
            return q_ref.at[pl.ds(5 * yy, 5 - yy)]
        def slots(yy, zz):
            return ag_ref.at[yy, zz], head_at(ah_ref, yy, zz), bg_ref.at[yy, zz], head_at(bh_ref, yy, zz)
        def lines(yy):
            mine = (r_ref, head_of(yy)) + slots(yy, z)[2:]
            return Line(4, lambda i: mine[i], lambda zz, i: slots(yy, zz)[i], zs_, zr)
        def keep(yy):
            a, b, _, _ = slots(yy, z)
            return [pltpu.make_async_copy(r_ref, a, own.at[0]), pltpu.make_async_copy(head_of(yy), b, own.at[1])]
        def give_own(yy):
            _, _, a, b = slots(yy, z)
            return [remote(r_ref, a, gs.at[0], gr.at[0], at(1, g, z, y)), remote(head_of(yy), b, gs.at[1], gr.at[1], at(1, g, z, y))]
        def along_y(place, zz, yy):
            src = slots(yy, zz) if place else (r_ref, head_of(yy)) + slots(yy, z)[2:]
            return [remote(src[i], slots(yy, zz)[i], ys.at[place, i], yr.at[place, i], at(p, g, z, 1 - y)) for i in range(4)]
        def bring(place, zz, yy):
            a, b, c, d = slots(yy, zz)
            return [remote(c, a, ws.at[yy, place, 0], wr.at[yy, place, 0], at(0, g, z, y)), remote(d, b, ws.at[yy, place, 1], wr.at[yy, place, 1], at(0, g, z, y))]
        def each(do, flipped=False):
            for yy in range(2):
                pl.when(y == (1 - yy if flipped else yy))(functools.partial(do, yy))
        def states_out(j, slot):
            return (pltpu.make_async_copy(lob.at[slot], sg_ref.at[pl.ds(4 * j, 4)], ls.at[slot]),
                    remote(upb.at[slot], sg_ref.at[pl.ds(4 * j, 4)], us.at[slot], ur.at[j], at(1 - p, g, z, y)))
        def gather(yy):
            def then(place, zz, i):
                along_y(place, zz, yy)[i].start()
                if i >= 2:
                    bring(place, zz, yy)[i - 2].start()
            for copy in give_own(yy):
                copy.wait_recv()
            lines(yy).start(0)
            for i in range(4):
                then(0, z, i)
            for copy in keep(yy):
                copy.start()
            for t in range(1, 4):
                lines(yy).arrive(t, then)
        def second(yy):
            def landed(place, zz):
                for copy in along_y(place, zz, yy):
                    copy.wait_recv()
                for copy in bring(place, zz, yy):
                    copy.start()
            lines(yy).each(landed)
        def finished(yy):
            def gone(place, zz):
                for copy in along_y(place, zz, yy) + bring(place, zz, yy):
                    copy.wait_send()
            for copy in keep(yy):
                copy.wait()
            lines(yy).sent()
            lines(yy).each(gone)
        def second_sent(yy):
            def gone(place, zz):
                for copy in bring(place, zz, yy):
                    copy.wait_send()
            lines(yy).each(gone)
        def brought(yy):
            def came(place, zz):
                for copy in bring(place, zz, yy):
                    copy.wait_recv()
            lines(yy).each(came)
    else:
        tot_ref, lo_ref, up_ref, xs, pre1_ref, xh, xl, d3f, d3h, d3l, d2h, d2l, d1h, d1l, h2h, h2l, acc2, a1, a2, a3, pay, lob, upb, x_sem, sem1, ls, us = rest
        def states_out(j, slot):
            return (pltpu.make_async_copy(lob.at[slot], lo_ref.at[pl.ds(4 * j, 4)], ls.at[slot]),
                    pltpu.make_async_copy(upb.at[slot], up_ref.at[pl.ds(4 * j, 4)], us.at[slot]))
    small_ref = pay.at[pl.ds(24, 648)]
    last = 20
    def x_in(j):
        return pltpu.make_async_copy(x_ref.at[pl.ds(4 * j, 4)], xs.at[pl.ds(4 * j, 4)], x_sem.at[j])
    pre1_in = pltpu.make_async_copy(pre1_hbm, pre1_ref, sem1)
    def fetch():
        pre1_in.start()
        for j in range(21):
            x_in(j).start()
    def upper():
        for ref in (d3h, d3l, d2h, d2l, acc2, a2, a3):
            ref[...] = jnp.zeros_like(ref)
        small_ref[...] = jnp.zeros((648, 128), F32)
        for ref in (d1h, d1l):
            ref[0] = jnp.zeros((704, 128), BF)
            ref[21] = jnp.zeros((704, 128), BF)
            ref[:, 0:32, :] = jnp.zeros((22, 32, 128), BF)
            ref[:, 672:704, :] = jnp.zeros((22, 32, 128), BF)
        d3f[...] = df_ref[...] * dsilu(pre3_ref[...])
        total = jnp.zeros((64, 128), F32)
        for y in range(7):
            for x in range(7):
                d = d3f[pl.ds(y * 7 + x, 64, stride=49), :]
                total = total + d
                hi, lo = split(d)
                d3h[y + 2, 64 * (x + 2):64 * (x + 3), :] = hi
                d3l[y + 2, 64 * (x + 2):64 * (x + 3), :] = lo
        small_ref[640:641, 0:64] = jnp.sum(jnp.transpose(total), axis=0, keepdims=True)
        w3 = (w3_ref[0], w3_ref[1])
        h2h[:, 576:, :] = jnp.zeros((9, 64, 128), BF)
        h2l[:, 576:, :] = jnp.zeros((9, 64, 128), BF)
        def split2(y, c):
            hi, lo = split(silu(pre2_ref[y]))
            h2h[y, 0:576, :] = hi
            h2l[y, 0:576, :] = lo
            return c
        lax.fori_loop(0, 9, split2, 0)
        def dgrad3(y, c):
            rh = jnp.concatenate([d3h[y + 2, 128 * i:128 * i + 256, :] for i in range(5)], axis=1)
            rl = jnp.concatenate([d3l[y + 2, 128 * i:128 * i + 256, :] for i in range(5)], axis=1)
            r = dot3(w3, (rh, rl))
            for ky in range(3):
                for i in range(5):
                    acc2[y + ky, 128 * i:128 * i + 128, :] += r[128 * ky:128 * ky + 128, 128 * i:128 * i + 128]
            return c
        lax.fori_loop(0, 7, dgrad3, 0)
        def wgrad3(y, c):
            def lhs(ref):
                return jnp.concatenate([jnp.concatenate([ref[y - ky + 2, 128 * (i + 1):128 * (i + 2), :] for i in range(4)], axis=1) for ky in range(3)], axis=0)
            def rhs(ref):
                return jnp.concatenate([ref[y, 128 * i:128 * i + 256, :] for i in range(4)], axis=1)
            a3[...] += dot3((lhs(d3h), lhs(d3l)), (rhs(h2h), rhs(h2l)), NT)
            return c
        lax.fori_loop(0, 9, wgrad3, 0)
        for ky in range(3):
            grad = a3[128 * ky:128 * ky + 64, 0:192] + a3[128 * ky + 64:128 * ky + 128, 64:256]
            small_ref[256 + 64 * ky:320 + 64 * ky, :] = grad[:, 0:128]
            small_ref[448 + 64 * ky:512 + 64 * ky, 0:64] = grad[:, 128:192]
        def step2(y, total):
            for x in range(9):
                d = acc2[y, 64 * x:64 * x + 64, :] * dsilu(pre2_ref[y, 64 * x:64 * x + 64, :])
                total = total + d
                hi, lo = split(d)
                d2h[y + 1, 64 * (x + 1):64 * (x + 2), :] = hi
                d2l[y + 1, 64 * (x + 1):64 * (x + 2), :] = lo
            return total
        total = lax.fori_loop(0, 9, step2, jnp.zeros((64, 128), F32))
        small_ref[641:642, 0:64] = jnp.sum(jnp.transpose(total), axis=0, keepdims=True)
    def block2(y, total):
        w2 = (w2_ref[0], w2_ref[1])
        rh = jnp.concatenate([d2h[pl.ds(y, 2), 64 * i:64 * i + 128, :].reshape(256, 128) for i in range(10)], axis=1)
        rl = jnp.concatenate([d2l[pl.ds(y, 2), 64 * i:64 * i + 128, :].reshape(256, 128) for i in range(10)], axis=1)
        r = dot3(w2, (rh, rl))
        h1h, h1l = [], []
        for py in range(2):
            rowh, rowl = [], []
            for i in range(10):
                v = pre1_ref[2 * y + py, 64 * i:64 * i + 64, :]
                s = jax.nn.sigmoid(v)
                d = r[64 * py:64 * py + 64, 128 * i:128 * i + 128] * (s * (1.0 + v * (1.0 - s)))
                total = total + d[0:32] + d[32:64]
                hi, lo = split(d)
                d1h[2 * y + py + 1, 64 * i + 32:64 * i + 96, :] = hi
                d1l[2 * y + py + 1, 64 * i + 32:64 * i + 96, :] = lo
                hi, lo = split(v * s)
                rowh.append(hi)
                rowl.append(lo)
            h1h.append(rowh)
            h1l.append(rowl)
        def lhs(ref):
            return jnp.concatenate([jnp.concatenate([ref[y + 1 - h, 64 * (i + 1):64 * (i + 2), :] for i in range(9)], axis=1) for h in range(2)], axis=0)
        def rhs(rows):
            return jnp.concatenate([jnp.concatenate([rows[0][i], rows[0][i + 1], rows[1][i], rows[1][i + 1]], axis=0) for i in range(9)], axis=1)
        a2[...] += dot3((lhs(d2h), lhs(d2l)), (rhs(h1h), rhs(h1l)), NT)
        return total
    def lower():
        pre1_in.wait()
        total = lax.fori_loop(0, 10, block2, jnp.zeros((32, 128), F32))
        small_ref[642:643, 0:32] = jnp.sum(jnp.transpose(total), axis=0, keepdims=True)
        small_ref[0:128, :] = a2[:, 0:128]
        small_ref[128:256, :] = a2[:, 128:256]
    def states_gone(j, slot):
        a, b = states_out(j, slot)
        a.wait()
        if net:
            b.wait_send()
        else:
            b.wait()
    def wgrad1(j, carry):
        x_in(j).wait()
        v = xs[pl.ds(4 * j, 4)]
        hi = v.astype(BF)
        xh[:, 0:336, :] = hi
        xl[:, 0:336, :] = (v - hi.astype(F32)).astype(BF)
        def lhs(ref):
            return jnp.concatenate([jnp.concatenate([ref[j + 1 - h, 96 * i + 32:96 * i + 128, :] for i in range(7)], axis=1) for h in range(2)], axis=0)
        def rhs(ref):
            return jnp.concatenate([ref[:, 48 * i:48 * i + 64, :].reshape(256, 128) for i in range(7)], axis=1)
        a1[...] += dot3((lhs(d1h), lhs(d1l)), (rhs(xh), rhs(xl)), NT)
        return carry
    def first_grad():
        lax.fori_loop(0, 21, wgrad1, 0)
        for h in range(2):
            for ky in range(4):
                grad = a1[96 * h:96 * h + 32, 64 * ky:64 * ky + 32]
                grad = grad + a1[96 * h + 32:96 * h + 64, 64 * ky + 16:64 * ky + 48]
                grad = grad + a1[96 * h + 64:96 * h + 96, 64 * ky + 32:64 * ky + 64]
                pay[672 + 32 * h:704 + 32 * h, 32 * ky:32 * ky + 32] = grad
    def dgrad1(j, carry):
        def both(ref):
            return jnp.concatenate([ref[pl.ds(j, 2), 96 * i:96 * i + 128, :].reshape(256, 128) for i in range(7)], axis=1)
        r = dot3((w1_ref[0], w1_ref[1]), (both(d1h), both(d1l)))
        slot = j % 2
        pl.when(j >= 2)(lambda: states_gone(j - 2, slot))
        lo_to, up_to = lob.at[slot], upb.at[slot]
        for ky in range(4):
            for i in range(7):
                lo_to[ky, 24 * i:24 * i + 24, :] = r[24 * ky:24 * ky + 24, 128 * i:128 * i + 128]
                up_to[ky, 24 * i:24 * i + 24, :] = r[96 + 24 * ky:96 + 24 * ky + 24, 128 * i:128 * i + 128]
        for copy in states_out(j, slot):
            copy.start()
        return carry
    if net:
        pl.when(p == 0)(fetch)
        pl.when(p == 0)(lambda: greet([chip((me + k) % chips) for k in range(1, chips)] + [at(1, g, z, y)]))
        pl.when(p == 1)(lambda: greet([at(1, g, flip(z, k), y) for k in range(1, 4)] + [at(1, g, z, 1 - y), at(0, g, z, y)]))
        def begin(yy):
            for copy in give_own(yy):
                copy.start()
        pl.when(p == 0)(lambda: each(begin))
        @pl.when(p == 1)
        def _():
            each(gather)
            each(second, flipped=True)
        pay[0:24, :] = s0_ref[...]
    else:
        pay[0:24, :] = jnp.zeros((24, 128), F32)
    pay[672:, :] = jnp.zeros((ROWS - 672, 128), F32)
    xh[:, 336:, :] = jnp.zeros((4, 16, 128), BF)
    xl[:, 336:, :] = jnp.zeros((4, 16, 128), BF)
    a1[...] = jnp.zeros_like(a1)
    if net:
        @pl.when(p == 0)
        def _():
            upper()
            lower()
            first_grad()
            for k in range(chips):
                give(k).start()
            for k in range(1, chips):
                show(k).start()
            got1[me] = pay[672:736, :]
            lax.fori_loop(0, 12, dgrad1, 0)
            give(0).wait()
            for k in range(1, chips):
                given(k).wait_recv()
            red[...] = jnp.sum(got[...], axis=0)
            tot[part(me), :] = red[...]
            for k in range(1, chips):
                tell(k).start()
            lax.fori_loop(12, 21, dgrad1, 0)
            for k in range(1, chips):
                told(k).wait_recv()
            for k in range(1, chips):
                shown(k).wait_recv()
            tot[672:736, :] = jnp.sum(got1[...], axis=0)
            hand.start()
            for k in range(1, chips):
                give(k).wait_send()
                tell(k).wait_send()
                show(k).wait_send()
            hand.wait_send()
            for j in (last - 1, last):
                states_gone(j, j % 2)
    else:
        fetch()
        upper()
        lower()
        first_grad()
        lax.fori_loop(0, 21, dgrad1, 0)
        for j in (last - 1, last):
            states_gone(j, j % 2)
    if net:
        @pl.when(p == 1)
        def _():
            hand.wait_recv()
            def arrive(i, c):
                states_out(i, 0)[1].wait_recv()
                return c
            lax.fori_loop(0, last + 1, arrive, 0)
        tot_ref[...] = tot[...]
        @pl.when(p == 0)
        def _():
            def given_own(yy):
                for copy in give_own(yy):
                    copy.wait_send()
            each(given_own)
            brought(0)
            brought(1)
        @pl.when(p == 1)
        def _():
            each(finished)
            each(second_sent, flipped=True)
    else:
        tot_ref[...] = pay[...]

def backward(net, x, pre1, pre2, pre3, df, w1, w2, w3, *wired):
    sds = lambda *s: jax.ShapeDtypeStruct(s, F32)
    vmb = lambda *s: pltpu.VMEM(s, BF)
    f32 = lambda *s: pltpu.VMEM(s, F32)
    dma = pltpu.SemaphoreType.DMA
    return pl.pallas_call(
        functools.partial(bwd_kernel, net),
        in_specs=[ANY, ANY] + [VMEM] * 6 + [VMEM] * 3 * net,
        out_specs=[VMEM] + [ANY] * (5 if net else 2),
        out_shape=[sds(ROWS, 128)] + ([sds(84, 168, 128)] + [sds(2, 4, 200, 512), sds(4, 9, 32, 128)] * 2 if net else [sds(84, 168, 128), sds(84, 168, 128)]),
        scratch_shapes=[f32(84, 336, 128), f32(20, 640, 128), vmb(4, 352, 128), vmb(4, 352, 128), f32(3136, 128), vmb(11, 768, 128), vmb(11, 768, 128), vmb(11, 704, 128),
                        vmb(11, 704, 128), vmb(22, 704, 128), vmb(22, 704, 128), vmb(9, 640, 128), vmb(9, 640, 128), f32(9, 640, 128), f32(192, 256), f32(128, 256),
                        f32(384, 256), f32(ROWS, 128), f32(2, 4, 168, 128), f32(2, 4, 168, 128), dma((21,)), dma, dma((2,)), dma((2,))]
        + ([f32(16, ROWS // 16, 128), f32(16, 64, 128), f32(ROWS // 16, 128), f32(ROWS, 128), dma((21,))]
           + line_sems(4) + [dma((7, 4))] * 2 + [dma((2,))] * 3 + [dma((2, 7, 2))] * 2 + [dma((16,))] * 6 + [dma] * 3) * net,
        compiler_params=pltpu.CompilerParams(vmem_limit_bytes=62 * 2**20, **(dict(collective_id=3, has_side_effects=True) if net else {})),
    )(x, pre1, pre2, pre3, df, w1, w2, w3, *wired)

def wide_kernel(f1a, f1b, f2a, f2b, d1, d2, d3, g1, g2, z1, z2, r_ref, q_ref, fv, dv, ev, gv, zv, acc, acq, da, sem):
    p, g = lax.axis_index("pair"), lax.axis_index("group")
    y = lax.axis_index("rep") % 2
    three, last = pl.ds(0, 3), 3
    head, tail = pl.ds(0, FIRST), pl.ds(FIRST, 200 - FIRST)
    pairs = [(f2a, fv.at[three, :, head]), (f1a.at[g], fv.at[last, :, head]), (f2b, fv.at[three, :, tail]), (f1b.at[g], fv.at[last, :, tail]),
             (d2, dv.at[three]), (d1.at[:, y], dv.at[last]), (d3, ev), (g2, gv.at[three]), (g1.at[:, g], gv.at[last]), (z2, zv.at[three]), (z1, zv.at[last])]
    copies = [pltpu.make_async_copy(a, b, sem.at[i]) for i, (a, b) in enumerate(pairs)]
    for copy in copies:
        copy.start()
    acc[...] = jnp.zeros_like(acc)
    acq[...] = jnp.zeros_like(acq)
    da[...] = jnp.zeros_like(da)
    for copy in copies:
        copy.wait()
    def block(ref, m):
        return jnp.concatenate([jnp.concatenate([ref[m, i, 128 * c:128 * c + 128, :] for c in range(2)], axis=1) for i in range(4)], axis=0)
    def step(m, carry):
        f = split(jnp.concatenate([fv[m, i] for i in range(4)], axis=1))
        acc[0] += dot3(f, split(block(dv, m)))
        acc[1] += dot3(f, split(block(ev, m)))
        dz = jnp.concatenate([zv[m, i] for i in range(4)], axis=1)
        row = lax.broadcasted_iota(jnp.int32, (PAD, 512), 0)
        chosen = dz[ATOMS:ATOMS + 1].astype(jnp.int32)
        d = jnp.where(row < ATOMS, dz, 0.0)
        da[0:PAD, :] = d
        for i in range(ACTIONS):
            da[128 + ATOMS * i:128 + ATOMS * i + PAD, :] = mask_of(chosen, i) * d
        def units(s):
            return split(jnp.concatenate([gv[m, i, s] for i in range(4)], axis=1))
        @pl.when(y == 0)
        def _():
            acq[:, 0:128] += dot3(units(0), split(da[0:128, :]), NT)
            acq[:, 128:640] += dot3(units(1), split(da[128:640, :]), NT)
        @pl.when(y == 1)
        def _():
            acq[:, 640:1152] += dot3(units(1), split(da[640:1152, :]), NT)
        return carry
    lax.fori_loop(0, 4, step, 0)
    r_ref[:, 0:256] = jnp.where(p == 0, acc[0], acc[1])
    r_ref[:, 256:512] = jnp.where(p == 0, acc[1], acc[0])
    for c in range(9):
        q_ref[c] = acq[:, 128 * c:128 * c + 128]

def wide_grads(*messages):
    sds = lambda *s: jax.ShapeDtypeStruct(s, F32)
    f32 = lambda *s: pltpu.VMEM(s, F32)
    return pl.pallas_call(
        wide_kernel, in_specs=[ANY] * 11, out_specs=[VMEM] * 2,
        out_shape=[sds(200, 512), sds(9, 32, 128)],
        scratch_shapes=[f32(4, 4, 200, 128), f32(4, 4, 256, 128), f32(4, 4, 256, 128), f32(4, 4, 2, 32, 128), f32(4, 4, PAD, 128),
                        f32(2, 200, 256), f32(32, 1152), f32(1152, 512), pltpu.SemaphoreType.DMA((11,))],
        compiler_params=pltpu.CompilerParams(vmem_limit_bytes=60 * 2**20),
    )(*messages)

def torso_out(tot, k1_ref, k2_ref, k3_ref, b1_ref, b2_ref, b3_ref, t1, t2):
    t1[:, 0:64] = jnp.transpose(tot[672:736, :])
    t1[:, 64:128] = jnp.zeros((128, 64), F32)
    for ky in range(4):
        for c in range(4):
            v = t1[pl.ds(32 * ky + c, 8, stride=4), :]
            for h in range(2):
                k1_ref[c, 4 * h + ky] = v[:, 32 * h:32 * h + 32]
    for py in range(2):
        t2[...] = jnp.transpose(tot[24 + 128 * py:152 + 128 * py, :])
        for h in range(2):
            for kx in range(4):
                k2_ref[:, 2 * h + py, kx, :] = t2[32 * kx:32 * kx + 32, 64 * h:64 * h + 64]
    for ky in range(3):
        for kx in range(3):
            base = (280 if kx < 2 else 472) + 64 * ky
            k3_ref[ky, kx] = tot[base:base + 64, 64 * (kx % 2):64 * (kx % 2) + 64]
    b3_ref[...] = tot[664:665, 0:64]
    b2_ref[...] = tot[665:666, 0:64]
    b1_ref[...] = tot[666:667, 0:32]

def finish_kernel(sg_ref, ag_ref, ah_ref, tot_ref, in_ref, out_ref, ein_ref, eout_ref, mean_ref, sigma_ref, hm_ref, hs_ref, k1_ref, k2_ref, k3_ref, b1_ref, b2_ref, b3_ref,
                  hb_ref, hbs_ref, bo_ref, bos_ref, loss_ref, states_ref, t1, t2, sv, sem):
    parts = [pl.ds(21 * i, 21) for i in range(4)]
    reads = [pltpu.make_async_copy(sg_ref.at[part], sv.at[part], sem.at[0, i]) for i, part in enumerate(parts)]
    moves = [pltpu.make_async_copy(sv.at[part], states_ref.at[part], sem.at[1, i]) for i, part in enumerate(parts)]
    for copy in reads:
        copy.start()
    for i in range(4):
        reads[i].wait()
        moves[i].start()
    for s in range(2):
        tall = column(in_ref[s:s + 1, :], 512) * out_ref[s:s + 1, :]
        for z, (start, n) in enumerate(((0, 200), (200, 200), (400, 184), (584, 200))):
            v = ag_ref[s, z, 0:n, :]
            mean_ref[s, start:start + n, :] = v
            sigma_ref[s, start:start + n, :] = v * tall[start:start + n]
    noise = column(eout_ref[...], 128)
    for c in range(9):
        start = 0 if c == 0 else ATOMS + 128 * (c - 1)
        n = min(128, (ATOMS if c == 0 else OUTS) - start)
        v = jnp.transpose(jnp.concatenate([ah_ref[z, c] for z in range(4)], axis=0))[0:n]
        hm_ref[start:start + n, :] = v
        hs_ref[start:start + n, :] = v * (noise[start:start + n] * ein_ref[min(c, 1):min(c, 1) + 1, :])
    torso_out(tot_ref, k1_ref, k2_ref, k3_ref, b1_ref, b2_ref, b3_ref, t1, t2)
    for s in range(2):
        for c in range(4):
            v = tot_ref[4 * s + c:4 * s + c + 1, :]
            hb_ref[s:s + 1, 128 * c:128 * c + 128] = v
            hbs_ref[s:s + 1, 128 * c:128 * c + 128] = v * out_ref[s:s + 1, 128 * c:128 * c + 128]
    for c in range(8):
        n = min(128, OUTS - 128 * c)
        v = tot_ref[8 + c:9 + c, 0:n]
        bo_ref[:, 128 * c:128 * c + n] = v
        bos_ref[:, 128 * c:128 * c + n] = v * eout_ref[:, 128 * c:128 * c + n]
    loss_ref[...] = tot_ref[16:17, :]
    for copy in moves:
        copy.wait()

def finish(sg, ag, ah, tot, n_in, n_out, e_in, e_out):
    sds = lambda *s: jax.ShapeDtypeStruct(s, F32)
    return pl.pallas_call(
        finish_kernel, in_specs=[ANY] + [VMEM] * 7, out_specs=[VMEM] * 15 + [ANY],
        out_shape=[sds(2, 784, 512), sds(2, 784, 512), sds(OUTS, 128), sds(OUTS, 128), sds(4, 8, 8, 32), sds(32, 4, 4, 64), sds(3, 3, 64, 64), sds(1, 32), sds(1, 64), sds(1, 64),
                   sds(2, 512), sds(2, 512), sds(1, OUTS), sds(1, OUTS), sds(1, 128), sds(84, 168, 128)],
        scratch_shapes=[pltpu.VMEM((128, 128), F32), pltpu.VMEM((128, 128), F32), pltpu.VMEM((84, 168, 128), F32), pltpu.SemaphoreType.DMA((2, 4))],
        compiler_params=pltpu.CompilerParams(vmem_limit_bytes=60 * 2**20),
    )(sg, ag, ah, tot, n_in, n_out, e_in, e_out)

def small_finish_kernel(tot_ref, k1_ref, k2_ref, k3_ref, b1_ref, b2_ref, b3_ref, t1, t2):
    torso_out(tot_ref, k1_ref, k2_ref, k3_ref, b1_ref, b2_ref, b3_ref, t1, t2)

def small_finish(tot):
    sds = lambda *s: jax.ShapeDtypeStruct(s, F32)
    return pl.pallas_call(
        small_finish_kernel, in_specs=[VMEM], out_specs=[VMEM] * 6,
        out_shape=[sds(4, 8, 8, 32), sds(32, 4, 4, 64), sds(3, 3, 64, 64), sds(1, 32), sds(1, 64), sds(1, 64)],
        scratch_shapes=[pltpu.VMEM((128, 128), F32), pltpu.VMEM((128, 128), F32)],
    )(tot)

def exchange(parts):
    groups = lax.axis_size("group")
    p, g = lax.axis_index("pair"), lax.axis_index("group")
    got = []
    for k in range(groups):
        to = (g + k) % groups
        mine = parts(0, to)
        if k:
            mine = lax.ppermute(mine, ("pair", "group"), [(i, (i + k) % groups) for i in range(groups)])
        theirs = lax.ppermute(parts(1, to), ("pair", "group"), [(i, groups + (i + k) % groups) for i in range(groups)])
        got.append(jnp.where(p == 0, mine, theirs))
    return got

HIGH = lax.Precision.HIGH

def local(states, actions, proj_lower, proj_upper, proj_weight, first_kernel, first_bias, second_kernel, second_bias,
          third_kernel, third_bias, hidden_mean, hidden_sigma, hidden_bias_mean, hidden_bias_sigma, head_mean, head_sigma,
          head_bias_mean, head_bias_sigma, hidden_noise_in, hidden_noise_out, head_noise_in, head_noise_out):
    pair = lax.axis_index("pair")
    groups = lax.axis_size("group")
    shards = 2 * groups
    net = int(groups == 2 and lax.axis_size("rep") == 8)
    n_in, n_out, e_in, e_out = hidden_noise_in[0], hidden_noise_out[0], head_noise_in[0], head_noise_out[0]
    own_noise = (n_in, n_out, e_in, e_out[None])
    feat_q, hid_q = 3136 // shards, 512 // shards
    shard = pair * groups + lax.axis_index("group")
    def of_shard(noise):
        on_in, on_out, on_ein, on_eout = (jnp.where(pair == 0, mine, other) for mine, other in zip(own_noise, noise))
        return (lax.dynamic_slice_in_dim(on_in, shard * feat_q, feat_q, axis=1), on_out, lax.dynamic_slice_in_dim(on_ein, shard * hid_q, hid_q, axis=1), on_eout)

    x = jnp.transpose(states[0], (2, 3, 1, 0)).reshape(84, 336, 128)
    fw1, fw2, fw3, bw1, bw2, bw3, c1, c2, c3 = prepare(first_kernel[0], second_kernel[0], third_kernel[0], first_bias, second_bias, third_bias)
    e_out = e_out[None]
    e_rows = jnp.where(jnp.arange(OUTS)[:, None] < ATOMS, e_in[0:1], e_in[1:2])
    wo = jnp.pad(head_mean[0].T + head_sigma[0].T * (e_rows * e_out.T), ((0, OUTP - OUTS), (0, 0)))
    bo = jnp.pad(head_bias_mean + head_bias_sigma * e_out, ((0, 0), (0, OUTP - OUTS)))
    hb = (hidden_bias_mean[0] + hidden_bias_sigma[0] * n_out).reshape(1, 1024)
    nin = jnp.transpose(n_in.reshape(2, STEPS, 3136 // STEPS), (1, 0, 2))
    pre1, pre2, pre3, feats = forward(x, fw1, fw2, fw3, c1, c2, c3)
    h, hid, logp, dist, *f12 = hidden(net, feats, hidden_mean[0], hidden_sigma[0], nin, n_out, hb, wo, bo, actions, proj_lower.T, proj_weight.T)
    back = (logp, h, hidden_mean[0], hidden_sigma[0], nin, n_out, wo, actions)
    if net:
        df, small_b, f2b, g1, d1, z1, g2, d2, z2, d3, *noise = hidden_bwd(net, dist, *back, f12[1], hid, *own_noise)
        part_r, part_q = wide_grads(f12[0], f12[1], f12[2], f2b, d1, d2, d3, g1, g2, z1, z2)
        total, grad_rows, ag, ah, _, _ = backward(net, x, pre1, pre2, pre3, df, bw1, bw2, bw3, part_r, part_q, small_b)
        (hidden_grad, hidden_sigma_grad, head_t, head_sigma_t, gk1, gk2, gk3, gb1, gb2, gb3, hb_grad, hbs_grad, bo_grad, bos_grad,
         loss, grad_rows) = finish(grad_rows, ag, ah, total, *of_shard(noise))
    else:
        df, small_b, msg, dz = hidden_bwd(net, lax.ppermute(dist, "pair", [(1, 0)]), *back)
        f_got = exchange(lambda p, g: lax.dynamic_slice_in_dim(feats, (p * groups + g) * feat_q, feat_q, axis=0))
        hid = jnp.transpose(hid, (3, 0, 2, 1, 4, 5)).reshape(1024, 128).T
        hid_got = exchange(lambda p, g: lax.dynamic_slice_in_dim(hid.reshape(128, 2, 512), (p * groups + g) * hid_q, hid_q, axis=2))
        dpre = jnp.transpose(msg.reshape(2, 2, 2, 128, 128), (3, 1, 0, 2, 4)).reshape(128, 1024)
        d_all = jnp.concatenate(exchange(lambda p, g: jnp.concatenate([dpre, dz.T, jnp.zeros((128, 72), F32)], axis=1)), axis=0)
        f_all = jnp.concatenate(f_got, axis=1)
        hid_all = jnp.concatenate(hid_got, axis=0)
        part_hidden = jnp.einsum("fb,bsh->sfh", f_all, d_all[:, :1024].reshape(-1, 2, 512), precision=HIGH)
        dz_all = d_all[:, 1024:1024 + ATOMS]
        picked = d_all[:, 1024 + ATOMS]
        mask = jnp.where(picked[None, :] == jnp.arange(ACTIONS, dtype=F32)[:, None], 1.0 - 1.0 / ACTIONS, -1.0 / ACTIONS)
        da = (mask[:, None, :] * dz_all.T[None]).reshape(ACTIONS * ATOMS, -1)
        part_head = jnp.concatenate([jnp.dot(dz_all.T, hid_all[:, 0], precision=HIGH), jnp.dot(da, hid_all[:, 1], precision=HIGH)], axis=0)
        hidden_grad, head_t = lax.psum((part_hidden, part_head), "rep")
        small_d, lo, up = backward(net, x, pre1, pre2, pre3, df, bw1, bw2, bw3)
        grad_rows = jnp.where(pair == 0, lo, lax.ppermute(up, "pair", [(0, 1)]))
        total = lax.psum(small_d + jnp.pad(small_b, ((0, ROWS - 24), (0, 0))), ("pair", "group", "rep"))
        in_q, on_out, e_q, on_eout = of_shard(lax.ppermute(own_noise, "pair", [(0, 1)]))
        hidden_sigma_grad = hidden_grad * (in_q[:, :, None] * on_out[:, None, :])
        head_sigma_t = head_t * (jnp.where(jnp.arange(OUTS)[:, None] < ATOMS, e_q[0:1], e_q[1:2]) * on_eout.T)
        gk1, gk2, gk3, gb1, gb2, gb3 = small_finish(total)
        hb_grad = total[0:8].reshape(2, 512)
        bo_grad = total[8:16].reshape(1, -1)[:, :OUTS]
        hbs_grad, bos_grad = hb_grad * on_out, bo_grad * on_eout
        loss = total[16:17]
    states_grad = jnp.transpose(grad_rows.reshape(84, 84, 2, 128), (3, 2, 0, 1))
    return (loss[0, 0], states_grad, jnp.transpose(gk1, (3, 0, 1, 2)), gb1[0], jnp.transpose(gk2, (3, 0, 1, 2)), gb2[0], jnp.transpose(gk3, (2, 3, 0, 1)), gb3[0],
            hidden_grad, hidden_sigma_grad, hb_grad, hbs_grad, head_t.T, head_sigma_t.T, bo_grad[0], bos_grad[0])


def solution(mesh):
    placed = (
        P("pair", ("group", "rep"), None, None, None),
        P("pair", ("group", "rep")),
        P(("group", "rep"), None),
        P(("group", "rep"), None),
        P(("group", "rep"), None),
        P("pair", None, None, None, None),
        P("pair", None),
        P("pair", None, None, None, None),
        P("pair", None),
        P("pair", None, None, None, None),
        P("pair", None),
        P("pair", None, None, None),
        P("pair", None, None, None),
        P("pair", None, None),
        P("pair", None, None),
        P("pair", None, None),
        P("pair", None, None),
        P("pair", None),
        P("pair", None),
        P("pair", None, None),
        P("pair", None, None),
        P("pair", None, None),
        P("pair", None),
    )
    return jax.shard_map(
        local,
        mesh=mesh,
        in_specs=placed,
        out_specs=(
            P(),
            P(("group", "rep"), "pair", None, None),
            P(),
            P(),
            P(),
            P(),
            P(),
            P(),
            P(None, ("pair", "group"), None),
            P(None, ("pair", "group"), None),
            P(),
            P(),
            P(("pair", "group"), None),
            P(("pair", "group"), None),
            P(),
            P(),
        ),
        check_vma=False,
    )
```

```python
import functools
import jax
import jax.numpy as jnp
from jax import lax
from jax.experimental import pallas as pl
from jax.experimental.pallas import tpu as pltpu
from jax.sharding import PartitionSpec as P

BF = jnp.bfloat16
F32 = jnp.float32
NN=(((1,),(0,)),((),()))
NT=(((1,),(1,)),((),()))
TN=(((0,),(0,)),((),()))

def split(v):
    hi = v.astype(BF)
    return hi, (v - hi.astype(F32)).astype(BF)

def dot(a, b, dims=NN):
    return lax.dot_general(a, b, dims, preferred_element_type=F32)

def dot3(a, b, dims=NN):
    ah, al = a; bh, bl = b
    return dot(ah, bh, dims) + (dot(ah, bl, dims) + dot(al, bh, dims))

def silu(v):
    return v * jax.nn.sigmoid(v)

def prep_kernel(k1_ref, k2_ref, k3_ref, b1_ref, b2_ref, b3_ref, f1_ref, f2_ref, f3_ref, r1_ref, r2_ref, r3_ref, c1_ref, c2_ref, c3_ref,
                t1a, t1b, u1a, u1b, m2, m3, n2, n3):
    for ref in (t1a, t1b, u1a, u1b, m2, m3, n2, n3):
        ref[...] = jnp.zeros_like(ref)
    def put(ref, start, stride, v, lane):
        n = v.shape[0]
        pieces = [jnp.zeros((n, lane), F32)] * (lane > 0) + [v] + [jnp.zeros((n, 96 - lane), F32)] * (lane < 96)
        rows = pl.ds(start, n, stride=stride)
        ref[rows, :] = ref[rows, :] + jnp.concatenate(pieces, axis=1)
    for c in range(4):
        for ky in range(8):
            v = k1_ref[c, ky]
            h, kq = ky // 4, ky % 4
            for w in range(3):
                put((t1a, t1b)[h], kq * 64 + 16 * w + c, 4, v, 32 * w)
            base = (c // 2) * 96 + kq * 24 + c % 2
            for q in range(4):
                if q == 0:
                    put((u1b, u1a)[h], base, 2, v[4:8], 0)
                elif q == 3:
                    put((u1b, u1a)[h], base + 16, 2, v[0:4], 96)
                else:
                    put((u1b, u1a)[h], base + 8 * (q - 1), 2, v, 32 * q)
    for ky in range(4):
        for kx in range(4):
            v = k2_ref[:, ky, kx, :]
            h, py, wx, px = ky // 2, ky % 2, 1 - kx // 2, kx % 2
            m2[py * 128 + kx * 32:py * 128 + kx * 32 + 32, 64 * h:64 * h + 64] = v
            n2[(py * 2 + px) * 32:(py * 2 + px) * 32 + 32, 128 * (1 - h) + 64 * wx:128 * (1 - h) + 64 * wx + 64] = v
    for ky in range(3):
        for kx in range(3):
            v = k3_ref[ky, kx]
            vt = jnp.transpose(v)
            for w in range(2):
                m3[ky * 128 + w * 64:ky * 128 + w * 64 + 64, 64 * (w + kx):64 * (w + kx) + 64] = v
                q = w + 2 - kx
                n3[ky * 128 + w * 64:ky * 128 + w * 64 + 64, 64 * q:64 * q + 64] = vt
    w1 = jnp.concatenate([jnp.transpose(t1a[...])[0:96], jnp.transpose(t1b[...])[0:96]], axis=0)
    pairs = ((f1_ref, w1), (f2_ref, jnp.transpose(m2[...])), (f3_ref, m3[...]), (r1_ref, jnp.concatenate([u1a[...], u1b[...]], axis=1)), (r2_ref, n2[...]), (r3_ref, n3[...]))
    for ref, v in pairs:
        hi, lo = split(v)
        ref[0] = hi
        ref[1] = lo
    for ref, b_ref, n, times in ((c1_ref, b1_ref, 32, 3), (c2_ref, b2_ref, 64, 1), (c3_ref, b3_ref, 64, 1)):
        col = jnp.transpose(jnp.broadcast_to(b_ref[...], (128, n)))
        for i in range(times):
            ref[n * i:n * i + n, :] = col

def prepare(k1, k2, k3, b1, b2, b3):
    vm = pl.BlockSpec(memory_space=pltpu.VMEM)
    bfs = lambda *s: jax.ShapeDtypeStruct(s, BF)
    sds = lambda *s: jax.ShapeDtypeStruct(s, F32)
    f32 = lambda *s: pltpu.VMEM(s, F32)
    return pl.pallas_call(
        prep_kernel, in_specs=[vm] * 6, out_specs=[vm] * 9,
        out_shape=[bfs(2, 192, 256), bfs(2, 128, 256), bfs(2, 384, 256), bfs(2, 192, 256), bfs(2, 128, 256), bfs(2, 384, 256), sds(96, 128), sds(64, 128), sds(64, 128)],
        scratch_shapes=[f32(256, 128), f32(256, 128), f32(192, 128), f32(192, 128), f32(256, 128), f32(384, 256), f32(128, 256), f32(384, 256)],
        compiler_params=pltpu.CompilerParams(vmem_limit_bytes=60 * 2**20),
    )(jnp.transpose(k1, (1, 2, 3, 0)), jnp.transpose(k2, (1, 2, 3, 0)), jnp.transpose(k3, (2, 3, 0, 1)), b1, b2, b3)

def fwd_kernel(x_ref, w1_ref, w2_ref, w3_ref, b1_ref, b2_ref, b3_ref, pre1_hbm, pre2_hbm, pre3_ref, f_ref,
               xs, pre1_ref, pre2_ref, xh, xl, top1, top2, acc3, h1h, h1l, h2h, h2l, x_sem, sem1, sem2):
    def x_in(j):
        return pltpu.make_async_copy(x_ref.at[pl.ds(4 * j, 4)], xs.at[pl.ds(4 * j, 4)], x_sem.at[j])
    def row_out(row):
        return pltpu.make_async_copy(pre1_ref.at[row], pre1_hbm.at[row], sem1.at[row])
    for j in range(21):
        x_in(j).start()
    xh[:, 336:, :] = jnp.zeros((4, 16, 128), BF)
    xl[:, 336:, :] = jnp.zeros((4, 16, 128), BF)
    top1[...] = jnp.zeros_like(top1)
    top2[...] = jnp.zeros_like(top2)
    acc3[...] = jnp.zeros_like(acc3)
    h2h[:, 576:, :] = jnp.zeros((9, 64, 128), BF)
    h2l[:, 576:, :] = jnp.zeros((9, 64, 128), BF)
    def step1(j, carry):
        x_in(j).wait()
        v = xs[pl.ds(4 * j, 4)]
        hi = v.astype(BF)
        xh[:, 0:336, :] = hi
        xl[:, 0:336, :] = (v - hi.astype(F32)).astype(BF)
        rh = jnp.concatenate([xh[:, 48 * i:48 * i + 64, :].reshape(256, 128) for i in range(7)], axis=1)
        rl = jnp.concatenate([xl[:, 48 * i:48 * i + 64, :].reshape(256, 128) for i in range(7)], axis=1)
        r = dot3((w1_ref[0], w1_ref[1]), (rh, rl))
        out = top1[...] + r[96:]
        top1[...] = r[:96]
        b1 = b1_ref[...]
        row = jnp.maximum(j - 1, 0)
        for i in range(7):
            n = 96 if i < 6 else 64
            p = out[:n, 128 * i:128 * i + 128] + b1[:n]
            pre1_ref[row, 96 * i:96 * i + n, :] = p
            hh, hl = split(silu(p))
            h1h[row, 96 * i:96 * i + n, :] = hh
            h1l[row, 96 * i:96 * i + n, :] = hl
        pl.when(j >= 1)(lambda: row_out(row).start())
        return carry
    lax.fori_loop(0, 21, step1, 0)
    w2 = (w2_ref[0], w2_ref[1])
    b2 = b2_ref[...]
    def step2(y, carry):
        rh = jnp.concatenate([h1h[pl.ds(2 * y, 2), 64 * i:64 * i + 128, :].reshape(256, 128) for i in range(9)], axis=1)
        rl = jnp.concatenate([h1l[pl.ds(2 * y, 2), 64 * i:64 * i + 128, :].reshape(256, 128) for i in range(9)], axis=1)
        r = dot3(w2, (rh, rl))
        o = top2[...] + r[64:]
        top2[...] = r[:64]
        row = jnp.maximum(y - 1, 0)
        for i in range(9):
            p = o[:, 128 * i:128 * i + 128] + b2
            pre2_ref[row, 64 * i:64 * i + 64, :] = p
            hh, hl = split(silu(p))
            h2h[row, 64 * i:64 * i + 64, :] = hh
            h2l[row, 64 * i:64 * i + 64, :] = hl
        return carry
    lax.fori_loop(0, 10, step2, 0)
    pre2_out = pltpu.make_async_copy(pre2_ref, pre2_hbm, sem2)
    pre2_out.start()
    w3 = (w3_ref[0], w3_ref[1])
    b3 = b3_ref[...]
    def step3(y, carry):
        rh = jnp.concatenate([h2h[y, 128 * i:128 * i + 256, :] for i in range(4)], axis=1)
        rl = jnp.concatenate([h2l[y, 128 * i:128 * i + 256, :] for i in range(4)], axis=1)
        r = dot3(w3, (rh, rl))
        for ky in range(3):
            for i in range(4):
                acc3[y - ky + 2, 128 * i:128 * i + 128, :] += r[128 * ky:128 * ky + 128, 128 * i:128 * i + 128]
        return carry
    lax.fori_loop(0, 9, step3, 0)
    for y in range(7):
        for x in range(7):
            p = acc3[y + 2, 64 * x:64 * x + 64, :] + b3
            pre3_ref[pl.ds(y * 7 + x, 64, stride=49), :] = p
            f_ref[pl.ds(y * 7 + x, 64, stride=49), :] = silu(p)
    pre2_out.wait()
    for row in range(20):
        row_out(row).wait()

def forward(x, w1, w2, w3, b1, b2, b3):
    vm = pl.BlockSpec(memory_space=pltpu.VMEM)
    hbm = pl.BlockSpec(memory_space=pl.ANY)
    sds = lambda *s: jax.ShapeDtypeStruct(s, F32)
    f32 = lambda *s: pltpu.VMEM(s, F32)
    bf = lambda *s: pltpu.VMEM(s, BF)
    dma = pltpu.SemaphoreType.DMA
    return pl.pallas_call(
        fwd_kernel,
        in_specs=[hbm] + [vm] * 6,
        out_specs=[hbm, hbm, vm, vm],
        out_shape=[sds(20, 640, 128), sds(9, 576, 128), sds(3136, 128), sds(3136, 128)],
        scratch_shapes=[f32(84, 336, 128), f32(20, 640, 128), f32(9, 576, 128), bf(4, 352, 128), bf(4, 352, 128),
                        f32(96, 896), f32(64, 1152), f32(11, 512, 128), bf(20, 640, 128), bf(20, 640, 128), bf(9, 640, 128), bf(9, 640, 128),
                        dma((21,)), dma((20,)), dma],
        compiler_params=pltpu.CompilerParams(vmem_limit_bytes=60 * 2**20),
    )(x, w1, w2, w3, b1, b2, b3)


MESH_ID = pl.DeviceIdType.MESH


def coords():
    r = lax.axis_index("rep")
    return lax.axis_index("pair"), lax.axis_index("group"), r // 2, r % 2


def at(p, g, z, y):
    return (p, g, z * 2 + y)


def flip(z, k):
    return (z, z + 1 - 2 * (z % 2), z + 2 - 4 * (z // 2), 3 - z)[k]


def line(p, g, z, y):
    return [at(q, g, flip(z, k), y) for k in range(4) for q in ((p, 1 - p) if k else (1 - p,))]


def plane(p, g, z, y):
    return [at(p, g, z, 1 - y), at(p, 1 - g, z, y), at(p, 1 - g, z, 1 - y)]


def greet(devices):
    barrier = pltpu.get_barrier_semaphore()
    for device in devices:
        pl.semaphore_signal(barrier, inc=1, device_id=device, device_id_type=MESH_ID)
    pl.semaphore_wait(barrier, len(devices))


def remote(src, dst, send, recv, device):
    return pltpu.make_async_remote_copy(src_ref=src, dst_ref=dst, send_sem=send, recv_sem=recv, device_id=device, device_id_type=MESH_ID)


class Scatter:
    def __init__(self, parts, src, dst, send, recv, own, hold=None, cores=2):
        self.parts, self.src, self.dst, self.send, self.recv, self.own, self.hold, self.cores = parts, src, dst, send, recv, own, hold, cores
        self.p, self.g, self.z, self.y = coords()

    def copies(self):
        for k in range(4):
            for q in range(self.cores):
                for i in range(self.parts):
                    zd = flip(self.z, k)
                    if k == 0 and q == 0:
                        yield pltpu.make_async_copy(self.src(q, zd, i), self.dst(self.z, i) if self.hold is None else self.hold.at[i], self.own.at[i]), True
                    else:
                        yield remote(self.src(q, zd, i), self.dst(self.z, i), self.send.at[k * 2 + q, i], self.recv.at[k, i], at(q, self.g, zd, self.y)), False

    def start(self):
        @pl.when(self.p == 0)
        def _():
            for copy, own in self.copies():
                copy.start()

    def arrived(self, k):
        if self.cores == 1:
            pl.when(self.p == 0)(lambda: self.landed(k))
        else:
            self.landed(k)

    def landed(self, k):
        for i in range(self.parts):
            zs = flip(self.z, k)
            wait = remote(self.src(0, zs, i), self.dst(zs, i), self.send.at[0, i], self.recv.at[k, i], at(1 - self.p, self.g, self.z, self.y)).wait_recv
            def local():
                if self.hold is None:
                    pltpu.make_async_copy(self.src(0, zs, i), self.dst(zs, i), self.own.at[i]).wait()
                else:
                    pltpu.make_async_copy(self.src(0, zs, i), self.hold.at[i], self.own.at[i]).wait()
                    out = pltpu.make_async_copy(self.hold.at[i], self.dst(zs, i), self.own.at[i])
                    out.start()
                    out.wait()
            if k:
                wait()
            elif self.cores == 1:
                local()
            else:
                pl.when(self.p == 1)(wait)
                pl.when(self.p == 0)(local)

    def sent(self):
        @pl.when(self.p == 0)
        def _():
            for copy, own in self.copies():
                if not own:
                    copy.wait_send()


def scatter_sems(parts, *hold):
    return [pltpu.SemaphoreType.DMA((8, parts)), pltpu.SemaphoreType.DMA((4, parts)), pltpu.SemaphoreType.DMA((parts,))] + [pltpu.VMEM((parts,) + hold, F32)] * bool(hold)


PIECES = ((0, 72), (72, 72), (144, 56))


def f_scatter(f_ref, f1_ref, piece, sems):
    start, rows = PIECES[piece]
    def src(q, zd, i):
        return f_ref.at[pl.ds(pl.multiple_of((2 * q + i) * 784 + jnp.minimum(200 * zd, 584) + start, 8), rows)]
    return Scatter(2, src, lambda z, i: f1_ref.at[i, z], *sems)


def f_fan(f1_ref, f2_ref, send, recv):
    return spread_plane(*coords(), lambda gd, yd: f1_ref.at[gd], lambda m: f2_ref.at[m], send, recv)


class Line:
    def __init__(self, parts, own, slot, send, recv):
        self.parts, self.own, self.slot, self.send, self.recv = parts, own, slot, send, recv
        self.p, self.g, self.z, self.y = coords()

    def block(self, t, way):
        return jnp.maximum(self.z - t, 0) if way == 0 else jnp.minimum(self.z + t, 3)

    def there(self, t, way):
        return self.z >= t if way == 0 else self.z + t <= 3

    def copies(self, t, way):
        to = at(self.p, self.g, jnp.minimum(self.z + 1, 3) if way == 0 else jnp.maximum(self.z - 1, 0), self.y)
        zz = self.block(t, way)
        return [remote(self.own(i) if t == 0 else self.slot(zz, i), self.slot(zz, i), self.send.at[t, way, i], self.recv.at[t, way, i], to) for i in range(self.parts)]

    def goes(self, t, way):
        return jnp.logical_and(self.there(t, way), self.z <= 2 if way == 0 else self.z >= 1)

    def start(self, t):
        for way in range(2):
            def go():
                for copy in self.copies(t, way):
                    copy.start()
            pl.when(self.goes(t, way))(go)

    def arrive(self, t, then):
        for i in range(self.parts):
            for way in range(2):
                def come():
                    zz = self.block(t, way)
                    remote(self.slot(zz, i), self.slot(zz, i), self.send.at[t - 1, way, i], self.recv.at[t - 1, way, i], at(1 - self.p, self.g, self.z, self.y)).wait_recv()
                    if t < 3:
                        pl.when(self.goes(t, way))(self.copies(t, way)[i].start)
                    then(2 * t - 1 + way, zz, i)
                pl.when(self.there(t, way))(come)

    def each(self, do):
        do(0, self.z)
        for t in range(1, 4):
            for way in range(2):
                pl.when(self.there(t, way))(lambda: do(2 * t - 1 + way, self.block(t, way)))

    def sent(self):
        for t in range(3):
            for way in range(2):
                def done():
                    for copy in self.copies(t, way):
                        copy.wait_send()
                pl.when(self.goes(t, way))(done)


def line_sems(parts):
    return [pltpu.SemaphoreType.DMA((3, 2, parts)), pltpu.SemaphoreType.DMA((3, 2, parts))]


def g_scatter(hid_ref, g1_ref, sems):
    return Scatter(1, lambda q, zd, i: hid_ref.at[q, zd], lambda z, i: g1_ref.at[z], *sems)


def z_scatter(dz_ref, dz1_ref, sems):
    return Scatter(1, lambda q, zd, i: dz_ref, lambda z, i: dz1_ref.at[z], *sems, cores=1)


def spread_plane(p, g, z, y, src, dst, send, recv):
    places = [(g, 1 - y), (1 - g, y), (1 - g, 1 - y)]
    return [remote(src(*to), dst(m), send.at[m], recv.at[m], at(p, to[0], z, to[1])) for m, to in enumerate(places)]
ATOMS, ACTIONS, PAD = 51, 18, 56
OUTS, OUTP = 969, 976
STEPS = 7
ANY = pl.BlockSpec(memory_space=pl.ANY)
VMEM = pl.BlockSpec(memory_space=pltpu.VMEM)

def column(row, lanes):
    tall = jnp.transpose(jnp.broadcast_to(row, (128, row.shape[1])))
    return jnp.concatenate([tall] * (lanes // 128), axis=1)

def noisy(mean_ref, sigma_ref, nin_ref, nout_ref, s):
    return mean_ref[s] + sigma_ref[s] * (column(nin_ref[0, s:s + 1, :], 512) * nout_ref[s:s + 1, :])

def mask_of(chosen, a):
    return jnp.where(chosen == a, 1.0 - 1.0 / ACTIONS, -1.0 / ACTIONS)

def hid_kernel(net, f_ref, m_ref, s_ref, nin_ref, nout_ref, hm_ref, hs_ref, wo_ref, bm_ref, bs_ref, eout_ref, c_ref, pl_ref, pw_ref, *rest):
    if net:
        f_all, h_ref, g_ref, logp_ref, dist_ref, t_ref = rest[:6]
        f1_refs, f2_refs = rest[6:9], rest[9:11]
        acc, adv, ts, tr, fs0, fr0, fs1, fr1 = rest[11:19]
        wires = [f_scatter(f_all, f1_refs[i], i, rest[19 + 4 * i:23 + 4 * i]) for i in range(3)]
        fans = [f_fan(f1_refs[0], f2_refs[0], fs0, fr0), f_fan(f1_refs[1], f2_refs[1], fs1, fr1)]
        p, g, z, y = coords()
        target = remote(dist_ref, t_ref, ts, tr, at(1 - p, g, z, y))
        def next_piece(i):
            wires[i].sent()
            wires[i + 1].start()
            for k in range(4):
                wires[i].arrived(k)
            for copy in fans[i]:
                copy.start()
    else:
        h_ref, g_ref, logp_ref, dist_ref, acc, adv = rest
    j = pl.program_id(0)
    @pl.when(j == 0)
    def _():
        if net:
            greet(line(p, g, z, y) + plane(p, g, z, y))
            wires[0].start()
        acc[...] = jnp.zeros_like(acc)
    if net:
        pl.when(j == 4)(lambda: next_piece(0))
        pl.when(j == 6)(lambda: next_piece(1))
    f = split(f_ref[...])
    for s in range(2):
        w = split(noisy(m_ref, s_ref, nin_ref, nout_ref, s))
        acc[:, 512 * s:512 * s + 512] += dot3(f, w, TN)
    @pl.when(j == pl.num_programs(0) - 1)
    def _():
        hb = hm_ref[...] + hs_ref[...] * nout_ref[...]
        h = jnp.concatenate([acc[:, 0:512] + hb[0:1], acc[:, 512:1024] + hb[1:2]], axis=1)
        h_ref[...] = h
        gt = jnp.transpose(silu(h))
        for s in range(2):
            for q in range(2):
                for gg in range(2):
                    for z in range(4):
                        at_row = 512 * s + 256 * q + 128 * gg + 32 * z
                        g_ref[q, z, gg, s] = gt[at_row:at_row + 32]
        both = dot3(split(wo_ref[...]), split(jnp.concatenate([gt[:512], gt[512:]], axis=1)))
        bias = column(jnp.concatenate([bm_ref[...] + bs_ref[...] * eout_ref[...], jnp.zeros((1, OUTP - OUTS), F32)], axis=1), 128)
        adv[...] = both[:, 128:] + bias
        z = both[0:PAD, 0:128] + bias[0:PAD]
        chosen = c_ref[...]
        for i in range(ACTIONS):
            z = z + mask_of(chosen, i) * adv[ATOMS * (i + 1):ATOMS * (i + 1) + PAD, :]
        row = lax.broadcasted_iota(jnp.int32, (PAD, 128), 0)
        z = jnp.where(row < ATOMS, z, -1e30)
        top = jnp.max(z, axis=0, keepdims=True)
        e = jnp.exp(z - top)
        tot = jnp.sum(e, axis=0, keepdims=True)
        logp_ref[...] = (z - top) - jnp.log(tot)
        prob = e / tot
        dist = jnp.zeros((PAD, 128), F32)
        for i in range(ATOMS):
            lower = pl_ref[i:i + 1, :]
            share = pw_ref[i:i + 1, :]
            pi = prob[i:i + 1, :]
            dist = dist + jnp.where(row == lower, pi * (1.0 - share), 0.0) + jnp.where(row == lower + 1, pi * share, 0.0)
        dist_ref[...] = dist
        if net:
            pl.when(p == 1)(target.start)
            for k in range(4):
                wires[2].arrived(k)
            wires[2].sent()
            for copy in fans[0] + fans[1]:
                copy.wait()
            pl.when(p == 1)(target.wait_send)
            pl.when(p == 0)(target.wait_recv)

def hidden(net, f, m, s, nin, nout, hm, hs, wo, bm, bs, eout, c, plow, pw):
    full = lambda *t: pl.BlockSpec(t, lambda j: (0,) * len(t))
    sds = lambda *t: jax.ShapeDtypeStruct(t, F32)
    k = 3136 // STEPS
    wspec = pl.BlockSpec((2, k, 512), lambda j: (0, j, 0))
    return pl.pallas_call(
        functools.partial(hid_kernel, net), grid=(STEPS,),
        in_specs=[pl.BlockSpec((k, 128), lambda j: (j, 0)), wspec, wspec, pl.BlockSpec((1, 2, k), lambda j: (j, 0, 0)), full(2, 512), full(2, 512), full(2, 512),
                  full(OUTP, 512), full(1, OUTS), full(1, OUTS), full(1, OUTS), full(1, 128), full(ATOMS, 128), full(ATOMS, 128)] + [ANY] * net,
        out_specs=[full(128, 1024), full(2, 4, 2, 2, 32, 128), full(PAD, 128), full(PAD, 128)] + [ANY] * (6 * net),
        out_shape=[sds(128, 1024), sds(2, 4, 2, 2, 32, 128), sds(PAD, 128), sds(PAD, 128)]
        + ([sds(PAD, 128)] + [sds(2, 4, n, 128) for _, n in PIECES] + [sds(3, 4, n, 128) for _, n in PIECES[:2]]) * net,
        scratch_shapes=[pltpu.VMEM((128, 1024), F32), pltpu.VMEM((OUTP, 128), F32)]
        + ([pltpu.SemaphoreType.DMA] * 2 + [pltpu.SemaphoreType.DMA((3,))] * 4 + sum([scatter_sems(2, n, 128) for _, n in PIECES], [])) * net,
        compiler_params=pltpu.CompilerParams(vmem_limit_bytes=60 * 2**20, **(dict(collective_id=1, has_side_effects=True) if net else {})),
    )(f, m, s, nin, nout, hm, hs, wo, bm, bs, eout, c, plow, pw, *([f] * net))

def hid_bwd_kernel(net, t_ref, logp_ref, h_ref, m_ref, s_ref, nin_ref, nout_ref, wo_ref, c_ref, *rest):
    if net:
        noise, rest = list(zip(rest[2:6], rest[16:20])), rest[:2] + rest[6:16] + rest[20:]
        f1b_ref, hid_ref, df_ref, small_ref, f2b_ref, g1_ref, d1_ref, dz1_ref, g2_ref, d2_ref, dz2_ref, d3_ref = rest[:12]
        dth, dtl, da, msg, dz_to = rest[12:17]
        ds, dr, gs, gr, qs, qr, fs, fr, hs, hr, ss, sr, ps, pr, own = rest[17:32]
        g_wire = g_scatter(hid_ref, g1_ref, rest[32:36])
        z_wire = z_scatter(dz_to, dz1_ref, rest[36:39])
        p, g, z, y = coords()
        d_line = Line(2, lambda i: d1_ref.at[z, i], lambda zz, i: d1_ref.at[zz, i], rest[39], rest[40])
        partner = at(1 - p, g, z, y)
        hands = [remote(dz2_ref, dz2_ref, hs.at[0], hr.at[0], partner), remote(dz1_ref, dz1_ref, hs.at[1], hr.at[1], partner)]
        tells = [remote(src, dst, rest[41].at[i], rest[42].at[i], partner) for i, (src, dst) in enumerate(noise)]
        own_tells = [pltpu.make_async_copy(src, dst, rest[43].at[i]) for i, (src, dst) in enumerate(noise)]
        give = remote(msg.at[1], d1_ref.at[z], ps, pr, partner)
        keep = pltpu.make_async_copy(msg.at[0], d1_ref.at[z], own)
        fan_f = f_fan(f1b_ref, f2b_ref, fs, fr)
        fan_g = spread_plane(p, g, z, y, lambda gd, yd: g1_ref.at[:, gd], lambda m: g2_ref.at[m], gs, gr)
        fan_z = spread_plane(p, g, z, y, lambda gd, yd: dz1_ref, lambda m: dz2_ref.at[m], qs, qr)
        def fan_d(place, zz):
            return spread_plane(p, g, z, y, lambda gd, yd: d1_ref.at[zz, yd], lambda m: d2_ref.at[m, zz], ds.at[place], dr.at[place])
        def swap_own(place, zz):
            return remote(d1_ref.at[zz, y], d3_ref.at[3, zz], ss.at[place, 0], sr.at[place, 0], partner)
        def swap(place, zz):
            return remote(d2_ref.at[:, zz], d3_ref.at[pl.ds(0, 3), zz], ss.at[place, 1], sr.at[place, 1], partner)
        def forward(place, zz, s):
            along_y, along_x, both = fan_d(place, zz)
            @pl.when(y == s)
            def _():
                along_x.start()
                swap_own(place, zz).start()
            @pl.when(y != s)
            def _():
                both.start()
                along_y.start()
        def forward_small():
            for k in range(4):
                g_wire.arrived(k)
            for copy in fan_g:
                copy.start()
            for k in range(4):
                z_wire.arrived(k)
            @pl.when(p == 0)
            def _():
                for copy in fan_z:
                    copy.start()
    else:
        df_ref, small_ref, msg, dz_to, dth, dtl, da = rest
    j = pl.program_id(0)
    def begin():
        t = t_ref[...]
        logp = logp_ref[...]
        chosen = c_ref[...]
        row = lax.broadcasted_iota(jnp.int32, (PAD, 128), 0)
        d = (jnp.exp(logp) * jnp.sum(t, axis=0, keepdims=True) - t) * (1.0 / 128)
        loss = -jnp.sum(jnp.where(row < ATOMS, t * logp, 0.0), axis=1, keepdims=True) * (1.0 / 128)
        dz_to[...] = jnp.where(row == ATOMS, chosen.astype(F32), d)
        da[...] = jnp.zeros_like(da)
        da[0:PAD, 0:128] = d
        for i in range(ACTIONS):
            da[ATOMS * (i + 1):ATOMS * (i + 1) + PAD, 128:256] = mask_of(chosen, i) * d
        every = da[...]
        eh, el = split(every)
        grads = dot3((eh, el), split(wo_ref[...]), TN)
        small_ref[...] = jnp.zeros_like(small_ref)
        for s in range(2):
            dp = grads[128 * s:128 * s + 128] * dsilu(h_ref[:, 512 * s:512 * s + 512])
            total = jnp.sum(dp, axis=0, keepdims=True)
            for c in range(4):
                msg[c // 2, s, 128 * (c % 2):128 * (c % 2) + 128, :] = dp[:, 128 * c:128 * c + 128]
                small_ref[4 * s + c:4 * s + c + 1, :] = total[:, 128 * c:128 * c + 128]
            hi, lo = split(jnp.transpose(dp))
            dth[s] = hi
            dtl[s] = lo
        if net:
            give.start()
            keep.start()
            z_wire.start()
            keep.wait()
        ones = jnp.ones((8, 256), BF)
        left = (every - eh.astype(F32)) - el.astype(F32)
        rows = dot(ones, eh, NT) + dot(ones, el, NT) + dot(ones, left.astype(BF), NT)
        for c in range(8):
            n = min(128, OUTP - 128 * c)
            small_ref[8 + c:9 + c, 0:n] = rows[0:1, 128 * c:128 * c + n]
        small_ref[16:17, :] = jnp.broadcast_to(jnp.sum(loss, axis=0, keepdims=True), (1, 128))
    def step():
        out = None
        for s in range(2):
            w = split(noisy(m_ref, s_ref, nin_ref, nout_ref, s))
            r = dot3(w, (dth[s], dtl[s]))
            out = r if out is None else out + r
        df_ref[...] = out
    if not net:
        pl.when(j == 0)(begin)
        step()
        return
    @pl.when(j == 0)
    def _():
        greet(line(p, g, z, y) + plane(p, g, z, y))
        for copy in fan_f:
            copy.start()
        g_wire.start()
        @pl.when(p == 0)
        def _():
            begin()
            for copy in tells + own_tells:
                copy.start()
        pl.when(p == 1)(give.wait_recv)
        d_line.start(0)
        for s in range(2):
            forward(0, z, s)
    pl.when(p == 0)(step)
    pl.when(j == 3)(forward_small)
    @pl.when(j == pl.num_programs(0) - 1)
    def _():
        for t in range(1, 4):
            d_line.arrive(t, forward)
        @pl.when(p == 0)
        def _():
            for copy in fan_z:
                copy.wait()
            for copy in hands:
                copy.start()
        def landed(place, zz):
            for copy in fan_d(place, zz):
                copy.wait_recv()
            swap(place, zz).start()
        d_line.each(landed)
        for copy in fan_f + fan_g:
            copy.wait()
        def gone(place, zz):
            for copy in fan_d(place, zz):
                copy.wait_send()
            swap(place, zz).wait()
            swap_own(place, zz).wait()
        d_line.each(gone)
        d_line.sent()
        @pl.when(p == 0)
        def _():
            give.wait_send()
            for copy in hands + tells:
                copy.wait_send()
            for copy in own_tells:
                copy.wait()
        @pl.when(p == 1)
        def _():
            for copy in hands + tells:
                copy.wait_recv()
        for wire in (g_wire, z_wire):
            wire.sent()

def hidden_bwd(net, t, logp, h, m, s, nin, nout, wo, c, *wired):
    full = lambda *u: pl.BlockSpec(u, lambda j: (0,) * len(u))
    sds = lambda *u: jax.ShapeDtypeStruct(u, F32)
    dma = pltpu.SemaphoreType.DMA
    k = 3136 // STEPS
    wspec = pl.BlockSpec((2, k, 512), lambda j: (0, j, 0))
    return pl.pallas_call(
        functools.partial(hid_bwd_kernel, net), grid=(STEPS,),
        in_specs=[full(PAD, 128), full(PAD, 128), full(128, 1024), wspec, wspec, pl.BlockSpec((1, 2, k), lambda j: (j, 0, 0)), full(2, 512),
                  full(OUTP, 512), full(1, 128)] + [ANY] * (6 * net),
        out_specs=[pl.BlockSpec((k, 128), lambda j: (j, 0)), full(24, 128)] + ([ANY] * 12 if net else [full(2, 2, 256, 128), full(PAD, 128)]),
        out_shape=[sds(3136, 128), sds(24, 128)] + ([sds(3, 4, PIECES[2][1], 128), sds(4, 2, 2, 32, 128), sds(4, 2, 256, 128), sds(4, PAD, 128), sds(3, 4, 2, 32, 128), sds(3, 4, 256, 128),
                                                     sds(3, 4, PAD, 128), sds(4, 4, 256, 128), sds(2, 3136), sds(2, 512), sds(2, 512), sds(1, OUTS)] if net else [sds(2, 2, 256, 128), sds(PAD, 128)]),
        scratch_shapes=[pltpu.VMEM((2, 512, 128), BF), pltpu.VMEM((2, 512, 128), BF), pltpu.VMEM((OUTP, 256), F32)]
        + ([pltpu.VMEM((2, 2, 256, 128), F32), pltpu.VMEM((PAD, 128), F32), dma((7, 3)), dma((7, 3))] + [dma((3,))] * 6 + [dma((2,)), dma((2,)), dma((7, 2)), dma((7, 2)), dma, dma, dma]
           + scatter_sems(1, 2, 2, 32, 128) + scatter_sems(1) + line_sems(2) + [dma((4,)), dma((4,)), dma((4,))]) * net,
        compiler_params=pltpu.CompilerParams(vmem_limit_bytes=60 * 2**20, **(dict(collective_id=2, has_side_effects=True) if net else {})),
    )(t, logp, h, m, s, nin, nout, wo, c, *wired)

def dsilu(v):
    s = jax.nn.sigmoid(v)
    return s * (1.0 + v * (1.0 - s))


ROWS = 768

def bwd_kernel(net, x_ref, pre1_hbm, pre2_ref, pre3_ref, df_ref, w1_ref, w2_ref, w3_ref, *rest):
    if net:
        r_ref, q_ref, s0_ref, tot_ref, sg_ref, ag_ref, ah_ref, bg_ref, bh_ref = rest[:9]
        xs, pre1_ref, xh, xl, d3f, d3h, d3l, d2h, d2l, d1h, d1l, h2h, h2l, acc2, a1, a2, a3, pay, lob, upb, x_sem, sem1, ls, us = rest[9:33]
        got, got1, red, tot, ur, zs_, zr, ys, yr, own, gs, gr, ws, wr, as_, ar, bs, br, es, er, cs, cr, one_ = rest[33:]
        p, g, z, y = coords()
        reps = lax.axis_size("rep")
        chips = 2 * reps
        me = g * reps + lax.axis_index("rep")
        size = ROWS // chips
        def chip(i):
            return (0, i // reps, i % reps)
        def part(i):
            return pl.ds(pl.multiple_of(i * size, 8), size)
        def give(k):
            to = (me + k) % chips
            if k:
                return remote(pay.at[part(to)], got.at[me], as_.at[k], ar.at[k], chip(to))
            return pltpu.make_async_copy(pay.at[part(me)], got.at[me], one_)
        def given(k):
            who = (me + chips - k) % chips
            return remote(pay.at[part(me)], got.at[who], as_.at[k], ar.at[k], chip(who))
        def show(k):
            return remote(pay.at[pl.ds(672, 64)], got1.at[me], es.at[k], er.at[k], chip((me + k) % chips))
        def shown(k):
            who = (me + chips - k) % chips
            return remote(pay.at[pl.ds(672, 64)], got1.at[who], es.at[k], er.at[k], chip(who))
        def tell(k):
            return remote(red, tot.at[part(me)], bs.at[k], br.at[k], chip((me + k) % chips))
        def told(k):
            who = (me + chips - k) % chips
            return remote(red, tot.at[part(who)], bs.at[k], br.at[k], chip(who))
        hand = remote(tot, tot, cs, cr, at(1 - p, g, z, y))
        def head_at(ref, yy, zz):
            return ref.at[zz, pl.ds(5 * yy, 5 - yy)]
        def head_of(yy):
            return q_ref.at[pl.ds(5 * yy, 5 - yy)]
        def slots(yy, zz):
            return ag_ref.at[yy, zz], head_at(ah_ref, yy, zz), bg_ref.at[yy, zz], head_at(bh_ref, yy, zz)
        def lines(yy):
            mine = (r_ref, head_of(yy)) + slots(yy, z)[2:]
            return Line(4, lambda i: mine[i], lambda zz, i: slots(yy, zz)[i], zs_, zr)
        def keep(yy):
            a, b, _, _ = slots(yy, z)
            return [pltpu.make_async_copy(r_ref, a, own.at[0]), pltpu.make_async_copy(head_of(yy), b, own.at[1])]
        def give_own(yy):
            _, _, a, b = slots(yy, z)
            return [remote(r_ref, a, gs.at[0], gr.at[0], at(1, g, z, y)), remote(head_of(yy), b, gs.at[1], gr.at[1], at(1, g, z, y))]
        def along_y(place, zz, yy):
            src = slots(yy, zz) if place else (r_ref, head_of(yy)) + slots(yy, z)[2:]
            return [remote(src[i], slots(yy, zz)[i], ys.at[place, i], yr.at[place, i], at(p, g, z, 1 - y)) for i in range(4)]
        def bring(place, zz, yy):
            a, b, c, d = slots(yy, zz)
            return [remote(c, a, ws.at[yy, place, 0], wr.at[yy, place, 0], at(0, g, z, y)), remote(d, b, ws.at[yy, place, 1], wr.at[yy, place, 1], at(0, g, z, y))]
        def each(do, flipped=False):
            for yy in range(2):
                pl.when(y == (1 - yy if flipped else yy))(functools.partial(do, yy))
        def states_out(j, slot):
            return (pltpu.make_async_copy(lob.at[slot], sg_ref.at[pl.ds(4 * j, 4)], ls.at[slot]),
                    remote(upb.at[slot], sg_ref.at[pl.ds(4 * j, 4)], us.at[slot], ur.at[j], at(1 - p, g, z, y)))
        def gather(yy):
            def then(place, zz, i):
                along_y(place, zz, yy)[i].start()
                if i >= 2:
                    bring(place, zz, yy)[i - 2].start()
            for copy in give_own(yy):
                copy.wait_recv()
            lines(yy).start(0)
            for i in range(4):
                then(0, z, i)
            for copy in keep(yy):
                copy.start()
            for t in range(1, 4):
                lines(yy).arrive(t, then)
        def second(yy):
            def landed(place, zz):
                for copy in along_y(place, zz, yy):
                    copy.wait_recv()
                for copy in bring(place, zz, yy):
                    copy.start()
            lines(yy).each(landed)
        def finished(yy):
            def gone(place, zz):
                for copy in along_y(place, zz, yy) + bring(place, zz, yy):
                    copy.wait_send()
            for copy in keep(yy):
                copy.wait()
            lines(yy).sent()
            lines(yy).each(gone)
        def second_sent(yy):
            def gone(place, zz):
                for copy in bring(place, zz, yy):
                    copy.wait_send()
            lines(yy).each(gone)
        def brought(yy):
            def came(place, zz):
                for copy in bring(place, zz, yy):
                    copy.wait_recv()
            lines(yy).each(came)
    else:
        tot_ref, lo_ref, up_ref, xs, pre1_ref, xh, xl, d3f, d3h, d3l, d2h, d2l, d1h, d1l, h2h, h2l, acc2, a1, a2, a3, pay, lob, upb, x_sem, sem1, ls, us = rest
        def states_out(j, slot):
            return (pltpu.make_async_copy(lob.at[slot], lo_ref.at[pl.ds(4 * j, 4)], ls.at[slot]),
                    pltpu.make_async_copy(upb.at[slot], up_ref.at[pl.ds(4 * j, 4)], us.at[slot]))
    small_ref = pay.at[pl.ds(24, 648)]
    last = 20
    def x_in(j):
        return pltpu.make_async_copy(x_ref.at[pl.ds(4 * j, 4)], xs.at[pl.ds(4 * j, 4)], x_sem.at[j])
    pre1_in = pltpu.make_async_copy(pre1_hbm, pre1_ref, sem1)
    def fetch():
        pre1_in.start()
        for j in range(21):
            x_in(j).start()
    def upper():
        for ref in (d3h, d3l, d2h, d2l, acc2, a2, a3):
            ref[...] = jnp.zeros_like(ref)
        small_ref[...] = jnp.zeros((648, 128), F32)
        for ref in (d1h, d1l):
            ref[0] = jnp.zeros((704, 128), BF)
            ref[21] = jnp.zeros((704, 128), BF)
            ref[:, 0:32, :] = jnp.zeros((22, 32, 128), BF)
            ref[:, 672:704, :] = jnp.zeros((22, 32, 128), BF)
        d3f[...] = df_ref[...] * dsilu(pre3_ref[...])
        total = jnp.zeros((64, 128), F32)
        for y in range(7):
            for x in range(7):
                d = d3f[pl.ds(y * 7 + x, 64, stride=49), :]
                total = total + d
                hi, lo = split(d)
                d3h[y + 2, 64 * (x + 2):64 * (x + 3), :] = hi
                d3l[y + 2, 64 * (x + 2):64 * (x + 3), :] = lo
        small_ref[640:641, 0:64] = jnp.sum(jnp.transpose(total), axis=0, keepdims=True)
        w3 = (w3_ref[0], w3_ref[1])
        h2h[:, 576:, :] = jnp.zeros((9, 64, 128), BF)
        h2l[:, 576:, :] = jnp.zeros((9, 64, 128), BF)
        def split2(y, c):
            hi, lo = split(silu(pre2_ref[y]))
            h2h[y, 0:576, :] = hi
            h2l[y, 0:576, :] = lo
            return c
        lax.fori_loop(0, 9, split2, 0)
        def dgrad3(y, c):
            rh = jnp.concatenate([d3h[y + 2, 128 * i:128 * i + 256, :] for i in range(5)], axis=1)
            rl = jnp.concatenate([d3l[y + 2, 128 * i:128 * i + 256, :] for i in range(5)], axis=1)
            r = dot3(w3, (rh, rl))
            for ky in range(3):
                for i in range(5):
                    acc2[y + ky, 128 * i:128 * i + 128, :] += r[128 * ky:128 * ky + 128, 128 * i:128 * i + 128]
            return c
        lax.fori_loop(0, 7, dgrad3, 0)
        def wgrad3(y, c):
            def lhs(ref):
                return jnp.concatenate([jnp.concatenate([ref[y - ky + 2, 128 * (i + 1):128 * (i + 2), :] for i in range(4)], axis=1) for ky in range(3)], axis=0)
            def rhs(ref):
                return jnp.concatenate([ref[y, 128 * i:128 * i + 256, :] for i in range(4)], axis=1)
            a3[...] += dot3((lhs(d3h), lhs(d3l)), (rhs(h2h), rhs(h2l)), NT)
            return c
        lax.fori_loop(0, 9, wgrad3, 0)
        for ky in range(3):
            grad = a3[128 * ky:128 * ky + 64, 0:192] + a3[128 * ky + 64:128 * ky + 128, 64:256]
            small_ref[256 + 64 * ky:320 + 64 * ky, :] = grad[:, 0:128]
            small_ref[448 + 64 * ky:512 + 64 * ky, 0:64] = grad[:, 128:192]
        def step2(y, total):
            for x in range(9):
                d = acc2[y, 64 * x:64 * x + 64, :] * dsilu(pre2_ref[y, 64 * x:64 * x + 64, :])
                total = total + d
                hi, lo = split(d)
                d2h[y + 1, 64 * (x + 1):64 * (x + 2), :] = hi
                d2l[y + 1, 64 * (x + 1):64 * (x + 2), :] = lo
            return total
        total = lax.fori_loop(0, 9, step2, jnp.zeros((64, 128), F32))
        small_ref[641:642, 0:64] = jnp.sum(jnp.transpose(total), axis=0, keepdims=True)
    def block2(y, total):
        w2 = (w2_ref[0], w2_ref[1])
        rh = jnp.concatenate([d2h[pl.ds(y, 2), 64 * i:64 * i + 128, :].reshape(256, 128) for i in range(10)], axis=1)
        rl = jnp.concatenate([d2l[pl.ds(y, 2), 64 * i:64 * i + 128, :].reshape(256, 128) for i in range(10)], axis=1)
        r = dot3(w2, (rh, rl))
        h1h, h1l = [], []
        for py in range(2):
            rowh, rowl = [], []
            for i in range(10):
                v = pre1_ref[2 * y + py, 64 * i:64 * i + 64, :]
                s = jax.nn.sigmoid(v)
                d = r[64 * py:64 * py + 64, 128 * i:128 * i + 128] * (s * (1.0 + v * (1.0 - s)))
                total = total + d[0:32] + d[32:64]
                hi, lo = split(d)
                d1h[2 * y + py + 1, 64 * i + 32:64 * i + 96, :] = hi
                d1l[2 * y + py + 1, 64 * i + 32:64 * i + 96, :] = lo
                hi, lo = split(v * s)
                rowh.append(hi)
                rowl.append(lo)
            h1h.append(rowh)
            h1l.append(rowl)
        def lhs(ref):
            return jnp.concatenate([jnp.concatenate([ref[y + 1 - h, 64 * (i + 1):64 * (i + 2), :] for i in range(9)], axis=1) for h in range(2)], axis=0)
        def rhs(rows):
            return jnp.concatenate([jnp.concatenate([rows[0][i], rows[0][i + 1], rows[1][i], rows[1][i + 1]], axis=0) for i in range(9)], axis=1)
        a2[...] += dot3((lhs(d2h), lhs(d2l)), (rhs(h1h), rhs(h1l)), NT)
        return total
    def lower():
        pre1_in.wait()
        total = lax.fori_loop(0, 10, block2, jnp.zeros((32, 128), F32))
        small_ref[642:643, 0:32] = jnp.sum(jnp.transpose(total), axis=0, keepdims=True)
        small_ref[0:128, :] = a2[:, 0:128]
        small_ref[128:256, :] = a2[:, 128:256]
    def states_gone(j, slot):
        a, b = states_out(j, slot)
        a.wait()
        if net:
            b.wait_send()
        else:
            b.wait()
    def wgrad1(j, carry):
        x_in(j).wait()
        v = xs[pl.ds(4 * j, 4)]
        hi = v.astype(BF)
        xh[:, 0:336, :] = hi
        xl[:, 0:336, :] = (v - hi.astype(F32)).astype(BF)
        def lhs(ref):
            return jnp.concatenate([jnp.concatenate([ref[j + 1 - h, 96 * i + 32:96 * i + 128, :] for i in range(7)], axis=1) for h in range(2)], axis=0)
        def rhs(ref):
            return jnp.concatenate([ref[:, 48 * i:48 * i + 64, :].reshape(256, 128) for i in range(7)], axis=1)
        a1[...] += dot3((lhs(d1h), lhs(d1l)), (rhs(xh), rhs(xl)), NT)
        return carry
    def first_grad():
        lax.fori_loop(0, 21, wgrad1, 0)
        for h in range(2):
            for ky in range(4):
                grad = a1[96 * h:96 * h + 32, 64 * ky:64 * ky + 32]
                grad = grad + a1[96 * h + 32:96 * h + 64, 64 * ky + 16:64 * ky + 48]
                grad = grad + a1[96 * h + 64:96 * h + 96, 64 * ky + 32:64 * ky + 64]
                pay[672 + 32 * h:704 + 32 * h, 32 * ky:32 * ky + 32] = grad
    def dgrad1(j, carry):
        def both(ref):
            return jnp.concatenate([ref[pl.ds(j, 2), 96 * i:96 * i + 128, :].reshape(256, 128) for i in range(7)], axis=1)
        r = dot3((w1_ref[0], w1_ref[1]), (both(d1h), both(d1l)))
        slot = j % 2
        pl.when(j >= 2)(lambda: states_gone(j - 2, slot))
        lo_to, up_to = lob.at[slot], upb.at[slot]
        for ky in range(4):
            for i in range(7):
                lo_to[ky, 24 * i:24 * i + 24, :] = r[24 * ky:24 * ky + 24, 128 * i:128 * i + 128]
                up_to[ky, 24 * i:24 * i + 24, :] = r[96 + 24 * ky:96 + 24 * ky + 24, 128 * i:128 * i + 128]
        for copy in states_out(j, slot):
            copy.start()
        return carry
    if net:
        pl.when(p == 0)(fetch)
        pl.when(p == 0)(lambda: greet([chip((me + k) % chips) for k in range(1, chips)] + [at(1, g, z, y)]))
        pl.when(p == 1)(lambda: greet([at(1, g, flip(z, k), y) for k in range(1, 4)] + [at(1, g, z, 1 - y), at(0, g, z, y)]))
        def begin(yy):
            for copy in give_own(yy):
                copy.start()
        pl.when(p == 0)(lambda: each(begin))
        @pl.when(p == 1)
        def _():
            each(gather)
            each(second, flipped=True)
        pay[0:24, :] = s0_ref[...]
    else:
        pay[0:24, :] = jnp.zeros((24, 128), F32)
    pay[672:, :] = jnp.zeros((ROWS - 672, 128), F32)
    xh[:, 336:, :] = jnp.zeros((4, 16, 128), BF)
    xl[:, 336:, :] = jnp.zeros((4, 16, 128), BF)
    a1[...] = jnp.zeros_like(a1)
    if net:
        @pl.when(p == 0)
        def _():
            upper()
            lower()
            first_grad()
            for k in range(chips):
                give(k).start()
            for k in range(1, chips):
                show(k).start()
            got1[me] = pay[672:736, :]
            lax.fori_loop(0, 12, dgrad1, 0)
            give(0).wait()
            for k in range(1, chips):
                given(k).wait_recv()
            red[...] = jnp.sum(got[...], axis=0)
            tot[part(me), :] = red[...]
            for k in range(1, chips):
                tell(k).start()
            lax.fori_loop(12, 21, dgrad1, 0)
            for k in range(1, chips):
                told(k).wait_recv()
            for k in range(1, chips):
                shown(k).wait_recv()
            tot[672:736, :] = jnp.sum(got1[...], axis=0)
            hand.start()
            for k in range(1, chips):
                give(k).wait_send()
                tell(k).wait_send()
                show(k).wait_send()
            hand.wait_send()
            for j in (last - 1, last):
                states_gone(j, j % 2)
    else:
        fetch()
        upper()
        lower()
        first_grad()
        lax.fori_loop(0, 21, dgrad1, 0)
        for j in (last - 1, last):
            states_gone(j, j % 2)
    if net:
        @pl.when(p == 1)
        def _():
            hand.wait_recv()
            def arrive(i, c):
                states_out(i, 0)[1].wait_recv()
                return c
            lax.fori_loop(0, last + 1, arrive, 0)
        tot_ref[...] = tot[...]
        @pl.when(p == 0)
        def _():
            def given_own(yy):
                for copy in give_own(yy):
                    copy.wait_send()
            each(given_own)
            brought(0)
            brought(1)
        @pl.when(p == 1)
        def _():
            each(finished)
            each(second_sent, flipped=True)
    else:
        tot_ref[...] = pay[...]

def backward(net, x, pre1, pre2, pre3, df, w1, w2, w3, *wired):
    sds = lambda *s: jax.ShapeDtypeStruct(s, F32)
    vmb = lambda *s: pltpu.VMEM(s, BF)
    f32 = lambda *s: pltpu.VMEM(s, F32)
    dma = pltpu.SemaphoreType.DMA
    return pl.pallas_call(
        functools.partial(bwd_kernel, net),
        in_specs=[ANY, ANY] + [VMEM] * 6 + [VMEM] * 3 * net,
        out_specs=[VMEM] + [ANY] * (5 if net else 2),
        out_shape=[sds(ROWS, 128)] + ([sds(84, 168, 128)] + [sds(2, 4, 200, 512), sds(4, 9, 32, 128)] * 2 if net else [sds(84, 168, 128), sds(84, 168, 128)]),
        scratch_shapes=[f32(84, 336, 128), f32(20, 640, 128), vmb(4, 352, 128), vmb(4, 352, 128), f32(3136, 128), vmb(11, 768, 128), vmb(11, 768, 128), vmb(11, 704, 128),
                        vmb(11, 704, 128), vmb(22, 704, 128), vmb(22, 704, 128), vmb(9, 640, 128), vmb(9, 640, 128), f32(9, 640, 128), f32(192, 256), f32(128, 256),
                        f32(384, 256), f32(ROWS, 128), f32(2, 4, 168, 128), f32(2, 4, 168, 128), dma((21,)), dma, dma((2,)), dma((2,))]
        + ([f32(16, ROWS // 16, 128), f32(16, 64, 128), f32(ROWS // 16, 128), f32(ROWS, 128), dma((21,))]
           + line_sems(4) + [dma((7, 4))] * 2 + [dma((2,))] * 3 + [dma((2, 7, 2))] * 2 + [dma((16,))] * 6 + [dma] * 3) * net,
        compiler_params=pltpu.CompilerParams(vmem_limit_bytes=62 * 2**20, **(dict(collective_id=3, has_side_effects=True) if net else {})),
    )(x, pre1, pre2, pre3, df, w1, w2, w3, *wired)

def wide_kernel(f1a, f1b, f1c, f2a, f2b, f2c, d1, d2, d3, g1, g2, z1, z2, r_ref, q_ref, fv, dv, ev, gv, zv, acc, acq, da, sem):
    p, g = lax.axis_index("pair"), lax.axis_index("group")
    y = lax.axis_index("rep") % 2
    three, last = pl.ds(0, 3), 3
    rows = [pl.ds(*piece) for piece in PIECES]
    pairs = [(ref, fv.at[three, :, rows[i]]) for i, ref in enumerate((f2a, f2b, f2c))] + [(ref.at[g], fv.at[last, :, rows[i]]) for i, ref in enumerate((f1a, f1b, f1c))]
    pairs += [(g2, gv.at[three]), (g1.at[:, g], gv.at[last]), (z2, zv.at[three]), (z1, zv.at[last])]
    first = len(pairs)
    for m in range(4):
        pairs += [(d2.at[m] if m < 3 else d1.at[:, y], dv.at[m]), (d3.at[m], ev.at[m])]
    copies = [pltpu.make_async_copy(a, b, sem.at[i]) for i, (a, b) in enumerate(pairs)]
    for copy in copies:
        copy.start()
    acc[...] = jnp.zeros_like(acc)
    acq[...] = jnp.zeros_like(acq)
    da[...] = jnp.zeros_like(da)
    for copy in copies[:first]:
        copy.wait()
    def block(ref, m):
        return jnp.concatenate([jnp.concatenate([ref[m, i, 128 * c:128 * c + 128, :] for c in range(2)], axis=1) for i in range(4)], axis=0)
    def step(m):
        for copy in copies[first + 2 * m:first + 2 * m + 2]:
            copy.wait()
        f = split(jnp.concatenate([fv[m, i] for i in range(4)], axis=1))
        acc[0] += dot3(f, split(block(dv, m)))
        acc[1] += dot3(f, split(block(ev, m)))
        dz = jnp.concatenate([zv[m, i] for i in range(4)], axis=1)
        row = lax.broadcasted_iota(jnp.int32, (PAD, 512), 0)
        chosen = dz[ATOMS:ATOMS + 1].astype(jnp.int32)
        d = jnp.where(row < ATOMS, dz, 0.0)
        da[0:PAD, :] = d
        for i in range(ACTIONS):
            da[128 + ATOMS * i:128 + ATOMS * i + PAD, :] = mask_of(chosen, i) * d
        def units(s):
            return split(jnp.concatenate([gv[m, i, s] for i in range(4)], axis=1))
        @pl.when(y == 0)
        def _():
            acq[:, 0:128] += dot3(units(0), split(da[0:128, :]), NT)
            acq[:, 128:640] += dot3(units(1), split(da[128:640, :]), NT)
        @pl.when(y == 1)
        def _():
            acq[:, 640:1152] += dot3(units(1), split(da[640:1152, :]), NT)
    for m in range(4):
        step(m)
    r_ref[:, 0:256] = jnp.where(p == 0, acc[0], acc[1])
    r_ref[:, 256:512] = jnp.where(p == 0, acc[1], acc[0])
    for c in range(9):
        q_ref[c] = acq[:, 128 * c:128 * c + 128]

def wide_grads(*messages):
    sds = lambda *s: jax.ShapeDtypeStruct(s, F32)
    f32 = lambda *s: pltpu.VMEM(s, F32)
    return pl.pallas_call(
        wide_kernel, in_specs=[ANY] * 13, out_specs=[VMEM] * 2,
        out_shape=[sds(200, 512), sds(9, 32, 128)],
        scratch_shapes=[f32(4, 4, 200, 128), f32(4, 4, 256, 128), f32(4, 4, 256, 128), f32(4, 4, 2, 32, 128), f32(4, 4, PAD, 128),
                        f32(2, 200, 256), f32(32, 1152), f32(1152, 512), pltpu.SemaphoreType.DMA((18,))],
        compiler_params=pltpu.CompilerParams(vmem_limit_bytes=60 * 2**20),
    )(*messages)

def torso_out(tot, k1_ref, k2_ref, k3_ref, b1_ref, b2_ref, b3_ref, t1, t2):
    t1[:, 0:64] = jnp.transpose(tot[672:736, :])
    t1[:, 64:128] = jnp.zeros((128, 64), F32)
    for ky in range(4):
        for c in range(4):
            v = t1[pl.ds(32 * ky + c, 8, stride=4), :]
            for h in range(2):
                k1_ref[c, 4 * h + ky] = v[:, 32 * h:32 * h + 32]
    for py in range(2):
        t2[...] = jnp.transpose(tot[24 + 128 * py:152 + 128 * py, :])
        for h in range(2):
            for kx in range(4):
                k2_ref[:, 2 * h + py, kx, :] = t2[32 * kx:32 * kx + 32, 64 * h:64 * h + 64]
    for ky in range(3):
        for kx in range(3):
            base = (280 if kx < 2 else 472) + 64 * ky
            k3_ref[ky, kx] = tot[base:base + 64, 64 * (kx % 2):64 * (kx % 2) + 64]
    b3_ref[...] = tot[664:665, 0:64]
    b2_ref[...] = tot[665:666, 0:64]
    b1_ref[...] = tot[666:667, 0:32]

def finish_kernel(sg_ref, ag_ref, ah_ref, tot_ref, in_ref, out_ref, ein_ref, eout_ref, mean_ref, sigma_ref, hm_ref, hs_ref, k1_ref, k2_ref, k3_ref, b1_ref, b2_ref, b3_ref,
                  hb_ref, hbs_ref, bo_ref, bos_ref, loss_ref, states_ref, t1, t2, sv, sem):
    parts = [pl.ds(21 * i, 21) for i in range(4)]
    reads = [pltpu.make_async_copy(sg_ref.at[part], sv.at[part], sem.at[0, i]) for i, part in enumerate(parts)]
    moves = [pltpu.make_async_copy(sv.at[part], states_ref.at[part], sem.at[1, i]) for i, part in enumerate(parts)]
    for copy in reads:
        copy.start()
    for i in range(4):
        reads[i].wait()
        moves[i].start()
    for s in range(2):
        tall = column(in_ref[s:s + 1, :], 512) * out_ref[s:s + 1, :]
        for z, (start, n) in enumerate(((0, 200), (200, 200), (400, 184), (584, 200))):
            v = ag_ref[s, z, 0:n, :]
            mean_ref[s, start:start + n, :] = v
            sigma_ref[s, start:start + n, :] = v * tall[start:start + n]
    noise = column(eout_ref[...], 128)
    for c in range(9):
        start = 0 if c == 0 else ATOMS + 128 * (c - 1)
        n = min(128, (ATOMS if c == 0 else OUTS) - start)
        v = jnp.transpose(jnp.concatenate([ah_ref[z, c] for z in range(4)], axis=0))[0:n]
        hm_ref[start:start + n, :] = v
        hs_ref[start:start + n, :] = v * (noise[start:start + n] * ein_ref[min(c, 1):min(c, 1) + 1, :])
    torso_out(tot_ref, k1_ref, k2_ref, k3_ref, b1_ref, b2_ref, b3_ref, t1, t2)
    for s in range(2):
        for c in range(4):
            v = tot_ref[4 * s + c:4 * s + c + 1, :]
            hb_ref[s:s + 1, 128 * c:128 * c + 128] = v
            hbs_ref[s:s + 1, 128 * c:128 * c + 128] = v * out_ref[s:s + 1, 128 * c:128 * c + 128]
    for c in range(8):
        n = min(128, OUTS - 128 * c)
        v = tot_ref[8 + c:9 + c, 0:n]
        bo_ref[:, 128 * c:128 * c + n] = v
        bos_ref[:, 128 * c:128 * c + n] = v * eout_ref[:, 128 * c:128 * c + n]
    loss_ref[...] = tot_ref[16:17, :]
    for copy in moves:
        copy.wait()

def finish(sg, ag, ah, tot, n_in, n_out, e_in, e_out):
    sds = lambda *s: jax.ShapeDtypeStruct(s, F32)
    return pl.pallas_call(
        finish_kernel, in_specs=[ANY] + [VMEM] * 7, out_specs=[VMEM] * 15 + [ANY],
        out_shape=[sds(2, 784, 512), sds(2, 784, 512), sds(OUTS, 128), sds(OUTS, 128), sds(4, 8, 8, 32), sds(32, 4, 4, 64), sds(3, 3, 64, 64), sds(1, 32), sds(1, 64), sds(1, 64),
                   sds(2, 512), sds(2, 512), sds(1, OUTS), sds(1, OUTS), sds(1, 128), sds(84, 168, 128)],
        scratch_shapes=[pltpu.VMEM((128, 128), F32), pltpu.VMEM((128, 128), F32), pltpu.VMEM((84, 168, 128), F32), pltpu.SemaphoreType.DMA((2, 4))],
        compiler_params=pltpu.CompilerParams(vmem_limit_bytes=60 * 2**20),
    )(sg, ag, ah, tot, n_in, n_out, e_in, e_out)

def small_finish_kernel(tot_ref, k1_ref, k2_ref, k3_ref, b1_ref, b2_ref, b3_ref, t1, t2):
    torso_out(tot_ref, k1_ref, k2_ref, k3_ref, b1_ref, b2_ref, b3_ref, t1, t2)

def small_finish(tot):
    sds = lambda *s: jax.ShapeDtypeStruct(s, F32)
    return pl.pallas_call(
        small_finish_kernel, in_specs=[VMEM], out_specs=[VMEM] * 6,
        out_shape=[sds(4, 8, 8, 32), sds(32, 4, 4, 64), sds(3, 3, 64, 64), sds(1, 32), sds(1, 64), sds(1, 64)],
        scratch_shapes=[pltpu.VMEM((128, 128), F32), pltpu.VMEM((128, 128), F32)],
    )(tot)

def exchange(parts):
    groups = lax.axis_size("group")
    p, g = lax.axis_index("pair"), lax.axis_index("group")
    got = []
    for k in range(groups):
        to = (g + k) % groups
        mine = parts(0, to)
        if k:
            mine = lax.ppermute(mine, ("pair", "group"), [(i, (i + k) % groups) for i in range(groups)])
        theirs = lax.ppermute(parts(1, to), ("pair", "group"), [(i, groups + (i + k) % groups) for i in range(groups)])
        got.append(jnp.where(p == 0, mine, theirs))
    return got

HIGH = lax.Precision.HIGH

def local(states, actions, proj_lower, proj_upper, proj_weight, first_kernel, first_bias, second_kernel, second_bias,
          third_kernel, third_bias, hidden_mean, hidden_sigma, hidden_bias_mean, hidden_bias_sigma, head_mean, head_sigma,
          head_bias_mean, head_bias_sigma, hidden_noise_in, hidden_noise_out, head_noise_in, head_noise_out):
    pair = lax.axis_index("pair")
    groups = lax.axis_size("group")
    shards = 2 * groups
    net = int(groups == 2 and lax.axis_size("rep") == 8)
    n_in, n_out, e_in, e_out = hidden_noise_in[0], hidden_noise_out[0], head_noise_in[0], head_noise_out[0]
    own_noise = (n_in, n_out, e_in, e_out[None])
    feat_q, hid_q = 3136 // shards, 512 // shards
    shard = pair * groups + lax.axis_index("group")
    def of_shard(noise):
        on_in, on_out, on_ein, on_eout = noise
        return (lax.dynamic_slice_in_dim(on_in, shard * feat_q, feat_q, axis=1), on_out, lax.dynamic_slice_in_dim(on_ein, shard * hid_q, hid_q, axis=1), on_eout)

    x = jnp.transpose(states[0], (2, 3, 1, 0)).reshape(84, 336, 128)
    fw1, fw2, fw3, bw1, bw2, bw3, c1, c2, c3 = prepare(first_kernel[0], second_kernel[0], third_kernel[0], first_bias, second_bias, third_bias)
    e_out = e_out[None]
    e_rows = jnp.where(jnp.arange(OUTS)[:, None] < ATOMS, e_in[0:1], e_in[1:2])
    wo = jnp.pad(head_mean[0].T + head_sigma[0].T * (e_rows * e_out.T), ((0, OUTP - OUTS), (0, 0)))
    nin = jnp.transpose(n_in.reshape(2, STEPS, 3136 // STEPS), (1, 0, 2))
    pre1, pre2, pre3, feats = forward(x, fw1, fw2, fw3, c1, c2, c3)
    h, hid, logp, dist, *f12 = hidden(net, feats, hidden_mean[0], hidden_sigma[0], nin, n_out, hidden_bias_mean[0], hidden_bias_sigma[0], wo, head_bias_mean, head_bias_sigma, e_out, actions, proj_lower.T, proj_weight.T)
    back = (logp, h, hidden_mean[0], hidden_sigma[0], nin, n_out, wo, actions)
    if net:
        target, *f12 = f12
        f1, f2 = f12[:3], f12[3:]
        df, small_b, f2c, g1, d1, z1, g2, d2, z2, d3, *noise = hidden_bwd(net, target, *back, f1[2], hid, *own_noise)
        part_r, part_q = wide_grads(*f1, *f2, f2c, d1, d2, d3, g1, g2, z1, z2)
        total, grad_rows, ag, ah, _, _ = backward(net, x, pre1, pre2, pre3, df, bw1, bw2, bw3, part_r, part_q, small_b)
        (hidden_grad, hidden_sigma_grad, head_t, head_sigma_t, gk1, gk2, gk3, gb1, gb2, gb3, hb_grad, hbs_grad, bo_grad, bos_grad,
         loss, grad_rows) = finish(grad_rows, ag, ah, total, *of_shard(noise))
    else:
        df, small_b, msg, dz = hidden_bwd(net, lax.ppermute(dist, "pair", [(1, 0)]), *back)
        f_got = exchange(lambda p, g: lax.dynamic_slice_in_dim(feats, (p * groups + g) * feat_q, feat_q, axis=0))
        hid = jnp.transpose(hid, (3, 0, 2, 1, 4, 5)).reshape(1024, 128).T
        hid_got = exchange(lambda p, g: lax.dynamic_slice_in_dim(hid.reshape(128, 2, 512), (p * groups + g) * hid_q, hid_q, axis=2))
        dpre = jnp.transpose(msg.reshape(2, 2, 2, 128, 128), (3, 1, 0, 2, 4)).reshape(128, 1024)
        d_all = jnp.concatenate(exchange(lambda p, g: jnp.concatenate([dpre, dz.T, jnp.zeros((128, 72), F32)], axis=1)), axis=0)
        f_all = jnp.concatenate(f_got, axis=1)
        hid_all = jnp.concatenate(hid_got, axis=0)
        part_hidden = jnp.einsum("fb,bsh->sfh", f_all, d_all[:, :1024].reshape(-1, 2, 512), precision=HIGH)
        dz_all = d_all[:, 1024:1024 + ATOMS]
        picked = d_all[:, 1024 + ATOMS]
        mask = jnp.where(picked[None, :] == jnp.arange(ACTIONS, dtype=F32)[:, None], 1.0 - 1.0 / ACTIONS, -1.0 / ACTIONS)
        da = (mask[:, None, :] * dz_all.T[None]).reshape(ACTIONS * ATOMS, -1)
        part_head = jnp.concatenate([jnp.dot(dz_all.T, hid_all[:, 0], precision=HIGH), jnp.dot(da, hid_all[:, 1], precision=HIGH)], axis=0)
        hidden_grad, head_t = lax.psum((part_hidden, part_head), "rep")
        small_d, lo, up = backward(net, x, pre1, pre2, pre3, df, bw1, bw2, bw3)
        grad_rows = jnp.where(pair == 0, lo, lax.ppermute(up, "pair", [(0, 1)]))
        total = lax.psum(small_d + jnp.pad(small_b, ((0, ROWS - 24), (0, 0))), ("pair", "group", "rep"))
        in_q, on_out, e_q, on_eout = of_shard([jnp.where(pair == 0, mine, lax.ppermute(mine, "pair", [(0, 1)])) for mine in own_noise])
        hidden_sigma_grad = hidden_grad * (in_q[:, :, None] * on_out[:, None, :])
        head_sigma_t = head_t * (jnp.where(jnp.arange(OUTS)[:, None] < ATOMS, e_q[0:1], e_q[1:2]) * on_eout.T)
        gk1, gk2, gk3, gb1, gb2, gb3 = small_finish(total)
        hb_grad = total[0:8].reshape(2, 512)
        bo_grad = total[8:16].reshape(1, -1)[:, :OUTS]
        hbs_grad, bos_grad = hb_grad * on_out, bo_grad * on_eout
        loss = total[16:17]
    states_grad = jnp.transpose(grad_rows.reshape(84, 84, 2, 128), (3, 2, 0, 1))
    return (loss[0, 0], states_grad, jnp.transpose(gk1, (3, 0, 1, 2)), gb1[0], jnp.transpose(gk2, (3, 0, 1, 2)), gb2[0], jnp.transpose(gk3, (2, 3, 0, 1)), gb3[0],
            hidden_grad, hidden_sigma_grad, hb_grad, hbs_grad, head_t.T, head_sigma_t.T, bo_grad[0], bos_grad[0])


def solution(mesh):
    placed = (
        P("pair", ("group", "rep"), None, None, None),
        P("pair", ("group", "rep")),
        P(("group", "rep"), None),
        P(("group", "rep"), None),
        P(("group", "rep"), None),
        P("pair", None, None, None, None),
        P("pair", None),
        P("pair", None, None, None, None),
        P("pair", None),
        P("pair", None, None, None, None),
        P("pair", None),
        P("pair", None, None, None),
        P("pair", None, None, None),
        P("pair", None, None),
        P("pair", None, None),
        P("pair", None, None),
        P("pair", None, None),
        P("pair", None),
        P("pair", None),
        P("pair", None, None),
        P("pair", None, None),
        P("pair", None, None),
        P("pair", None),
    )
    return jax.shard_map(
        local,
        mesh=mesh,
        in_specs=placed,
        out_specs=(
            P(),
            P(("group", "rep"), "pair", None, None),
            P(),
            P(),
            P(),
            P(),
            P(),
            P(),
            P(None, ("pair", "group"), None),
            P(None, ("pair", "group"), None),
            P(),
            P(),
            P(("pair", "group"), None),
            P(("pair", "group"), None),
            P(),
            P(),
        ),
        check_vma=False,
    )
```

```python
import functools
import jax
import jax.numpy as jnp
from jax import lax
from jax.experimental import pallas as pl
from jax.experimental.pallas import tpu as pltpu
from jax.sharding import PartitionSpec as P

BF = jnp.bfloat16
F32 = jnp.float32
NN=(((1,),(0,)),((),()))
NT=(((1,),(1,)),((),()))
TN=(((0,),(0,)),((),()))

def split(v):
    hi = v.astype(BF)
    return hi, (v - hi.astype(F32)).astype(BF)

def dot(a, b, dims=NN):
    return lax.dot_general(a, b, dims, preferred_element_type=F32)

def dot3(a, b, dims=NN):
    ah, al = a; bh, bl = b
    return dot(ah, bh, dims) + (dot(ah, bl, dims) + dot(al, bh, dims))

def silu(v):
    return v * jax.nn.sigmoid(v)

def prep_kernel(k1_ref, k2_ref, k3_ref, b1_ref, b2_ref, b3_ref, f1_ref, f2_ref, f3_ref, r1_ref, r2_ref, r3_ref, c1_ref, c2_ref, c3_ref,
                t1a, t1b, u1a, u1b, m2, m3, n2, n3):
    for ref in (t1a, t1b, u1a, u1b, m2, m3, n2, n3):
        ref[...] = jnp.zeros_like(ref)
    def put(ref, start, stride, v, lane):
        n = v.shape[0]
        pieces = [jnp.zeros((n, lane), F32)] * (lane > 0) + [v] + [jnp.zeros((n, 96 - lane), F32)] * (lane < 96)
        rows = pl.ds(start, n, stride=stride)
        ref[rows, :] = ref[rows, :] + jnp.concatenate(pieces, axis=1)
    for c in range(4):
        for ky in range(8):
            v = k1_ref[c, ky]
            h, kq = ky // 4, ky % 4
            for w in range(3):
                put((t1a, t1b)[h], kq * 64 + 16 * w + c, 4, v, 32 * w)
            base = (c // 2) * 96 + kq * 24 + c % 2
            for q in range(4):
                if q == 0:
                    put((u1b, u1a)[h], base, 2, v[4:8], 0)
                elif q == 3:
                    put((u1b, u1a)[h], base + 16, 2, v[0:4], 96)
                else:
                    put((u1b, u1a)[h], base + 8 * (q - 1), 2, v, 32 * q)
    for ky in range(4):
        for kx in range(4):
            v = k2_ref[:, ky, kx, :]
            h, py, wx, px = ky // 2, ky % 2, 1 - kx // 2, kx % 2
            m2[py * 128 + kx * 32:py * 128 + kx * 32 + 32, 64 * h:64 * h + 64] = v
            n2[(py * 2 + px) * 32:(py * 2 + px) * 32 + 32, 128 * (1 - h) + 64 * wx:128 * (1 - h) + 64 * wx + 64] = v
    for ky in range(3):
        for kx in range(3):
            v = k3_ref[ky, kx]
            vt = jnp.transpose(v)
            for w in range(2):
                m3[ky * 128 + w * 64:ky * 128 + w * 64 + 64, 64 * (w + kx):64 * (w + kx) + 64] = v
                q = w + 2 - kx
                n3[ky * 128 + w * 64:ky * 128 + w * 64 + 64, 64 * q:64 * q + 64] = vt
    w1 = jnp.concatenate([jnp.transpose(t1a[...])[0:96], jnp.transpose(t1b[...])[0:96]], axis=0)
    pairs = ((f1_ref, w1), (f2_ref, jnp.transpose(m2[...])), (f3_ref, m3[...]), (r1_ref, jnp.concatenate([u1a[...], u1b[...]], axis=1)), (r2_ref, n2[...]), (r3_ref, n3[...]))
    for ref, v in pairs:
        hi, lo = split(v)
        ref[0] = hi
        ref[1] = lo
    for ref, b_ref, n, times in ((c1_ref, b1_ref, 32, 3), (c2_ref, b2_ref, 64, 1), (c3_ref, b3_ref, 64, 1)):
        col = jnp.transpose(jnp.broadcast_to(b_ref[...], (128, n)))
        for i in range(times):
            ref[n * i:n * i + n, :] = col

def prepare(k1, k2, k3, b1, b2, b3):
    vm = pl.BlockSpec(memory_space=pltpu.VMEM)
    bfs = lambda *s: jax.ShapeDtypeStruct(s, BF)
    sds = lambda *s: jax.ShapeDtypeStruct(s, F32)
    f32 = lambda *s: pltpu.VMEM(s, F32)
    return pl.pallas_call(
        prep_kernel, in_specs=[vm] * 6, out_specs=[vm] * 9,
        out_shape=[bfs(2, 192, 256), bfs(2, 128, 256), bfs(2, 384, 256), bfs(2, 192, 256), bfs(2, 128, 256), bfs(2, 384, 256), sds(96, 128), sds(64, 128), sds(64, 128)],
        scratch_shapes=[f32(256, 128), f32(256, 128), f32(192, 128), f32(192, 128), f32(256, 128), f32(384, 256), f32(128, 256), f32(384, 256)],
        compiler_params=pltpu.CompilerParams(vmem_limit_bytes=60 * 2**20),
    )(jnp.transpose(k1, (1, 2, 3, 0)), jnp.transpose(k2, (1, 2, 3, 0)), jnp.transpose(k3, (2, 3, 0, 1)), b1, b2, b3)

def fwd_kernel(x_ref, w1_ref, w2_ref, w3_ref, b1_ref, b2_ref, b3_ref, pre1_hbm, pre2_hbm, pre3_ref, f_ref,
               xs, pre1_ref, pre2_ref, xh, xl, top1, top2, acc3, h1h, h1l, h2h, h2l, x_sem, sem1, sem2):
    def x_in(j):
        return pltpu.make_async_copy(x_ref.at[pl.ds(4 * j, 4)], xs.at[pl.ds(4 * j, 4)], x_sem.at[j])
    def row_out(row):
        return pltpu.make_async_copy(pre1_ref.at[row], pre1_hbm.at[row], sem1.at[row])
    for j in range(21):
        x_in(j).start()
    xh[:, 336:, :] = jnp.zeros((4, 16, 128), BF)
    xl[:, 336:, :] = jnp.zeros((4, 16, 128), BF)
    top1[...] = jnp.zeros_like(top1)
    top2[...] = jnp.zeros_like(top2)
    acc3[...] = jnp.zeros_like(acc3)
    h2h[:, 576:, :] = jnp.zeros((9, 64, 128), BF)
    h2l[:, 576:, :] = jnp.zeros((9, 64, 128), BF)
    def step1(j, carry):
        x_in(j).wait()
        v = xs[pl.ds(4 * j, 4)]
        hi = v.astype(BF)
        xh[:, 0:336, :] = hi
        xl[:, 0:336, :] = (v - hi.astype(F32)).astype(BF)
        rh = jnp.concatenate([xh[:, 48 * i:48 * i + 64, :].reshape(256, 128) for i in range(7)], axis=1)
        rl = jnp.concatenate([xl[:, 48 * i:48 * i + 64, :].reshape(256, 128) for i in range(7)], axis=1)
        r = dot3((w1_ref[0], w1_ref[1]), (rh, rl))
        out = top1[...] + r[96:]
        top1[...] = r[:96]
        b1 = b1_ref[...]
        row = jnp.maximum(j - 1, 0)
        for i in range(7):
            n = 96 if i < 6 else 64
            p = out[:n, 128 * i:128 * i + 128] + b1[:n]
            pre1_ref[row, 96 * i:96 * i + n, :] = p
            hh, hl = split(silu(p))
            h1h[row, 96 * i:96 * i + n, :] = hh
            h1l[row, 96 * i:96 * i + n, :] = hl
        pl.when(j >= 1)(lambda: row_out(row).start())
        return carry
    lax.fori_loop(0, 21, step1, 0)
    w2 = (w2_ref[0], w2_ref[1])
    b2 = b2_ref[...]
    def step2(y, carry):
        rh = jnp.concatenate([h1h[pl.ds(2 * y, 2), 64 * i:64 * i + 128, :].reshape(256, 128) for i in range(9)], axis=1)
        rl = jnp.concatenate([h1l[pl.ds(2 * y, 2), 64 * i:64 * i + 128, :].reshape(256, 128) for i in range(9)], axis=1)
        r = dot3(w2, (rh, rl))
        o = top2[...] + r[64:]
        top2[...] = r[:64]
        row = jnp.maximum(y - 1, 0)
        for i in range(9):
            p = o[:, 128 * i:128 * i + 128] + b2
            pre2_ref[row, 64 * i:64 * i + 64, :] = p
            hh, hl = split(silu(p))
            h2h[row, 64 * i:64 * i + 64, :] = hh
            h2l[row, 64 * i:64 * i + 64, :] = hl
        return carry
    lax.fori_loop(0, 10, step2, 0)
    pre2_out = pltpu.make_async_copy(pre2_ref, pre2_hbm, sem2)
    pre2_out.start()
    w3 = (w3_ref[0], w3_ref[1])
    b3 = b3_ref[...]
    def step3(y, carry):
        rh = jnp.concatenate([h2h[y, 128 * i:128 * i + 256, :] for i in range(4)], axis=1)
        rl = jnp.concatenate([h2l[y, 128 * i:128 * i + 256, :] for i in range(4)], axis=1)
        r = dot3(w3, (rh, rl))
        for ky in range(3):
            for i in range(4):
                acc3[y - ky + 2, 128 * i:128 * i + 128, :] += r[128 * ky:128 * ky + 128, 128 * i:128 * i + 128]
        return carry
    lax.fori_loop(0, 9, step3, 0)
    for y in range(7):
        for x in range(7):
            p = acc3[y + 2, 64 * x:64 * x + 64, :] + b3
            pre3_ref[pl.ds(y * 7 + x, 64, stride=49), :] = p
            f_ref[pl.ds(y * 7 + x, 64, stride=49), :] = silu(p)
    pre2_out.wait()
    for row in range(20):
        row_out(row).wait()

def forward(x, w1, w2, w3, b1, b2, b3):
    vm = pl.BlockSpec(memory_space=pltpu.VMEM)
    hbm = pl.BlockSpec(memory_space=pl.ANY)
    sds = lambda *s: jax.ShapeDtypeStruct(s, F32)
    f32 = lambda *s: pltpu.VMEM(s, F32)
    bf = lambda *s: pltpu.VMEM(s, BF)
    dma = pltpu.SemaphoreType.DMA
    return pl.pallas_call(
        fwd_kernel,
        in_specs=[hbm] + [vm] * 6,
        out_specs=[hbm, hbm, vm, vm],
        out_shape=[sds(20, 640, 128), sds(9, 576, 128), sds(3136, 128), sds(3136, 128)],
        scratch_shapes=[f32(84, 336, 128), f32(20, 640, 128), f32(9, 576, 128), bf(4, 352, 128), bf(4, 352, 128),
                        f32(96, 896), f32(64, 1152), f32(11, 512, 128), bf(20, 640, 128), bf(20, 640, 128), bf(9, 640, 128), bf(9, 640, 128),
                        dma((21,)), dma((20,)), dma],
        compiler_params=pltpu.CompilerParams(vmem_limit_bytes=60 * 2**20),
    )(x, w1, w2, w3, b1, b2, b3)


MESH_ID = pl.DeviceIdType.MESH


def coords():
    r = lax.axis_index("rep")
    return lax.axis_index("pair"), lax.axis_index("group"), r // 2, r % 2


def at(p, g, z, y):
    return (p, g, z * 2 + y)


def flip(z, k):
    return (z, z + 1 - 2 * (z % 2), z + 2 - 4 * (z // 2), 3 - z)[k]


def line(p, g, z, y):
    return [at(q, g, flip(z, k), y) for k in range(4) for q in ((p, 1 - p) if k else (1 - p,))]


def plane(p, g, z, y):
    return [at(p, g, z, 1 - y), at(p, 1 - g, z, y), at(p, 1 - g, z, 1 - y)]


def greet(devices):
    barrier = pltpu.get_barrier_semaphore()
    for device in devices:
        pl.semaphore_signal(barrier, inc=1, device_id=device, device_id_type=MESH_ID)
    pl.semaphore_wait(barrier, len(devices))


def remote(src, dst, send, recv, device):
    return pltpu.make_async_remote_copy(src_ref=src, dst_ref=dst, send_sem=send, recv_sem=recv, device_id=device, device_id_type=MESH_ID)


class Scatter:
    def __init__(self, parts, src, dst, send, recv, own, hold=None, cores=2):
        self.parts, self.src, self.dst, self.send, self.recv, self.own, self.hold, self.cores = parts, src, dst, send, recv, own, hold, cores
        self.p, self.g, self.z, self.y = coords()

    def copies(self):
        for k in range(4):
            for q in range(self.cores):
                for i in range(self.parts):
                    zd = flip(self.z, k)
                    if k == 0 and q == 0:
                        yield pltpu.make_async_copy(self.src(q, zd, i), self.dst(self.z, i) if self.hold is None else self.hold.at[i], self.own.at[i]), True
                    else:
                        yield remote(self.src(q, zd, i), self.dst(self.z, i), self.send.at[k * 2 + q, i], self.recv.at[k, i], at(q, self.g, zd, self.y)), False

    def start(self):
        @pl.when(self.p == 0)
        def _():
            for copy, own in self.copies():
                copy.start()

    def arrived(self, k):
        if self.cores == 1:
            pl.when(self.p == 0)(lambda: self.landed(k))
        else:
            self.landed(k)

    def landed(self, k):
        for i in range(self.parts):
            zs = flip(self.z, k)
            wait = remote(self.src(0, zs, i), self.dst(zs, i), self.send.at[0, i], self.recv.at[k, i], at(1 - self.p, self.g, self.z, self.y)).wait_recv
            def local():
                if self.hold is None:
                    pltpu.make_async_copy(self.src(0, zs, i), self.dst(zs, i), self.own.at[i]).wait()
                else:
                    pltpu.make_async_copy(self.src(0, zs, i), self.hold.at[i], self.own.at[i]).wait()
                    out = pltpu.make_async_copy(self.hold.at[i], self.dst(zs, i), self.own.at[i])
                    out.start()
                    out.wait()
            if k:
                wait()
            elif self.cores == 1:
                local()
            else:
                pl.when(self.p == 1)(wait)
                pl.when(self.p == 0)(local)

    def sent(self):
        @pl.when(self.p == 0)
        def _():
            for copy, own in self.copies():
                if not own:
                    copy.wait_send()


def scatter_sems(parts, *hold):
    return [pltpu.SemaphoreType.DMA((8, parts)), pltpu.SemaphoreType.DMA((4, parts)), pltpu.SemaphoreType.DMA((parts,))] + [pltpu.VMEM((parts,) + hold, F32)] * bool(hold)


PIECES = ((0, 64), (64, 64), (128, 72))


def f_scatter(f_ref, f1_ref, piece, sems):
    start, rows = PIECES[piece]
    def src(q, zd, i):
        return f_ref.at[pl.ds(pl.multiple_of((2 * q + i) * 784 + jnp.minimum(200 * zd, 584) + start, 8), rows)]
    return Scatter(2, src, lambda z, i: f1_ref.at[i, z], *sems)


def f_fan(f1_ref, f2_ref, send, recv):
    return spread_plane(*coords(), lambda gd, yd: f1_ref.at[gd], lambda m: f2_ref.at[m], send, recv)


class Line:
    def __init__(self, parts, own, slot, send, recv):
        self.parts, self.own, self.slot, self.send, self.recv = parts, own, slot, send, recv
        self.p, self.g, self.z, self.y = coords()

    def block(self, t, way):
        return jnp.maximum(self.z - t, 0) if way == 0 else jnp.minimum(self.z + t, 3)

    def there(self, t, way):
        return self.z >= t if way == 0 else self.z + t <= 3

    def copies(self, t, way):
        to = at(self.p, self.g, jnp.minimum(self.z + 1, 3) if way == 0 else jnp.maximum(self.z - 1, 0), self.y)
        zz = self.block(t, way)
        return [remote(self.own(i) if t == 0 else self.slot(zz, i), self.slot(zz, i), self.send.at[t, way, i], self.recv.at[t, way, i], to) for i in range(self.parts)]

    def goes(self, t, way):
        return jnp.logical_and(self.there(t, way), self.z <= 2 if way == 0 else self.z >= 1)

    def start(self, t):
        for way in range(2):
            def go():
                for copy in self.copies(t, way):
                    copy.start()
            pl.when(self.goes(t, way))(go)

    def arrive(self, t, then):
        for i in range(self.parts):
            for way in range(2):
                def come():
                    zz = self.block(t, way)
                    remote(self.slot(zz, i), self.slot(zz, i), self.send.at[t - 1, way, i], self.recv.at[t - 1, way, i], at(1 - self.p, self.g, self.z, self.y)).wait_recv()
                    if t < 3:
                        pl.when(self.goes(t, way))(self.copies(t, way)[i].start)
                    then(2 * t - 1 + way, zz, i)
                pl.when(self.there(t, way))(come)

    def each(self, do):
        do(0, self.z)
        for t in range(1, 4):
            for way in range(2):
                pl.when(self.there(t, way))(lambda: do(2 * t - 1 + way, self.block(t, way)))

    def sent(self):
        for t in range(3):
            for way in range(2):
                def done():
                    for copy in self.copies(t, way):
                        copy.wait_send()
                pl.when(self.goes(t, way))(done)


def line_sems(parts):
    return [pltpu.SemaphoreType.DMA((3, 2, parts)), pltpu.SemaphoreType.DMA((3, 2, parts))]


def g_scatter(hid_ref, g1_ref, sems):
    return Scatter(1, lambda q, zd, i: hid_ref.at[q, zd], lambda z, i: g1_ref.at[z], *sems)


def z_scatter(dz_ref, dz1_ref, sems):
    return Scatter(1, lambda q, zd, i: dz_ref, lambda z, i: dz1_ref.at[z], *sems, cores=1)


def spread_plane(p, g, z, y, src, dst, send, recv):
    places = [(g, 1 - y), (1 - g, y), (1 - g, 1 - y)]
    return [remote(src(*to), dst(m), send.at[m], recv.at[m], at(p, to[0], z, to[1])) for m, to in enumerate(places)]
ATOMS, ACTIONS, PAD = 51, 18, 56
OUTS, OUTP = 969, 976
STEPS = 7
ANY = pl.BlockSpec(memory_space=pl.ANY)
VMEM = pl.BlockSpec(memory_space=pltpu.VMEM)

def column(row, lanes):
    tall = jnp.transpose(jnp.broadcast_to(row, (128, row.shape[1])))
    return jnp.concatenate([tall] * (lanes // 128), axis=1)

def noisy(mean_ref, sigma_ref, nin_ref, nout_ref, s):
    return mean_ref[s] + sigma_ref[s] * (column(nin_ref[0, s:s + 1, :], 512) * nout_ref[s:s + 1, :])

def mask_of(chosen, a):
    return jnp.where(chosen == a, 1.0 - 1.0 / ACTIONS, -1.0 / ACTIONS)

def hid_kernel(net, f_ref, m_ref, s_ref, nin_ref, nout_ref, hm_ref, hs_ref, wo_ref, bm_ref, bs_ref, eout_ref, c_ref, pl_ref, pw_ref, *rest):
    if net:
        f_all, h_ref, g_ref, logp_ref, dist_ref, t_ref = rest[:6]
        f1_refs, f2_refs = rest[6:9], rest[9:11]
        acc, adv, ts, tr, fs0, fr0, fs1, fr1 = rest[11:19]
        wires = [f_scatter(f_all, f1_refs[i], i, rest[19 + 4 * i:23 + 4 * i]) for i in range(3)]
        fans = [f_fan(f1_refs[0], f2_refs[0], fs0, fr0), f_fan(f1_refs[1], f2_refs[1], fs1, fr1)]
        p, g, z, y = coords()
        target = remote(dist_ref, t_ref, ts, tr, at(1 - p, g, z, y))
        def next_piece(i):
            wires[i].sent()
            wires[i + 1].start()
            for k in range(4):
                wires[i].arrived(k)
            for copy in fans[i]:
                copy.start()
    else:
        h_ref, g_ref, logp_ref, dist_ref, acc, adv = rest
    j = pl.program_id(0)
    @pl.when(j == 0)
    def _():
        if net:
            greet(line(p, g, z, y) + plane(p, g, z, y))
            wires[0].start()
        acc[...] = jnp.zeros_like(acc)
    if net:
        pl.when(j == 3)(lambda: next_piece(0))
        pl.when(j == 5)(lambda: next_piece(1))
    f = split(f_ref[...])
    for s in range(2):
        w = split(noisy(m_ref, s_ref, nin_ref, nout_ref, s))
        acc[:, 512 * s:512 * s + 512] += dot3(f, w, TN)
    @pl.when(j == pl.num_programs(0) - 1)
    def _():
        hb = hm_ref[...] + hs_ref[...] * nout_ref[...]
        h = jnp.concatenate([acc[:, 0:512] + hb[0:1], acc[:, 512:1024] + hb[1:2]], axis=1)
        h_ref[...] = h
        gt = jnp.transpose(silu(h))
        for s in range(2):
            for q in range(2):
                for gg in range(2):
                    for z in range(4):
                        at_row = 512 * s + 256 * q + 128 * gg + 32 * z
                        g_ref[q, z, gg, s] = gt[at_row:at_row + 32]
        both = dot3(split(wo_ref[...]), split(jnp.concatenate([gt[:512], gt[512:]], axis=1)))
        bias = column(jnp.concatenate([bm_ref[...] + bs_ref[...] * eout_ref[...], jnp.zeros((1, OUTP - OUTS), F32)], axis=1), 128)
        adv[...] = both[:, 128:] + bias
        z = both[0:PAD, 0:128] + bias[0:PAD]
        chosen = c_ref[...]
        for i in range(ACTIONS):
            z = z + mask_of(chosen, i) * adv[ATOMS * (i + 1):ATOMS * (i + 1) + PAD, :]
        row = lax.broadcasted_iota(jnp.int32, (PAD, 128), 0)
        z = jnp.where(row < ATOMS, z, -1e30)
        top = jnp.max(z, axis=0, keepdims=True)
        e = jnp.exp(z - top)
        tot = jnp.sum(e, axis=0, keepdims=True)
        logp_ref[...] = (z - top) - jnp.log(tot)
        prob = e / tot
        dist = jnp.zeros((PAD, 128), F32)
        for i in range(ATOMS):
            lower = pl_ref[i:i + 1, :]
            share = pw_ref[i:i + 1, :]
            pi = prob[i:i + 1, :]
            dist = dist + jnp.where(row == lower, pi * (1.0 - share), 0.0) + jnp.where(row == lower + 1, pi * share, 0.0)
        dist_ref[...] = dist
        if net:
            pl.when(p == 1)(target.start)
            for k in range(4):
                wires[2].arrived(k)
            wires[2].sent()
            for copy in fans[0] + fans[1]:
                copy.wait()
            pl.when(p == 1)(target.wait_send)
            pl.when(p == 0)(target.wait_recv)

def hidden(net, f, m, s, nin, nout, hm, hs, wo, bm, bs, eout, c, plow, pw):
    full = lambda *t: pl.BlockSpec(t, lambda j: (0,) * len(t))
    sds = lambda *t: jax.ShapeDtypeStruct(t, F32)
    k = 3136 // STEPS
    wspec = pl.BlockSpec((2, k, 512), lambda j: (0, j, 0))
    return pl.pallas_call(
        functools.partial(hid_kernel, net), grid=(STEPS,),
        in_specs=[pl.BlockSpec((k, 128), lambda j: (j, 0)), wspec, wspec, pl.BlockSpec((1, 2, k), lambda j: (j, 0, 0)), full(2, 512), full(2, 512), full(2, 512),
                  full(OUTP, 512), full(1, OUTS), full(1, OUTS), full(1, OUTS), full(1, 128), full(ATOMS, 128), full(ATOMS, 128)] + [ANY] * net,
        out_specs=[full(128, 1024), full(2, 4, 2, 2, 32, 128), full(PAD, 128), full(PAD, 128)] + [ANY] * (6 * net),
        out_shape=[sds(128, 1024), sds(2, 4, 2, 2, 32, 128), sds(PAD, 128), sds(PAD, 128)]
        + ([sds(PAD, 128)] + [sds(2, 4, n, 128) for _, n in PIECES] + [sds(3, 4, n, 128) for _, n in PIECES[:2]]) * net,
        scratch_shapes=[pltpu.VMEM((128, 1024), F32), pltpu.VMEM((OUTP, 128), F32)]
        + ([pltpu.SemaphoreType.DMA] * 2 + [pltpu.SemaphoreType.DMA((3,))] * 4 + sum([scatter_sems(2, n, 128) for _, n in PIECES], [])) * net,
        compiler_params=pltpu.CompilerParams(vmem_limit_bytes=60 * 2**20, **(dict(collective_id=1, has_side_effects=True) if net else {})),
    )(f, m, s, nin, nout, hm, hs, wo, bm, bs, eout, c, plow, pw, *([f] * net))

def hid_bwd_kernel(net, t_ref, logp_ref, h_ref, m_ref, s_ref, nin_ref, nout_ref, wo_ref, c_ref, *rest):
    if net:
        noise, rest = list(zip(rest[2:6], rest[16:20])), rest[:2] + rest[6:16] + rest[20:]
        f1b_ref, hid_ref, df_ref, small_ref, f2b_ref, g1_ref, d1_ref, dz1_ref, g2_ref, d2_ref, dz2_ref, d3_ref = rest[:12]
        dth, dtl, da, msg, dz_to = rest[12:17]
        ds, dr, gs, gr, qs, qr, fs, fr, hs, hr, ss, sr, ps, pr, own = rest[17:32]
        g_wire = g_scatter(hid_ref, g1_ref, rest[32:36])
        z_wire = z_scatter(dz_to, dz1_ref, rest[36:39])
        p, g, z, y = coords()
        d_line = Line(2, lambda i: d1_ref.at[z, i], lambda zz, i: d1_ref.at[zz, i], rest[39], rest[40])
        partner = at(1 - p, g, z, y)
        hands = [remote(dz2_ref, dz2_ref, hs.at[0], hr.at[0], partner), remote(dz1_ref, dz1_ref, hs.at[1], hr.at[1], partner)]
        tells = [remote(src, dst, rest[41].at[i], rest[42].at[i], partner) for i, (src, dst) in enumerate(noise)]
        own_tells = [pltpu.make_async_copy(src, dst, rest[43].at[i]) for i, (src, dst) in enumerate(noise)]
        give = remote(msg.at[1], d1_ref.at[z], ps, pr, partner)
        keep = pltpu.make_async_copy(msg.at[0], d1_ref.at[z], own)
        fan_f = f_fan(f1b_ref, f2b_ref, fs, fr)
        fan_g = spread_plane(p, g, z, y, lambda gd, yd: g1_ref.at[:, gd], lambda m: g2_ref.at[m], gs, gr)
        fan_z = spread_plane(p, g, z, y, lambda gd, yd: dz1_ref, lambda m: dz2_ref.at[m], qs, qr)
        def fan_d(place, zz):
            return spread_plane(p, g, z, y, lambda gd, yd: d1_ref.at[zz, yd], lambda m: d2_ref.at[m, zz], ds.at[place], dr.at[place])
        def swap_own(place, zz):
            return remote(d1_ref.at[zz, y], d3_ref.at[3, zz], ss.at[place, 0], sr.at[place, 0], partner)
        def swap(place, zz):
            return remote(d2_ref.at[:, zz], d3_ref.at[pl.ds(0, 3), zz], ss.at[place, 1], sr.at[place, 1], partner)
        def forward(place, zz, s):
            along_y, along_x, both = fan_d(place, zz)
            @pl.when(y == s)
            def _():
                along_x.start()
                swap_own(place, zz).start()
            @pl.when(y != s)
            def _():
                both.start()
                along_y.start()
        def forward_small():
            for k in range(4):
                g_wire.arrived(k)
            for copy in fan_g:
                copy.start()
            for k in range(4):
                z_wire.arrived(k)
            @pl.when(p == 0)
            def _():
                for copy in fan_z:
                    copy.start()
    else:
        df_ref, small_ref, msg, dz_to, dth, dtl, da = rest
    j = pl.program_id(0)
    def begin():
        t = t_ref[...]
        logp = logp_ref[...]
        chosen = c_ref[...]
        row = lax.broadcasted_iota(jnp.int32, (PAD, 128), 0)
        d = (jnp.exp(logp) * jnp.sum(t, axis=0, keepdims=True) - t) * (1.0 / 128)
        loss = -jnp.sum(jnp.where(row < ATOMS, t * logp, 0.0), axis=1, keepdims=True) * (1.0 / 128)
        dz_to[...] = jnp.where(row == ATOMS, chosen.astype(F32), d)
        da[...] = jnp.zeros_like(da)
        da[0:PAD, 0:128] = d
        for i in range(ACTIONS):
            da[ATOMS * (i + 1):ATOMS * (i + 1) + PAD, 128:256] = mask_of(chosen, i) * d
        every = da[...]
        eh, el = split(every)
        grads = dot3((eh, el), split(wo_ref[...]), TN)
        small_ref[...] = jnp.zeros_like(small_ref)
        for s in range(2):
            dp = grads[128 * s:128 * s + 128] * dsilu(h_ref[:, 512 * s:512 * s + 512])
            total = jnp.sum(dp, axis=0, keepdims=True)
            for c in range(4):
                msg[c // 2, s, 128 * (c % 2):128 * (c % 2) + 128, :] = dp[:, 128 * c:128 * c + 128]
                small_ref[4 * s + c:4 * s + c + 1, :] = total[:, 128 * c:128 * c + 128]
            hi, lo = split(jnp.transpose(dp))
            dth[s] = hi
            dtl[s] = lo
        if net:
            give.start()
            keep.start()
            z_wire.start()
            keep.wait()
        ones = jnp.ones((8, 256), BF)
        left = (every - eh.astype(F32)) - el.astype(F32)
        rows = dot(ones, eh, NT) + dot(ones, el, NT) + dot(ones, left.astype(BF), NT)
        for c in range(8):
            n = min(128, OUTP - 128 * c)
            small_ref[8 + c:9 + c, 0:n] = rows[0:1, 128 * c:128 * c + n]
        small_ref[16:17, :] = jnp.broadcast_to(jnp.sum(loss, axis=0, keepdims=True), (1, 128))
    def step():
        out = None
        for s in range(2):
            w = split(noisy(m_ref, s_ref, nin_ref, nout_ref, s))
            r = dot3(w, (dth[s], dtl[s]))
            out = r if out is None else out + r
        df_ref[...] = out
    if not net:
        pl.when(j == 0)(begin)
        step()
        return
    @pl.when(j == 0)
    def _():
        greet(line(p, g, z, y) + plane(p, g, z, y))
        for copy in fan_f:
            copy.start()
        g_wire.start()
        @pl.when(p == 0)
        def _():
            begin()
            for copy in tells + own_tells:
                copy.start()
        pl.when(p == 1)(give.wait_recv)
        d_line.start(0)
        for s in range(2):
            forward(0, z, s)
    pl.when(p == 0)(step)
    pl.when(j == 2)(forward_small)
    @pl.when(j == pl.num_programs(0) - 1)
    def _():
        for t in range(1, 4):
            d_line.arrive(t, forward)
        @pl.when(p == 0)
        def _():
            for copy in fan_z:
                copy.wait()
            for copy in hands:
                copy.start()
        def landed(place, zz):
            for copy in fan_d(place, zz):
                copy.wait_recv()
            swap(place, zz).start()
        d_line.each(landed)
        for copy in fan_f + fan_g:
            copy.wait()
        def gone(place, zz):
            for copy in fan_d(place, zz):
                copy.wait_send()
            swap(place, zz).wait()
            swap_own(place, zz).wait()
        d_line.each(gone)
        d_line.sent()
        @pl.when(p == 0)
        def _():
            give.wait_send()
            for copy in hands + tells:
                copy.wait_send()
            for copy in own_tells:
                copy.wait()
        @pl.when(p == 1)
        def _():
            for copy in hands + tells:
                copy.wait_recv()
        for wire in (g_wire, z_wire):
            wire.sent()

def hidden_bwd(net, t, logp, h, m, s, nin, nout, wo, c, *wired):
    full = lambda *u: pl.BlockSpec(u, lambda j: (0,) * len(u))
    sds = lambda *u: jax.ShapeDtypeStruct(u, F32)
    dma = pltpu.SemaphoreType.DMA
    k = 3136 // STEPS
    wspec = pl.BlockSpec((2, k, 512), lambda j: (0, j, 0))
    return pl.pallas_call(
        functools.partial(hid_bwd_kernel, net), grid=(STEPS,),
        in_specs=[full(PAD, 128), full(PAD, 128), full(128, 1024), wspec, wspec, pl.BlockSpec((1, 2, k), lambda j: (j, 0, 0)), full(2, 512),
                  full(OUTP, 512), full(1, 128)] + [ANY] * (6 * net),
        out_specs=[pl.BlockSpec((k, 128), lambda j: (j, 0)), full(24, 128)] + ([ANY] * 12 if net else [full(2, 2, 256, 128), full(PAD, 128)]),
        out_shape=[sds(3136, 128), sds(24, 128)] + ([sds(3, 4, PIECES[2][1], 128), sds(4, 2, 2, 32, 128), sds(4, 2, 256, 128), sds(4, PAD, 128), sds(3, 4, 2, 32, 128), sds(3, 4, 256, 128),
                                                     sds(3, 4, PAD, 128), sds(4, 4, 256, 128), sds(2, 3136), sds(2, 512), sds(2, 512), sds(1, OUTS)] if net else [sds(2, 2, 256, 128), sds(PAD, 128)]),
        scratch_shapes=[pltpu.VMEM((2, 512, 128), BF), pltpu.VMEM((2, 512, 128), BF), pltpu.VMEM((OUTP, 256), F32)]
        + ([pltpu.VMEM((2, 2, 256, 128), F32), pltpu.VMEM((PAD, 128), F32), dma((7, 3)), dma((7, 3))] + [dma((3,))] * 6 + [dma((2,)), dma((2,)), dma((7, 2)), dma((7, 2)), dma, dma, dma]
           + scatter_sems(1, 2, 2, 32, 128) + scatter_sems(1) + line_sems(2) + [dma((4,)), dma((4,)), dma((4,))]) * net,
        compiler_params=pltpu.CompilerParams(vmem_limit_bytes=60 * 2**20, **(dict(collective_id=2, has_side_effects=True) if net else {})),
    )(t, logp, h, m, s, nin, nout, wo, c, *wired)

def dsilu(v):
    s = jax.nn.sigmoid(v)
    return s * (1.0 + v * (1.0 - s))


ROWS = 768

def bwd_kernel(net, x_ref, pre1_hbm, pre2_ref, pre3_ref, df_ref, w1_ref, w2_ref, w3_ref, *rest):
    if net:
        r_ref, q_ref, s0_ref, tot_ref, sg_ref, ag_ref, ah_ref, bg_ref, bh_ref = rest[:9]
        xs, pre1_ref, xh, xl, d3f, d3h, d3l, d2h, d2l, d1h, d1l, h2h, h2l, acc2, a1, a2, a3, pay, lob, upb, x_sem, sem1, ls, us = rest[9:33]
        got, got1, red, tot, ur, zs_, zr, ys, yr, own, gs, gr, ws, wr, as_, ar, bs, br, es, er, cs, cr, one_ = rest[33:]
        p, g, z, y = coords()
        reps = lax.axis_size("rep")
        chips = 2 * reps
        me = g * reps + lax.axis_index("rep")
        size = ROWS // chips
        def chip(i):
            return (0, i // reps, i % reps)
        def part(i):
            return pl.ds(pl.multiple_of(i * size, 8), size)
        def give(k):
            to = (me + k) % chips
            if k:
                return remote(pay.at[part(to)], got.at[me], as_.at[k], ar.at[k], chip(to))
            return pltpu.make_async_copy(pay.at[part(me)], got.at[me], one_)
        def given(k):
            who = (me + chips - k) % chips
            return remote(pay.at[part(me)], got.at[who], as_.at[k], ar.at[k], chip(who))
        def show(k):
            return remote(pay.at[pl.ds(672, 64)], got1.at[me], es.at[k], er.at[k], chip((me + k) % chips))
        def shown(k):
            who = (me + chips - k) % chips
            return remote(pay.at[pl.ds(672, 64)], got1.at[who], es.at[k], er.at[k], chip(who))
        def tell(k):
            return remote(red, tot.at[part(me)], bs.at[k], br.at[k], chip((me + k) % chips))
        def told(k):
            who = (me + chips - k) % chips
            return remote(red, tot.at[part(who)], bs.at[k], br.at[k], chip(who))
        hand = remote(tot, tot, cs, cr, at(1 - p, g, z, y))
        def head_at(ref, yy, zz):
            return ref.at[zz, pl.ds(5 * yy, 5 - yy)]
        def head_of(yy):
            return q_ref.at[pl.ds(5 * yy, 5 - yy)]
        def slots(yy, zz):
            return ag_ref.at[yy, zz], head_at(ah_ref, yy, zz), bg_ref.at[yy, zz], head_at(bh_ref, yy, zz)
        def lines(yy):
            mine = (r_ref, head_of(yy)) + slots(yy, z)[2:]
            return Line(4, lambda i: mine[i], lambda zz, i: slots(yy, zz)[i], zs_, zr)
        def keep(yy):
            a, b, _, _ = slots(yy, z)
            return [pltpu.make_async_copy(r_ref, a, own.at[0]), pltpu.make_async_copy(head_of(yy), b, own.at[1])]
        def give_own(yy):
            _, _, a, b = slots(yy, z)
            return [remote(r_ref, a, gs.at[0], gr.at[0], at(1, g, z, y)), remote(head_of(yy), b, gs.at[1], gr.at[1], at(1, g, z, y))]
        def along_y(place, zz, yy):
            src = slots(yy, zz) if place else (r_ref, head_of(yy)) + slots(yy, z)[2:]
            return [remote(src[i], slots(yy, zz)[i], ys.at[place, i], yr.at[place, i], at(p, g, z, 1 - y)) for i in range(4)]
        def bring(place, zz, yy):
            a, b, c, d = slots(yy, zz)
            return [remote(c, a, ws.at[yy, place, 0], wr.at[yy, place, 0], at(0, g, z, y)), remote(d, b, ws.at[yy, place, 1], wr.at[yy, place, 1], at(0, g, z, y))]
        def each(do, flipped=False):
            for yy in range(2):
                pl.when(y == (1 - yy if flipped else yy))(functools.partial(do, yy))
        def states_out(j, slot):
            return (pltpu.make_async_copy(lob.at[slot], sg_ref.at[pl.ds(4 * j, 4)], ls.at[slot]),
                    remote(upb.at[slot], sg_ref.at[pl.ds(4 * j, 4)], us.at[slot], ur.at[j], at(1 - p, g, z, y)))
        def gather(yy):
            def then(place, zz, i):
                along_y(place, zz, yy)[i].start()
                if i >= 2:
                    bring(place, zz, yy)[i - 2].start()
            for copy in give_own(yy):
                copy.wait_recv()
            lines(yy).start(0)
            for i in range(4):
                then(0, z, i)
            for copy in keep(yy):
                copy.start()
            for t in range(1, 4):
                lines(yy).arrive(t, then)
        def second(yy):
            def landed(place, zz):
                for copy in along_y(place, zz, yy):
                    copy.wait_recv()
                for copy in bring(place, zz, yy):
                    copy.start()
            lines(yy).each(landed)
        def finished(yy):
            def gone(place, zz):
                for copy in along_y(place, zz, yy) + bring(place, zz, yy):
                    copy.wait_send()
            for copy in keep(yy):
                copy.wait()
            lines(yy).sent()
            lines(yy).each(gone)
        def second_sent(yy):
            def gone(place, zz):
                for copy in bring(place, zz, yy):
                    copy.wait_send()
            lines(yy).each(gone)
        def brought(yy):
            def came(place, zz):
                for copy in bring(place, zz, yy):
                    copy.wait_recv()
            lines(yy).each(came)
    else:
        tot_ref, lo_ref, up_ref, xs, pre1_ref, xh, xl, d3f, d3h, d3l, d2h, d2l, d1h, d1l, h2h, h2l, acc2, a1, a2, a3, pay, lob, upb, x_sem, sem1, ls, us = rest
        def states_out(j, slot):
            return (pltpu.make_async_copy(lob.at[slot], lo_ref.at[pl.ds(4 * j, 4)], ls.at[slot]),
                    pltpu.make_async_copy(upb.at[slot], up_ref.at[pl.ds(4 * j, 4)], us.at[slot]))
    small_ref = pay.at[pl.ds(24, 648)]
    last = 20
    def x_in(j):
        return pltpu.make_async_copy(x_ref.at[pl.ds(4 * j, 4)], xs.at[pl.ds(4 * j, 4)], x_sem.at[j])
    pre1_in = pltpu.make_async_copy(pre1_hbm, pre1_ref, sem1)
    def fetch():
        pre1_in.start()
        for j in range(21):
            x_in(j).start()
    def upper():
        for ref in (d3h, d3l, d2h, d2l, acc2, a2, a3):
            ref[...] = jnp.zeros_like(ref)
        small_ref[...] = jnp.zeros((648, 128), F32)
        for ref in (d1h, d1l):
            ref[0] = jnp.zeros((704, 128), BF)
            ref[21] = jnp.zeros((704, 128), BF)
            ref[:, 0:32, :] = jnp.zeros((22, 32, 128), BF)
            ref[:, 672:704, :] = jnp.zeros((22, 32, 128), BF)
        d3f[...] = df_ref[...] * dsilu(pre3_ref[...])
        total = jnp.zeros((64, 128), F32)
        for y in range(7):
            for x in range(7):
                d = d3f[pl.ds(y * 7 + x, 64, stride=49), :]
                total = total + d
                hi, lo = split(d)
                d3h[y + 2, 64 * (x + 2):64 * (x + 3), :] = hi
                d3l[y + 2, 64 * (x + 2):64 * (x + 3), :] = lo
        small_ref[640:641, 0:64] = jnp.sum(jnp.transpose(total), axis=0, keepdims=True)
        w3 = (w3_ref[0], w3_ref[1])
        h2h[:, 576:, :] = jnp.zeros((9, 64, 128), BF)
        h2l[:, 576:, :] = jnp.zeros((9, 64, 128), BF)
        def split2(y, c):
            hi, lo = split(silu(pre2_ref[y]))
            h2h[y, 0:576, :] = hi
            h2l[y, 0:576, :] = lo
            return c
        lax.fori_loop(0, 9, split2, 0)
        def dgrad3(y, c):
            rh = jnp.concatenate([d3h[y + 2, 128 * i:128 * i + 256, :] for i in range(5)], axis=1)
            rl = jnp.concatenate([d3l[y + 2, 128 * i:128 * i + 256, :] for i in range(5)], axis=1)
            r = dot3(w3, (rh, rl))
            for ky in range(3):
                for i in range(5):
                    acc2[y + ky, 128 * i:128 * i + 128, :] += r[128 * ky:128 * ky + 128, 128 * i:128 * i + 128]
            return c
        lax.fori_loop(0, 7, dgrad3, 0)
        def wgrad3(y, c):
            def lhs(ref):
                return jnp.concatenate([jnp.concatenate([ref[y - ky + 2, 128 * (i + 1):128 * (i + 2), :] for i in range(4)], axis=1) for ky in range(3)], axis=0)
            def rhs(ref):
                return jnp.concatenate([ref[y, 128 * i:128 * i + 256, :] for i in range(4)], axis=1)
            a3[...] += dot3((lhs(d3h), lhs(d3l)), (rhs(h2h), rhs(h2l)), NT)
            return c
        lax.fori_loop(0, 9, wgrad3, 0)
        for ky in range(3):
            grad = a3[128 * ky:128 * ky + 64, 0:192] + a3[128 * ky + 64:128 * ky + 128, 64:256]
            small_ref[256 + 64 * ky:320 + 64 * ky, :] = grad[:, 0:128]
            small_ref[448 + 64 * ky:512 + 64 * ky, 0:64] = grad[:, 128:192]
        def step2(y, total):
            for x in range(9):
                d = acc2[y, 64 * x:64 * x + 64, :] * dsilu(pre2_ref[y, 64 * x:64 * x + 64, :])
                total = total + d
                hi, lo = split(d)
                d2h[y + 1, 64 * (x + 1):64 * (x + 2), :] = hi
                d2l[y + 1, 64 * (x + 1):64 * (x + 2), :] = lo
            return total
        total = lax.fori_loop(0, 9, step2, jnp.zeros((64, 128), F32))
        small_ref[641:642, 0:64] = jnp.sum(jnp.transpose(total), axis=0, keepdims=True)
    def block2(y, total):
        w2 = (w2_ref[0], w2_ref[1])
        rh = jnp.concatenate([d2h[pl.ds(y, 2), 64 * i:64 * i + 128, :].reshape(256, 128) for i in range(10)], axis=1)
        rl = jnp.concatenate([d2l[pl.ds(y, 2), 64 * i:64 * i + 128, :].reshape(256, 128) for i in range(10)], axis=1)
        r = dot3(w2, (rh, rl))
        h1h, h1l = [], []
        for py in range(2):
            rowh, rowl = [], []
            for i in range(10):
                v = pre1_ref[2 * y + py, 64 * i:64 * i + 64, :]
                s = jax.nn.sigmoid(v)
                d = r[64 * py:64 * py + 64, 128 * i:128 * i + 128] * (s * (1.0 + v * (1.0 - s)))
                total = total + d[0:32] + d[32:64]
                hi, lo = split(d)
                d1h[2 * y + py + 1, 64 * i + 32:64 * i + 96, :] = hi
                d1l[2 * y + py + 1, 64 * i + 32:64 * i + 96, :] = lo
                hi, lo = split(v * s)
                rowh.append(hi)
                rowl.append(lo)
            h1h.append(rowh)
            h1l.append(rowl)
        def lhs(ref):
            return jnp.concatenate([jnp.concatenate([ref[y + 1 - h, 64 * (i + 1):64 * (i + 2), :] for i in range(9)], axis=1) for h in range(2)], axis=0)
        def rhs(rows):
            return jnp.concatenate([jnp.concatenate([rows[0][i], rows[0][i + 1], rows[1][i], rows[1][i + 1]], axis=0) for i in range(9)], axis=1)
        a2[...] += dot3((lhs(d2h), lhs(d2l)), (rhs(h1h), rhs(h1l)), NT)
        return total
    def lower():
        pre1_in.wait()
        total = lax.fori_loop(0, 10, block2, jnp.zeros((32, 128), F32))
        small_ref[642:643, 0:32] = jnp.sum(jnp.transpose(total), axis=0, keepdims=True)
        small_ref[0:128, :] = a2[:, 0:128]
        small_ref[128:256, :] = a2[:, 128:256]
    def states_gone(j, slot):
        a, b = states_out(j, slot)
        a.wait()
        if net:
            b.wait_send()
        else:
            b.wait()
    def wgrad1(j, carry):
        x_in(j).wait()
        v = xs[pl.ds(4 * j, 4)]
        hi = v.astype(BF)
        xh[:, 0:336, :] = hi
        xl[:, 0:336, :] = (v - hi.astype(F32)).astype(BF)
        def lhs(ref):
            return jnp.concatenate([jnp.concatenate([ref[j + 1 - h, 96 * i + 32:96 * i + 128, :] for i in range(7)], axis=1) for h in range(2)], axis=0)
        def rhs(ref):
            return jnp.concatenate([ref[:, 48 * i:48 * i + 64, :].reshape(256, 128) for i in range(7)], axis=1)
        a1[...] += dot3((lhs(d1h), lhs(d1l)), (rhs(xh), rhs(xl)), NT)
        return carry
    def first_grad():
        lax.fori_loop(0, 21, wgrad1, 0)
        for h in range(2):
            for ky in range(4):
                grad = a1[96 * h:96 * h + 32, 64 * ky:64 * ky + 32]
                grad = grad + a1[96 * h + 32:96 * h + 64, 64 * ky + 16:64 * ky + 48]
                grad = grad + a1[96 * h + 64:96 * h + 96, 64 * ky + 32:64 * ky + 64]
                pay[672 + 32 * h:704 + 32 * h, 32 * ky:32 * ky + 32] = grad
    def dgrad1(j, carry):
        def both(ref):
            return jnp.concatenate([ref[pl.ds(j, 2), 96 * i:96 * i + 128, :].reshape(256, 128) for i in range(7)], axis=1)
        r = dot3((w1_ref[0], w1_ref[1]), (both(d1h), both(d1l)))
        slot = j % 2
        pl.when(j >= 2)(lambda: states_gone(j - 2, slot))
        lo_to, up_to = lob.at[slot], upb.at[slot]
        for ky in range(4):
            for i in range(7):
                lo_to[ky, 24 * i:24 * i + 24, :] = r[24 * ky:24 * ky + 24, 128 * i:128 * i + 128]
                up_to[ky, 24 * i:24 * i + 24, :] = r[96 + 24 * ky:96 + 24 * ky + 24, 128 * i:128 * i + 128]
        for copy in states_out(j, slot):
            copy.start()
        return carry
    if net:
        pl.when(p == 0)(fetch)
        pl.when(p == 0)(lambda: greet([chip((me + k) % chips) for k in range(1, chips)] + [at(1, g, z, y)]))
        pl.when(p == 1)(lambda: greet([at(1, g, flip(z, k), y) for k in range(1, 4)] + [at(1, g, z, 1 - y), at(0, g, z, y)]))
        def begin(yy):
            for copy in give_own(yy):
                copy.start()
        pl.when(p == 0)(lambda: each(begin))
        @pl.when(p == 1)
        def _():
            each(gather)
            each(second, flipped=True)
        pay[0:24, :] = s0_ref[...]
    else:
        pay[0:24, :] = jnp.zeros((24, 128), F32)
    pay[672:, :] = jnp.zeros((ROWS - 672, 128), F32)
    xh[:, 336:, :] = jnp.zeros((4, 16, 128), BF)
    xl[:, 336:, :] = jnp.zeros((4, 16, 128), BF)
    a1[...] = jnp.zeros_like(a1)
    if net:
        @pl.when(p == 0)
        def _():
            upper()
            lower()
            first_grad()
            for k in range(chips):
                give(k).start()
            for k in range(1, chips):
                show(k).start()
            got1[me] = pay[672:736, :]
            lax.fori_loop(0, 12, dgrad1, 0)
            give(0).wait()
            for k in range(1, chips):
                given(k).wait_recv()
            red[...] = jnp.sum(got[...], axis=0)
            tot[part(me), :] = red[...]
            for k in range(1, chips):
                tell(k).start()
            lax.fori_loop(12, 21, dgrad1, 0)
            for k in range(1, chips):
                told(k).wait_recv()
            for k in range(1, chips):
                shown(k).wait_recv()
            tot[672:736, :] = jnp.sum(got1[...], axis=0)
            hand.start()
            for k in range(1, chips):
                give(k).wait_send()
                tell(k).wait_send()
                show(k).wait_send()
            hand.wait_send()
            for j in (last - 1, last):
                states_gone(j, j % 2)
    else:
        fetch()
        upper()
        lower()
        first_grad()
        lax.fori_loop(0, 21, dgrad1, 0)
        for j in (last - 1, last):
            states_gone(j, j % 2)
    if net:
        @pl.when(p == 1)
        def _():
            hand.wait_recv()
            def arrive(i, c):
                states_out(i, 0)[1].wait_recv()
                return c
            lax.fori_loop(0, last + 1, arrive, 0)
        tot_ref[...] = tot[...]
        @pl.when(p == 0)
        def _():
            def given_own(yy):
                for copy in give_own(yy):
                    copy.wait_send()
            each(given_own)
            brought(0)
            brought(1)
        @pl.when(p == 1)
        def _():
            each(finished)
            each(second_sent, flipped=True)
    else:
        tot_ref[...] = pay[...]

def backward(net, x, pre1, pre2, pre3, df, w1, w2, w3, *wired):
    sds = lambda *s: jax.ShapeDtypeStruct(s, F32)
    vmb = lambda *s: pltpu.VMEM(s, BF)
    f32 = lambda *s: pltpu.VMEM(s, F32)
    dma = pltpu.SemaphoreType.DMA
    return pl.pallas_call(
        functools.partial(bwd_kernel, net),
        in_specs=[ANY, ANY] + [VMEM] * 6 + [VMEM] * 3 * net,
        out_specs=[VMEM] + [ANY] * (5 if net else 2),
        out_shape=[sds(ROWS, 128)] + ([sds(84, 168, 128)] + [sds(2, 4, 200, 512), sds(4, 9, 32, 128)] * 2 if net else [sds(84, 168, 128), sds(84, 168, 128)]),
        scratch_shapes=[f32(84, 336, 128), f32(20, 640, 128), vmb(4, 352, 128), vmb(4, 352, 128), f32(3136, 128), vmb(11, 768, 128), vmb(11, 768, 128), vmb(11, 704, 128),
                        vmb(11, 704, 128), vmb(22, 704, 128), vmb(22, 704, 128), vmb(9, 640, 128), vmb(9, 640, 128), f32(9, 640, 128), f32(192, 256), f32(128, 256),
                        f32(384, 256), f32(ROWS, 128), f32(2, 4, 168, 128), f32(2, 4, 168, 128), dma((21,)), dma, dma((2,)), dma((2,))]
        + ([f32(16, ROWS // 16, 128), f32(16, 64, 128), f32(ROWS // 16, 128), f32(ROWS, 128), dma((21,))]
           + line_sems(4) + [dma((7, 4))] * 2 + [dma((2,))] * 3 + [dma((2, 7, 2))] * 2 + [dma((16,))] * 6 + [dma] * 3) * net,
        compiler_params=pltpu.CompilerParams(vmem_limit_bytes=62 * 2**20, **(dict(collective_id=3, has_side_effects=True) if net else {})),
    )(x, pre1, pre2, pre3, df, w1, w2, w3, *wired)

def wide_kernel(f1a, f1b, f1c, f2a, f2b, f2c, d1, d2, d3, g1, g2, z1, z2, r_ref, q_ref, fv, dv, ev, gv, zv, acc, acq, da, sem):
    p, g = lax.axis_index("pair"), lax.axis_index("group")
    y = lax.axis_index("rep") % 2
    three, last = pl.ds(0, 3), 3
    rows = [pl.ds(*piece) for piece in PIECES]
    pairs = [(ref, fv.at[three, :, rows[i]]) for i, ref in enumerate((f2a, f2b, f2c))] + [(ref.at[g], fv.at[last, :, rows[i]]) for i, ref in enumerate((f1a, f1b, f1c))]
    pairs += [(g2, gv.at[three]), (g1.at[:, g], gv.at[last]), (z2, zv.at[three]), (z1, zv.at[last])]
    first = len(pairs)
    for m in range(4):
        pairs += [(d2.at[m] if m < 3 else d1.at[:, y], dv.at[m]), (d3.at[m], ev.at[m])]
    copies = [pltpu.make_async_copy(a, b, sem.at[i]) for i, (a, b) in enumerate(pairs)]
    for copy in copies:
        copy.start()
    acc[...] = jnp.zeros_like(acc)
    acq[...] = jnp.zeros_like(acq)
    da[...] = jnp.zeros_like(da)
    for copy in copies[:first]:
        copy.wait()
    def block(ref, m):
        return jnp.concatenate([jnp.concatenate([ref[m, i, 128 * c:128 * c + 128, :] for c in range(2)], axis=1) for i in range(4)], axis=0)
    def step(m):
        for copy in copies[first + 2 * m:first + 2 * m + 2]:
            copy.wait()
        f = split(jnp.concatenate([fv[m, i] for i in range(4)], axis=1))
        acc[0] += dot3(f, split(block(dv, m)))
        acc[1] += dot3(f, split(block(ev, m)))
        dz = jnp.concatenate([zv[m, i] for i in range(4)], axis=1)
        row = lax.broadcasted_iota(jnp.int32, (PAD, 512), 0)
        chosen = dz[ATOMS:ATOMS + 1].astype(jnp.int32)
        d = jnp.where(row < ATOMS, dz, 0.0)
        da[0:PAD, :] = d
        for i in range(ACTIONS):
            da[128 + ATOMS * i:128 + ATOMS * i + PAD, :] = mask_of(chosen, i) * d
        def units(s):
            return split(jnp.concatenate([gv[m, i, s] for i in range(4)], axis=1))
        @pl.when(y == 0)
        def _():
            acq[:, 0:128] += dot3(units(0), split(da[0:128, :]), NT)
            acq[:, 128:640] += dot3(units(1), split(da[128:640, :]), NT)
        @pl.when(y == 1)
        def _():
            acq[:, 640:1152] += dot3(units(1), split(da[640:1152, :]), NT)
    for m in range(4):
        step(m)
    r_ref[:, 0:256] = jnp.where(p == 0, acc[0], acc[1])
    r_ref[:, 256:512] = jnp.where(p == 0, acc[1], acc[0])
    for c in range(9):
        q_ref[c] = acq[:, 128 * c:128 * c + 128]

def wide_grads(*messages):
    sds = lambda *s: jax.ShapeDtypeStruct(s, F32)
    f32 = lambda *s: pltpu.VMEM(s, F32)
    return pl.pallas_call(
        wide_kernel, in_specs=[ANY] * 13, out_specs=[VMEM] * 2,
        out_shape=[sds(200, 512), sds(9, 32, 128)],
        scratch_shapes=[f32(4, 4, 200, 128), f32(4, 4, 256, 128), f32(4, 4, 256, 128), f32(4, 4, 2, 32, 128), f32(4, 4, PAD, 128),
                        f32(2, 200, 256), f32(32, 1152), f32(1152, 512), pltpu.SemaphoreType.DMA((18,))],
        compiler_params=pltpu.CompilerParams(vmem_limit_bytes=60 * 2**20),
    )(*messages)

def torso_out(tot, k1_ref, k2_ref, k3_ref, b1_ref, b2_ref, b3_ref, t1, t2):
    t1[:, 0:64] = jnp.transpose(tot[672:736, :])
    t1[:, 64:128] = jnp.zeros((128, 64), F32)
    for ky in range(4):
        for c in range(4):
            v = t1[pl.ds(32 * ky + c, 8, stride=4), :]
            for h in range(2):
                k1_ref[c, 4 * h + ky] = v[:, 32 * h:32 * h + 32]
    for py in range(2):
        t2[...] = jnp.transpose(tot[24 + 128 * py:152 + 128 * py, :])
        for h in range(2):
            for kx in range(4):
                k2_ref[:, 2 * h + py, kx, :] = t2[32 * kx:32 * kx + 32, 64 * h:64 * h + 64]
    for ky in range(3):
        for kx in range(3):
            base = (280 if kx < 2 else 472) + 64 * ky
            k3_ref[ky, kx] = tot[base:base + 64, 64 * (kx % 2):64 * (kx % 2) + 64]
    b3_ref[...] = tot[664:665, 0:64]
    b2_ref[...] = tot[665:666, 0:64]
    b1_ref[...] = tot[666:667, 0:32]

def finish_kernel(sg_ref, ag_ref, ah_ref, tot_ref, in_ref, out_ref, ein_ref, eout_ref, mean_ref, sigma_ref, hm_ref, hs_ref, k1_ref, k2_ref, k3_ref, b1_ref, b2_ref, b3_ref,
                  hb_ref, hbs_ref, bo_ref, bos_ref, loss_ref, states_ref, t1, t2, sv, sem):
    parts = [pl.ds(21 * i, 21) for i in range(4)]
    reads = [pltpu.make_async_copy(sg_ref.at[part], sv.at[part], sem.at[0, i]) for i, part in enumerate(parts)]
    moves = [pltpu.make_async_copy(sv.at[part], states_ref.at[part], sem.at[1, i]) for i, part in enumerate(parts)]
    for copy in reads:
        copy.start()
    for i in range(4):
        reads[i].wait()
        moves[i].start()
    for s in range(2):
        tall = column(in_ref[s:s + 1, :], 512) * out_ref[s:s + 1, :]
        for z, (start, n) in enumerate(((0, 200), (200, 200), (400, 184), (584, 200))):
            v = ag_ref[s, z, 0:n, :]
            mean_ref[s, start:start + n, :] = v
            sigma_ref[s, start:start + n, :] = v * tall[start:start + n]
    noise = column(eout_ref[...], 128)
    for c in range(9):
        start = 0 if c == 0 else ATOMS + 128 * (c - 1)
        n = min(128, (ATOMS if c == 0 else OUTS) - start)
        v = jnp.transpose(jnp.concatenate([ah_ref[z, c] for z in range(4)], axis=0))[0:n]
        hm_ref[start:start + n, :] = v
        hs_ref[start:start + n, :] = v * (noise[start:start + n] * ein_ref[min(c, 1):min(c, 1) + 1, :])
    torso_out(tot_ref, k1_ref, k2_ref, k3_ref, b1_ref, b2_ref, b3_ref, t1, t2)
    for s in range(2):
        for c in range(4):
            v = tot_ref[4 * s + c:4 * s + c + 1, :]
            hb_ref[s:s + 1, 128 * c:128 * c + 128] = v
            hbs_ref[s:s + 1, 128 * c:128 * c + 128] = v * out_ref[s:s + 1, 128 * c:128 * c + 128]
    for c in range(8):
        n = min(128, OUTS - 128 * c)
        v = tot_ref[8 + c:9 + c, 0:n]
        bo_ref[:, 128 * c:128 * c + n] = v
        bos_ref[:, 128 * c:128 * c + n] = v * eout_ref[:, 128 * c:128 * c + n]
    loss_ref[...] = tot_ref[16:17, :]
    for copy in moves:
        copy.wait()

def finish(sg, ag, ah, tot, n_in, n_out, e_in, e_out):
    sds = lambda *s: jax.ShapeDtypeStruct(s, F32)
    return pl.pallas_call(
        finish_kernel, in_specs=[ANY] + [VMEM] * 7, out_specs=[VMEM] * 15 + [ANY],
        out_shape=[sds(2, 784, 512), sds(2, 784, 512), sds(OUTS, 128), sds(OUTS, 128), sds(4, 8, 8, 32), sds(32, 4, 4, 64), sds(3, 3, 64, 64), sds(1, 32), sds(1, 64), sds(1, 64),
                   sds(2, 512), sds(2, 512), sds(1, OUTS), sds(1, OUTS), sds(1, 128), sds(84, 168, 128)],
        scratch_shapes=[pltpu.VMEM((128, 128), F32), pltpu.VMEM((128, 128), F32), pltpu.VMEM((84, 168, 128), F32), pltpu.SemaphoreType.DMA((2, 4))],
        compiler_params=pltpu.CompilerParams(vmem_limit_bytes=60 * 2**20),
    )(sg, ag, ah, tot, n_in, n_out, e_in, e_out)

def small_finish_kernel(tot_ref, k1_ref, k2_ref, k3_ref, b1_ref, b2_ref, b3_ref, t1, t2):
    torso_out(tot_ref, k1_ref, k2_ref, k3_ref, b1_ref, b2_ref, b3_ref, t1, t2)

def small_finish(tot):
    sds = lambda *s: jax.ShapeDtypeStruct(s, F32)
    return pl.pallas_call(
        small_finish_kernel, in_specs=[VMEM], out_specs=[VMEM] * 6,
        out_shape=[sds(4, 8, 8, 32), sds(32, 4, 4, 64), sds(3, 3, 64, 64), sds(1, 32), sds(1, 64), sds(1, 64)],
        scratch_shapes=[pltpu.VMEM((128, 128), F32), pltpu.VMEM((128, 128), F32)],
    )(tot)

def exchange(parts):
    groups = lax.axis_size("group")
    p, g = lax.axis_index("pair"), lax.axis_index("group")
    got = []
    for k in range(groups):
        to = (g + k) % groups
        mine = parts(0, to)
        if k:
            mine = lax.ppermute(mine, ("pair", "group"), [(i, (i + k) % groups) for i in range(groups)])
        theirs = lax.ppermute(parts(1, to), ("pair", "group"), [(i, groups + (i + k) % groups) for i in range(groups)])
        got.append(jnp.where(p == 0, mine, theirs))
    return got

HIGH = lax.Precision.HIGH

def local(states, actions, proj_lower, proj_upper, proj_weight, first_kernel, first_bias, second_kernel, second_bias,
          third_kernel, third_bias, hidden_mean, hidden_sigma, hidden_bias_mean, hidden_bias_sigma, head_mean, head_sigma,
          head_bias_mean, head_bias_sigma, hidden_noise_in, hidden_noise_out, head_noise_in, head_noise_out):
    pair = lax.axis_index("pair")
    groups = lax.axis_size("group")
    shards = 2 * groups
    net = int(groups == 2 and lax.axis_size("rep") == 8)
    n_in, n_out, e_in, e_out = hidden_noise_in[0], hidden_noise_out[0], head_noise_in[0], head_noise_out[0]
    own_noise = (n_in, n_out, e_in, e_out[None])
    feat_q, hid_q = 3136 // shards, 512 // shards
    shard = pair * groups + lax.axis_index("group")
    def of_shard(noise):
        on_in, on_out, on_ein, on_eout = noise
        return (lax.dynamic_slice_in_dim(on_in, shard * feat_q, feat_q, axis=1), on_out, lax.dynamic_slice_in_dim(on_ein, shard * hid_q, hid_q, axis=1), on_eout)

    x = jnp.transpose(states[0], (2, 3, 1, 0)).reshape(84, 336, 128)
    fw1, fw2, fw3, bw1, bw2, bw3, c1, c2, c3 = prepare(first_kernel[0], second_kernel[0], third_kernel[0], first_bias, second_bias, third_bias)
    e_out = e_out[None]
    e_rows = jnp.where(jnp.arange(OUTS)[:, None] < ATOMS, e_in[0:1], e_in[1:2])
    wo = jnp.pad(head_mean[0].T + head_sigma[0].T * (e_rows * e_out.T), ((0, OUTP - OUTS), (0, 0)))
    nin = jnp.transpose(n_in.reshape(2, STEPS, 3136 // STEPS), (1, 0, 2))
    pre1, pre2, pre3, feats = forward(x, fw1, fw2, fw3, c1, c2, c3)
    h, hid, logp, dist, *f12 = hidden(net, feats, hidden_mean[0], hidden_sigma[0], nin, n_out, hidden_bias_mean[0], hidden_bias_sigma[0], wo, head_bias_mean, head_bias_sigma, e_out, actions, proj_lower.T, proj_weight.T)
    back = (logp, h, hidden_mean[0], hidden_sigma[0], nin, n_out, wo, actions)
    if net:
        target, *f12 = f12
        f1, f2 = f12[:3], f12[3:]
        df, small_b, f2c, g1, d1, z1, g2, d2, z2, d3, *noise = hidden_bwd(net, target, *back, f1[2], hid, *own_noise)
        part_r, part_q = wide_grads(*f1, *f2, f2c, d1, d2, d3, g1, g2, z1, z2)
        total, grad_rows, ag, ah, _, _ = backward(net, x, pre1, pre2, pre3, df, bw1, bw2, bw3, part_r, part_q, small_b)
        (hidden_grad, hidden_sigma_grad, head_t, head_sigma_t, gk1, gk2, gk3, gb1, gb2, gb3, hb_grad, hbs_grad, bo_grad, bos_grad,
         loss, grad_rows) = finish(grad_rows, ag, ah, total, *of_shard(noise))
    else:
        df, small_b, msg, dz = hidden_bwd(net, lax.ppermute(dist, "pair", [(1, 0)]), *back)
        f_got = exchange(lambda p, g: lax.dynamic_slice_in_dim(feats, (p * groups + g) * feat_q, feat_q, axis=0))
        hid = jnp.transpose(hid, (3, 0, 2, 1, 4, 5)).reshape(1024, 128).T
        hid_got = exchange(lambda p, g: lax.dynamic_slice_in_dim(hid.reshape(128, 2, 512), (p * groups + g) * hid_q, hid_q, axis=2))
        dpre = jnp.transpose(msg.reshape(2, 2, 2, 128, 128), (3, 1, 0, 2, 4)).reshape(128, 1024)
        d_all = jnp.concatenate(exchange(lambda p, g: jnp.concatenate([dpre, dz.T, jnp.zeros((128, 72), F32)], axis=1)), axis=0)
        f_all = jnp.concatenate(f_got, axis=1)
        hid_all = jnp.concatenate(hid_got, axis=0)
        part_hidden = jnp.einsum("fb,bsh->sfh", f_all, d_all[:, :1024].reshape(-1, 2, 512), precision=HIGH)
        dz_all = d_all[:, 1024:1024 + ATOMS]
        picked = d_all[:, 1024 + ATOMS]
        mask = jnp.where(picked[None, :] == jnp.arange(ACTIONS, dtype=F32)[:, None], 1.0 - 1.0 / ACTIONS, -1.0 / ACTIONS)
        da = (mask[:, None, :] * dz_all.T[None]).reshape(ACTIONS * ATOMS, -1)
        part_head = jnp.concatenate([jnp.dot(dz_all.T, hid_all[:, 0], precision=HIGH), jnp.dot(da, hid_all[:, 1], precision=HIGH)], axis=0)
        hidden_grad, head_t = lax.psum((part_hidden, part_head), "rep")
        small_d, lo, up = backward(net, x, pre1, pre2, pre3, df, bw1, bw2, bw3)
        grad_rows = jnp.where(pair == 0, lo, lax.ppermute(up, "pair", [(0, 1)]))
        total = lax.psum(small_d + jnp.pad(small_b, ((0, ROWS - 24), (0, 0))), ("pair", "group", "rep"))
        in_q, on_out, e_q, on_eout = of_shard([jnp.where(pair == 0, mine, lax.ppermute(mine, "pair", [(0, 1)])) for mine in own_noise])
        hidden_sigma_grad = hidden_grad * (in_q[:, :, None] * on_out[:, None, :])
        head_sigma_t = head_t * (jnp.where(jnp.arange(OUTS)[:, None] < ATOMS, e_q[0:1], e_q[1:2]) * on_eout.T)
        gk1, gk2, gk3, gb1, gb2, gb3 = small_finish(total)
        hb_grad = total[0:8].reshape(2, 512)
        bo_grad = total[8:16].reshape(1, -1)[:, :OUTS]
        hbs_grad, bos_grad = hb_grad * on_out, bo_grad * on_eout
        loss = total[16:17]
    states_grad = jnp.transpose(grad_rows.reshape(84, 84, 2, 128), (3, 2, 0, 1))
    return (loss[0, 0], states_grad, jnp.transpose(gk1, (3, 0, 1, 2)), gb1[0], jnp.transpose(gk2, (3, 0, 1, 2)), gb2[0], jnp.transpose(gk3, (2, 3, 0, 1)), gb3[0],
            hidden_grad, hidden_sigma_grad, hb_grad, hbs_grad, head_t.T, head_sigma_t.T, bo_grad[0], bos_grad[0])


def solution(mesh):
    placed = (
        P("pair", ("group", "rep"), None, None, None),
        P("pair", ("group", "rep")),
        P(("group", "rep"), None),
        P(("group", "rep"), None),
        P(("group", "rep"), None),
        P("pair", None, None, None, None),
        P("pair", None),
        P("pair", None, None, None, None),
        P("pair", None),
        P("pair", None, None, None, None),
        P("pair", None),
        P("pair", None, None, None),
        P("pair", None, None, None),
        P("pair", None, None),
        P("pair", None, None),
        P("pair", None, None),
        P("pair", None, None),
        P("pair", None),
        P("pair", None),
        P("pair", None, None),
        P("pair", None, None),
        P("pair", None, None),
        P("pair", None),
    )
    return jax.shard_map(
        local,
        mesh=mesh,
        in_specs=placed,
        out_specs=(
            P(),
            P(("group", "rep"), "pair", None, None),
            P(),
            P(),
            P(),
            P(),
            P(),
            P(),
            P(None, ("pair", "group"), None),
            P(None, ("pair", "group"), None),
            P(),
            P(),
            P(("pair", "group"), None),
            P(("pair", "group"), None),
            P(),
            P(),
        ),
        check_vma=False,
    )
```

```python
import functools
import jax
import jax.numpy as jnp
from jax import lax
from jax.experimental import pallas as pl
from jax.experimental.pallas import tpu as pltpu
from jax.sharding import PartitionSpec as P

BF = jnp.bfloat16
F32 = jnp.float32
NN=(((1,),(0,)),((),()))
NT=(((1,),(1,)),((),()))
TN=(((0,),(0,)),((),()))

def split(v):
    hi = v.astype(BF)
    return hi, (v - hi.astype(F32)).astype(BF)

def dot(a, b, dims=NN):
    return lax.dot_general(a, b, dims, preferred_element_type=F32)

def dot3(a, b, dims=NN):
    ah, al = a; bh, bl = b
    return dot(ah, bh, dims) + (dot(ah, bl, dims) + dot(al, bh, dims))

def silu(v):
    return v * jax.nn.sigmoid(v)

def prep_kernel(k1_ref, k2_ref, k3_ref, b1_ref, b2_ref, b3_ref, f1_ref, f2_ref, f3_ref, r1_ref, r2_ref, r3_ref, c1_ref, c2_ref, c3_ref,
                t1a, t1b, u1a, u1b, m2, m3, n2, n3):
    for ref in (t1a, t1b, u1a, u1b, m2, m3, n2, n3):
        ref[...] = jnp.zeros_like(ref)
    def put(ref, start, stride, v, lane):
        n = v.shape[0]
        pieces = [jnp.zeros((n, lane), F32)] * (lane > 0) + [v] + [jnp.zeros((n, 96 - lane), F32)] * (lane < 96)
        rows = pl.ds(start, n, stride=stride)
        ref[rows, :] = ref[rows, :] + jnp.concatenate(pieces, axis=1)
    for c in range(4):
        for ky in range(8):
            v = k1_ref[c, ky]
            h, kq = ky // 4, ky % 4
            for w in range(3):
                put((t1a, t1b)[h], kq * 64 + 16 * w + c, 4, v, 32 * w)
            base = (c // 2) * 96 + kq * 24 + c % 2
            for q in range(4):
                if q == 0:
                    put((u1b, u1a)[h], base, 2, v[4:8], 0)
                elif q == 3:
                    put((u1b, u1a)[h], base + 16, 2, v[0:4], 96)
                else:
                    put((u1b, u1a)[h], base + 8 * (q - 1), 2, v, 32 * q)
    for ky in range(4):
        for kx in range(4):
            v = k2_ref[:, ky, kx, :]
            h, py, wx, px = ky // 2, ky % 2, 1 - kx // 2, kx % 2
            m2[py * 128 + kx * 32:py * 128 + kx * 32 + 32, 64 * h:64 * h + 64] = v
            n2[(py * 2 + px) * 32:(py * 2 + px) * 32 + 32, 128 * (1 - h) + 64 * wx:128 * (1 - h) + 64 * wx + 64] = v
    for ky in range(3):
        for kx in range(3):
            v = k3_ref[ky, kx]
            vt = jnp.transpose(v)
            for w in range(2):
                m3[ky * 128 + w * 64:ky * 128 + w * 64 + 64, 64 * (w + kx):64 * (w + kx) + 64] = v
                q = w + 2 - kx
                n3[ky * 128 + w * 64:ky * 128 + w * 64 + 64, 64 * q:64 * q + 64] = vt
    w1 = jnp.concatenate([jnp.transpose(t1a[...])[0:96], jnp.transpose(t1b[...])[0:96]], axis=0)
    pairs = ((f1_ref, w1), (f2_ref, jnp.transpose(m2[...])), (f3_ref, m3[...]), (r1_ref, jnp.concatenate([u1a[...], u1b[...]], axis=1)), (r2_ref, n2[...]), (r3_ref, n3[...]))
    for ref, v in pairs:
        hi, lo = split(v)
        ref[0] = hi
        ref[1] = lo
    for ref, b_ref, n, times in ((c1_ref, b1_ref, 32, 3), (c2_ref, b2_ref, 64, 1), (c3_ref, b3_ref, 64, 1)):
        col = jnp.transpose(jnp.broadcast_to(b_ref[...], (128, n)))
        for i in range(times):
            ref[n * i:n * i + n, :] = col

def prepare(k1, k2, k3, b1, b2, b3):
    vm = pl.BlockSpec(memory_space=pltpu.VMEM)
    bfs = lambda *s: jax.ShapeDtypeStruct(s, BF)
    sds = lambda *s: jax.ShapeDtypeStruct(s, F32)
    f32 = lambda *s: pltpu.VMEM(s, F32)
    return pl.pallas_call(
        prep_kernel, in_specs=[vm] * 6, out_specs=[vm] * 9,
        out_shape=[bfs(2, 192, 256), bfs(2, 128, 256), bfs(2, 384, 256), bfs(2, 192, 256), bfs(2, 128, 256), bfs(2, 384, 256), sds(96, 128), sds(64, 128), sds(64, 128)],
        scratch_shapes=[f32(256, 128), f32(256, 128), f32(192, 128), f32(192, 128), f32(256, 128), f32(384, 256), f32(128, 256), f32(384, 256)],
        compiler_params=pltpu.CompilerParams(vmem_limit_bytes=60 * 2**20),
    )(jnp.transpose(k1, (1, 2, 3, 0)), jnp.transpose(k2, (1, 2, 3, 0)), jnp.transpose(k3, (2, 3, 0, 1)), b1, b2, b3)

def fwd_kernel(x_ref, w1_ref, w2_ref, w3_ref, b1_ref, b2_ref, b3_ref, pre1_hbm, pre2_hbm, pre3_ref, f_ref,
               xs, pre1_ref, pre2_ref, xh, xl, top1, top2, acc3, h1h, h1l, h2h, h2l, x_sem, sem1, sem2):
    def x_in(j):
        return pltpu.make_async_copy(x_ref.at[pl.ds(4 * j, 4)], xs.at[pl.ds(4 * j, 4)], x_sem.at[j])
    def row_out(row):
        return pltpu.make_async_copy(pre1_ref.at[row], pre1_hbm.at[row], sem1.at[row])
    for j in range(21):
        x_in(j).start()
    xh[:, 336:, :] = jnp.zeros((4, 16, 128), BF)
    xl[:, 336:, :] = jnp.zeros((4, 16, 128), BF)
    top1[...] = jnp.zeros_like(top1)
    top2[...] = jnp.zeros_like(top2)
    acc3[...] = jnp.zeros_like(acc3)
    h2h[:, 576:, :] = jnp.zeros((9, 64, 128), BF)
    h2l[:, 576:, :] = jnp.zeros((9, 64, 128), BF)
    def step1(j, carry):
        x_in(j).wait()
        v = xs[pl.ds(4 * j, 4)]
        hi = v.astype(BF)
        xh[:, 0:336, :] = hi
        xl[:, 0:336, :] = (v - hi.astype(F32)).astype(BF)
        rh = jnp.concatenate([xh[:, 48 * i:48 * i + 64, :].reshape(256, 128) for i in range(7)], axis=1)
        rl = jnp.concatenate([xl[:, 48 * i:48 * i + 64, :].reshape(256, 128) for i in range(7)], axis=1)
        r = dot3((w1_ref[0], w1_ref[1]), (rh, rl))
        out = top1[...] + r[96:]
        top1[...] = r[:96]
        b1 = b1_ref[...]
        row = jnp.maximum(j - 1, 0)
        for i in range(7):
            n = 96 if i < 6 else 64
            p = out[:n, 128 * i:128 * i + 128] + b1[:n]
            pre1_ref[row, 96 * i:96 * i + n, :] = p
            hh, hl = split(silu(p))
            h1h[row, 96 * i:96 * i + n, :] = hh
            h1l[row, 96 * i:96 * i + n, :] = hl
        pl.when(j >= 1)(lambda: row_out(row).start())
        return carry
    lax.fori_loop(0, 21, step1, 0)
    w2 = (w2_ref[0], w2_ref[1])
    b2 = b2_ref[...]
    def step2(y, carry):
        rh = jnp.concatenate([h1h[pl.ds(2 * y, 2), 64 * i:64 * i + 128, :].reshape(256, 128) for i in range(9)], axis=1)
        rl = jnp.concatenate([h1l[pl.ds(2 * y, 2), 64 * i:64 * i + 128, :].reshape(256, 128) for i in range(9)], axis=1)
        r = dot3(w2, (rh, rl))
        o = top2[...] + r[64:]
        top2[...] = r[:64]
        row = jnp.maximum(y - 1, 0)
        for i in range(9):
            p = o[:, 128 * i:128 * i + 128] + b2
            pre2_ref[row, 64 * i:64 * i + 64, :] = p
            hh, hl = split(silu(p))
            h2h[row, 64 * i:64 * i + 64, :] = hh
            h2l[row, 64 * i:64 * i + 64, :] = hl
        return carry
    lax.fori_loop(0, 10, step2, 0)
    pre2_out = pltpu.make_async_copy(pre2_ref, pre2_hbm, sem2)
    pre2_out.start()
    w3 = (w3_ref[0], w3_ref[1])
    b3 = b3_ref[...]
    def step3(y, carry):
        rh = jnp.concatenate([h2h[y, 128 * i:128 * i + 256, :] for i in range(4)], axis=1)
        rl = jnp.concatenate([h2l[y, 128 * i:128 * i + 256, :] for i in range(4)], axis=1)
        r = dot3(w3, (rh, rl))
        for ky in range(3):
            for i in range(4):
                acc3[y - ky + 2, 128 * i:128 * i + 128, :] += r[128 * ky:128 * ky + 128, 128 * i:128 * i + 128]
        return carry
    lax.fori_loop(0, 9, step3, 0)
    for y in range(7):
        for x in range(7):
            p = acc3[y + 2, 64 * x:64 * x + 64, :] + b3
            pre3_ref[pl.ds(y * 7 + x, 64, stride=49), :] = p
            f_ref[pl.ds(y * 7 + x, 64, stride=49), :] = silu(p)
    pre2_out.wait()
    for row in range(20):
        row_out(row).wait()

def forward(x, w1, w2, w3, b1, b2, b3):
    vm = pl.BlockSpec(memory_space=pltpu.VMEM)
    hbm = pl.BlockSpec(memory_space=pl.ANY)
    sds = lambda *s: jax.ShapeDtypeStruct(s, F32)
    f32 = lambda *s: pltpu.VMEM(s, F32)
    bf = lambda *s: pltpu.VMEM(s, BF)
    dma = pltpu.SemaphoreType.DMA
    return pl.pallas_call(
        fwd_kernel,
        in_specs=[hbm] + [vm] * 6,
        out_specs=[hbm, hbm, vm, vm],
        out_shape=[sds(20, 640, 128), sds(9, 576, 128), sds(3136, 128), sds(3136, 128)],
        scratch_shapes=[f32(84, 336, 128), f32(20, 640, 128), f32(9, 576, 128), bf(4, 352, 128), bf(4, 352, 128),
                        f32(96, 896), f32(64, 1152), f32(11, 512, 128), bf(20, 640, 128), bf(20, 640, 128), bf(9, 640, 128), bf(9, 640, 128),
                        dma((21,)), dma((20,)), dma],
        compiler_params=pltpu.CompilerParams(vmem_limit_bytes=60 * 2**20),
    )(x, w1, w2, w3, b1, b2, b3)


MESH_ID = pl.DeviceIdType.MESH


def coords():
    r = lax.axis_index("rep")
    return lax.axis_index("pair"), lax.axis_index("group"), r // 2, r % 2


def at(p, g, z, y):
    return (p, g, z * 2 + y)


def flip(z, k):
    return (z, z + 1 - 2 * (z % 2), z + 2 - 4 * (z // 2), 3 - z)[k]


def line(p, g, z, y):
    return [at(q, g, flip(z, k), y) for k in range(4) for q in ((p, 1 - p) if k else (1 - p,))]


def plane(p, g, z, y):
    return [at(p, g, z, 1 - y), at(p, 1 - g, z, y), at(p, 1 - g, z, 1 - y)]


def greet(devices):
    barrier = pltpu.get_barrier_semaphore()
    for device in devices:
        pl.semaphore_signal(barrier, inc=1, device_id=device, device_id_type=MESH_ID)
    pl.semaphore_wait(barrier, len(devices))


def remote(src, dst, send, recv, device):
    return pltpu.make_async_remote_copy(src_ref=src, dst_ref=dst, send_sem=send, recv_sem=recv, device_id=device, device_id_type=MESH_ID)


class Scatter:
    def __init__(self, parts, src, dst, send, recv, own, hold=None, cores=2):
        self.parts, self.src, self.dst, self.send, self.recv, self.own, self.hold, self.cores = parts, src, dst, send, recv, own, hold, cores
        self.p, self.g, self.z, self.y = coords()

    def copies(self):
        for k in range(4):
            for q in range(self.cores):
                for i in range(self.parts):
                    zd = flip(self.z, k)
                    if k == 0 and q == 0:
                        yield pltpu.make_async_copy(self.src(q, zd, i), self.dst(self.z, i) if self.hold is None else self.hold.at[i], self.own.at[i]), True
                    else:
                        yield remote(self.src(q, zd, i), self.dst(self.z, i), self.send.at[k * 2 + q, i], self.recv.at[k, i], at(q, self.g, zd, self.y)), False

    def start(self):
        @pl.when(self.p == 0)
        def _():
            for copy, own in self.copies():
                copy.start()

    def arrived(self, k):
        if self.cores == 1:
            pl.when(self.p == 0)(lambda: self.landed(k))
        else:
            self.landed(k)

    def landed(self, k):
        for i in range(self.parts):
            zs = flip(self.z, k)
            wait = remote(self.src(0, zs, i), self.dst(zs, i), self.send.at[0, i], self.recv.at[k, i], at(1 - self.p, self.g, self.z, self.y)).wait_recv
            def local():
                if self.hold is None:
                    pltpu.make_async_copy(self.src(0, zs, i), self.dst(zs, i), self.own.at[i]).wait()
                else:
                    pltpu.make_async_copy(self.src(0, zs, i), self.hold.at[i], self.own.at[i]).wait()
                    out = pltpu.make_async_copy(self.hold.at[i], self.dst(zs, i), self.own.at[i])
                    out.start()
                    out.wait()
            if k:
                wait()
            elif self.cores == 1:
                local()
            else:
                pl.when(self.p == 1)(wait)
                pl.when(self.p == 0)(local)

    def sent(self):
        @pl.when(self.p == 0)
        def _():
            for copy, own in self.copies():
                if not own:
                    copy.wait_send()


def scatter_sems(parts, *hold):
    return [pltpu.SemaphoreType.DMA((8, parts)), pltpu.SemaphoreType.DMA((4, parts)), pltpu.SemaphoreType.DMA((parts,))] + [pltpu.VMEM((parts,) + hold, F32)] * bool(hold)


PIECES = ((0, 72), (72, 72), (144, 56))


def f_scatter(f_ref, f1_ref, piece, sems):
    start, rows = PIECES[piece]
    def src(q, zd, i):
        return f_ref.at[pl.ds(pl.multiple_of((2 * q + i) * 784 + jnp.minimum(200 * zd, 584) + start, 8), rows)]
    return Scatter(2, src, lambda z, i: f1_ref.at[i, z], *sems)


def f_fan(f1_ref, f2_ref, send, recv):
    return spread_plane(*coords(), lambda gd, yd: f1_ref.at[gd], lambda m: f2_ref.at[m], send, recv)


class Line:
    def __init__(self, parts, own, slot, send, recv):
        self.parts, self.own, self.slot, self.send, self.recv = parts, own, slot, send, recv
        self.p, self.g, self.z, self.y = coords()

    def block(self, t, way):
        return jnp.maximum(self.z - t, 0) if way == 0 else jnp.minimum(self.z + t, 3)

    def there(self, t, way):
        return self.z >= t if way == 0 else self.z + t <= 3

    def copies(self, t, way):
        to = at(self.p, self.g, jnp.minimum(self.z + 1, 3) if way == 0 else jnp.maximum(self.z - 1, 0), self.y)
        zz = self.block(t, way)
        return [remote(self.own(i) if t == 0 else self.slot(zz, i), self.slot(zz, i), self.send.at[t, way, i], self.recv.at[t, way, i], to) for i in range(self.parts)]

    def goes(self, t, way):
        return jnp.logical_and(self.there(t, way), self.z <= 2 if way == 0 else self.z >= 1)

    def start(self, t):
        for way in range(2):
            def go():
                for copy in self.copies(t, way):
                    copy.start()
            pl.when(self.goes(t, way))(go)

    def arrive(self, t, then):
        for i in range(self.parts):
            for way in range(2):
                def come():
                    zz = self.block(t, way)
                    remote(self.slot(zz, i), self.slot(zz, i), self.send.at[t - 1, way, i], self.recv.at[t - 1, way, i], at(1 - self.p, self.g, self.z, self.y)).wait_recv()
                    if t < 3:
                        pl.when(self.goes(t, way))(self.copies(t, way)[i].start)
                    then(2 * t - 1 + way, zz, i)
                pl.when(self.there(t, way))(come)

    def each(self, do):
        do(0, self.z)
        for t in range(1, 4):
            for way in range(2):
                pl.when(self.there(t, way))(lambda: do(2 * t - 1 + way, self.block(t, way)))

    def sent(self):
        for t in range(3):
            for way in range(2):
                def done():
                    for copy in self.copies(t, way):
                        copy.wait_send()
                pl.when(self.goes(t, way))(done)


def line_sems(parts):
    return [pltpu.SemaphoreType.DMA((3, 2, parts)), pltpu.SemaphoreType.DMA((3, 2, parts))]


def g_scatter(hid_ref, g1_ref, sems):
    return Scatter(1, lambda q, zd, i: hid_ref.at[q, zd], lambda z, i: g1_ref.at[z], *sems)


def z_scatter(dz_ref, dz1_ref, sems):
    return Scatter(1, lambda q, zd, i: dz_ref, lambda z, i: dz1_ref.at[z], *sems, cores=1)


def spread_plane(p, g, z, y, src, dst, send, recv):
    places = [(g, 1 - y), (1 - g, y), (1 - g, 1 - y)]
    return [remote(src(*to), dst(m), send.at[m], recv.at[m], at(p, to[0], z, to[1])) for m, to in enumerate(places)]
ATOMS, ACTIONS, PAD = 51, 18, 56
OUTS, OUTP = 969, 976
STEPS = 7
ANY = pl.BlockSpec(memory_space=pl.ANY)
VMEM = pl.BlockSpec(memory_space=pltpu.VMEM)

def column(row, lanes):
    tall = jnp.transpose(jnp.broadcast_to(row, (128, row.shape[1])))
    return jnp.concatenate([tall] * (lanes // 128), axis=1)

def noisy(mean_ref, sigma_ref, nin_ref, nout_ref, s):
    return mean_ref[s] + sigma_ref[s] * (column(nin_ref[0, s:s + 1, :], 512) * nout_ref[s:s + 1, :])

def mask_of(chosen, a):
    return jnp.where(chosen == a, 1.0 - 1.0 / ACTIONS, -1.0 / ACTIONS)

def hid_kernel(net, f_ref, m_ref, s_ref, nin_ref, nout_ref, hm_ref, hs_ref, wo_ref, bm_ref, bs_ref, eout_ref, c_ref, pl_ref, pw_ref, *rest):
    if net:
        f_all, h_ref, g_ref, logp_ref, dist_ref, t_ref = rest[:6]
        f1_refs, f2_refs = rest[6:9], rest[9:11]
        acc, adv, ts, tr, fs0, fr0, fs1, fr1 = rest[11:19]
        wires = [f_scatter(f_all, f1_refs[i], i, rest[19 + 4 * i:23 + 4 * i]) for i in range(3)]
        fans = [f_fan(f1_refs[0], f2_refs[0], fs0, fr0), f_fan(f1_refs[1], f2_refs[1], fs1, fr1)]
        p, g, z, y = coords()
        target = remote(dist_ref, t_ref, ts, tr, at(1 - p, g, z, y))
        def next_piece(i):
            wires[i].sent()
            wires[i + 1].start()
            for k in range(4):
                wires[i].arrived(k)
            for copy in fans[i]:
                copy.start()
    else:
        h_ref, g_ref, logp_ref, dist_ref, acc, adv = rest
    j = pl.program_id(0)
    @pl.when(j == 0)
    def _():
        if net:
            greet(line(p, g, z, y) + plane(p, g, z, y))
            wires[0].start()
        acc[...] = jnp.zeros_like(acc)
    if net:
        pl.when(j == 4)(lambda: next_piece(0))
        pl.when(j == 6)(lambda: next_piece(1))
    f = split(f_ref[...])
    for s in range(2):
        w = split(noisy(m_ref, s_ref, nin_ref, nout_ref, s))
        acc[:, 512 * s:512 * s + 512] += dot3(f, w, TN)
    @pl.when(j == pl.num_programs(0) - 1)
    def _():
        hb = hm_ref[...] + hs_ref[...] * nout_ref[...]
        h = jnp.concatenate([acc[:, 0:512] + hb[0:1], acc[:, 512:1024] + hb[1:2]], axis=1)
        h_ref[...] = h
        gt = jnp.transpose(silu(h))
        for s in range(2):
            for q in range(2):
                for gg in range(2):
                    for z in range(4):
                        at_row = 512 * s + 256 * q + 128 * gg + 32 * z
                        g_ref[q, z, gg, s] = gt[at_row:at_row + 32]
        both = dot3(split(wo_ref[...]), split(jnp.concatenate([gt[:512], gt[512:]], axis=1)))
        bias = column(jnp.concatenate([bm_ref[...] + bs_ref[...] * eout_ref[...], jnp.zeros((1, OUTP - OUTS), F32)], axis=1), 128)
        adv[...] = both[:, 128:] + bias
        z = both[0:PAD, 0:128] + bias[0:PAD]
        chosen = c_ref[...]
        for i in range(ACTIONS):
            z = z + mask_of(chosen, i) * adv[ATOMS * (i + 1):ATOMS * (i + 1) + PAD, :]
        row = lax.broadcasted_iota(jnp.int32, (PAD, 128), 0)
        z = jnp.where(row < ATOMS, z, -1e30)
        top = jnp.max(z, axis=0, keepdims=True)
        e = jnp.exp(z - top)
        tot = jnp.sum(e, axis=0, keepdims=True)
        logp_ref[...] = (z - top) - jnp.log(tot)
        prob = e / tot
        dist = jnp.zeros((PAD, 128), F32)
        for i in range(ATOMS):
            lower = pl_ref[i:i + 1, :]
            share = pw_ref[i:i + 1, :]
            pi = prob[i:i + 1, :]
            dist = dist + jnp.where(row == lower, pi * (1.0 - share), 0.0) + jnp.where(row == lower + 1, pi * share, 0.0)
        dist_ref[...] = dist
        if net:
            pl.when(p == 1)(target.start)
            for k in range(4):
                wires[2].arrived(k)
            wires[2].sent()
            for copy in fans[0] + fans[1]:
                copy.wait()
            pl.when(p == 1)(target.wait_send)
            pl.when(p == 0)(target.wait_recv)

def hidden(net, f, m, s, nin, nout, hm, hs, wo, bm, bs, eout, c, plow, pw):
    full = lambda *t: pl.BlockSpec(t, lambda j: (0,) * len(t))
    sds = lambda *t: jax.ShapeDtypeStruct(t, F32)
    k = 3136 // STEPS
    wspec = pl.BlockSpec((2, k, 512), lambda j: (0, j, 0))
    return pl.pallas_call(
        functools.partial(hid_kernel, net), grid=(STEPS,),
        in_specs=[pl.BlockSpec((k, 128), lambda j: (j, 0)), wspec, wspec, pl.BlockSpec((1, 2, k), lambda j: (j, 0, 0)), full(2, 512), full(2, 512), full(2, 512),
                  full(OUTP, 512), full(1, OUTS), full(1, OUTS), full(1, OUTS), full(1, 128), full(ATOMS, 128), full(ATOMS, 128)] + [ANY] * net,
        out_specs=[full(128, 1024), full(2, 4, 2, 2, 32, 128), full(PAD, 128), full(PAD, 128)] + [ANY] * (6 * net),
        out_shape=[sds(128, 1024), sds(2, 4, 2, 2, 32, 128), sds(PAD, 128), sds(PAD, 128)]
        + ([sds(PAD, 128)] + [sds(2, 4, n, 128) for _, n in PIECES] + [sds(3, 4, n, 128) for _, n in PIECES[:2]]) * net,
        scratch_shapes=[pltpu.VMEM((128, 1024), F32), pltpu.VMEM((OUTP, 128), F32)]
        + ([pltpu.SemaphoreType.DMA] * 2 + [pltpu.SemaphoreType.DMA((3,))] * 4 + sum([scatter_sems(2, n, 128) for _, n in PIECES], [])) * net,
        compiler_params=pltpu.CompilerParams(vmem_limit_bytes=60 * 2**20, **(dict(collective_id=1, has_side_effects=True) if net else {})),
    )(f, m, s, nin, nout, hm, hs, wo, bm, bs, eout, c, plow, pw, *([f] * net))

def hid_bwd_kernel(net, t_ref, logp_ref, h_ref, m_ref, s_ref, nin_ref, nout_ref, wo_ref, c_ref, *rest):
    if net:
        noise, rest = list(zip(rest[2:6], rest[16:20])), rest[:2] + rest[6:16] + rest[20:]
        f1b_ref, hid_ref, df_ref, small_ref, f2b_ref, g1_ref, d1_ref, dz1_ref, g2_ref, d2_ref, dz2_ref, d3_ref = rest[:12]
        dth, dtl, da, msg, dz_to = rest[12:17]
        ds, dr, gs, gr, qs, qr, fs, fr, hs, hr, ss, sr, ps, pr, own = rest[17:32]
        g_wire = g_scatter(hid_ref, g1_ref, rest[32:36])
        z_wire = z_scatter(dz_to, dz1_ref, rest[36:39])
        p, g, z, y = coords()
        d_line = Line(2, lambda i: d1_ref.at[z, i], lambda zz, i: d1_ref.at[zz, i], rest[39], rest[40])
        partner = at(1 - p, g, z, y)
        hands = [remote(dz2_ref, dz2_ref, hs.at[0], hr.at[0], partner), remote(dz1_ref, dz1_ref, hs.at[1], hr.at[1], partner)]
        tells = [remote(src, dst, rest[41].at[i], rest[42].at[i], partner) for i, (src, dst) in enumerate(noise)]
        own_tells = [pltpu.make_async_copy(src, dst, rest[43].at[i]) for i, (src, dst) in enumerate(noise)]
        give = remote(msg.at[1], d1_ref.at[z], ps, pr, partner)
        keep = pltpu.make_async_copy(msg.at[0], d1_ref.at[z], own)
        fan_f = f_fan(f1b_ref, f2b_ref, fs, fr)
        fan_g = spread_plane(p, g, z, y, lambda gd, yd: g1_ref.at[:, gd], lambda m: g2_ref.at[m], gs, gr)
        fan_z = spread_plane(p, g, z, y, lambda gd, yd: dz1_ref, lambda m: dz2_ref.at[m], qs, qr)
        def fan_d(place, zz):
            return spread_plane(p, g, z, y, lambda gd, yd: d1_ref.at[zz, yd], lambda m: d2_ref.at[m, zz], ds.at[place], dr.at[place])
        def swap_own(place, zz):
            return remote(d1_ref.at[zz, y], d3_ref.at[3, zz], ss.at[place, 0], sr.at[place, 0], partner)
        def swap(place, zz):
            return remote(d2_ref.at[:, zz], d3_ref.at[pl.ds(0, 3), zz], ss.at[place, 1], sr.at[place, 1], partner)
        def forward(place, zz, s):
            along_y, along_x, both = fan_d(place, zz)
            @pl.when(y == s)
            def _():
                along_x.start()
                swap_own(place, zz).start()
            @pl.when(y != s)
            def _():
                both.start()
                along_y.start()
        def forward_small():
            for k in range(4):
                g_wire.arrived(k)
            for copy in fan_g:
                copy.start()
            for k in range(4):
                z_wire.arrived(k)
            @pl.when(p == 0)
            def _():
                for copy in fan_z:
                    copy.start()
    else:
        df_ref, small_ref, msg, dz_to, dth, dtl, da = rest
    j = pl.program_id(0)
    def begin():
        t = t_ref[...]
        logp = logp_ref[...]
        chosen = c_ref[...]
        row = lax.broadcasted_iota(jnp.int32, (PAD, 128), 0)
        d = (jnp.exp(logp) * jnp.sum(t, axis=0, keepdims=True) - t) * (1.0 / 128)
        loss = -jnp.sum(jnp.where(row < ATOMS, t * logp, 0.0), axis=1, keepdims=True) * (1.0 / 128)
        dz_to[...] = jnp.where(row == ATOMS, chosen.astype(F32), d)
        da[...] = jnp.zeros_like(da)
        da[0:PAD, 0:128] = d
        for i in range(ACTIONS):
            da[ATOMS * (i + 1):ATOMS * (i + 1) + PAD, 128:256] = mask_of(chosen, i) * d
        every = da[...]
        eh, el = split(every)
        grads = dot3((eh, el), split(wo_ref[...]), TN)
        small_ref[...] = jnp.zeros_like(small_ref)
        for s in range(2):
            dp = grads[128 * s:128 * s + 128] * dsilu(h_ref[:, 512 * s:512 * s + 512])
            total = jnp.sum(dp, axis=0, keepdims=True)
            for c in range(4):
                msg[c // 2, s, 128 * (c % 2):128 * (c % 2) + 128, :] = dp[:, 128 * c:128 * c + 128]
                small_ref[4 * s + c:4 * s + c + 1, :] = total[:, 128 * c:128 * c + 128]
            hi, lo = split(jnp.transpose(dp))
            dth[s] = hi
            dtl[s] = lo
        if net:
            give.start()
            keep.start()
            z_wire.start()
            keep.wait()
        ones = jnp.ones((8, 256), BF)
        left = (every - eh.astype(F32)) - el.astype(F32)
        rows = dot(ones, eh, NT) + dot(ones, el, NT) + dot(ones, left.astype(BF), NT)
        for c in range(8):
            n = min(128, OUTP - 128 * c)
            small_ref[8 + c:9 + c, 0:n] = rows[0:1, 128 * c:128 * c + n]
        small_ref[16:17, :] = jnp.broadcast_to(jnp.sum(loss, axis=0, keepdims=True), (1, 128))
    def step():
        out = None
        for s in range(2):
            w = split(noisy(m_ref, s_ref, nin_ref, nout_ref, s))
            r = dot3(w, (dth[s], dtl[s]))
            out = r if out is None else out + r
        df_ref[...] = out
    if not net:
        pl.when(j == 0)(begin)
        step()
        return
    @pl.when(j == 0)
    def _():
        greet(line(p, g, z, y) + plane(p, g, z, y))
        for copy in fan_f:
            copy.start()
        g_wire.start()
        @pl.when(p == 0)
        def _():
            begin()
            for copy in tells + own_tells:
                copy.start()
        pl.when(p == 1)(give.wait_recv)
        d_line.start(0)
        for s in range(2):
            forward(0, z, s)
    pl.when(p == 0)(step)
    pl.when(j == 3)(forward_small)
    @pl.when(j == pl.num_programs(0) - 1)
    def _():
        for t in range(1, 4):
            d_line.arrive(t, forward)
        @pl.when(p == 0)
        def _():
            for copy in fan_z:
                copy.wait()
            for copy in hands:
                copy.start()
        def landed(place, zz):
            for copy in fan_d(place, zz):
                copy.wait_recv()
            swap(place, zz).start()
        d_line.each(landed)
        for copy in fan_f + fan_g:
            copy.wait()
        def gone(place, zz):
            for copy in fan_d(place, zz):
                copy.wait_send()
            swap(place, zz).wait()
            swap_own(place, zz).wait()
        d_line.each(gone)
        d_line.sent()
        @pl.when(p == 0)
        def _():
            give.wait_send()
            for copy in hands + tells:
                copy.wait_send()
            for copy in own_tells:
                copy.wait()
        @pl.when(p == 1)
        def _():
            for copy in hands + tells:
                copy.wait_recv()
        for wire in (g_wire, z_wire):
            wire.sent()

def hidden_bwd(net, t, logp, h, m, s, nin, nout, wo, c, *wired):
    full = lambda *u: pl.BlockSpec(u, lambda j: (0,) * len(u))
    sds = lambda *u: jax.ShapeDtypeStruct(u, F32)
    dma = pltpu.SemaphoreType.DMA
    k = 3136 // STEPS
    wspec = pl.BlockSpec((2, k, 512), lambda j: (0, j, 0))
    return pl.pallas_call(
        functools.partial(hid_bwd_kernel, net), grid=(STEPS,),
        in_specs=[full(PAD, 128), full(PAD, 128), full(128, 1024), wspec, wspec, pl.BlockSpec((1, 2, k), lambda j: (j, 0, 0)), full(2, 512),
                  full(OUTP, 512), full(1, 128)] + [ANY] * (6 * net),
        out_specs=[pl.BlockSpec((k, 128), lambda j: (j, 0)), full(24, 128)] + ([ANY] * 12 if net else [full(2, 2, 256, 128), full(PAD, 128)]),
        out_shape=[sds(3136, 128), sds(24, 128)] + ([sds(3, 4, PIECES[2][1], 128), sds(4, 2, 2, 32, 128), sds(4, 2, 256, 128), sds(4, PAD, 128), sds(3, 4, 2, 32, 128), sds(3, 4, 256, 128),
                                                     sds(3, 4, PAD, 128), sds(4, 4, 256, 128), sds(2, 3136), sds(2, 512), sds(2, 512), sds(1, OUTS)] if net else [sds(2, 2, 256, 128), sds(PAD, 128)]),
        scratch_shapes=[pltpu.VMEM((2, 512, 128), BF), pltpu.VMEM((2, 512, 128), BF), pltpu.VMEM((OUTP, 256), F32)]
        + ([pltpu.VMEM((2, 2, 256, 128), F32), pltpu.VMEM((PAD, 128), F32), dma((7, 3)), dma((7, 3))] + [dma((3,))] * 6 + [dma((2,)), dma((2,)), dma((7, 2)), dma((7, 2)), dma, dma, dma]
           + scatter_sems(1, 2, 2, 32, 128) + scatter_sems(1) + line_sems(2) + [dma((4,)), dma((4,)), dma((4,))]) * net,
        compiler_params=pltpu.CompilerParams(vmem_limit_bytes=60 * 2**20, **(dict(collective_id=2, has_side_effects=True) if net else {})),
    )(t, logp, h, m, s, nin, nout, wo, c, *wired)

def dsilu(v):
    s = jax.nn.sigmoid(v)
    return s * (1.0 + v * (1.0 - s))


ROWS = 768

def bwd_kernel(net, x_ref, pre1_hbm, pre2_ref, pre3_ref, df_ref, w1_ref, w2_ref, w3_ref, *rest):
    if net:
        r_ref, q_ref, s0_ref, tot_ref, sg_ref, ag_ref, ah_ref, bg_ref, bh_ref = rest[:9]
        xs, pre1_ref, xh, xl, d3f, d3h, d3l, d2h, d2l, d1h, d1l, h2h, h2l, acc2, a1, a2, a3, pay, lob, upb, x_sem, sem1, ls, us = rest[9:33]
        got, got1, red, tot, ur, zs_, zr, ys, yr, own, gs, gr, ws, wr, as_, ar, bs, br, es, er, cs, cr, one_ = rest[33:]
        p, g, z, y = coords()
        reps = lax.axis_size("rep")
        chips = 2 * reps
        me = g * reps + lax.axis_index("rep")
        size = ROWS // chips
        def chip(i):
            return (0, i // reps, i % reps)
        def part(i):
            return pl.ds(pl.multiple_of(i * size, 8), size)
        def give(k):
            to = (me + k) % chips
            if k:
                return remote(pay.at[part(to)], got.at[me], as_.at[k], ar.at[k], chip(to))
            return pltpu.make_async_copy(pay.at[part(me)], got.at[me], one_)
        def given(k):
            who = (me + chips - k) % chips
            return remote(pay.at[part(me)], got.at[who], as_.at[k], ar.at[k], chip(who))
        def show(k):
            return remote(pay.at[pl.ds(672, 64)], got1.at[me], es.at[k], er.at[k], chip((me + k) % chips))
        def shown(k):
            who = (me + chips - k) % chips
            return remote(pay.at[pl.ds(672, 64)], got1.at[who], es.at[k], er.at[k], chip(who))
        def tell(k):
            return remote(red, tot.at[part(me)], bs.at[k], br.at[k], chip((me + k) % chips))
        def told(k):
            who = (me + chips - k) % chips
            return remote(red, tot.at[part(who)], bs.at[k], br.at[k], chip(who))
        hand = remote(tot, tot, cs, cr, at(1 - p, g, z, y))
        def head_at(ref, yy, zz):
            return ref.at[zz, pl.ds(5 * yy, 5 - yy)]
        def head_of(yy):
            return q_ref.at[pl.ds(5 * yy, 5 - yy)]
        def slots(yy, zz):
            return ag_ref.at[yy, zz], head_at(ah_ref, yy, zz), bg_ref.at[yy, zz], head_at(bh_ref, yy, zz)
        def lines(yy):
            mine = (r_ref, head_of(yy)) + slots(yy, z)[2:]
            return Line(4, lambda i: mine[i], lambda zz, i: slots(yy, zz)[i], zs_, zr)
        def keep(yy):
            a, b, _, _ = slots(yy, z)
            return [pltpu.make_async_copy(r_ref, a, own.at[0]), pltpu.make_async_copy(head_of(yy), b, own.at[1])]
        def give_own(yy):
            _, _, a, b = slots(yy, z)
            return [remote(r_ref, a, gs.at[0], gr.at[0], at(1, g, z, y)), remote(head_of(yy), b, gs.at[1], gr.at[1], at(1, g, z, y))]
        def along_y(place, zz, yy):
            src = slots(yy, zz) if place else (r_ref, head_of(yy)) + slots(yy, z)[2:]
            return [remote(src[i], slots(yy, zz)[i], ys.at[place, i], yr.at[place, i], at(p, g, z, 1 - y)) for i in range(4)]
        def bring(place, zz, yy):
            a, b, c, d = slots(yy, zz)
            return [remote(c, a, ws.at[yy, place, 0], wr.at[yy, place, 0], at(0, g, z, y)), remote(d, b, ws.at[yy, place, 1], wr.at[yy, place, 1], at(0, g, z, y))]
        def each(do, flipped=False):
            for yy in range(2):
                pl.when(y == (1 - yy if flipped else yy))(functools.partial(do, yy))
        def states_out(j, slot):
            return (pltpu.make_async_copy(lob.at[slot], sg_ref.at[pl.ds(4 * j, 4)], ls.at[slot]),
                    remote(upb.at[slot], sg_ref.at[pl.ds(4 * j, 4)], us.at[slot], ur.at[j], at(1 - p, g, z, y)))
        def gather(yy):
            def then(place, zz, i):
                along_y(place, zz, yy)[i].start()
                if i >= 2:
                    bring(place, zz, yy)[i - 2].start()
            for copy in give_own(yy):
                copy.wait_recv()
            lines(yy).start(0)
            for i in range(4):
                then(0, z, i)
            for copy in keep(yy):
                copy.start()
            for t in range(1, 4):
                lines(yy).arrive(t, then)
        def second(yy):
            def landed(place, zz):
                for copy in along_y(place, zz, yy):
                    copy.wait_recv()
                for copy in bring(place, zz, yy):
                    copy.start()
            lines(yy).each(landed)
        def finished(yy):
            def gone(place, zz):
                for copy in along_y(place, zz, yy) + bring(place, zz, yy):
                    copy.wait_send()
            for copy in keep(yy):
                copy.wait()
            lines(yy).sent()
            lines(yy).each(gone)
        def second_sent(yy):
            def gone(place, zz):
                for copy in bring(place, zz, yy):
                    copy.wait_send()
            lines(yy).each(gone)
        def brought(yy):
            def came(place, zz):
                for copy in bring(place, zz, yy):
                    copy.wait_recv()
            lines(yy).each(came)
    else:
        tot_ref, lo_ref, up_ref, xs, pre1_ref, xh, xl, d3f, d3h, d3l, d2h, d2l, d1h, d1l, h2h, h2l, acc2, a1, a2, a3, pay, lob, upb, x_sem, sem1, ls, us = rest
        def states_out(j, slot):
            return (pltpu.make_async_copy(lob.at[slot], lo_ref.at[pl.ds(4 * j, 4)], ls.at[slot]),
                    pltpu.make_async_copy(upb.at[slot], up_ref.at[pl.ds(4 * j, 4)], us.at[slot]))
    small_ref = pay.at[pl.ds(24, 648)]
    last = 20
    def x_in(j):
        return pltpu.make_async_copy(x_ref.at[pl.ds(4 * j, 4)], xs.at[pl.ds(4 * j, 4)], x_sem.at[j])
    pre1_in = pltpu.make_async_copy(pre1_hbm, pre1_ref, sem1)
    def fetch():
        pre1_in.start()
        for j in range(21):
            x_in(j).start()
    def upper():
        for ref in (d3h, d3l, d2h, d2l, acc2, a2, a3):
            ref[...] = jnp.zeros_like(ref)
        small_ref[...] = jnp.zeros((648, 128), F32)
        for ref in (d1h, d1l):
            ref[0] = jnp.zeros((704, 128), BF)
            ref[21] = jnp.zeros((704, 128), BF)
            ref[:, 0:32, :] = jnp.zeros((22, 32, 128), BF)
            ref[:, 672:704, :] = jnp.zeros((22, 32, 128), BF)
        d3f[...] = df_ref[...] * dsilu(pre3_ref[...])
        total = jnp.zeros((64, 128), F32)
        for y in range(7):
            for x in range(7):
                d = d3f[pl.ds(y * 7 + x, 64, stride=49), :]
                total = total + d
                hi, lo = split(d)
                d3h[y + 2, 64 * (x + 2):64 * (x + 3), :] = hi
                d3l[y + 2, 64 * (x + 2):64 * (x + 3), :] = lo
        small_ref[640:641, 0:64] = jnp.sum(jnp.transpose(total), axis=0, keepdims=True)
        w3 = (w3_ref[0], w3_ref[1])
        h2h[:, 576:, :] = jnp.zeros((9, 64, 128), BF)
        h2l[:, 576:, :] = jnp.zeros((9, 64, 128), BF)
        def split2(y, c):
            hi, lo = split(silu(pre2_ref[y]))
            h2h[y, 0:576, :] = hi
            h2l[y, 0:576, :] = lo
            return c
        lax.fori_loop(0, 9, split2, 0)
        def dgrad3(y, c):
            rh = jnp.concatenate([d3h[y + 2, 128 * i:128 * i + 256, :] for i in range(5)], axis=1)
            rl = jnp.concatenate([d3l[y + 2, 128 * i:128 * i + 256, :] for i in range(5)], axis=1)
            r = dot3(w3, (rh, rl))
            for ky in range(3):
                for i in range(5):
                    acc2[y + ky, 128 * i:128 * i + 128, :] += r[128 * ky:128 * ky + 128, 128 * i:128 * i + 128]
            return c
        lax.fori_loop(0, 7, dgrad3, 0)
        def wgrad3(y, c):
            def lhs(ref):
                return jnp.concatenate([jnp.concatenate([ref[y - ky + 2, 128 * (i + 1):128 * (i + 2), :] for i in range(4)], axis=1) for ky in range(3)], axis=0)
            def rhs(ref):
                return jnp.concatenate([ref[y, 128 * i:128 * i + 256, :] for i in range(4)], axis=1)
            a3[...] += dot3((lhs(d3h), lhs(d3l)), (rhs(h2h), rhs(h2l)), NT)
            return c
        lax.fori_loop(0, 9, wgrad3, 0)
        for ky in range(3):
            grad = a3[128 * ky:128 * ky + 64, 0:192] + a3[128 * ky + 64:128 * ky + 128, 64:256]
            small_ref[256 + 64 * ky:320 + 64 * ky, :] = grad[:, 0:128]
            small_ref[448 + 64 * ky:512 + 64 * ky, 0:64] = grad[:, 128:192]
        def step2(y, total):
            for x in range(9):
                d = acc2[y, 64 * x:64 * x + 64, :] * dsilu(pre2_ref[y, 64 * x:64 * x + 64, :])
                total = total + d
                hi, lo = split(d)
                d2h[y + 1, 64 * (x + 1):64 * (x + 2), :] = hi
                d2l[y + 1, 64 * (x + 1):64 * (x + 2), :] = lo
            return total
        total = lax.fori_loop(0, 9, step2, jnp.zeros((64, 128), F32))
        small_ref[641:642, 0:64] = jnp.sum(jnp.transpose(total), axis=0, keepdims=True)
    def block2(y, total):
        w2 = (w2_ref[0], w2_ref[1])
        rh = jnp.concatenate([d2h[pl.ds(y, 2), 64 * i:64 * i + 128, :].reshape(256, 128) for i in range(10)], axis=1)
        rl = jnp.concatenate([d2l[pl.ds(y, 2), 64 * i:64 * i + 128, :].reshape(256, 128) for i in range(10)], axis=1)
        r = dot3(w2, (rh, rl))
        h1h, h1l = [], []
        for py in range(2):
            rowh, rowl = [], []
            for i in range(10):
                v = pre1_ref[2 * y + py, 64 * i:64 * i + 64, :]
                s = jax.nn.sigmoid(v)
                d = r[64 * py:64 * py + 64, 128 * i:128 * i + 128] * (s * (1.0 + v * (1.0 - s)))
                total = total + d[0:32] + d[32:64]
                hi, lo = split(d)
                d1h[2 * y + py + 1, 64 * i + 32:64 * i + 96, :] = hi
                d1l[2 * y + py + 1, 64 * i + 32:64 * i + 96, :] = lo
                hi, lo = split(v * s)
                rowh.append(hi)
                rowl.append(lo)
            h1h.append(rowh)
            h1l.append(rowl)
        def lhs(ref):
            return jnp.concatenate([jnp.concatenate([ref[y + 1 - h, 64 * (i + 1):64 * (i + 2), :] for i in range(9)], axis=1) for h in range(2)], axis=0)
        def rhs(rows):
            return jnp.concatenate([jnp.concatenate([rows[0][i], rows[0][i + 1], rows[1][i], rows[1][i + 1]], axis=0) for i in range(9)], axis=1)
        a2[...] += dot3((lhs(d2h), lhs(d2l)), (rhs(h1h), rhs(h1l)), NT)
        return total
    def lower():
        pre1_in.wait()
        total = lax.fori_loop(0, 10, block2, jnp.zeros((32, 128), F32))
        small_ref[642:643, 0:32] = jnp.sum(jnp.transpose(total), axis=0, keepdims=True)
        small_ref[0:128, :] = a2[:, 0:128]
        small_ref[128:256, :] = a2[:, 128:256]
    def states_gone(j, slot):
        a, b = states_out(j, slot)
        a.wait()
        if net:
            b.wait_send()
        else:
            b.wait()
    def wgrad1(j, carry):
        x_in(j).wait()
        v = xs[pl.ds(4 * j, 4)]
        hi = v.astype(BF)
        xh[:, 0:336, :] = hi
        xl[:, 0:336, :] = (v - hi.astype(F32)).astype(BF)
        def lhs(ref):
            return jnp.concatenate([jnp.concatenate([ref[j + 1 - h, 96 * i + 32:96 * i + 128, :] for i in range(7)], axis=1) for h in range(2)], axis=0)
        def rhs(ref):
            return jnp.concatenate([ref[:, 48 * i:48 * i + 64, :].reshape(256, 128) for i in range(7)], axis=1)
        a1[...] += dot3((lhs(d1h), lhs(d1l)), (rhs(xh), rhs(xl)), NT)
        return carry
    def first_grad():
        lax.fori_loop(0, 21, wgrad1, 0)
        if net:
            give(0).wait()
            for k in range(1, chips):
                give(k).wait_send()
        for h in range(2):
            for ky in range(4):
                grad = a1[96 * h:96 * h + 32, 64 * ky:64 * ky + 32]
                grad = grad + a1[96 * h + 32:96 * h + 64, 64 * ky + 16:64 * ky + 48]
                grad = grad + a1[96 * h + 64:96 * h + 96, 64 * ky + 32:64 * ky + 64]
                pay[672 + 32 * h:704 + 32 * h, 32 * ky:32 * ky + 32] = grad
    def dgrad1(j, carry):
        def both(ref):
            return jnp.concatenate([ref[pl.ds(j, 2), 96 * i:96 * i + 128, :].reshape(256, 128) for i in range(7)], axis=1)
        r = dot3((w1_ref[0], w1_ref[1]), (both(d1h), both(d1l)))
        slot = j % 2
        pl.when(j >= 2)(lambda: states_gone(j - 2, slot))
        lo_to, up_to = lob.at[slot], upb.at[slot]
        for ky in range(4):
            for i in range(7):
                lo_to[ky, 24 * i:24 * i + 24, :] = r[24 * ky:24 * ky + 24, 128 * i:128 * i + 128]
                up_to[ky, 24 * i:24 * i + 24, :] = r[96 + 24 * ky:96 + 24 * ky + 24, 128 * i:128 * i + 128]
        for copy in states_out(j, slot):
            copy.start()
        return carry
    if net:
        pl.when(p == 0)(fetch)
        pl.when(p == 0)(lambda: greet([chip((me + k) % chips) for k in range(1, chips)] + [at(1, g, z, y)]))
        pl.when(p == 1)(lambda: greet([at(1, g, flip(z, k), y) for k in range(1, 4)] + [at(1, g, z, 1 - y), at(0, g, z, y)]))
        def begin(yy):
            for copy in give_own(yy):
                copy.start()
        pl.when(p == 0)(lambda: each(begin))
        @pl.when(p == 1)
        def _():
            each(gather)
            each(second, flipped=True)
        pay[0:24, :] = s0_ref[...]
    else:
        pay[0:24, :] = jnp.zeros((24, 128), F32)
    pay[672:, :] = jnp.zeros((ROWS - 672, 128), F32)
    xh[:, 336:, :] = jnp.zeros((4, 16, 128), BF)
    xl[:, 336:, :] = jnp.zeros((4, 16, 128), BF)
    a1[...] = jnp.zeros_like(a1)
    if net:
        @pl.when(p == 0)
        def _():
            upper()
            lower()
            for k in range(chips):
                give(k).start()
            first_grad()
            for k in range(1, chips):
                show(k).start()
            got1[me] = pay[672:736, :]
            lax.fori_loop(0, 12, dgrad1, 0)
            for k in range(1, chips):
                given(k).wait_recv()
            red[...] = jnp.sum(got[...], axis=0)
            tot[part(me), :] = red[...]
            for k in range(1, chips):
                tell(k).start()
            lax.fori_loop(12, 21, dgrad1, 0)
            for k in range(1, chips):
                told(k).wait_recv()
            for k in range(1, chips):
                shown(k).wait_recv()
            tot[672:736, :] = jnp.sum(got1[...], axis=0)
            hand.start()
            for k in range(1, chips):
                tell(k).wait_send()
                show(k).wait_send()
            hand.wait_send()
            for j in (last - 1, last):
                states_gone(j, j % 2)
    else:
        fetch()
        upper()
        lower()
        first_grad()
        lax.fori_loop(0, 21, dgrad1, 0)
        for j in (last - 1, last):
            states_gone(j, j % 2)
    if net:
        @pl.when(p == 1)
        def _():
            hand.wait_recv()
            def arrive(i, c):
                states_out(i, 0)[1].wait_recv()
                return c
            lax.fori_loop(0, last + 1, arrive, 0)
        tot_ref[...] = tot[...]
        @pl.when(p == 0)
        def _():
            def given_own(yy):
                for copy in give_own(yy):
                    copy.wait_send()
            each(given_own)
            brought(0)
            brought(1)
        @pl.when(p == 1)
        def _():
            each(finished)
            each(second_sent, flipped=True)
    else:
        tot_ref[...] = pay[...]

def backward(net, x, pre1, pre2, pre3, df, w1, w2, w3, *wired):
    sds = lambda *s: jax.ShapeDtypeStruct(s, F32)
    vmb = lambda *s: pltpu.VMEM(s, BF)
    f32 = lambda *s: pltpu.VMEM(s, F32)
    dma = pltpu.SemaphoreType.DMA
    return pl.pallas_call(
        functools.partial(bwd_kernel, net),
        in_specs=[ANY, ANY] + [VMEM] * 6 + [VMEM] * 3 * net,
        out_specs=[VMEM] + [ANY] * (5 if net else 2),
        out_shape=[sds(ROWS, 128)] + ([sds(84, 168, 128)] + [sds(2, 4, 200, 512), sds(4, 9, 32, 128)] * 2 if net else [sds(84, 168, 128), sds(84, 168, 128)]),
        scratch_shapes=[f32(84, 336, 128), f32(20, 640, 128), vmb(4, 352, 128), vmb(4, 352, 128), f32(3136, 128), vmb(11, 768, 128), vmb(11, 768, 128), vmb(11, 704, 128),
                        vmb(11, 704, 128), vmb(22, 704, 128), vmb(22, 704, 128), vmb(9, 640, 128), vmb(9, 640, 128), f32(9, 640, 128), f32(192, 256), f32(128, 256),
                        f32(384, 256), f32(ROWS, 128), f32(2, 4, 168, 128), f32(2, 4, 168, 128), dma((21,)), dma, dma((2,)), dma((2,))]
        + ([f32(16, ROWS // 16, 128), f32(16, 64, 128), f32(ROWS // 16, 128), f32(ROWS, 128), dma((21,))]
           + line_sems(4) + [dma((7, 4))] * 2 + [dma((2,))] * 3 + [dma((2, 7, 2))] * 2 + [dma((16,))] * 6 + [dma] * 3) * net,
        compiler_params=pltpu.CompilerParams(vmem_limit_bytes=62 * 2**20, **(dict(collective_id=3, has_side_effects=True) if net else {})),
    )(x, pre1, pre2, pre3, df, w1, w2, w3, *wired)

def wide_kernel(f1a, f1b, f1c, f2a, f2b, f2c, d1, d2, d3, g1, g2, z1, z2, r_ref, q_ref, fv, dv, ev, gv, zv, acc, acq, da, sem):
    p, g = lax.axis_index("pair"), lax.axis_index("group")
    y = lax.axis_index("rep") % 2
    three, last = pl.ds(0, 3), 3
    rows = [pl.ds(*piece) for piece in PIECES]
    pairs = [(ref, fv.at[three, :, rows[i]]) for i, ref in enumerate((f2a, f2b, f2c))] + [(ref.at[g], fv.at[last, :, rows[i]]) for i, ref in enumerate((f1a, f1b, f1c))]
    pairs += [(g2, gv.at[three]), (g1.at[:, g], gv.at[last]), (z2, zv.at[three]), (z1, zv.at[last])]
    first = len(pairs)
    for m in range(4):
        pairs += [(d2.at[m] if m < 3 else d1.at[:, y], dv.at[m]), (d3.at[m], ev.at[m])]
    copies = [pltpu.make_async_copy(a, b, sem.at[i]) for i, (a, b) in enumerate(pairs)]
    for copy in copies:
        copy.start()
    acc[...] = jnp.zeros_like(acc)
    acq[...] = jnp.zeros_like(acq)
    da[...] = jnp.zeros_like(da)
    for copy in copies[:first]:
        copy.wait()
    def block(ref, m):
        return jnp.concatenate([jnp.concatenate([ref[m, i, 128 * c:128 * c + 128, :] for c in range(2)], axis=1) for i in range(4)], axis=0)
    def step(m):
        for copy in copies[first + 2 * m:first + 2 * m + 2]:
            copy.wait()
        f = split(jnp.concatenate([fv[m, i] for i in range(4)], axis=1))
        acc[0] += dot3(f, split(block(dv, m)))
        acc[1] += dot3(f, split(block(ev, m)))
        dz = jnp.concatenate([zv[m, i] for i in range(4)], axis=1)
        row = lax.broadcasted_iota(jnp.int32, (PAD, 512), 0)
        chosen = dz[ATOMS:ATOMS + 1].astype(jnp.int32)
        d = jnp.where(row < ATOMS, dz, 0.0)
        da[0:PAD, :] = d
        for i in range(ACTIONS):
            da[128 + ATOMS * i:128 + ATOMS * i + PAD, :] = mask_of(chosen, i) * d
        def units(s):
            return split(jnp.concatenate([gv[m, i, s] for i in range(4)], axis=1))
        @pl.when(y == 0)
        def _():
            acq[:, 0:128] += dot3(units(0), split(da[0:128, :]), NT)
            acq[:, 128:640] += dot3(units(1), split(da[128:640, :]), NT)
        @pl.when(y == 1)
        def _():
            acq[:, 640:1152] += dot3(units(1), split(da[640:1152, :]), NT)
    for m in range(4):
        step(m)
    r_ref[:, 0:256] = jnp.where(p == 0, acc[0], acc[1])
    r_ref[:, 256:512] = jnp.where(p == 0, acc[1], acc[0])
    for c in range(9):
        q_ref[c] = acq[:, 128 * c:128 * c + 128]

def wide_grads(*messages):
    sds = lambda *s: jax.ShapeDtypeStruct(s, F32)
    f32 = lambda *s: pltpu.VMEM(s, F32)
    return pl.pallas_call(
        wide_kernel, in_specs=[ANY] * 13, out_specs=[VMEM] * 2,
        out_shape=[sds(200, 512), sds(9, 32, 128)],
        scratch_shapes=[f32(4, 4, 200, 128), f32(4, 4, 256, 128), f32(4, 4, 256, 128), f32(4, 4, 2, 32, 128), f32(4, 4, PAD, 128),
                        f32(2, 200, 256), f32(32, 1152), f32(1152, 512), pltpu.SemaphoreType.DMA((18,))],
        compiler_params=pltpu.CompilerParams(vmem_limit_bytes=60 * 2**20),
    )(*messages)

def torso_out(tot, k1_ref, k2_ref, k3_ref, b1_ref, b2_ref, b3_ref, t1, t2):
    t1[:, 0:64] = jnp.transpose(tot[672:736, :])
    t1[:, 64:128] = jnp.zeros((128, 64), F32)
    for ky in range(4):
        for c in range(4):
            v = t1[pl.ds(32 * ky + c, 8, stride=4), :]
            for h in range(2):
                k1_ref[c, 4 * h + ky] = v[:, 32 * h:32 * h + 32]
    for py in range(2):
        t2[...] = jnp.transpose(tot[24 + 128 * py:152 + 128 * py, :])
        for h in range(2):
            for kx in range(4):
                k2_ref[:, 2 * h + py, kx, :] = t2[32 * kx:32 * kx + 32, 64 * h:64 * h + 64]
    for ky in range(3):
        for kx in range(3):
            base = (280 if kx < 2 else 472) + 64 * ky
            k3_ref[ky, kx] = tot[base:base + 64, 64 * (kx % 2):64 * (kx % 2) + 64]
    b3_ref[...] = tot[664:665, 0:64]
    b2_ref[...] = tot[665:666, 0:64]
    b1_ref[...] = tot[666:667, 0:32]

def finish_kernel(sg_ref, ag_ref, ah_ref, tot_ref, in_ref, out_ref, ein_ref, eout_ref, mean_ref, sigma_ref, hm_ref, hs_ref, k1_ref, k2_ref, k3_ref, b1_ref, b2_ref, b3_ref,
                  hb_ref, hbs_ref, bo_ref, bos_ref, loss_ref, states_ref, t1, t2, sv, sem):
    parts = [pl.ds(21 * i, 21) for i in range(4)]
    reads = [pltpu.make_async_copy(sg_ref.at[part], sv.at[part], sem.at[0, i]) for i, part in enumerate(parts)]
    moves = [pltpu.make_async_copy(sv.at[part], states_ref.at[part], sem.at[1, i]) for i, part in enumerate(parts)]
    for copy in reads:
        copy.start()
    for i in range(4):
        reads[i].wait()
        moves[i].start()
    for s in range(2):
        tall = column(in_ref[s:s + 1, :], 512) * out_ref[s:s + 1, :]
        for z, (start, n) in enumerate(((0, 200), (200, 200), (400, 184), (584, 200))):
            v = ag_ref[s, z, 0:n, :]
            mean_ref[s, start:start + n, :] = v
            sigma_ref[s, start:start + n, :] = v * tall[start:start + n]
    noise = column(eout_ref[...], 128)
    for c in range(9):
        start = 0 if c == 0 else ATOMS + 128 * (c - 1)
        n = min(128, (ATOMS if c == 0 else OUTS) - start)
        v = jnp.transpose(jnp.concatenate([ah_ref[z, c] for z in range(4)], axis=0))[0:n]
        hm_ref[start:start + n, :] = v
        hs_ref[start:start + n, :] = v * (noise[start:start + n] * ein_ref[min(c, 1):min(c, 1) + 1, :])
    torso_out(tot_ref, k1_ref, k2_ref, k3_ref, b1_ref, b2_ref, b3_ref, t1, t2)
    for s in range(2):
        for c in range(4):
            v = tot_ref[4 * s + c:4 * s + c + 1, :]
            hb_ref[s:s + 1, 128 * c:128 * c + 128] = v
            hbs_ref[s:s + 1, 128 * c:128 * c + 128] = v * out_ref[s:s + 1, 128 * c:128 * c + 128]
    for c in range(8):
        n = min(128, OUTS - 128 * c)
        v = tot_ref[8 + c:9 + c, 0:n]
        bo_ref[:, 128 * c:128 * c + n] = v
        bos_ref[:, 128 * c:128 * c + n] = v * eout_ref[:, 128 * c:128 * c + n]
    loss_ref[...] = tot_ref[16:17, :]
    for copy in moves:
        copy.wait()

def finish(sg, ag, ah, tot, n_in, n_out, e_in, e_out):
    sds = lambda *s: jax.ShapeDtypeStruct(s, F32)
    return pl.pallas_call(
        finish_kernel, in_specs=[ANY] + [VMEM] * 7, out_specs=[VMEM] * 15 + [ANY],
        out_shape=[sds(2, 784, 512), sds(2, 784, 512), sds(OUTS, 128), sds(OUTS, 128), sds(4, 8, 8, 32), sds(32, 4, 4, 64), sds(3, 3, 64, 64), sds(1, 32), sds(1, 64), sds(1, 64),
                   sds(2, 512), sds(2, 512), sds(1, OUTS), sds(1, OUTS), sds(1, 128), sds(84, 168, 128)],
        scratch_shapes=[pltpu.VMEM((128, 128), F32), pltpu.VMEM((128, 128), F32), pltpu.VMEM((84, 168, 128), F32), pltpu.SemaphoreType.DMA((2, 4))],
        compiler_params=pltpu.CompilerParams(vmem_limit_bytes=60 * 2**20),
    )(sg, ag, ah, tot, n_in, n_out, e_in, e_out)

def small_finish_kernel(tot_ref, k1_ref, k2_ref, k3_ref, b1_ref, b2_ref, b3_ref, t1, t2):
    torso_out(tot_ref, k1_ref, k2_ref, k3_ref, b1_ref, b2_ref, b3_ref, t1, t2)

def small_finish(tot):
    sds = lambda *s: jax.ShapeDtypeStruct(s, F32)
    return pl.pallas_call(
        small_finish_kernel, in_specs=[VMEM], out_specs=[VMEM] * 6,
        out_shape=[sds(4, 8, 8, 32), sds(32, 4, 4, 64), sds(3, 3, 64, 64), sds(1, 32), sds(1, 64), sds(1, 64)],
        scratch_shapes=[pltpu.VMEM((128, 128), F32), pltpu.VMEM((128, 128), F32)],
    )(tot)

def exchange(parts):
    groups = lax.axis_size("group")
    p, g = lax.axis_index("pair"), lax.axis_index("group")
    got = []
    for k in range(groups):
        to = (g + k) % groups
        mine = parts(0, to)
        if k:
            mine = lax.ppermute(mine, ("pair", "group"), [(i, (i + k) % groups) for i in range(groups)])
        theirs = lax.ppermute(parts(1, to), ("pair", "group"), [(i, groups + (i + k) % groups) for i in range(groups)])
        got.append(jnp.where(p == 0, mine, theirs))
    return got

HIGH = lax.Precision.HIGH

def local(states, actions, proj_lower, proj_upper, proj_weight, first_kernel, first_bias, second_kernel, second_bias,
          third_kernel, third_bias, hidden_mean, hidden_sigma, hidden_bias_mean, hidden_bias_sigma, head_mean, head_sigma,
          head_bias_mean, head_bias_sigma, hidden_noise_in, hidden_noise_out, head_noise_in, head_noise_out):
    pair = lax.axis_index("pair")
    groups = lax.axis_size("group")
    shards = 2 * groups
    net = int(groups == 2 and lax.axis_size("rep") == 8)
    n_in, n_out, e_in, e_out = hidden_noise_in[0], hidden_noise_out[0], head_noise_in[0], head_noise_out[0]
    own_noise = (n_in, n_out, e_in, e_out[None])
    feat_q, hid_q = 3136 // shards, 512 // shards
    shard = pair * groups + lax.axis_index("group")
    def of_shard(noise):
        on_in, on_out, on_ein, on_eout = noise
        return (lax.dynamic_slice_in_dim(on_in, shard * feat_q, feat_q, axis=1), on_out, lax.dynamic_slice_in_dim(on_ein, shard * hid_q, hid_q, axis=1), on_eout)

    x = jnp.transpose(states[0], (2, 3, 1, 0)).reshape(84, 336, 128)
    fw1, fw2, fw3, bw1, bw2, bw3, c1, c2, c3 = prepare(first_kernel[0], second_kernel[0], third_kernel[0], first_bias, second_bias, third_bias)
    e_out = e_out[None]
    e_rows = jnp.where(jnp.arange(OUTS)[:, None] < ATOMS, e_in[0:1], e_in[1:2])
    wo = jnp.pad(head_mean[0].T + head_sigma[0].T * (e_rows * e_out.T), ((0, OUTP - OUTS), (0, 0)))
    nin = jnp.transpose(n_in.reshape(2, STEPS, 3136 // STEPS), (1, 0, 2))
    pre1, pre2, pre3, feats = forward(x, fw1, fw2, fw3, c1, c2, c3)
    h, hid, logp, dist, *f12 = hidden(net, feats, hidden_mean[0], hidden_sigma[0], nin, n_out, hidden_bias_mean[0], hidden_bias_sigma[0], wo, head_bias_mean, head_bias_sigma, e_out, actions, proj_lower.T, proj_weight.T)
    back = (logp, h, hidden_mean[0], hidden_sigma[0], nin, n_out, wo, actions)
    if net:
        target, *f12 = f12
        f1, f2 = f12[:3], f12[3:]
        df, small_b, f2c, g1, d1, z1, g2, d2, z2, d3, *noise = hidden_bwd(net, target, *back, f1[2], hid, *own_noise)
        part_r, part_q = wide_grads(*f1, *f2, f2c, d1, d2, d3, g1, g2, z1, z2)
        total, grad_rows, ag, ah, _, _ = backward(net, x, pre1, pre2, pre3, df, bw1, bw2, bw3, part_r, part_q, small_b)
        (hidden_grad, hidden_sigma_grad, head_t, head_sigma_t, gk1, gk2, gk3, gb1, gb2, gb3, hb_grad, hbs_grad, bo_grad, bos_grad,
         loss, grad_rows) = finish(grad_rows, ag, ah, total, *of_shard(noise))
    else:
        df, small_b, msg, dz = hidden_bwd(net, lax.ppermute(dist, "pair", [(1, 0)]), *back)
        f_got = exchange(lambda p, g: lax.dynamic_slice_in_dim(feats, (p * groups + g) * feat_q, feat_q, axis=0))
        hid = jnp.transpose(hid, (3, 0, 2, 1, 4, 5)).reshape(1024, 128).T
        hid_got = exchange(lambda p, g: lax.dynamic_slice_in_dim(hid.reshape(128, 2, 512), (p * groups + g) * hid_q, hid_q, axis=2))
        dpre = jnp.transpose(msg.reshape(2, 2, 2, 128, 128), (3, 1, 0, 2, 4)).reshape(128, 1024)
        d_all = jnp.concatenate(exchange(lambda p, g: jnp.concatenate([dpre, dz.T, jnp.zeros((128, 72), F32)], axis=1)), axis=0)
        f_all = jnp.concatenate(f_got, axis=1)
        hid_all = jnp.concatenate(hid_got, axis=0)
        part_hidden = jnp.einsum("fb,bsh->sfh", f_all, d_all[:, :1024].reshape(-1, 2, 512), precision=HIGH)
        dz_all = d_all[:, 1024:1024 + ATOMS]
        picked = d_all[:, 1024 + ATOMS]
        mask = jnp.where(picked[None, :] == jnp.arange(ACTIONS, dtype=F32)[:, None], 1.0 - 1.0 / ACTIONS, -1.0 / ACTIONS)
        da = (mask[:, None, :] * dz_all.T[None]).reshape(ACTIONS * ATOMS, -1)
        part_head = jnp.concatenate([jnp.dot(dz_all.T, hid_all[:, 0], precision=HIGH), jnp.dot(da, hid_all[:, 1], precision=HIGH)], axis=0)
        hidden_grad, head_t = lax.psum((part_hidden, part_head), "rep")
        small_d, lo, up = backward(net, x, pre1, pre2, pre3, df, bw1, bw2, bw3)
        grad_rows = jnp.where(pair == 0, lo, lax.ppermute(up, "pair", [(0, 1)]))
        total = lax.psum(small_d + jnp.pad(small_b, ((0, ROWS - 24), (0, 0))), ("pair", "group", "rep"))
        in_q, on_out, e_q, on_eout = of_shard([jnp.where(pair == 0, mine, lax.ppermute(mine, "pair", [(0, 1)])) for mine in own_noise])
        hidden_sigma_grad = hidden_grad * (in_q[:, :, None] * on_out[:, None, :])
        head_sigma_t = head_t * (jnp.where(jnp.arange(OUTS)[:, None] < ATOMS, e_q[0:1], e_q[1:2]) * on_eout.T)
        gk1, gk2, gk3, gb1, gb2, gb3 = small_finish(total)
        hb_grad = total[0:8].reshape(2, 512)
        bo_grad = total[8:16].reshape(1, -1)[:, :OUTS]
        hbs_grad, bos_grad = hb_grad * on_out, bo_grad * on_eout
        loss = total[16:17]
    states_grad = jnp.transpose(grad_rows.reshape(84, 84, 2, 128), (3, 2, 0, 1))
    return (loss[0, 0], states_grad, jnp.transpose(gk1, (3, 0, 1, 2)), gb1[0], jnp.transpose(gk2, (3, 0, 1, 2)), gb2[0], jnp.transpose(gk3, (2, 3, 0, 1)), gb3[0],
            hidden_grad, hidden_sigma_grad, hb_grad, hbs_grad, head_t.T, head_sigma_t.T, bo_grad[0], bos_grad[0])


def solution(mesh):
    placed = (
        P("pair", ("group", "rep"), None, None, None),
        P("pair", ("group", "rep")),
        P(("group", "rep"), None),
        P(("group", "rep"), None),
        P(("group", "rep"), None),
        P("pair", None, None, None, None),
        P("pair", None),
        P("pair", None, None, None, None),
        P("pair", None),
        P("pair", None, None, None, None),
        P("pair", None),
        P("pair", None, None, None),
        P("pair", None, None, None),
        P("pair", None, None),
        P("pair", None, None),
        P("pair", None, None),
        P("pair", None, None),
        P("pair", None),
        P("pair", None),
        P("pair", None, None),
        P("pair", None, None),
        P("pair", None, None),
        P("pair", None),
    )
    return jax.shard_map(
        local,
        mesh=mesh,
        in_specs=placed,
        out_specs=(
            P(),
            P(("group", "rep"), "pair", None, None),
            P(),
            P(),
            P(),
            P(),
            P(),
            P(),
            P(None, ("pair", "group"), None),
            P(None, ("pair", "group"), None),
            P(),
            P(),
            P(("pair", "group"), None),
            P(("pair", "group"), None),
            P(),
            P(),
        ),
        check_vma=False,
    )
```
